32 devices in a mesh: dp: 4 (over y, x), blk: 8 (over z, core).
Axes of the slice: x: 2, y: 2, z: 4, core: 2. Of those that a mesh axis runs over, the one named last changes fastest.
Arguments:
- tokens: bfloat16 [32, 64, 64, 320], P('dp', 'blk'), may hold values from -6 to 6
- mask: int32 [32, 64, 64], P('dp', 'blk'), may hold values from 0 to 1, as said below
- labels: int32 [32, 64, 64], P('dp', 'blk'), may hold values from 0 to 18
- predicted: int32 [32, 64, 64], P('dp', 'blk'), may hold values from 0 to 18
- cotangent: bfloat16 [32, 64, 64, 320], P('dp', 'blk'), may hold values from -6 to 6
- norm1_gain: float32 [320], replicated, may hold values from 0.1 to 1.9
- norm1_bias: float32 [320], replicated, may hold values from -3 to 3
- query_weight: bfloat16 [320, 320], replicated, may hold values from -0.3125 to 0.3125
- query_bias: float32 [320], replicated, may hold values from -3 to 3
- reduce_weight: bfloat16 [1280, 320], replicated, may hold values from -0.15625 to 0.15625
- reduce_bias: float32 [320], replicated, may hold values from -3 to 3
- rnorm_gain: float32 [320], replicated, may hold values from 0.1 to 1.9
- rnorm_bias: float32 [320], replicated, may hold values from -3 to 3
- kv_weight: bfloat16 [320, 640], replicated, may hold values from -0.3125 to 0.3125
- value_bias: float32 [320], replicated, may hold values from -3 to 3
- proj_weight: bfloat16 [320, 320], replicated, may hold values from -6 to 6
- proj_bias: float32 [320], replicated, may hold values from -3 to 3
- norm2_gain: float32 [320], replicated, may hold values from 0.1 to 1.9
- norm2_bias: float32 [320], replicated, may hold values from -3 to 3
- expand_weight: bfloat16 [320, 1280], replicated, may hold values from -0.3125 to 0.3125
- expand_bias: float32 [1280], replicated, may hold values from -3 to 3
- depth_weight: float32 [9, 1280], replicated, may hold values from -2 to 2
- depth_bias: float32 [1280], replicated, may hold values from -3 to 3
- shrink_weight: bfloat16 [1280, 320], replicated, may hold values from -0.15625 to 0.15625
- shrink_bias: float32 [320], replicated, may hold values from -3 to 3
Outputs:
- output: bfloat16 [32, 64, 64, 320], P('dp', 'blk')
- input_grad: float32 [32, 64, 64, 320], P('dp', 'blk')
- norm1_gain_grad: float32 [320], replicated
- norm1_bias_grad: float32 [320], replicated
- query_weight_grad: float32 [320, 320], replicated
- query_bias_grad: float32 [320], replicated
- reduce_weight_grad: float32 [1280, 320], replicated
- reduce_bias_grad: float32 [320], replicated
- rnorm_gain_grad: float32 [320], replicated
- rnorm_bias_grad: float32 [320], replicated
- kv_weight_grad: float32 [320, 640], replicated
- value_bias_grad: float32 [320], replicated
- proj_weight_grad: float32 [320, 320], replicated
- proj_bias_grad: float32 [320], replicated
- norm2_gain_grad: float32 [320], replicated
- norm2_bias_grad: float32 [320], replicated
- expand_weight_grad: float32 [320, 1280], replicated
- expand_bias_grad: float32 [1280], replicated
- depth_weight_grad: float32 [9, 1280], replicated
- depth_bias_grad: float32 [1280], replicated
- shrink_weight_grad: float32 [1280, 320], replicated
- shrink_bias_grad: float32 [320], replicated
- confusion: int32 [19, 19], replicated
The draws below stay inside these ranges and needn't reach their ends.
Inputs may be any that keep to these rules, and one draw needn't show every extreme that they name: `mask`: in every scene the 1s fill a rectangle at the top left: the first rows, from 32 to 48 of them, and in these rows the first columns, from 32 to 63 of them; all other entries are 0.
All inputs are finite; a program needn't handle non-finite values.
Results may differ from the reference program's by a relative error of at most 0.018.
Values may be sent and summed in bfloat16 or wider, within the bound.
A program may use at most 448 MiB of HBM per device.

```python
import jax
import jax.numpy as jnp
from jax import lax

C = 320
HEADS = 5
FF = 1280
H = 64
W = 64
CLASSES = 19
SCENES = 32


def draw_mask(key, part):
    key = jax.random.fold_in(key, 11)
    row_key, col_key = jax.random.split(key)
    row_bounds = jax.random.randint(row_key, (SCENES,), H // 2, 3 * H // 4 + 1)
    col_bounds = jax.random.randint(col_key, (SCENES,), W // 2, W)
    rows = jnp.arange(H, dtype=jnp.int32)
    columns = jnp.arange(W, dtype=jnp.int32)
    inside_rows = rows[None, :, None] < row_bounds[:, None, None]
    inside_cols = columns[None, None, :] < col_bounds[:, None, None]
    return jnp.logical_and(inside_rows, inside_cols).astype(jnp.int32)


def place_ends(entries, stream_key, least, top_value):
    shape = entries.shape
    index_at = [jax.random.randint(jax.random.fold_in(stream_key, axis), (), 0, shape[axis]) for axis in range(len(shape))]
    entries = entries.at[tuple(index_at)].set(least)
    longest = shape.index(max(shape))
    index_at[longest] = (index_at[longest] + 1) % shape[longest]
    return entries.at[tuple(index_at)].set(top_value)


def block_scale(key, extent, cuts, low, top_value):
    level, own = 1.0, jax.random.fold_in(key, 6)
    for position, parts in cuts:
        heights = jnp.exp(jax.random.uniform(jax.random.fold_in(own, position), (parts,), jnp.float32, low / len(cuts), top_value / len(cuts)))
        level = level * jnp.repeat(heights, extent[position] // parts).reshape([-1 if axis == position else 1 for axis in range(len(extent))])
    return level


def noise(rng, extent, scale, limit, cuts=(), kind=jnp.bfloat16):
    factor_of = block_scale(rng, extent, cuts, -0.22, 0.18) if cuts else 1.0
    values = jax.random.normal(rng, extent, jnp.float32) * scale * factor_of
    return jnp.minimum(jnp.maximum(values, -limit), limit).astype(kind)


def setup_inputs(seed: int = 0) -> dict:
    seeds = jax.random.split(jax.random.key(seed), 26)
    tokens = noise(seeds[0], (SCENES, H, W, C), 1.0, 6.0, ((0, 4), (1, 8)))
    mask = draw_mask(jax.random.fold_in(seeds[25], 71), 0)
    labels = place_ends(jax.random.randint(seeds[2], (SCENES, H, W), 0, CLASSES), jax.random.fold_in(seeds[2], 1), 0, CLASSES - 1).astype(jnp.int32)
    predicted = place_ends(jax.random.randint(seeds[3], (SCENES, H, W), 0, CLASSES), jax.random.fold_in(seeds[3], 1), 0, CLASSES - 1).astype(jnp.int32)
    cotangent = noise(seeds[4], (SCENES, H, W, C), 1.0, 6.0, ((0, 4), (1, 8)))
    norm1_gain = jnp.clip(1.0 + 0.18 * jax.random.normal(seeds[5], (C,), jnp.float32), 0.1, 1.9)
    norm1_bias = noise(seeds[6], (C,), 0.5, 3.0, (), jnp.float32)
    query_weight = noise(seeds[7], (C, C), C ** -0.5, 0.3125)
    query_bias = noise(seeds[8], (C,), 0.5, 3.0, (), jnp.float32)
    reduce_weight = noise(seeds[9], (4 * C, C), (4 * C) ** -0.5, 0.15625)
    reduce_bias = noise(seeds[10], (C,), 0.5, 3.0, (), jnp.float32)
    rnorm_gain = jnp.clip(1.0 + 0.18 * jax.random.normal(seeds[11], (C,), jnp.float32), 0.1, 1.9)
    rnorm_bias = noise(seeds[12], (C,), 0.5, 3.0, (), jnp.float32)
    kv_weight = noise(seeds[13], (C, 2 * C), C ** -0.5, 0.3125)
    value_bias = noise(seeds[14], (C,), 0.5, 3.0, (), jnp.float32)
    proj_weight = noise(seeds[15], (C, C), (max(C // 256, 1)) ** -0.5, 6.0)
    proj_bias = noise(seeds[16], (C,), 0.5, 3.0, (), jnp.float32)
    norm2_gain = jnp.clip(1.0 + 0.18 * jax.random.normal(seeds[17], (C,), jnp.float32), 0.1, 1.9)
    norm2_bias = noise(seeds[18], (C,), 0.5, 3.0, (), jnp.float32)
    expand_weight = noise(seeds[19], (C, FF), C ** -0.5, 0.3125)
    expand_bias = noise(seeds[20], (FF,), 0.5, 3.0, (), jnp.float32)
    depth_weight = noise(seeds[21], (9, FF), 9 ** -0.5, 2.0, (), jnp.float32)
    depth_bias = noise(seeds[22], (FF,), 0.5, 3.0, (), jnp.float32)
    shrink_weight = noise(seeds[23], (FF, C), FF ** -0.5, 0.15625)
    shrink_bias = noise(seeds[24], (C,), 0.5, 3.0, (), jnp.float32)
    return {"tokens": tokens, "mask": mask, "labels": labels, "predicted": predicted, "cotangent": cotangent, "norm1_gain": norm1_gain, "norm1_bias": norm1_bias, "query_weight": query_weight, "query_bias": query_bias, "reduce_weight": reduce_weight, "reduce_bias": reduce_bias, "rnorm_gain": rnorm_gain, "rnorm_bias": rnorm_bias, "kv_weight": kv_weight, "value_bias": value_bias, "proj_weight": proj_weight, "proj_bias": proj_bias, "norm2_gain": norm2_gain, "norm2_bias": norm2_bias, "expand_weight": expand_weight, "expand_bias": expand_bias, "depth_weight": depth_weight, "depth_bias": depth_bias, "shrink_weight": shrink_weight, "shrink_bias": shrink_bias}


EPSILON = 1e-06
NEGATIVE = -32768.0
HIGHEST = lax.Precision.HIGHEST

@jax.custom_vjp
def low(v):
    return lax.optimization_barrier(v.astype(jnp.bfloat16)).astype(jnp.float32)

@jax.custom_vjp
def low_back(v):
    return v

def low_keep(v):
    return (low(v), None)

def low_pass(kept, grad):
    return (grad,)

def back_keep(v):
    return (v, None)

def back_low(kept, grad):
    return (low(grad),)
low.defvjp(low_keep, low_pass)
low_back.defvjp(back_keep, back_low)

def layer_norm(value, gain, shift):
    center = value - lax.optimization_barrier(jnp.mean(value, -1, keepdims=True))
    spread = lax.optimization_barrier(jnp.mean(center * center, -1, keepdims=True))
    return center * lax.rsqrt(spread + EPSILON) * gain + shift

def depthwise(hidden, taps):
    height, width = (hidden.shape[0], hidden.shape[1])
    padded = jnp.pad(hidden, ((1, 1), (1, 1), (0, 0)))
    total = jnp.zeros(hidden.shape, jnp.float32)
    for index in range(9):
        total = total + taps[index] * padded[index // 3:index // 3 + height, index % 3:index % 3 + width]
    return total

def key_bias(mask):
    scenes, height, width = mask.shape
    grid = lax.optimization_barrier(jnp.sum(mask.reshape(scenes, height // 2, 2, width // 2, 2), axis=(2, 4)))
    return jnp.where(grid > 0, jnp.float32(0.0), jnp.float32(NEGATIVE)).reshape(scenes, -1)

def scene_block(scene, keybias, params):
    norm1_gain, norm1_bias, query_weight, query_bias, reduce_weight, reduce_bias, rnorm_gain, rnorm_bias, kv_weight, value_bias, proj_weight, proj_bias, norm2_gain, norm2_bias, expand_weight, expand_bias, depth_weight, depth_bias, shrink_weight, shrink_bias = params
    height, width, channels = scene.shape
    head_size = channels // HEADS
    scale = head_size ** (-0.5)
    flat = scene.reshape(height * width, channels)
    normed = low(layer_norm(flat, norm1_gain, norm1_bias))
    query = low(low_back(jnp.dot(normed, query_weight, precision=HIGHEST) + query_bias))
    patches = normed.reshape(height // 2, 2, width // 2, 2, channels).transpose(0, 2, 1, 3, 4)
    patches = patches.reshape(height * width // 4, 4 * channels)
    reduced = low_back(jnp.dot(patches, reduce_weight, precision=HIGHEST) + reduce_bias)
    rnormed = low(layer_norm(reduced, rnorm_gain, rnorm_bias))
    offsets = jnp.concatenate([jnp.zeros_like(value_bias), value_bias])
    keyval = low(low_back(jnp.dot(rnormed, kv_weight, precision=HIGHEST) + offsets))
    query_heads = query.reshape(-1, HEADS, head_size)
    key_heads = keyval[:, :channels].reshape(-1, HEADS, head_size)
    value_heads = keyval[:, channels:].reshape(-1, HEADS, head_size)
    scores = jnp.einsum('qhd,khd->hqk', query_heads, key_heads, precision=HIGHEST) * scale + keybias
    scores = low_back(scores)
    powers = jnp.exp(scores - lax.optimization_barrier(jnp.max(scores, -1, keepdims=True)))
    weights = powers / lax.optimization_barrier(jnp.sum(powers, -1, keepdims=True))
    attended = jnp.einsum('hqk,khd->qhd', low(weights), value_heads, precision=HIGHEST)
    attended = low(low_back(attended.reshape(height * width, channels)))
    branch = low_back(jnp.dot(attended, proj_weight, precision=HIGHEST) + proj_bias)
    resid = flat + branch
    cnormed = low(layer_norm(resid, norm2_gain, norm2_bias))
    hidden = low(low_back(jnp.dot(cnormed, expand_weight, precision=HIGHEST) + expand_bias))
    mixed = low_back(depthwise(hidden.reshape(height, width, -1), depth_weight) + depth_bias)
    active = low(jax.nn.gelu(mixed, approximate=False)).reshape(height * width, -1)
    result = resid + jnp.dot(active, shrink_weight, precision=HIGHEST) + shrink_bias
    return result.reshape(height, width, channels)

def reference(tokens, mask, labels, predicted, cotangent, norm1_gain, norm1_bias, query_weight, query_bias, reduce_weight, reduce_bias, rnorm_gain, rnorm_bias, kv_weight, value_bias, proj_weight, proj_bias, norm2_gain, norm2_bias, expand_weight, expand_bias, depth_weight, depth_bias, shrink_weight, shrink_bias):
    params = tuple((item.astype(jnp.float32) for item in (norm1_gain, norm1_bias, query_weight, query_bias, reduce_weight, reduce_bias, rnorm_gain, rnorm_bias, kv_weight, value_bias, proj_weight, proj_bias, norm2_gain, norm2_bias, expand_weight, expand_bias, depth_weight, depth_bias, shrink_weight, shrink_bias)))
    keybias = key_bias(mask)

    def forward(inputs, *weights):

        def one_scene(pair):
            return scene_block(pair[0], pair[1], weights)
        return lax.map(jax.checkpoint(one_scene), (inputs, keybias))
    result, pullback = jax.vjp(forward, tokens.astype(jnp.float32), *params)
    grads = pullback(cotangent.astype(jnp.float32))
    codes = (labels.reshape(-1) * CLASSES + predicted.reshape(-1)).astype(jnp.int32)
    counted = jax.ops.segment_sum(mask.reshape(-1).astype(jnp.int32), codes, num_segments=CLASSES * CLASSES)
    confusion = counted.astype(jnp.int32).reshape(CLASSES, CLASSES)
    return (result.astype(jnp.bfloat16), grads[0], grads[1], grads[2], grads[3], grads[4], grads[5], grads[6], grads[7], grads[8], grads[9], grads[10], grads[11], grads[12], grads[13], grads[14], grads[15], grads[16], grads[17], grads[18], grads[19], grads[20], confusion)
```

```python
import functools

import jax
import jax.numpy as jnp
from jax import lax
from jax.experimental import pallas as pl
from jax.experimental.pallas import tpu as pltpu
from jax.sharding import PartitionSpec as P
import ml_dtypes
import numpy as np

HEADS = 5
CLASSES = 19
EPSILON = 1e-06
NEGATIVE = -32768.0
LOG2E = 1.4426950408889634
LN2 = 0.6931471805599453
F32 = jnp.float32
BF16 = jnp.bfloat16
LANE = 128
HALF = 64
KEY_CHUNK = 256
MASK_ROWS = 48
VMEM = 62 * 2**20
FF_CHUNK = 256


def up_to(value, step):
    return -(-value // step) * step


def dot(a, b):
    return lax.dot_general(a, b, (((1,), (0,)), ((), ())), preferred_element_type=F32)


def dot_nt(a, b):
    return lax.dot_general(a, b, (((1,), (1,)), ((), ())), preferred_element_type=F32)


def dot_tn(a, b):
    return lax.dot_general(a, b, (((0,), (0,)), ((), ())), preferred_element_type=F32)


def lanes(shape):
    return lax.broadcasted_iota(jnp.int32, shape, len(shape) - 1)


def whole(shape):
    return pl.BlockSpec(shape, lambda *_: (0,) * len(shape))


def per_scene(shape):
    return pl.BlockSpec((1,) + shape, lambda s: (s,) + (0,) * len(shape))


def centered(value, channels):
    mean = jnp.sum(value, -1, keepdims=True) * (1.0 / channels)
    center = jnp.where(lanes(value.shape) < channels, value - mean, 0.0)
    var = jnp.sum(center * center, -1, keepdims=True) * (1.0 / channels)
    rstd = lax.rsqrt(var + EPSILON)
    return center * rstd, rstd


def norm_back(up, gain, xhat, rstd, channels):
    u = up * gain
    mean = jnp.sum(u, -1, keepdims=True) * (1.0 / channels)
    proj = jnp.sum(u * xhat, -1, keepdims=True) * (1.0 / channels)
    return (u - mean - xhat * proj) * rstd


def ext_lane(head):
    return HALF if head % 2 == 0 else 0


def widen(value, width):
    pad = width - value.shape[-1]
    return jnp.concatenate([value, jnp.zeros(value.shape[:-1] + (pad,), value.dtype)], -1)


def place(blk):
    me = lax.axis_index("blk")
    core = lax.rem(me, 2)
    chip = me // 2
    return chip, core, {"blk": me + 2}, {"blk": me - 2}, {"blk": me + 1 - 2 * core}


def greet(chip, chips, up, down, sib):
    barrier = pltpu.get_barrier_semaphore()
    MESH = pl.DeviceIdType.MESH
    has_up, has_down = chip < chips - 1, chip > 0
    pl.semaphore_signal(barrier, inc=1, device_id=sib, device_id_type=MESH)

    @pl.when(has_up)
    def _():
        pl.semaphore_signal(barrier, inc=1, device_id=up, device_id_type=MESH)

    @pl.when(has_down)
    def _():
        pl.semaphore_signal(barrier, inc=1, device_id=down, device_id_type=MESH)

    pl.semaphore_wait(barrier, 1 + has_up.astype(jnp.int32) + has_down.astype(jnp.int32))


def remote(src, dst, send, recv, device):
    return pltpu.make_async_remote_copy(
        src_ref=src, dst_ref=dst, send_sem=send, recv_sem=recv, device_id=device,
        device_id_type=pl.DeviceIdType.MESH,
    )


def attend_kernel(
    dims, blk, used, tok_ref, mask_ref, label_ref, pred_ref, tok2_ref, vec_ref, wr_ref, wq_ref,
    one_ref, wk_ref, wv_ref, wp_ref,
    red_ref, cnt_ref, q_ref, att_ref, ke_ref, ve_ref, rn_ref, res_ref,
    scr, qbuf, oe, rnbuf, up_send, down_send, sib_send, line_recv, sib_recv,
):
    scenes, height, width, channels, cp = dims
    n = height * width
    keys = n // 4
    chips = blk // 2
    lag = chips
    step = pl.program_id(0)
    head_size = channels // HEADS
    chip, core, up, down, sib = place(blk)

    @pl.when(step == 0)
    def _():
        greet(chip, chips, up, down, sib)
        cnt_ref[...] = jnp.zeros(cnt_ref.shape, F32)

    def slot(origin, c):
        return c * used + origin

    def send_up(s, origin):
        place_ = rnbuf.at[s, slot(origin, core)]
        return remote(place_, place_, up_send.at[s, origin], line_recv.at[s, origin], up)

    def send_down(s, origin):
        place_ = rnbuf.at[s, slot(origin, core)]
        return remote(place_, place_, down_send.at[s, origin], line_recv.at[s, origin], down)

    def send_sib(s, origin):
        place_ = rnbuf.at[s, slot(origin, core)]
        return remote(place_, place_, sib_send.at[s, origin], sib_recv.at[s, origin], sib)

    @pl.when(step < scenes)
    def _():
        s = step
        x = widen(tok_ref[0].astype(F32), cp)
        xhat, _ = centered(x, channels)
        low = (xhat * vec_ref[0:1] + vec_ref[1:2]).astype(BF16)
        lowf = low.astype(F32)
        for t in range(cp // LANE):
            scr[t] = lowf[:, t * LANE : (t + 1) * LANE]
        total = jnp.zeros((keys, cp), F32)
        for b in range(2):
            part = [scr[t, pl.ds(b, n // 2, stride=2), :] for t in range(cp // LANE)]
            part = jnp.concatenate(part, -1).reshape(height // 2, 2, width // 2, cp)
            for a in range(2):
                total = total + dot(part[:, a].reshape(keys, cp).astype(BF16), wr_ref[2 * a + b])
        red_ref[0] = total
        rhat, _ = centered(total, channels)
        m = mask_ref[0].astype(F32)
        shape = (width // 2, width)
        near = lanes(shape) // 2 == lax.broadcasted_iota(jnp.int32, shape, 0)
        flags = []
        for i in range(height // 2):
            both = m[2 * i : 2 * i + 1] + m[2 * i + 1 : 2 * i + 2]
            flags.append(jnp.sum(jnp.where(near, both, 0.0), -1, keepdims=True))
        unc = jnp.where(jnp.concatenate(flags, 0) > 0.0, 0.0, 1.0)
        flag = jnp.where(lanes((keys, cp)) == channels, unc, 0.0)
        own = (rhat * vec_ref[2:3] + vec_ref[3:4] + flag).astype(BF16)

        @pl.when(chip < used)
        def _():
            rnbuf[s, slot(chip, core)] = own
            send_sib(s, chip).start()

            @pl.when(chip < chips - 1)
            def _():
                send_up(s, chip).start()

            @pl.when(chip > 0)
            def _():
                send_down(s, chip).start()

        qf = dot(low, wq_ref[...]) * (LOG2E * head_size**-0.5) + one_ref[...]
        qbuf[lax.rem(s, lag + 1)] = qf.astype(BF16)
        shape = (cnt_ref.shape[0], width)
        classes = lax.broadcasted_iota(jnp.int32, shape, 0)
        wide = lax.broadcasted_iota(jnp.int32, (LANE, width), 0)
        total = jnp.zeros(cnt_ref.shape, F32)
        for r in range(height):
            label = jnp.where(mask_ref[0, r : r + 1] > 0, label_ref[0, r : r + 1], -1)
            hot = jnp.where(label == classes, 1.0, 0.0).astype(BF16)
            pred = jnp.where(pred_ref[0, r : r + 1] == wide, 1.0, 0.0).astype(BF16)
            total = total + dot_nt(hot, pred)
        cnt_ref[...] += total

    for age in range(1, chips):
        s = step - age

        @pl.when(jnp.logical_and(s >= 0, s < scenes))
        def _(s=s, age=age):
            below = chip - age

            @pl.when(jnp.logical_and(below >= 0, below < used))
            def _():
                send_up(s, below).wait_recv()
                send_sib(s, below).start()

                @pl.when(chip < chips - 1)
                def _():
                    send_up(s, below).start()

            above = chip + age

            @pl.when(above < used)
            def _():
                send_down(s, above).wait_recv()
                send_sib(s, above).start()

                @pl.when(chip > 0)
                def _():
                    send_down(s, above).start()

    @pl.when(step >= lag)
    def _():
        s = step - lag

        for origin in range(used):
            send_sib(s, origin).wait_recv()

        rn_all = rnbuf[s].reshape(2 * used * keys, cp)
        rn_ref[0] = rn_all
        ke_ref[0] = dot(rn_all, wk_ref[...]).astype(BF16)
        ve_ref[0] = dot(rn_all, wv_ref[...]).astype(BF16)
        mine = lax.rem(s, lag + 1)
        count = 2 * used * keys // KEY_CHUNK
        for h in range(HEADS):
            block = slice(h * LANE, (h + 1) * LANE)
            e = ext_lane(h)
            q = qbuf[mine, :, block]
            parts = [
                dot_nt(q, ke_ref[0, j * KEY_CHUNK : (j + 1) * KEY_CHUNK, block])
                for j in range(count)
            ]
            top = functools.reduce(jnp.maximum, parts)
            top = jnp.max(top, -1, keepdims=True)
            out = jnp.zeros((n, LANE), F32)
            for j in range(count):
                p = jnp.exp2(parts[j] - top).astype(BF16)
                out = out + dot(p, ve_ref[0, j * KEY_CHUNK : (j + 1) * KEY_CHUNK, block])
            total = out[:, e : e + 1]
            oe[h] = out / total
            lse = top + jnp.log2(total)
            hi = lse.astype(BF16).astype(F32)
            mid = (lse - hi).astype(BF16).astype(F32)
            lo = lse - hi - mid
            lane = lanes((n, LANE))
            q2 = q.astype(F32)
            q2 = jnp.where(lane == e + 3, -hi, q2)
            q2 = jnp.where(lane == e + 4, -mid, q2)
            q2 = jnp.where(lane == e + 5, -lo, q2)
            q_ref[0, :, block] = q2.astype(BF16)

        tiles = []
        low_half = lanes((n, LANE)) < HALF
        for t in range(cp // LANE):
            other = oe[2 * t + 1] if 2 * t + 1 < HEADS else jnp.zeros((n, LANE), F32)
            tiles.append(jnp.where(low_half, oe[2 * t], other))
        att = jnp.concatenate(tiles, -1)
        att_ref[0] = att
        x = widen(tok2_ref[0].astype(F32), cp)
        resid = x + dot(att.astype(BF16), wp_ref[...]) + vec_ref[4:5]
        for t in range(cp // LANE):
            for r in range(height):
                for half in range(2):
                    base = r * width + half * (width // 2)
                    at = r * scenes * width + half * scenes + s
                    res_ref[t, pl.ds(at, width // 2, stride=2 * scenes), :] = resid[
                        base : base + width // 2, t * LANE : (t + 1) * LANE
                    ]

    @pl.when(step == scenes + lag - 1)
    def _():
        @pl.loop(0, scenes)
        def _(s):
            for origin in range(used):
                send_sib(s, origin).wait_send()

                @pl.when(jnp.logical_and(origin <= chip, chip < chips - 1))
                def _(origin=origin):
                    send_up(s, origin).wait_send()

                @pl.when(jnp.logical_and(origin >= chip, chip > 0))
                def _(origin=origin):
                    send_down(s, origin).wait_send()


def attend(dims, blk, used, cid, tok, mask, labels, predicted, vec, wr, wq, ones, wk, wv, wp):
    scenes, height, width, channels, cp = dims
    n = height * width
    keys = n // 4
    chips = blk // 2
    lag = chips
    k = blk * keys
    live = 2 * used * keys
    he = HEADS * LANE

    def early(shape):
        return pl.BlockSpec(
            (1,) + shape, lambda t: (jnp.minimum(t, scenes - 1),) + (0,) * len(shape)
        )

    def late(shape):
        return pl.BlockSpec((1,) + shape, lambda t: (jnp.maximum(t - lag, 0),) + (0,) * len(shape))

    return pl.pallas_call(
        functools.partial(attend_kernel, dims, blk, used),
        grid=(scenes + lag,),
        in_specs=[early((n, channels))]
        + [early((height, width))] * 3
        + [late((n, channels))]
        + [whole(v.shape) for v in (vec, wr, wq, ones, wk, wv, wp)],
        out_specs=[
            early((keys, cp)),
            whole((32, LANE)),
            late((n, he)),
            late((n, cp)),
            late((live, he)),
            late((live, he)),
            late((live, cp)),
            whole((cp // LANE, scenes * n, LANE)),
        ],
        out_shape=[
            jax.ShapeDtypeStruct((scenes, keys, cp), F32),
            jax.ShapeDtypeStruct((32, LANE), F32),
            jax.ShapeDtypeStruct((scenes, n, he), BF16),
            jax.ShapeDtypeStruct((scenes, n, cp), F32),
            jax.ShapeDtypeStruct((scenes, k, he), BF16),
            jax.ShapeDtypeStruct((scenes, k, he), BF16),
            jax.ShapeDtypeStruct((scenes, k, cp), BF16),
            jax.ShapeDtypeStruct((cp // LANE, scenes * n, LANE), F32),
        ],
        scratch_shapes=[
            pltpu.VMEM((cp // LANE, n, LANE), F32),
            pltpu.VMEM((lag + 1, n, he), BF16),
            pltpu.VMEM((HEADS, n, LANE), F32),
            pltpu.VMEM((scenes, 2 * used, keys, cp), BF16),
        ]
        + [pltpu.SemaphoreType.DMA((scenes, used))] * 5,
        compiler_params=pltpu.CompilerParams(
            vmem_limit_bytes=VMEM, collective_id=cid, has_side_effects=True
        ),
    )(tok, mask, labels, predicted, tok, vec, wr, wq, ones, wk, wv, wp)


def ffn_kernel(
    dims, ff, blk, res_ref, ct_ref, vec_ref, we_ref, ws_ref, taps_ref, tb_ref,
    out_hbm, gres_hbm, dwe_ref, dwst, dtap_ref, dtb_ref, dvec_ref,
    cn, cnt, ctt, ctx, oacc, gacc, hid, gm, halo, tapacc, out_stage, gres_stage,
    out_sem, gres_sem, cn_send, cn_recv, gm_send, gm_recv,
):
    scenes, height, width, channels, cp = dims
    n = height * width
    rw = scenes * width
    lt = cp // LANE
    fc = FF_CHUNK
    nchunk = ff // fc
    cols = width // 2
    pair = 2 * scenes
    me = lax.axis_index("blk")
    has_left = me > 0
    has_right = me < blk - 1
    left, right = {"blk": me - 1}, {"blk": me + 1}
    MESH = pl.DeviceIdType.MESH

    barrier = pltpu.get_barrier_semaphore()

    @pl.when(has_left)
    def _():
        pl.semaphore_signal(barrier, inc=1, device_id=left, device_id_type=MESH)

    @pl.when(has_right)
    def _():
        pl.semaphore_signal(barrier, inc=1, device_id=right, device_id_type=MESH)

    pl.semaphore_wait(barrier, has_left.astype(jnp.int32) + has_right.astype(jnp.int32))

    def row(r, size=rw):
        return pl.ds(pl.multiple_of(r * rw, rw), size)

    g2, b2 = vec_ref[5:6], vec_ref[6:7]

    def load3(ref, r):
        return jnp.concatenate([ref[t, row(r), :] for t in range(lt)], -1)

    def store3(ref, r, value):
        for t in range(lt):
            ref[t, row(r), :] = value[:, t * LANE : (t + 1) * LANE]

    @pl.loop(0, height)
    def _(r):
        x = load3(res_ref, r)
        xhat, _ = centered(x, channels)
        c = (xhat * g2 + b2).astype(BF16)
        cn[row(r + 1), :] = c
        cnt[:, row(r)] = c.T
        store3(oacc, r, x + vec_ref[7:8])

    def cn_copy(up):
        return pltpu.make_async_remote_copy(
            src_ref=cn.at[row(1 if up else height), :],
            dst_ref=cn.at[row(height + 1 if up else 0), :],
            send_sem=cn_send.at[0 if up else 1],
            recv_sem=cn_recv.at[0 if up else 1],
            device_id=left if up else right,
            device_id_type=MESH,
        )

    @pl.when(has_left)
    def _():
        cn_copy(True).start()

    @pl.when(has_right)
    def _():
        cn_copy(False).start()

    @pl.loop(0, scenes)
    def _(s):
        c = widen(ct_ref[s].astype(F32), cp)
        for t in range(lt):
            for r in range(height):
                for half in range(2):
                    base = r * width + half * cols
                    gacc[t, pl.ds(r * rw + half * scenes + s, cols, stride=pair), :] = c[
                        base : base + cols, t * LANE : (t + 1) * LANE
                    ]

    dvec_ref[...] = jnp.zeros(dvec_ref.shape, F32)

    @pl.loop(0, height)
    def _(r):
        c = load3(gacc, r)
        dvec_ref[2:3] += jnp.sum(c, 0, keepdims=True)
        low = c.astype(BF16)
        ctt[row(r), :] = low
        ctx[:, row(r)] = low.T
        store3(gacc, r, jnp.zeros((rw, cp), F32))

    dwe_ref[...] = jnp.zeros(dwe_ref.shape, F32)
    dwst[...] = jnp.zeros(dwst.shape, F32)

    @pl.when(has_left)
    def _():
        cn_copy(False).wait_recv()

    @pl.when(jnp.logical_not(has_left))
    def _():
        cn[row(0), :] = jnp.zeros((rw, cp), BF16)

    @pl.when(has_right)
    def _():
        cn_copy(True).wait_recv()

    @pl.when(jnp.logical_not(has_right))
    def _():
        cn[row(height + 1), :] = jnp.zeros((rw, cp), BF16)

    def put(ref, slot, r, value):
        v = value.reshape(cols, pair, fc)
        z = jnp.zeros((scenes, fc), F32)
        ref[slot, r, 1 : cols + 1] = v.astype(BF16)
        ref[slot, r, 0] = jnp.concatenate([z, v[cols - 1, :scenes]], 0).astype(BF16)
        ref[slot, r, cols + 1] = jnp.concatenate([v[0, scenes:], z], 0).astype(BF16)

    def gm_copy(k, slot, up):
        return pltpu.make_async_remote_copy(
            src_ref=gm.at[slot, 1 if up else height],
            dst_ref=halo.at[k, 1 if up else 0],
            send_sem=gm_send.at[k, 0 if up else 1],
            recv_sem=gm_recv.at[k, 0 if up else 1],
            device_id=left if up else right,
            device_id_type=MESH,
        )

    def phase_a(k, slot):
        span = pl.ds(pl.multiple_of(k * fc, fc), fc)

        @pl.loop(0, height + 2)
        def _(r):
            put(hid, slot, r, dot(cn[row(r), :], we_ref[:, span]))

        @pl.loop(0, height)
        def _(r):
            acc = None
            for a in range(3):
                line = hid[slot, r + a]
                for b in range(3):
                    tap = taps_ref[pl.ds(3 * a + b, 1), span].astype(BF16).reshape(1, 1, fc)
                    term = line[b : b + cols] * tap
                    acc = term if acc is None else acc + term
            mixed = acc.astype(F32).reshape(rw, fc) + tb_ref[:, span]
            phi = 0.5 + 0.5 * lax.erf(mixed * 0.7071067811865476)
            dens = jnp.exp2(mixed * mixed * (-0.5 * LOG2E)) * 0.3989422804014327
            active = (mixed * phi).astype(BF16)
            slope = phi + mixed * dens
            grad = dot(ctt[row(r), :], ws_ref[:, span]) * slope
            put(gm, slot, r + 1, grad)
            dtb_ref[:, span] += jnp.sum(grad.reshape(rw // 8, 8, fc), 0)
            o = dot_nt(active, ws_ref[:, span])
            for t in range(lt):
                oacc[t, row(r), :] += o[:, t * LANE : (t + 1) * LANE]
            dwst[:, span] += dot(ctx[:, row(r)], active)

        @pl.when(has_left)
        def _():
            gm_copy(k, slot, True).start()

        @pl.when(has_right)
        def _():
            gm_copy(k, slot, False).start()

    def phase_b(k, slot):
        span = pl.ds(pl.multiple_of(k * fc, fc), fc)

        @pl.when(has_left)
        def _():
            gm_copy(k, slot, False).wait_recv()
            gm[slot, 0] = halo[k, 0]

        @pl.when(jnp.logical_not(has_left))
        def _():
            gm[slot, 0] = jnp.zeros((cols + 2, pair, fc), BF16)

        @pl.when(has_right)
        def _():
            gm_copy(k, slot, True).wait_recv()
            gm[slot, height + 1] = halo[k, 1]

        @pl.when(jnp.logical_not(has_right))
        def _():
            gm[slot, height + 1] = jnp.zeros((cols + 2, pair, fc), BF16)

        tapacc[...] = jnp.zeros(tapacc.shape, F32)

        @pl.loop(0, height)
        def _(r):
            acc = None
            own = hid[slot, r + 1, 1 : cols + 1]
            for a in range(3):
                line = gm[slot, r + 2 - a]
                for b in range(3):
                    tap = taps_ref[pl.ds(3 * a + b, 1), span].astype(BF16).reshape(1, 1, fc)
                    window = line[2 - b : 2 - b + cols]
                    term = window * tap
                    acc = term if acc is None else acc + term
                    prod = own * window
                    q = cols // 4
                    prod = (prod[:q] + prod[q : 2 * q]) + (prod[2 * q : 3 * q] + prod[3 * q :])
                    tapacc[3 * a + b] += jnp.sum(prod.astype(F32), 0)
            low = acc.reshape(rw, fc)
            dwe_ref[:, span] += dot(cnt[:, row(r)], low)
            g = dot_nt(low, we_ref[:, span])
            for t in range(lt):
                gacc[t, row(r), :] += g[:, t * LANE : (t + 1) * LANE]

        for tap in range(9):
            dtap_ref[pl.ds(tap, 1), span] = jnp.sum(tapacc[tap], 0, keepdims=True)

        @pl.when(has_left)
        def _():
            gm_copy(k, slot, True).wait_send()

        @pl.when(has_right)
        def _():
            gm_copy(k, slot, False).wait_send()

    dtb_ref[...] = jnp.zeros(dtb_ref.shape, F32)

    @pl.loop(0, nchunk + 1)
    def _(k):
        slot = lax.rem(k, 2)

        @pl.when(k < nchunk)
        def _():
            phase_a(k, slot)

        @pl.when(k > 0)
        def _():
            phase_b(k - 1, 1 - slot)

    @pl.when(has_left)
    def _():
        cn_copy(True).wait_send()

    @pl.when(has_right)
    def _():
        cn_copy(False).wait_send()

    @pl.loop(0, height)
    def _(r):
        x = load3(res_ref, r)
        xhat, rstd = centered(x, channels)
        upstream = load3(gacc, r)
        dvec_ref[0:1] += jnp.sum(upstream * xhat, 0, keepdims=True)
        dvec_ref[1:2] += jnp.sum(upstream, 0, keepdims=True)
        g = ctt[row(r), :].astype(F32) + norm_back(upstream, g2, xhat, rstd, channels)
        store3(gacc, r, g)

    def gather(ref, s):
        rows = []
        for r in range(height):
            for half in range(2):
                rows.append(
                    jnp.concatenate(
                        [
                            ref[t, pl.ds(r * rw + half * scenes + s, cols, stride=pair), :]
                            for t in range(lt)
                        ],
                        -1,
                    )
                )
        return jnp.concatenate(rows, 0)[:, :channels]

    def out_copy(s, slot):
        return pltpu.make_async_copy(out_stage.at[slot], out_hbm.at[s], out_sem.at[slot])

    def gres_copy(s, slot):
        return pltpu.make_async_copy(gres_stage.at[slot], gres_hbm.at[s], gres_sem.at[slot])

    @pl.loop(0, scenes)
    def _(s):
        slot = lax.rem(s, 2)

        @pl.when(s >= 2)
        def _():
            out_copy(s - 2, slot).wait()
            gres_copy(s - 2, slot).wait()

        out_stage[slot] = gather(oacc, s).astype(BF16)
        gres_stage[slot] = gather(gacc, s)
        out_copy(s, slot).start()
        gres_copy(s, slot).start()

    for s in range(scenes - 2, scenes):
        out_copy(s, s % 2).wait()
        gres_copy(s, s % 2).wait()


def ffn(dims, blk, res, ct, vec, we, ws, taps, tb):
    scenes, height, width, channels, cp = dims
    n = height * width
    total = scenes * n
    rw = scenes * width
    ff = ws.shape[1]
    lt = cp // LANE
    nchunk = ff // FF_CHUNK
    strip = (width // 2 + 2, 2 * scenes, FF_CHUNK)
    vm = pl.BlockSpec(memory_space=pltpu.VMEM)
    hbm = pl.BlockSpec(memory_space=pl.ANY)
    return pl.pallas_call(
        functools.partial(ffn_kernel, dims, ff, blk),
        in_specs=[vm] * 7,
        out_specs=[hbm, hbm] + [vm] * 5,
        out_shape=[
            jax.ShapeDtypeStruct((scenes, n, channels), BF16),
            jax.ShapeDtypeStruct((scenes, n, channels), F32),
            jax.ShapeDtypeStruct((cp, ff), F32),
            jax.ShapeDtypeStruct((cp, ff), F32),
            jax.ShapeDtypeStruct((9, ff), F32),
            jax.ShapeDtypeStruct((8, ff), F32),
            jax.ShapeDtypeStruct((8, cp), F32),
        ],
        scratch_shapes=[
            pltpu.VMEM((total + 2 * rw, cp), BF16),
            pltpu.VMEM((cp, total), BF16),
            pltpu.VMEM((total, cp), BF16),
            pltpu.VMEM((cp, total), BF16),
            pltpu.VMEM((lt, total, LANE), F32),
            pltpu.VMEM((lt, total, LANE), F32),
            pltpu.VMEM((2, height + 2) + strip, BF16),
            pltpu.VMEM((2, height + 2) + strip, BF16),
            pltpu.VMEM((nchunk, 2) + strip, BF16),
            pltpu.VMEM((9, 2 * scenes, FF_CHUNK), F32),
            pltpu.VMEM((2, n, channels), BF16),
            pltpu.VMEM((2, n, channels), F32),
            pltpu.SemaphoreType.DMA((2,)),
            pltpu.SemaphoreType.DMA((2,)),
            pltpu.SemaphoreType.DMA((2,)),
            pltpu.SemaphoreType.DMA((2,)),
            pltpu.SemaphoreType.DMA((nchunk, 2)),
            pltpu.SemaphoreType.DMA((nchunk, 2)),
        ],
        compiler_params=pltpu.CompilerParams(
            vmem_limit_bytes=VMEM, collective_id=0, has_side_effects=True
        ),
    )(res, ct, vec, we, ws, taps, tb)


def attback_kernel(
    dims, blk, used, q_ref, att_ref, gres_ref, ke_ref, ve_ref, rn_ref, wpe_ref, wkv_ref,
    grn_ref, gqt_ref, dwp_ref, dwkv_ref, dbp_ref,
    ge, dqt, own, acc, sib_land, up_land, down_land,
    sib_send, sib_recv, up_send, up_recv, down_send, down_recv,
):
    scenes, height, width, channels, cp = dims
    n = height * width
    keys = n // 4
    chips = blk // 2
    lt = cp // LANE
    head_size = channels // HEADS
    step = pl.program_id(0)
    chip, core, up, down, sib = place(blk)
    count = 2 * used * keys // KEY_CHUNK

    @pl.when(step == 0)
    def _():
        greet(chip, chips, up, down, sib)
        dwp_ref[...] = jnp.zeros(dwp_ref.shape, F32)
        dwkv_ref[...] = jnp.zeros(dwkv_ref.shape, F32)
        dbp_ref[...] = jnp.zeros(dbp_ref.shape, F32)

    def to_sib(s):
        return remote(
            own.at[lax.rem(s, 2), 1 - core], sib_land.at[s], sib_send.at[s], sib_recv.at[s], sib
        )

    def to_up(s, target):
        return remote(
            acc.at[s, target], up_land.at[s, target], up_send.at[s, target], up_recv.at[s, target], up
        )

    def to_down(s, target):
        return remote(
            acc.at[s, target], down_land.at[s, target], down_send.at[s, target],
            down_recv.at[s, target], down,
        )

    def plus(a, b):
        return (a.astype(F32) + b.astype(F32)).astype(BF16)

    def chunk(j):
        s = step
        per = KEY_CHUNK // keys
        span = slice(j * KEY_CHUNK, (j + 1) * KEY_CHUNK)
        dks, dvs = [], []
        for h in range(HEADS):
            block = slice(h * LANE, (h + 1) * LANE)
            k, v = ke_ref[0, span, block], ve_ref[0, span, block]
            q, g = q_ref[0, :, block], ge[:, block]
            p = jnp.exp2(dot_nt(k, q))
            gs = (p * dot_nt(v, g)).astype(BF16)
            dvs.append(dot(p.astype(BF16), g))
            dks.append(dot(gs, q))
            dqt[block, :] += dot_tn(k, gs)
        low_half = lanes((KEY_CHUNK, LANE)) < HALF
        tiles = []
        for group, scale in ((dks, LN2), (dvs, 1.0)):
            for t in range(lt):
                other = (
                    group[2 * t + 1] if 2 * t + 1 < HEADS else jnp.zeros((KEY_CHUNK, LANE), F32)
                )
                tiles.append((jnp.where(low_half, group[2 * t], other) * scale).astype(BF16))
        gkv = jnp.concatenate(tiles, -1)
        grn = dot_nt(gkv, wkv_ref[...]).astype(BF16)
        for i in range(per):
            at = j * per + i
            own[lax.rem(s, 2), at // used, at % used] = grn[i * keys : (i + 1) * keys]
        dwkv_ref[...] += dot(rn_ref[0, span].T, gkv)

    @pl.when(step < scenes)
    def _():
        s = step
        gb = widen(gres_ref[0], cp).astype(BF16)
        dbp_ref[...] += jnp.sum(gb.astype(F32).reshape(n // 8, 8, cp), 0)
        att = att_ref[0]
        dwp_ref[...] += dot(att.astype(BF16).T, gb)
        gatt = dot_nt(gb, wpe_ref[...])
        lane = lanes((n, LANE))
        for h in range(HEADS):
            e = ext_lane(h)
            g = gatt[:, h * LANE : (h + 1) * LANE].astype(BF16).astype(F32)
            o = att[:, (h // 2) * LANE : (h // 2 + 1) * LANE]
            inner = jnp.sum(g * o, -1, keepdims=True)
            hi = inner.astype(BF16).astype(F32)
            g = jnp.where(lane == e, -hi, g)
            g = jnp.where(lane == e + 1, hi - inner, g)
            ge[:, h * LANE : (h + 1) * LANE] = g.astype(BF16)
        dqt[...] = jnp.zeros(dqt.shape, F32)
        chunk(0)

    s1 = step - 1

    @pl.when(jnp.logical_and(s1 >= 0, s1 < scenes))
    def _():
        to_sib(s1).wait()
        acc[s1] = plus(own[lax.rem(s1, 2), core], sib_land[s1])

    s_up = step - 1 - chip

    @pl.when(jnp.logical_and(s_up >= 0, s_up < scenes))
    def _():
        for target in range(1, used):

            @pl.when(target > chip)
            def _(target=target):
                @pl.when(chip > 0)
                def _():
                    to_up(s_up, target).wait_recv()
                    acc[s_up, target] = plus(acc[s_up, target], up_land[s_up, target])

                to_up(s_up, target).start()

    s_down = step - chips + chip

    @pl.when(jnp.logical_and(s_down >= 0, s_down < scenes))
    def _():
        for target in range(used):

            @pl.when(target < chip)
            def _(target=target):
                @pl.when(chip < chips - 1)
                def _():
                    to_down(s_down, target).wait_recv()
                    acc[s_down, target] = plus(acc[s_down, target], down_land[s_down, target])

                to_down(s_down, target).start()

    s_end = step - chips

    @pl.when(s_end >= 0)
    def _():
        @pl.when(chip < used)
        def _():
            grn_ref[0] = acc[s_end, chip].astype(F32)

            @pl.when(chip > 0)
            def _():
                to_up(s_end, chip).wait_recv()
                grn_ref[0] += up_land[s_end, chip].astype(F32)

            @pl.when(chip < chips - 1)
            def _():
                to_down(s_end, chip).wait_recv()
                grn_ref[0] += down_land[s_end, chip].astype(F32)

        @pl.when(chip >= used)
        def _():
            grn_ref[0] = jnp.zeros((keys, cp), F32)

    @pl.when(step < scenes)
    def _():
        s = step
        for j in range(1, count):
            chunk(j)
        to_sib(s).start()
        for h in range(HEADS):
            base = h * LANE + (0 if h % 2 == 0 else HALF)
            gqt_ref[0, h * HALF : (h + 1) * HALF] = (
                dqt[base : base + HALF, :] * head_size**-0.5
            ).astype(BF16)

    @pl.when(step == scenes + chips - 1)
    def _():
        @pl.loop(0, scenes)
        def _(s):
            for target in range(used):

                @pl.when(target > chip)
                def _(target=target):
                    to_up(s, target).wait_send()

                @pl.when(target < chip)
                def _(target=target):
                    to_down(s, target).wait_send()


def attback(dims, blk, used, cid, q, att, gres, ke, ve, rn, wpe, wkv):
    scenes, height, width, channels, cp = dims
    n = height * width
    keys = n // 4
    chips = blk // 2
    live = 2 * used * keys
    he = HEADS * LANE

    def early(shape):
        return pl.BlockSpec(
            (1,) + shape, lambda t: (jnp.minimum(t, scenes - 1),) + (0,) * len(shape)
        )

    def late(shape):
        return pl.BlockSpec((1,) + shape, lambda t: (jnp.maximum(t - chips, 0),) + (0,) * len(shape))

    land = (scenes, used, keys, cp)
    return pl.pallas_call(
        functools.partial(attback_kernel, dims, blk, used),
        grid=(scenes + chips,),
        in_specs=[
            early((n, he)),
            early((n, cp)),
            early((n, channels)),
            early((live, he)),
            early((live, he)),
            early((live, cp)),
            whole(wpe.shape),
            whole(wkv.shape),
        ],
        out_specs=[
            late((keys, cp)),
            early((channels, n)),
            whole((cp, cp)),
            whole((cp, 2 * cp)),
            whole((8, cp)),
        ],
        out_shape=[
            jax.ShapeDtypeStruct((scenes, keys, cp), F32),
            jax.ShapeDtypeStruct((scenes, channels, n), BF16),
            jax.ShapeDtypeStruct((cp, cp), F32),
            jax.ShapeDtypeStruct((cp, 2 * cp), F32),
            jax.ShapeDtypeStruct((8, cp), F32),
        ],
        scratch_shapes=[
            pltpu.VMEM((n, he), BF16),
            pltpu.VMEM((he, n), F32),
            pltpu.VMEM((2, 2, used, keys, cp), BF16),
            pltpu.VMEM(land, BF16),
            pltpu.VMEM(land, BF16),
            pltpu.VMEM(land, BF16),
            pltpu.VMEM(land, BF16),
            pltpu.SemaphoreType.DMA((scenes,)),
            pltpu.SemaphoreType.DMA((scenes,)),
        ]
        + [pltpu.SemaphoreType.DMA((scenes, used))] * 4,
        compiler_params=pltpu.CompilerParams(
            vmem_limit_bytes=VMEM, collective_id=cid, has_side_effects=True
        ),
    )(q, att, gres, ke, ve, rn, wpe, wkv)


def tail_kernel(
    dims, tok_ref, gqt_ref, gres_ref, grn_ref, red_ref, vec_ref, wq_ref, wr_ref,
    ig_ref, dwqt, dwrt, dvec_ref, scr, gscr,
):
    scenes, height, width, channels, cp = dims
    n = height * width
    keys = n // 4
    lt = cp // LANE
    s_id = pl.program_id(0)

    @pl.when(s_id == 0)
    def _():
        dwqt[...] = jnp.zeros(dwqt.shape, F32)
        dwrt[...] = jnp.zeros(dwrt.shape, F32)
        dvec_ref[...] = jnp.zeros(dvec_ref.shape, F32)

    rhat, rstd = centered(red_ref[0], channels)
    up = grn_ref[0].astype(F32)
    dvec_ref[0:1] += jnp.sum(up * rhat, 0, keepdims=True)
    dvec_ref[1:2] += jnp.sum(up, 0, keepdims=True)
    gred = norm_back(jnp.where(lanes(up.shape) < channels, up, 0.0), vec_ref[2:3], rhat, rstd, channels)
    gred = jnp.where(lanes(up.shape) < channels, gred, 0.0).astype(BF16)
    dvec_ref[2:3] += jnp.sum(gred.astype(F32), 0, keepdims=True)
    gred_t = gred.T

    x = widen(tok_ref[0].astype(F32), cp)
    xhat, xstd = centered(x, channels)
    low = (xhat * vec_ref[0:1] + vec_ref[1:2]).astype(BF16)
    lowf = low.astype(F32)
    for t in range(lt):
        scr[t] = lowf[:, t * LANE : (t + 1) * LANE]
    for b in range(2):
        part = [scr[t, pl.ds(b, n // 2, stride=2), :] for t in range(lt)]
        part = jnp.concatenate(part, -1).reshape(height // 2, 2, width // 2, cp)
        for a in range(2):
            ab = 2 * a + b
            dwrt[ab] += dot(gred_t, part[:, a].reshape(keys, cp).astype(BF16))
            back = dot_nt(gred, wr_ref[ab])
            for t in range(lt):
                for i in range(height // 2):
                    gscr[t, pl.ds((2 * i + a) * width + b, width // 2, stride=2), :] = back[
                        i * (width // 2) : (i + 1) * (width // 2), t * LANE : (t + 1) * LANE
                    ]
    gqt = gqt_ref[0]
    dwqt[...] += dot(gqt, low)
    gn = widen(dot_nt(gqt.T, wq_ref[...]), cp) + jnp.concatenate([gscr[t] for t in range(lt)], -1)
    dvec_ref[3:4] += jnp.sum(gn * xhat, 0, keepdims=True)
    dvec_ref[4:5] += jnp.sum(gn, 0, keepdims=True)
    gx = norm_back(gn, vec_ref[0:1], xhat, xstd, channels)
    ig_ref[0] = gres_ref[0] + gx[:, :channels]


def tail(dims, tok, gqt, gres, grn, red, vec, wqt, wr):
    scenes, height, width, channels, cp = dims
    n = height * width
    keys = n // 4
    lt = cp // LANE
    return pl.pallas_call(
        functools.partial(tail_kernel, dims),
        grid=(scenes,),
        in_specs=[
            per_scene((n, channels)),
            per_scene((channels, n)),
            per_scene((n, channels)),
            per_scene((keys, cp)),
            per_scene((keys, cp)),
            whole(vec.shape),
            whole(wqt.shape),
            whole(wr.shape),
        ],
        out_specs=[
            per_scene((n, channels)),
            whole((channels, cp)),
            whole((4, cp, cp)),
            whole((8, cp)),
        ],
        out_shape=[
            jax.ShapeDtypeStruct((scenes, n, channels), F32),
            jax.ShapeDtypeStruct((channels, cp), F32),
            jax.ShapeDtypeStruct((4, cp, cp), F32),
            jax.ShapeDtypeStruct((8, cp), F32),
        ],
        scratch_shapes=[
            pltpu.VMEM((lt, n, LANE), F32),
            pltpu.VMEM((lt, n, LANE), F32),
        ],
        compiler_params=pltpu.CompilerParams(vmem_limit_bytes=VMEM),
    )(tok, gqt, gres, grn, red, vec, wqt, wr)


def bit_orders(ndp, nblk):
    dp_bits, blk_bits = ndp.bit_length() - 1, nblk.bit_length() - 1
    assert ndp == 1 << dp_bits and nblk == 1 << blk_bits
    core = [("blk", 0)] if blk_bits else []
    xs = [("dp", b) for b in range(dp_bits // 2)]
    ys = [("dp", b) for b in range(dp_bits // 2, dp_bits)]
    zs = [("blk", b) for b in range(1, blk_bits)]
    return [core + xs + ys + zs, core + ys + zs + xs, core + zs + xs + ys]


def pack_plan(channels, ff, ndev):
    cp = up_to(channels, LANE)
    tall = up_to(channels + 2, 16)
    items = [
        ("we", tall, ff // LANE), ("ws", channels, ff // LANE), ("wr", channels, 4 * cp // LANE),
        ("wkv", tall, 2 * cp // LANE), ("wp", channels, cp // LANE), ("wq", channels, cp // LANE),
    ]
    plan, at = {}, 0
    for name, rows, slabs in items:
        plan[name] = (at, rows, slabs)
        at += rows * slabs
    unit = 16 * ndev
    units = -(-at // unit)
    last = units // 3 - (1 if units > 6 else 0)
    mid = (units - last) // 2
    sizes = [(units - last - mid) * unit, mid * unit, last * unit]
    return plan, at, sizes


def small_plan(channels, ff, ndev):
    cp = up_to(channels, LANE)
    plan = {"tap": (0, 16, ff // LANE)}
    at = 16 * (ff // LANE)
    plan["vec"] = (at, 16, cp // LANE)
    at += 16 * (cp // LANE)
    plan["count"] = (at, 32, 1)
    at += 32
    return plan, up_to(at, 8 * ndev)


def reduce_kernel(
    channels, ff, ndp, nblk, dwe, dws, dwr, dwkv, dwp, dwq, dtap, dtb, dvec2, dvec1, dbp, cnt,
    out_hbm, small_hbm, work, recv, done, swork, srecv, sdone, send_sem, recv_sem, out_sem,
):
    ndev = ndp * nblk
    cp = up_to(channels, LANE)
    orders = bit_orders(ndp, nblk)
    rounds = len(orders[0])
    plan, used, sizes = pack_plan(channels, ff, ndev)
    splan, srows = small_plan(channels, ff, ndev)
    MESH = pl.DeviceIdType.MESH
    index = {"dp": lax.axis_index("dp"), "blk": lax.axis_index("blk")}

    def partner(axis, bit):
        step = 1 << bit
        value = lax.rem(index[axis] // step, 2)
        return value, {axis: index[axis] + (1 - 2 * value) * step}

    barrier = pltpu.get_barrier_semaphore()
    for axis, bit in orders[0]:
        pl.semaphore_signal(barrier, inc=1, device_id=partner(axis, bit)[1], device_id_type=MESH)

    def put(name, ref, rows_from=None):
        at, rows, slabs = plan[name]
        for t in range(slabs):
            work[at + t * rows : at + (t + 1) * rows, :] = ref(t, rows).astype(BF16)

    def lane_slabs(ref):
        return lambda t, rows: ref[:rows, t * LANE : (t + 1) * LANE]

    put("we", lane_slabs(dwe))
    put("ws", lane_slabs(dws))
    per = cp // LANE
    put("wr", lambda t, rows: dwr[t // per, :rows, (t % per) * LANE : (t % per + 1) * LANE])
    put("wkv", lane_slabs(dwkv))
    put("wp", lane_slabs(dwp))
    put("wq", lane_slabs(dwq))
    if used < sum(sizes):
        work[used:, :] = jnp.zeros((sum(sizes) - used, LANE), BF16)
    swork[...] = jnp.zeros(swork.shape, F32)
    at, rows, slabs = splan["tap"]
    db = jnp.sum(dtb[...], 0, keepdims=True)
    for t in range(slabs):
        cut = slice(t * LANE, (t + 1) * LANE)
        swork[at + t * rows : at + t * rows + 9, :] = dtap[:, cut]
        swork[at + t * rows + 9 : at + t * rows + 10, :] = db[:, cut]
    at, rows, slabs = splan["vec"]
    pb = jnp.sum(dbp[...], 0, keepdims=True)
    for t in range(slabs):
        cut = slice(t * LANE, (t + 1) * LANE)
        swork[at + t * rows : at + t * rows + 3, :] = dvec2[0:3, cut]
        swork[at + t * rows + 3 : at + t * rows + 8, :] = dvec1[0:5, cut]
        swork[at + t * rows + 8 : at + t * rows + 9, :] = pb[:, cut]
    at, rows, _ = splan["count"]
    swork[at : at + rows, :] = cnt[...]

    pl.semaphore_wait(barrier, rounds)

    parts, at = [], 0
    for size, order in zip(sizes, orders):
        if size:
            parts.append([work, recv, at, size, order])
        at += size
    parts.append([swork, srecv, 0, srows, orders[0]])

    state = [(first, size) for _, _, first, size, _ in parts]
    landing = [first for _, _, first, _, _ in parts]
    for i in range(rounds):
        copies = []
        for p, (buf, land, _, _, order) in enumerate(parts):
            start, size = state[p]
            size //= 2
            bit, device = partner(*order[i])
            unit = 16 if buf is work else 8
            send = pl.multiple_of(start + (1 - bit) * size, unit)
            keep = pl.multiple_of(start + bit * size, unit)
            copy = pltpu.make_async_remote_copy(
                src_ref=buf.at[pl.ds(send, size), :],
                dst_ref=land.at[pl.ds(landing[p], size), :],
                send_sem=send_sem.at[p, i],
                recv_sem=recv_sem.at[p, i],
                device_id=device,
                device_id_type=MESH,
            )
            copy.start()
            copies.append((copy, keep, size, landing[p], unit))
            state[p] = (keep, size)
            landing[p] += size
        for p, (copy, keep, size, low, unit) in enumerate(copies):
            buf, land = parts[p][:2]
            copy.wait()
            step = next(c for c in (256, 128, 64, 32, 16, 8) if size % c == 0)

            @pl.loop(0, size // step)
            def _(j, buf=buf, land=land, keep=keep, low=low, step=step, unit=unit):
                mine = pl.ds(pl.multiple_of(keep + j * step, unit), step)
                theirs = pl.ds(pl.multiple_of(low + j * step, unit), step)
                buf[mine, :] = (buf[mine, :].astype(F32) + land[theirs, :].astype(F32)).astype(buf.dtype)

    for p, (buf, _, _, _, _) in enumerate(parts):
        start, size = state[p]
        unit = 16 if buf is work else 8
        rows = pl.ds(pl.multiple_of(start, unit), size)
        final = done if buf is work else sdone
        final[rows, :] = buf[rows, :]

    for i in reversed(range(rounds)):
        copies = []
        for p, (buf, _, _, _, order) in enumerate(parts):
            start, size = state[p]
            final = done if buf is work else sdone
            bit, device = partner(*order[i])
            unit = 16 if buf is work else 8
            rows = pl.ds(pl.multiple_of(start, unit), size)
            copy = pltpu.make_async_remote_copy(
                src_ref=final.at[rows, :],
                dst_ref=final.at[rows, :],
                send_sem=send_sem.at[p, rounds + i],
                recv_sem=recv_sem.at[p, rounds + i],
                device_id=device,
                device_id_type=MESH,
            )
            copy.start()
            copies.append(copy)
            state[p] = (start - bit * size, 2 * size)
        for copy in copies:
            copy.wait()

    a = pltpu.make_async_copy(done, out_hbm, out_sem.at[0])
    b = pltpu.make_async_copy(sdone, small_hbm, out_sem.at[1])
    a.start()
    b.start()
    a.wait()
    b.wait()


def reduce_all(channels, ff, ndp, nblk, *grads):
    ndev = ndp * nblk
    rounds = len(bit_orders(ndp, nblk)[0])
    _, _, sizes = pack_plan(channels, ff, ndev)
    _, srows = small_plan(channels, ff, ndev)
    total = sum(sizes)
    vm = pl.BlockSpec(memory_space=pltpu.VMEM)
    hbm = pl.BlockSpec(memory_space=pl.ANY)
    return pl.pallas_call(
        functools.partial(reduce_kernel, channels, ff, ndp, nblk),
        in_specs=[vm] * len(grads),
        out_specs=[hbm, hbm],
        out_shape=[
            jax.ShapeDtypeStruct((total, LANE), BF16),
            jax.ShapeDtypeStruct((srows, LANE), F32),
        ],
        scratch_shapes=[
            pltpu.VMEM((total, LANE), BF16),
            pltpu.VMEM((total, LANE), BF16),
            pltpu.VMEM((total, LANE), BF16),
            pltpu.VMEM((srows, LANE), F32),
            pltpu.VMEM((srows, LANE), F32),
            pltpu.VMEM((srows, LANE), F32),
            pltpu.SemaphoreType.DMA((4, 2 * rounds)),
            pltpu.SemaphoreType.DMA((4, 2 * rounds)),
            pltpu.SemaphoreType.DMA((2,)),
        ],
        compiler_params=pltpu.CompilerParams(
            vmem_limit_bytes=VMEM, collective_id=1, has_side_effects=True
        ),
    )(*grads)


def unpack_kernel(channels, ff, ndev, packed, small, *outs):
    cp = up_to(channels, LANE)
    plan, _, _ = pack_plan(channels, ff, ndev)
    splan, _ = small_plan(channels, ff, ndev)
    (g1, b1, wq, qb, wr, rb, rg, rbn, wkv, vb, wp, pb, g2, b2, we, eb, dt, db, ws, sb, cm) = outs
    lt = cp // LANE

    def slab(name, t, first=0, count=None):
        at, rows, _ = plan[name]
        count = rows if count is None else count
        return packed[at + t * rows + first : at + t * rows + first + count, :].astype(F32)

    for t in range(ff // LANE):
        cut = slice(t * LANE, (t + 1) * LANE)
        we[:, cut] = slab("we", t, 0, channels)
        eb[cut] = slab("we", t, channels, 16)[0]
        ws[:, cut] = slab("ws", t)
        at, rows, _ = splan["tap"]
        dt[:, cut] = small[at + t * rows : at + t * rows + 9, :]
        db[cut] = small[at + t * rows + 9, :]

    def wide(name, first, count=None, base=0):
        return jnp.concatenate([slab(name, base + t, first, count) for t in range(lt)], -1)

    parts = [wide("wr", 0, base=ab * lt) for ab in range(4)]
    wr[...] = jnp.concatenate([v[:, :channels] for v in parts], -1)
    rb[...] = parts[0].T[channels]
    turned = wide("wq", 0).T
    wq[...] = turned[:channels]
    qb[...] = turned[channels]
    wp[...] = wide("wp", 0)[:, :channels]
    wkv[...] = jnp.concatenate(
        [wide("wkv", 0, channels)[:, :channels], wide("wkv", 0, channels, lt)[:, :channels]], -1
    )
    vb[...] = wide("wkv", channels, 16, lt)[1, :channels]
    at, rows, _ = splan["vec"]
    vec = jnp.concatenate([small[at + t * rows : at + (t + 1) * rows, :] for t in range(lt)], -1)
    vec = vec[:, :channels]
    for k, ref in enumerate((g2, b2, sb, rg, rbn, None, g1, b1, pb)):
        if ref is not None:
            ref[...] = vec[k]
    at, rows, _ = splan["count"]
    cm[...] = small[at : at + rows, :].astype(jnp.int32)[:CLASSES, :CLASSES]


def unpack(channels, ff, ndev, packed, small):
    one = (channels,)
    shapes = [
        one, one, (channels, channels), one, (channels, 4 * channels), one, one, one,
        (channels, 2 * channels), one, (channels, channels), one, one, one, (channels, ff), (ff,),
        (9, ff), (ff,), (channels, ff), one,
    ]
    outs = [jax.ShapeDtypeStruct(v, F32) for v in shapes]
    outs.append(jax.ShapeDtypeStruct((CLASSES, CLASSES), jnp.int32))
    return pl.pallas_call(
        functools.partial(unpack_kernel, channels, ff, ndev),
        out_shape=outs,
        compiler_params=pltpu.CompilerParams(vmem_limit_bytes=VMEM),
    )(packed, small)


NEG = np.float32(NEGATIVE * LOG2E)
NEG_HI = np.float32(ml_dtypes.bfloat16(NEG))
NEG_MID = np.float32(ml_dtypes.bfloat16(NEG - NEG_HI))
NEG_LO = np.float32(ml_dtypes.bfloat16(NEG - NEG_HI - NEG_MID))


def ext_row(values):
    lane = lanes((1, HEADS * LANE))
    row = jnp.zeros((1, HEADS * LANE), F32)
    for h in range(HEADS):
        for k, value in values.items():
            row = jnp.where(lane == h * LANE + ext_lane(h) + k, value, row)
    return row


def spread(value, cp):
    value = widen(value, cp)
    half = lanes((1, LANE)) // HALF
    blocks = []
    for h in range(HEADS):
        tile = value[:, (h // 2) * LANE : (h // 2 + 1) * LANE]
        blocks.append(jnp.where(half == h % 2, tile, jnp.zeros_like(tile)))
    return jnp.concatenate(blocks, -1)


def split_low(value):
    hi = value.astype(BF16).astype(F32)
    return hi, value - hi


def rows16(*rows):
    width = rows[0].shape[-1]
    at = lax.broadcasted_iota(jnp.int32, (16, width), 0)
    block = jnp.zeros((16, width), F32)
    for k, row in enumerate(rows):
        block = jnp.where(at == k, row, block)
    return block.astype(BF16)


def prep_kernel(
    channels, g1, b1, qw, qb, rw, rb, rg, rbn, kvw, vb, pw, pb, g2, b2, ew, eb, tb, sw, sb,
    vec, wq, wk, wv, wp, wpe, wkv, wr, we, ws, one, dbias, full,
):
    cp = up_to(channels, LANE)
    he = HEADS * LANE
    ff = ew.shape[1]
    head_size = channels // HEADS
    rest = cp - channels - 16

    def row(ref):
        return ref[...].reshape(1, ref.shape[-1])

    lane = lanes((1, cp))

    def padded(ref, *at):
        v = widen(row(ref), cp)
        for k in at:
            v = jnp.where(lane == channels + k, 1.0, v)
        return v

    for k, v in enumerate(
        (
            padded(g1), padded(b1, 0, 1), padded(rg), padded(rbn, 1, 2), padded(pb), padded(g2),
            padded(b2, 0, 1), padded(sb),
        )
    ):
        vec[k : k + 1, :] = v

    def fill(ref, top, *rows):
        width = ref.shape[-1]
        ref[:channels, :] = top
        ref[channels : channels + 16, :] = (
            rows16(*rows) if rows else jnp.zeros((16, width), BF16)
        )
        if rest:
            ref[channels + 16 :, :] = jnp.zeros((rest, width), BF16)

    ones = ext_row({0: 1.0, 1: 1.0, 2: 1.0})
    one[...] = ones
    dbias[...] = row(tb)
    qs = spread(qw[...], cp)
    qb_hi, qb_lo = split_low(row(qb))
    fill(wq, qs, spread(qb_hi, cp), spread(qb_lo, cp))
    kw = widen(kvw[:, :channels], cp)
    vw = widen(kvw[:, channels:], cp)
    ks = spread(kvw[:, :channels], cp)
    nil = jnp.zeros((1, he), F32)
    fill(
        wk, ks, ext_row({0: float(NEG_HI), 1: float(NEG_MID), 2: float(NEG_LO)}),
        ext_row({3: 1.0, 4: 1.0, 5: 1.0}),
    )
    vb_hi, vb_lo = split_low(row(vb))
    fill(wv, spread(kvw[:, channels:], cp), nil, spread(vb_hi, cp) + ones, spread(vb_lo, cp))
    p = widen(pw[...], cp)
    fill(wp, p)
    zero = jnp.zeros((HALF, cp), BF16)
    for h in range(HEADS):
        data, other = (0, HALF) if h % 2 == 0 else (HALF, 0)
        wpe[h * LANE + data : h * LANE + data + HALF, :] = p[h * HALF : (h + 1) * HALF]
        wpe[h * LANE + other : h * LANE + other + HALF, :] = zero
    fill(wkv, jnp.concatenate([kw, vw], -1))
    rb_rows = [widen(v, cp) for v in split_low(row(rb))]
    rw_rows = rw[...].T
    for ab in range(4):
        fill(
            wr.at[ab], widen(rw_rows[ab * channels : (ab + 1) * channels, :], cp),
            *rb_rows[ab : ab + 1],
        )
    fill(we, ew[...], *split_low(row(eb)))
    fill(ws, sw[...])

    def norm(v):
        return jnp.sqrt(jnp.sum(v * v, (0, 1), keepdims=True))

    root = channels**0.5

    def reach(gain, bias):
        top = jnp.max(jnp.abs(row(gain)), (0, 1), keepdims=True)
        return root * top + norm(row(bias))

    query_in, key_in = reach(g1, b1), reach(rg, rbn)
    qb_wide = spread(row(qb), cp)
    bound = jnp.zeros((1, 1), F32)
    for h in range(HEADS):
        cut = slice(h * LANE, (h + 1) * LANE)
        query = query_in * norm(qs[:, cut].astype(F32)) + norm(qb_wide[:, cut])
        key = key_in * norm(ks[:, cut].astype(F32))
        bound = jnp.maximum(bound, query * key)
    bound = bound * (head_size**-0.5 * 1.05)
    full[...] = jnp.where(2.0 * bound + 256.0 < -NEGATIVE, 0, 1).astype(jnp.int32)


def prep(channels, *weights):
    cp = up_to(channels, LANE)
    he = HEADS * LANE
    ff = weights[14].shape[1]
    shapes = [
        ((8, cp), F32), ((cp, he), BF16), ((cp, he), BF16), ((cp, he), BF16), ((cp, cp), BF16),
        ((he, cp), BF16), ((cp, 2 * cp), BF16), ((4, cp, cp), BF16), ((cp, ff), BF16),
        ((cp, ff), BF16), ((1, he), F32), ((1, ff), F32), ((1, 1), jnp.int32),
    ]
    return pl.pallas_call(
        functools.partial(prep_kernel, channels),
        out_shape=[jax.ShapeDtypeStruct(*v) for v in shapes],
        compiler_params=pltpu.CompilerParams(vmem_limit_bytes=VMEM),
    )(*weights)


def body(
    tokens, mask, labels, predicted, cotangent, norm1_gain, norm1_bias, query_weight, query_bias,
    reduce_weight, reduce_bias, rnorm_gain, rnorm_bias, kv_weight, value_bias, proj_weight,
    proj_bias, norm2_gain, norm2_bias, expand_weight, expand_bias, depth_weight, depth_bias,
    shrink_weight, shrink_bias,
):
    scenes, height, width, channels = tokens.shape
    ndp, blk = lax.axis_size("dp"), lax.axis_size("blk")
    n = height * width
    ff = expand_weight.shape[1]
    dims = (scenes, height, width, channels, up_to(channels, LANE))
    chips = blk // 2
    used = min(chips, -(-MASK_ROWS // (2 * height)))

    vec, wq, wk, wv, wp, wpe, wkv, wr, we, ws, ones, tap_bias, full = prep(
        channels, norm1_gain, norm1_bias, query_weight, query_bias, reduce_weight.T, reduce_bias,
        rnorm_gain, rnorm_bias, kv_weight, value_bias, proj_weight, proj_bias, norm2_gain,
        norm2_bias, expand_weight, expand_bias, depth_bias, shrink_weight.T, shrink_bias,
    )
    full = full[0, 0] > 0

    def either(call, cids, *operands):
        if used == chips:
            return call(dims, blk, chips, cids[1], *operands)
        return lax.cond(
            full,
            functools.partial(call, dims, blk, chips, cids[1]),
            functools.partial(call, dims, blk, used, cids[0]),
            *operands,
        )

    tok = tokens.reshape(scenes, n, channels)
    ct = cotangent.reshape(scenes, n, channels)
    red, counts, q, att, ke, ve, rn, res = either(
        attend, (2, 3), tok, mask, labels, predicted, vec, wr, wq, ones, wk, wv, wp
    )
    out, gres, dwe, dwst, dtap, dtb, dvec2 = ffn(
        dims, blk, res, ct, vec, we, ws, depth_weight, tap_bias
    )
    grn, gqt, dwp, dwkv, dbp = either(attback, (4, 5), q, att, gres, ke, ve, rn, wpe, wkv)
    ig, dwqt, dwrt, dvec1 = tail(dims, tok, gqt, gres, grn, red, vec, query_weight, wr)
    packed, small = reduce_all(
        channels, ff, ndp, blk, dwe, dwst, dwrt, dwkv, dwp, dwqt, dtap, dtb, dvec2, dvec1, dbp, counts
    )
    grads = list(unpack(channels, ff, ndp * blk, packed, small))
    grads[4], grads[18] = grads[4].T, grads[18].T
    return (out.reshape(tokens.shape), ig.reshape(tokens.shape), *grads)


def solution(mesh):
    banded = P("dp", "blk", None, None)
    plane = P("dp", "blk", None)
    in_specs = (banded, plane, plane, plane, banded) + (P(),) * 20
    out_specs = (banded, banded) + (P(),) * 21
    return jax.shard_map(body, mesh=mesh, in_specs=in_specs, out_specs=out_specs, check_vma=False)
```

```python
import functools

import jax
import jax.numpy as jnp
from jax import lax
from jax.experimental import pallas as pl
from jax.experimental.pallas import tpu as pltpu
from jax.sharding import PartitionSpec as P
import ml_dtypes
import numpy as np

HEADS = 5
CLASSES = 19
EPSILON = 1e-06
NEGATIVE = -32768.0
LOG2E = 1.4426950408889634
LN2 = 0.6931471805599453
F32 = jnp.float32
BF16 = jnp.bfloat16
LANE = 128
HALF = 64
KEY_CHUNK = 256
MASK_ROWS = 48
VMEM = 62 * 2**20
FF_CHUNK = 256
GROUP = 8


def up_to(value, step):
    return -(-value // step) * step


def dot(a, b):
    return lax.dot_general(a, b, (((1,), (0,)), ((), ())), preferred_element_type=F32)


def dot_nt(a, b):
    return lax.dot_general(a, b, (((1,), (1,)), ((), ())), preferred_element_type=F32)


def dot_tn(a, b):
    return lax.dot_general(a, b, (((0,), (0,)), ((), ())), preferred_element_type=F32)


def lanes(shape):
    return lax.broadcasted_iota(jnp.int32, shape, len(shape) - 1)


def whole(shape):
    return pl.BlockSpec(shape, lambda *_: (0,) * len(shape))


def per_scene(shape):
    return pl.BlockSpec((1,) + shape, lambda s: (s,) + (0,) * len(shape))


def centered(value, channels):
    mean = jnp.sum(value, -1, keepdims=True) * (1.0 / channels)
    center = jnp.where(lanes(value.shape) < channels, value - mean, 0.0)
    var = jnp.sum(center * center, -1, keepdims=True) * (1.0 / channels)
    rstd = lax.rsqrt(var + EPSILON)
    return center * rstd, rstd


def norm_back(up, gain, xhat, rstd, channels):
    u = up * gain
    mean = jnp.sum(u, -1, keepdims=True) * (1.0 / channels)
    proj = jnp.sum(u * xhat, -1, keepdims=True) * (1.0 / channels)
    return (u - mean - xhat * proj) * rstd


def ext_lane(head):
    return HALF if head % 2 == 0 else 0


def widen(value, width):
    pad = width - value.shape[-1]
    return jnp.concatenate([value, jnp.zeros(value.shape[:-1] + (pad,), value.dtype)], -1)


def place(blk):
    me = lax.axis_index("blk")
    core = lax.rem(me, 2)
    chip = me // 2
    return chip, core, {"blk": me + 2}, {"blk": me - 2}, {"blk": me + 1 - 2 * core}


def greet(chip, chips, up, down, sib):
    barrier = pltpu.get_barrier_semaphore()
    MESH = pl.DeviceIdType.MESH
    has_up, has_down = chip < chips - 1, chip > 0
    pl.semaphore_signal(barrier, inc=1, device_id=sib, device_id_type=MESH)

    @pl.when(has_up)
    def _():
        pl.semaphore_signal(barrier, inc=1, device_id=up, device_id_type=MESH)

    @pl.when(has_down)
    def _():
        pl.semaphore_signal(barrier, inc=1, device_id=down, device_id_type=MESH)

    pl.semaphore_wait(barrier, 1 + has_up.astype(jnp.int32) + has_down.astype(jnp.int32))


def remote(src, dst, send, recv, device):
    return pltpu.make_async_remote_copy(
        src_ref=src, dst_ref=dst, send_sem=send, recv_sem=recv, device_id=device,
        device_id_type=pl.DeviceIdType.MESH,
    )


def groups_of(ndp, nblk):
    dp_bits, blk_bits = ndp.bit_length() - 1, nblk.bit_length() - 1
    assert ndp == 1 << dp_bits and nblk == 1 << blk_bits
    core = [("blk", 0, 2)] if blk_bits else []
    if dp_bits > 2:
        plane = [("dp", 0, 1 << dp_bits // 2), ("dp", dp_bits // 2, 1 << (dp_bits - dp_bits // 2))]
    else:
        plane = [("dp", 0, ndp)] if dp_bits else []
    line = [("blk", 1, nblk // 2)] if blk_bits > 1 else []
    return core, plane, line


def lay_out(items, ndev):
    plan, at = {}, 0
    for name, rows, slabs in items:
        plan[name] = (at, rows, slabs)
        at += rows * slabs
    unit = 16 * ndev
    units = -(-at // unit)
    last = units // 3 - (1 if units > 6 else 0)
    mid = (units - last) // 2
    return plan, at, [(units - last - mid) * unit, mid * unit, last * unit]


def ffn_plan(channels, ff, ndev):
    tall = up_to(channels + 2, 16)
    return lay_out([("we", tall, ff // LANE), ("ws", channels, ff // LANE)], ndev)


def rest_plan(channels, ndev):
    cp = up_to(channels, LANE)
    tall = up_to(channels + 2, 16)
    return lay_out(
        [
            ("wr", channels, 4 * cp // LANE), ("wkv", tall, 2 * cp // LANE),
            ("wp", channels, cp // LANE), ("wq", channels, cp // LANE),
        ],
        ndev,
    )


def small_plan(channels, ff, ndev):
    cp = up_to(channels, LANE)
    plan = {"tap": (0, 16, ff // LANE)}
    at = 16 * (ff // LANE)
    plan["vec"] = (at, 16, cp // LANE)
    at += 16 * (cp // LANE)
    plan["count"] = (at, 32, 1)
    at += 32
    return plan, up_to(at, 8 * ndev)


def member(group):
    axis, bit, size = group
    return lax.rem(lax.axis_index(axis) // (1 << bit), size)


def other(group, index):
    axis, bit, _ = group
    return {axis: lax.axis_index(axis) + (index - member(group)) * (1 << bit)}


def peers_of(order):
    return [
        other(group, lax.rem(member(group) + d, group[2])) for group in order for d in range(1, group[2])
    ]


class Sums:
    def __init__(self, parts, send_sem, recv_sem):
        self.parts, self.send_sem, self.recv_sem = parts, send_sem, recv_sem
        self.rounds = len(parts[0][5])
        self.ops = 2 * self.rounds

    def unit(self, p):
        return 16 if self.parts[p][0].dtype == BF16 else 8

    def segment(self, p, i):
        _, _, _, start, rows, order = self.parts[p]
        for group in order[:i]:
            rows //= group[2]
            start = start + member(group) * rows
        return start, rows

    def landing(self, p, i):
        _, _, _, first, rows, order = self.parts[p]
        for group in order[:i]:
            first += rows // group[2] * (group[2] - 1)
            rows //= group[2]
        return first

    def copies(self, p, k):
        buf, land, done, _, _, order = self.parts[p]
        unit = self.unit(p)
        halving = k < self.rounds
        i = k if halving else self.ops - 1 - k
        group = order[i]
        size = group[2]
        me = member(group)
        result = []
        for d in range(1, size):
            to = lax.rem(me + d, size)
            if halving:
                start, rows = self.segment(p, i)
                rows //= size
                src = buf.at[pl.ds(pl.multiple_of(start + to * rows, unit), rows), :]
                low = self.landing(p, i) + (size - 1 - d) * rows
                dst = land.at[pl.ds(low, rows), :]
            else:
                start, rows = self.segment(p, i + 1)
                src = done.at[pl.ds(pl.multiple_of(start, unit), rows), :]
                dst = src
            result.append(
                remote(
                    src, dst, self.send_sem.at[p, k, d - 1], self.recv_sem.at[p, k, d - 1],
                    other(group, to),
                )
            )
        return result

    def start(self, p, k):
        for copy in self.copies(p, k):
            copy.start()

    def finish(self, p, k):
        for copy in self.copies(p, k):
            copy.wait()
        if k >= self.rounds:
            return
        buf, land, done, _, _, order = self.parts[p]
        unit = self.unit(p)
        keep, rows = self.segment(p, k + 1)
        low = self.landing(p, k)
        step = next(c for c in (256, 128, 64, 32, 16, 8) if rows % c == 0)
        into = done if k == self.rounds - 1 else buf

        @pl.loop(0, rows // step)
        def _(j):
            mine = pl.ds(pl.multiple_of(keep + j * step, unit), step)
            total = buf[mine, :].astype(F32)
            for d in range(order[k][2] - 1):
                theirs = pl.ds(pl.multiple_of(low + d * rows + j * step, unit), step)
                total = total + land[theirs, :].astype(F32)
            into[mine, :] = total.astype(buf.dtype)

    def advance(self, k):
        for p in range(len(self.parts)):
            if k > 0:
                self.finish(p, k - 1)
            if k < self.ops:
                self.start(p, k)


def three_parts(buf, land, done, sizes, orders):
    parts, at = [], 0
    for size, order in zip(sizes, orders):
        if size:
            parts.append((buf, land, done, at, size, order))
        at += size
    return parts


def orders_of(ndp, nblk):
    core, plane, line = groups_of(ndp, nblk)
    return [core + plane + line, core + plane + line, core + line + plane]


def widest(ndp, nblk):
    return max(group[2] for group in orders_of(ndp, nblk)[0]) - 1


def attend_kernel(
    dims, blk, used, tok_ref, mask_ref, label_ref, pred_ref, tok2_ref, vec_ref, wr_ref, wq_ref,
    one_ref, wk_ref, wv_ref, wp_ref,
    red_ref, cnt_ref, q_ref, att_ref, ke_ref, ve_ref, rn_ref, res_ref,
    scr, qbuf, oe, rnbuf, up_send, down_send, sib_send, line_recv, sib_recv,
):
    scenes, height, width, channels, cp = dims
    n = height * width
    keys = n // 4
    chips = blk // 2
    lag = chips
    step = pl.program_id(0)
    head_size = channels // HEADS
    chip, core, up, down, sib = place(blk)

    @pl.when(step == 0)
    def _():
        greet(chip, chips, up, down, sib)
        cnt_ref[...] = jnp.zeros(cnt_ref.shape, F32)

    def slot(origin, c):
        return c * used + origin

    def send_up(s, origin):
        place_ = rnbuf.at[s, slot(origin, core)]
        return remote(place_, place_, up_send.at[s, origin], line_recv.at[s, origin], up)

    def send_down(s, origin):
        place_ = rnbuf.at[s, slot(origin, core)]
        return remote(place_, place_, down_send.at[s, origin], line_recv.at[s, origin], down)

    def send_sib(s, origin):
        place_ = rnbuf.at[s, slot(origin, core)]
        return remote(place_, place_, sib_send.at[s, origin], sib_recv.at[s, origin], sib)

    @pl.when(step < scenes)
    def _():
        s = step
        x = widen(tok_ref[0].astype(F32), cp)
        xhat, _ = centered(x, channels)
        low = (xhat * vec_ref[0:1] + vec_ref[1:2]).astype(BF16)
        lowf = low.astype(F32)
        for t in range(cp // LANE):
            scr[t] = lowf[:, t * LANE : (t + 1) * LANE]
        total = jnp.zeros((keys, cp), F32)
        for b in range(2):
            part = [scr[t, pl.ds(b, n // 2, stride=2), :] for t in range(cp // LANE)]
            part = jnp.concatenate(part, -1).reshape(height // 2, 2, width // 2, cp)
            for a in range(2):
                total = total + dot(part[:, a].reshape(keys, cp).astype(BF16), wr_ref[2 * a + b])
        red_ref[0] = total
        rhat, _ = centered(total, channels)
        m = mask_ref[0].astype(F32)
        shape = (width // 2, width)
        near = lanes(shape) // 2 == lax.broadcasted_iota(jnp.int32, shape, 0)
        flags = []
        for i in range(height // 2):
            both = m[2 * i : 2 * i + 1] + m[2 * i + 1 : 2 * i + 2]
            flags.append(jnp.sum(jnp.where(near, both, 0.0), -1, keepdims=True))
        unc = jnp.where(jnp.concatenate(flags, 0) > 0.0, 0.0, 1.0)
        flag = jnp.where(lanes((keys, cp)) == channels, unc, 0.0)
        own = (rhat * vec_ref[2:3] + vec_ref[3:4] + flag).astype(BF16)

        @pl.when(chip < used)
        def _():
            rnbuf[s, slot(chip, core)] = own
            send_sib(s, chip).start()

            @pl.when(chip < chips - 1)
            def _():
                send_up(s, chip).start()

            @pl.when(chip > 0)
            def _():
                send_down(s, chip).start()

        qf = dot(low, wq_ref[...]) * (LOG2E * head_size**-0.5) + one_ref[...]
        qbuf[lax.rem(s, lag + 1)] = qf.astype(BF16)
        shape = (cnt_ref.shape[0], width)
        classes = lax.broadcasted_iota(jnp.int32, shape, 0)
        wide = lax.broadcasted_iota(jnp.int32, (LANE, width), 0)
        total = jnp.zeros(cnt_ref.shape, F32)
        for r in range(height):
            label = jnp.where(mask_ref[0, r : r + 1] > 0, label_ref[0, r : r + 1], -1)
            hot = jnp.where(label == classes, 1.0, 0.0).astype(BF16)
            pred = jnp.where(pred_ref[0, r : r + 1] == wide, 1.0, 0.0).astype(BF16)
            total = total + dot_nt(hot, pred)
        cnt_ref[...] += total

    for age in range(1, chips):
        s = step - age

        @pl.when(jnp.logical_and(s >= 0, s < scenes))
        def _(s=s, age=age):
            below = chip - age

            @pl.when(jnp.logical_and(below >= 0, below < used))
            def _():
                send_up(s, below).wait_recv()
                send_sib(s, below).start()

                @pl.when(chip < chips - 1)
                def _():
                    send_up(s, below).start()

            above = chip + age

            @pl.when(above < used)
            def _():
                send_down(s, above).wait_recv()
                send_sib(s, above).start()

                @pl.when(chip > 0)
                def _():
                    send_down(s, above).start()

    @pl.when(step >= lag)
    def _():
        s = step - lag

        for origin in range(used):
            send_sib(s, origin).wait_recv()

        rn_all = rnbuf[s].reshape(2 * used * keys, cp)
        rn_ref[0] = rn_all
        ke_ref[0] = dot(rn_all, wk_ref[...]).astype(BF16)
        ve_ref[0] = dot(rn_all, wv_ref[...]).astype(BF16)
        mine = lax.rem(s, lag + 1)
        count = 2 * used * keys // KEY_CHUNK
        for h in range(HEADS):
            block = slice(h * LANE, (h + 1) * LANE)
            e = ext_lane(h)
            q = qbuf[mine, :, block]
            parts = [
                dot_nt(q, ke_ref[0, j * KEY_CHUNK : (j + 1) * KEY_CHUNK, block])
                for j in range(count)
            ]
            top = functools.reduce(jnp.maximum, parts)
            top = jnp.max(top, -1, keepdims=True)
            out = jnp.zeros((n, LANE), F32)
            for j in range(count):
                p = jnp.exp2(parts[j] - top).astype(BF16)
                out = out + dot(p, ve_ref[0, j * KEY_CHUNK : (j + 1) * KEY_CHUNK, block])
            total = out[:, e : e + 1]
            oe[h] = out / total
            lse = top + jnp.log2(total)
            hi = lse.astype(BF16).astype(F32)
            mid = (lse - hi).astype(BF16).astype(F32)
            lo = lse - hi - mid
            lane = lanes((n, LANE))
            q2 = q.astype(F32)
            q2 = jnp.where(lane == e + 3, -hi, q2)
            q2 = jnp.where(lane == e + 4, -mid, q2)
            q2 = jnp.where(lane == e + 5, -lo, q2)
            q_ref[0, :, block] = q2.astype(BF16)

        tiles = []
        low_half = lanes((n, LANE)) < HALF
        for t in range(cp // LANE):
            other = oe[2 * t + 1] if 2 * t + 1 < HEADS else jnp.zeros((n, LANE), F32)
            tiles.append(jnp.where(low_half, oe[2 * t], other))
        att = jnp.concatenate(tiles, -1)
        att_ref[0] = att
        x = widen(tok2_ref[0].astype(F32), cp)
        resid = x + dot(att.astype(BF16), wp_ref[...]) + vec_ref[4:5]
        for t in range(cp // LANE):
            for r in range(height):
                for half in range(2):
                    base = r * width + half * (width // 2)
                    at = r * scenes * width + half * scenes + s
                    res_ref[t, pl.ds(at, width // 2, stride=2 * scenes), :] = resid[
                        base : base + width // 2, t * LANE : (t + 1) * LANE
                    ]

    @pl.when(step == scenes + lag - 1)
    def _():
        @pl.loop(0, scenes)
        def _(s):
            for origin in range(used):
                send_sib(s, origin).wait_send()

                @pl.when(jnp.logical_and(origin <= chip, chip < chips - 1))
                def _(origin=origin):
                    send_up(s, origin).wait_send()

                @pl.when(jnp.logical_and(origin >= chip, chip > 0))
                def _(origin=origin):
                    send_down(s, origin).wait_send()


def attend(dims, blk, used, cid, tok, mask, labels, predicted, vec, wr, wq, ones, wk, wv, wp):
    scenes, height, width, channels, cp = dims
    n = height * width
    keys = n // 4
    chips = blk // 2
    lag = chips
    k = blk * keys
    live = 2 * used * keys
    he = HEADS * LANE

    def early(shape):
        return pl.BlockSpec(
            (1,) + shape, lambda t: (jnp.minimum(t, scenes - 1),) + (0,) * len(shape)
        )

    def late(shape):
        return pl.BlockSpec((1,) + shape, lambda t: (jnp.maximum(t - lag, 0),) + (0,) * len(shape))

    return pl.pallas_call(
        functools.partial(attend_kernel, dims, blk, used),
        grid=(scenes + lag,),
        in_specs=[early((n, channels))]
        + [early((height, width))] * 3
        + [late((n, channels))]
        + [whole(v.shape) for v in (vec, wr, wq, ones, wk, wv, wp)],
        out_specs=[
            early((keys, cp)),
            whole((32, LANE)),
            late((n, he)),
            late((n, cp)),
            late((live, he)),
            late((live, he)),
            late((live, cp)),
            whole((cp // LANE, scenes * n, LANE)),
        ],
        out_shape=[
            jax.ShapeDtypeStruct((scenes, keys, cp), F32),
            jax.ShapeDtypeStruct((32, LANE), F32),
            jax.ShapeDtypeStruct((scenes, n, he), BF16),
            jax.ShapeDtypeStruct((scenes, n, cp), F32),
            jax.ShapeDtypeStruct((scenes, k, he), BF16),
            jax.ShapeDtypeStruct((scenes, k, he), BF16),
            jax.ShapeDtypeStruct((scenes, k, cp), BF16),
            jax.ShapeDtypeStruct((cp // LANE, scenes * n, LANE), F32),
        ],
        scratch_shapes=[
            pltpu.VMEM((cp // LANE, n, LANE), F32),
            pltpu.VMEM((lag + 1, n, he), BF16),
            pltpu.VMEM((HEADS, n, LANE), F32),
            pltpu.VMEM((scenes, 2 * used, keys, cp), BF16),
        ]
        + [pltpu.SemaphoreType.DMA((scenes, used))] * 5,
        compiler_params=pltpu.CompilerParams(
            vmem_limit_bytes=VMEM, collective_id=cid, has_side_effects=True
        ),
    )(tok, mask, labels, predicted, tok, vec, wr, wq, ones, wk, wv, wp)


def ffn_kernel(
    dims, ff, blk, ndev, res_hbm, ct_hbm, vec_ref, we_ref, ws_ref, taps_ref, tb_ref,
    out_hbm, gres_hbm, pack_hbm, dtap_ref, dtb_ref, dvec_ref,
    dwe_ref, dwst, packed, res_ref, ct_ref, cn, cnt, ctt, ctx, oacc, gacc, hid, gm, halo, act, back, tapacc, out_stage, gres_stage,
    pack_sem, res_sem, ct_sem, out_sem, gres_sem, cn_send, cn_recv, gm_send, gm_recv,
):
    scenes, height, width, channels, cp = dims
    n = height * width
    rw = scenes * width
    lt = cp // LANE
    fc = FF_CHUNK
    nchunk = ff // fc
    cols = width // 2
    pair = 2 * scenes
    group = GROUP if cols % GROUP == 0 else cols
    me = lax.axis_index("blk")
    has_left = me > 0
    has_right = me < blk - 1
    left, right = {"blk": me - 1}, {"blk": me + 1}
    MESH = pl.DeviceIdType.MESH

    def res_copy(r):
        rows = pl.ds(pl.multiple_of(r * rw, rw), rw)
        return pltpu.make_async_copy(res_hbm.at[:, rows, :], res_ref.at[:, rows, :], res_sem.at[r])

    def ct_copy(s):
        return pltpu.make_async_copy(ct_hbm.at[s], ct_ref.at[s], ct_sem.at[s])

    for r in range(height):
        res_copy(r).start()
    for s in range(scenes):
        ct_copy(s).start()

    barrier = pltpu.get_barrier_semaphore()

    @pl.when(has_left)
    def _():
        pl.semaphore_signal(barrier, inc=1, device_id=left, device_id_type=MESH)

    @pl.when(has_right)
    def _():
        pl.semaphore_signal(barrier, inc=1, device_id=right, device_id_type=MESH)

    pl.semaphore_wait(barrier, has_left.astype(jnp.int32) + has_right.astype(jnp.int32))

    def row(r, size=rw):
        return pl.ds(pl.multiple_of(r * rw, rw), size)

    g2, b2 = vec_ref[5:6], vec_ref[6:7]

    def load3(ref, r):
        return jnp.concatenate([ref[t, row(r), :] for t in range(lt)], -1)

    def store3(ref, r, value):
        for t in range(lt):
            ref[t, row(r), :] = value[:, t * LANE : (t + 1) * LANE]

    @pl.loop(0, height)
    def _(r):
        res_copy(r).wait()
        x = load3(res_ref, r)
        xhat, rstd = centered(x, channels)
        c = (xhat * g2 + b2).astype(BF16)
        cn[row(r + 1), :] = c
        cnt[:, row(r)] = c.T
        store3(oacc, r, x + vec_ref[7:8])
        store3(res_ref, r, jnp.where(lanes(xhat.shape) == channels, rstd, xhat))

    def cn_copy(up):
        return pltpu.make_async_remote_copy(
            src_ref=cn.at[row(1 if up else height), :],
            dst_ref=cn.at[row(height + 1 if up else 0), :],
            send_sem=cn_send.at[0 if up else 1],
            recv_sem=cn_recv.at[0 if up else 1],
            device_id=left if up else right,
            device_id_type=MESH,
        )

    @pl.when(has_left)
    def _():
        cn_copy(True).start()

    @pl.when(has_right)
    def _():
        cn_copy(False).start()

    @pl.loop(0, scenes)
    def _(s):
        ct_copy(s).wait()
        c = widen(ct_ref[s].astype(F32), cp)
        for t in range(lt):
            for r in range(height):
                for half in range(2):
                    base = r * width + half * cols
                    gacc[t, pl.ds(r * rw + half * scenes + s, cols, stride=pair), :] = c[
                        base : base + cols, t * LANE : (t + 1) * LANE
                    ]

    dvec_ref[...] = jnp.zeros(dvec_ref.shape, F32)

    @pl.loop(0, height)
    def _(r):
        c = load3(gacc, r)
        dvec_ref[2:3] += jnp.sum(c, 0, keepdims=True)
        low = c.astype(BF16)
        ctt[row(r), :] = low
        ctx[:, row(r)] = low.T
        store3(gacc, r, jnp.zeros((rw, cp), F32))

    dwe_ref[...] = jnp.zeros(dwe_ref.shape, F32)
    dwst[...] = jnp.zeros(dwst.shape, F32)

    @pl.when(has_left)
    def _():
        cn_copy(False).wait_recv()

    @pl.when(jnp.logical_not(has_left))
    def _():
        cn[row(0), :] = jnp.zeros((rw, cp), BF16)

    @pl.when(has_right)
    def _():
        cn_copy(True).wait_recv()

    @pl.when(jnp.logical_not(has_right))
    def _():
        cn[row(height + 1), :] = jnp.zeros((rw, cp), BF16)

    def put(ref, slot, r, value):
        v = value.reshape(cols, pair, fc)
        z = jnp.zeros((scenes, fc), F32)
        ref[slot, r, 1 : cols + 1] = v.astype(BF16)
        ref[slot, r, 0] = jnp.concatenate([z, v[cols - 1, :scenes]], 0).astype(BF16)
        ref[slot, r, cols + 1] = jnp.concatenate([v[0, scenes:], z], 0).astype(BF16)

    def gm_copy(k, slot, up):
        return pltpu.make_async_remote_copy(
            src_ref=gm.at[slot, 1 if up else height],
            dst_ref=halo.at[k, 1 if up else 0],
            send_sem=gm_send.at[k, 0 if up else 1],
            recv_sem=gm_recv.at[k, 0 if up else 1],
            device_id=left if up else right,
            device_id_type=MESH,
        )

    def phase_a(k, slot):
        span = pl.ds(pl.multiple_of(k * fc, fc), fc)
        taps = [
            taps_ref[pl.ds(i, 1), span].astype(BF16).reshape(1, 1, fc) for i in range(9)
        ]
        bias = tb_ref[:, span]

        def hidden(r):
            put(hid, slot, r, dot(cn[r * rw : (r + 1) * rw, :], we_ref[:, span]))

        def products(r):
            active = act[r * rw : (r + 1) * rw, :]
            o = dot_nt(active, ws_ref[:, span])
            for t in range(lt):
                oacc[t, r * rw : (r + 1) * rw, :] += o[:, t * LANE : (t + 1) * LANE]
            dwst[:, span] += dot(ctx[:, r * rw : (r + 1) * rw], active)

        hidden(0)
        hidden(1)
        hidden(2)
        sums = jnp.zeros((8, fc), F32)
        for r in range(height):
            if r + 3 < height + 2:
                hidden(r + 3)
            back[...] = dot(ctt[r * rw : (r + 1) * rw, :], ws_ref[:, span])
            if r:
                products(r - 1)
            for g in range(0, cols, group):
                acc = None
                for a in range(3):
                    line = hid[slot, r + a, g : g + group + 2]
                    for b in range(3):
                        term = line[b : b + group] * taps[3 * a + b]
                        acc = term if acc is None else acc + term
                mixed = acc.astype(F32).reshape(group * pair, fc) + bias
                arg = mixed * 0.7071067811865476
                phi = 0.5 + 0.5 * lax.erf(arg)
                dens = jnp.exp2(arg * arg * -LOG2E) * mixed
                act[r * rw + g * pair : r * rw + (g + group) * pair, :] = (mixed * phi).astype(BF16)
                slope = phi + dens * 0.3989422804014327
                grad = back[g * pair : (g + group) * pair, :] * slope
                sums = sums + jnp.sum(grad.reshape(group * pair // 8, 8, fc), 0)
                v = grad.reshape(group, pair, fc)
                gm[slot, r + 1, g + 1 : g + group + 1] = v.astype(BF16)
                z = jnp.zeros((scenes, fc), F32)
                if g == 0:
                    gm[slot, r + 1, cols + 1] = jnp.concatenate([v[0, scenes:], z], 0).astype(BF16)
                if g + group == cols:
                    gm[slot, r + 1, 0] = jnp.concatenate([z, v[group - 1, :scenes]], 0).astype(BF16)
        products(height - 1)
        dtb_ref[:, span] = sums

        @pl.when(has_left)
        def _():
            gm_copy(k, slot, True).start()

        @pl.when(has_right)
        def _():
            gm_copy(k, slot, False).start()

    def phase_b(k, slot):
        span = pl.ds(pl.multiple_of(k * fc, fc), fc)

        @pl.when(has_left)
        def _():
            gm_copy(k, slot, False).wait_recv()
            gm[slot, 0] = halo[k, 0]

        @pl.when(jnp.logical_not(has_left))
        def _():
            gm[slot, 0] = jnp.zeros((cols + 2, pair, fc), BF16)

        @pl.when(has_right)
        def _():
            gm_copy(k, slot, True).wait_recv()
            gm[slot, height + 1] = halo[k, 1]

        @pl.when(jnp.logical_not(has_right))
        def _():
            gm[slot, height + 1] = jnp.zeros((cols + 2, pair, fc), BF16)

        taps = [
            taps_ref[pl.ds(i, 1), span].astype(BF16).reshape(1, 1, fc) for i in range(9)
        ]
        tapacc[...] = jnp.zeros(tapacc.shape, F32)

        def products(r):
            low = act[r * rw : (r + 1) * rw, :]
            dwe_ref[:, span] += dot(cnt[:, r * rw : (r + 1) * rw], low)
            g = dot_nt(low, we_ref[:, span])
            for t in range(lt):
                gacc[t, r * rw : (r + 1) * rw, :] += g[:, t * LANE : (t + 1) * LANE]

        for r in range(height):
            if r:
                products(r - 1)
            tapsum = [None] * 9
            for g in range(0, cols, group):
                acc = None
                own = hid[slot, r + 1, g + 1 : g + group + 1]
                for a in range(3):
                    line = gm[slot, r + 2 - a, g : g + group + 2]
                    for b in range(3):
                        window = line[2 - b : 2 - b + group]
                        term = window * taps[3 * a + b]
                        acc = term if acc is None else acc + term
                        prod = own * window
                        while prod.shape[0] > 1:
                            cut = prod.shape[0] // 2
                            prod = prod[:cut] + prod[cut:]
                        i = 3 * a + b
                        tapsum[i] = prod[0] if tapsum[i] is None else tapsum[i] + prod[0]
                act[r * rw + g * pair : r * rw + (g + group) * pair, :] = acc.reshape(group * pair, fc)
            for i in range(9):
                tapacc[i] += tapsum[i].astype(F32)
        products(height - 1)

        for tap in range(9):
            dtap_ref[pl.ds(tap, 1), span] = jnp.sum(tapacc[tap], 0, keepdims=True)

        @pl.when(has_left)
        def _():
            gm_copy(k, slot, True).wait_send()

        @pl.when(has_right)
        def _():
            gm_copy(k, slot, False).wait_send()

    @pl.loop(0, nchunk + 1)
    def _(k):
        slot = lax.rem(k, 2)

        @pl.when(k < nchunk)
        def _():
            phase_a(k, slot)

        @pl.when(k > 0)
        def _():
            phase_b(k - 1, 1 - slot)

    @pl.when(has_left)
    def _():
        cn_copy(True).wait_send()

    @pl.when(has_right)
    def _():
        cn_copy(False).wait_send()

    plan, filled, _ = ffn_plan(channels, ff, ndev)
    for name, ref in (("we", dwe_ref), ("ws", dwst)):
        at, rows, slabs = plan[name]
        for t in range(slabs):
            packed[at + t * rows : at + (t + 1) * rows, :] = ref[
                :rows, t * LANE : (t + 1) * LANE
            ].astype(BF16)
    if filled < packed.shape[0]:
        packed[filled:, :] = jnp.zeros((packed.shape[0] - filled, LANE), BF16)
    pack_copy = pltpu.make_async_copy(packed, pack_hbm, pack_sem.at[0])
    pack_copy.start()

    def gather(ref, s):
        rows = []
        for r in range(height):
            for half in range(2):
                rows.append(
                    jnp.concatenate(
                        [
                            ref[t, pl.ds(r * rw + half * scenes + s, cols, stride=pair), :]
                            for t in range(lt)
                        ],
                        -1,
                    )
                )
        return jnp.concatenate(rows, 0)[:, :channels]

    def out_copy(s, slot):
        return pltpu.make_async_copy(out_stage.at[slot], out_hbm.at[s], out_sem.at[slot])

    def gres_copy(s, slot):
        return pltpu.make_async_copy(gres_stage.at[slot], gres_hbm.at[s], gres_sem.at[slot])

    @pl.loop(0, scenes)
    def _(s):
        slot = lax.rem(s, 2)

        @pl.when(s >= 2)
        def _():
            out_copy(s - 2, slot).wait()

        out_stage[slot] = gather(oacc, s).astype(BF16)
        out_copy(s, slot).start()

    @pl.loop(0, height)
    def _(r):
        kept = load3(res_ref, r)
        rstd = kept[:, channels : channels + 1]
        xhat = jnp.where(lanes(kept.shape) < channels, kept, 0.0)
        upstream = load3(gacc, r)
        dvec_ref[0:1] += jnp.sum(upstream * xhat, 0, keepdims=True)
        dvec_ref[1:2] += jnp.sum(upstream, 0, keepdims=True)
        g = ctt[row(r), :].astype(F32) + norm_back(upstream, g2, xhat, rstd, channels)
        store3(gacc, r, g)

    @pl.loop(0, scenes)
    def _(s):
        slot = lax.rem(s, 2)

        @pl.when(s >= 2)
        def _():
            gres_copy(s - 2, slot).wait()

        gres_stage[slot] = gather(gacc, s)
        gres_copy(s, slot).start()

    for s in range(scenes - 2, scenes):
        out_copy(s, s % 2).wait()
        gres_copy(s, s % 2).wait()
    pack_copy.wait()


def ffn(dims, blk, ndev, res, ct, vec, we, ws, taps, tb):
    scenes, height, width, channels, cp = dims
    n = height * width
    total = scenes * n
    rw = scenes * width
    ff = ws.shape[1]
    lt = cp // LANE
    nchunk = ff // FF_CHUNK
    strip = (width // 2 + 2, 2 * scenes, FF_CHUNK)
    pack_rows = sum(ffn_plan(channels, ff, ndev)[2])
    vm = pl.BlockSpec(memory_space=pltpu.VMEM)
    hbm = pl.BlockSpec(memory_space=pl.ANY)
    return pl.pallas_call(
        functools.partial(ffn_kernel, dims, ff, blk, ndev),
        in_specs=[hbm, hbm] + [vm] * 5,
        out_specs=[hbm, hbm, hbm] + [vm] * 3,
        out_shape=[
            jax.ShapeDtypeStruct((scenes, n, channels), BF16),
            jax.ShapeDtypeStruct((scenes, n, channels), F32),
            jax.ShapeDtypeStruct((pack_rows, LANE), BF16),
            jax.ShapeDtypeStruct((9, ff), F32),
            jax.ShapeDtypeStruct((8, ff), F32),
            jax.ShapeDtypeStruct((8, cp), F32),
        ],
        scratch_shapes=[
            pltpu.VMEM((cp, ff), F32),
            pltpu.VMEM((cp, ff), F32),
            pltpu.VMEM((pack_rows, LANE), BF16),
            pltpu.VMEM((lt, total, LANE), F32),
            pltpu.VMEM((scenes, n, channels), BF16),
            pltpu.VMEM((total + 2 * rw, cp), BF16),
            pltpu.VMEM((cp, total), BF16),
            pltpu.VMEM((total, cp), BF16),
            pltpu.VMEM((cp, total), BF16),
            pltpu.VMEM((lt, total, LANE), F32),
            pltpu.VMEM((lt, total, LANE), F32),
            pltpu.VMEM((2, height + 2) + strip, BF16),
            pltpu.VMEM((2, height + 2) + strip, BF16),
            pltpu.VMEM((nchunk, 2) + strip, BF16),
            pltpu.VMEM((total, FF_CHUNK), BF16),
            pltpu.VMEM((rw, FF_CHUNK), F32),
            pltpu.VMEM((9, 2 * scenes, FF_CHUNK), F32),
            pltpu.VMEM((2, n, channels), BF16),
            pltpu.VMEM((2, n, channels), F32),
            pltpu.SemaphoreType.DMA((1,)),
            pltpu.SemaphoreType.DMA((height,)),
            pltpu.SemaphoreType.DMA((scenes,)),
            pltpu.SemaphoreType.DMA((2,)),
            pltpu.SemaphoreType.DMA((2,)),
            pltpu.SemaphoreType.DMA((2,)),
            pltpu.SemaphoreType.DMA((2,)),
            pltpu.SemaphoreType.DMA((nchunk, 2)),
            pltpu.SemaphoreType.DMA((nchunk, 2)),
        ],
        compiler_params=pltpu.CompilerParams(
            vmem_limit_bytes=VMEM, collective_id=0, has_side_effects=True
        ),
    )(res, ct, vec, we, ws, taps, tb)


def attback_kernel(
    dims, ff, ndp, blk, used, q_ref, att_ref, gres_ref, ke_ref, ve_ref, rn_ref, tok_ref, gres2_ref,
    red_ref, vec_ref, wpe_ref, wkv_ref, wq_ref, wr_ref, first_hbm,
    ig_ref, dwqt, dwrt, dwp_ref, dwkv_ref, dbp_ref, dvec_ref, sum_hbm,
    ge, dqt, gqt_ref, grn_ref, scr, gscr, own, acc, sib_land, up_land, down_land,
    work, land, done,
    sib_send, sib_recv, up_send, up_recv, down_send, down_recv, sum_send, sum_recv, sum_sem,
):
    scenes, height, width, channels, cp = dims
    n = height * width
    keys = n // 4
    chips = blk // 2
    lt = cp // LANE
    head_size = channels // HEADS
    step = pl.program_id(0)
    chip, core, up, down, sib = place(blk)
    count = 2 * used * keys // KEY_CHUNK
    steps = scenes + chips
    together = -(-scenes // chips)
    ndev = ndp * blk
    order = orders_of(ndp, blk)[0]
    parts = three_parts(work, land, done, ffn_plan(channels, ff, ndev)[2], [order] * 3)
    sums = Sums(parts, sum_send, sum_recv)
    each = -(-(sums.ops + 1) // (steps - 1))

    @pl.when(step == 0)
    def _():
        load = pltpu.make_async_copy(first_hbm, work, sum_sem.at[0])
        load.start()
        barrier = pltpu.get_barrier_semaphore()
        peers = peers_of(order)
        for peer in peers:
            pl.semaphore_signal(barrier, inc=1, device_id=peer, device_id_type=pl.DeviceIdType.MESH)
        pl.semaphore_wait(barrier, len(peers))
        load.wait()
        for k in range(each):
            sums.advance(k)
        dwqt[...] = jnp.zeros(dwqt.shape, F32)
        dwrt[...] = jnp.zeros(dwrt.shape, F32)
        dvec_ref[...] = jnp.zeros(dvec_ref.shape, F32)
        dwp_ref[...] = jnp.zeros(dwp_ref.shape, F32)
        dwkv_ref[...] = jnp.zeros(dwkv_ref.shape, F32)
        dbp_ref[...] = jnp.zeros(dbp_ref.shape, F32)

    def to_sib(s, target):
        return remote(
            own.at[lax.rem(s, 2), 1 - core, target], sib_land.at[s, target], sib_send.at[s, target],
            sib_recv.at[s, target], sib,
        )

    def to_up(s, target):
        return remote(
            acc.at[s, target], up_land.at[s, target], up_send.at[s, target], up_recv.at[s, target], up
        )

    def to_down(s, target):
        return remote(
            acc.at[s, target], down_land.at[s, target], down_send.at[s, target],
            down_recv.at[s, target], down,
        )

    def plus(a, b):
        return (a.astype(F32) + b.astype(F32)).astype(BF16)

    def chunk(j):
        s = step
        per = KEY_CHUNK // keys
        span = slice(j * KEY_CHUNK, (j + 1) * KEY_CHUNK)
        dks, dvs = [], []
        for h in range(HEADS):
            block = slice(h * LANE, (h + 1) * LANE)
            k, v = ke_ref[0, span, block], ve_ref[0, span, block]
            q, g = q_ref[0, :, block], ge[:, block]
            p = jnp.exp2(dot_nt(k, q))
            gs = (p * dot_nt(v, g)).astype(BF16)
            dvs.append(dot(p.astype(BF16), g))
            dks.append(dot(gs, q))
            dqt[block, :] += dot_tn(k, gs)
        low_half = lanes((KEY_CHUNK, LANE)) < HALF
        tiles = []
        for group, scale in ((dks, LN2), (dvs, 1.0)):
            for t in range(lt):
                other = (
                    group[2 * t + 1] if 2 * t + 1 < HEADS else jnp.zeros((KEY_CHUNK, LANE), F32)
                )
                tiles.append((jnp.where(low_half, group[2 * t], other) * scale).astype(BF16))
        gkv = jnp.concatenate(tiles, -1)
        grn = dot_nt(gkv, wkv_ref[...]).astype(BF16)
        for i in range(per):
            at = j * per + i
            own[lax.rem(s, 2), at // used, at % used] = grn[i * keys : (i + 1) * keys]

            @pl.when(core != at // used)
            def _(at=at):
                to_sib(s, at % used).start()

        dwkv_ref[...] += dot(rn_ref[0, span].T, gkv)

    @pl.when(step < scenes)
    def _():
        s = step
        gb = widen(gres_ref[0], cp).astype(BF16)
        dbp_ref[...] += jnp.sum(gb.astype(F32).reshape(n // 8, 8, cp), 0)
        att = att_ref[0]
        dwp_ref[...] += dot(att.astype(BF16).T, gb)
        gatt = dot_nt(gb, wpe_ref[...])
        lane = lanes((n, LANE))
        for h in range(HEADS):
            e = ext_lane(h)
            g = gatt[:, h * LANE : (h + 1) * LANE].astype(BF16).astype(F32)
            o = att[:, (h // 2) * LANE : (h // 2 + 1) * LANE]
            inner = jnp.sum(g * o, -1, keepdims=True)
            hi = inner.astype(BF16).astype(F32)
            g = jnp.where(lane == e, -hi, g)
            g = jnp.where(lane == e + 1, hi - inner, g)
            ge[:, h * LANE : (h + 1) * LANE] = g.astype(BF16)
        dqt[...] = jnp.zeros(dqt.shape, F32)
        chunk(0)

    s1 = step - 1

    @pl.when(jnp.logical_and(s1 >= 0, s1 < scenes))
    def _():
        for target in range(used):
            to_sib(s1, target).wait()
            acc[s1, target] = plus(own[lax.rem(s1, 2), core, target], sib_land[s1, target])

    s_up = step - 1 - chip

    @pl.when(jnp.logical_and(s_up >= 0, s_up < scenes))
    def _():
        for target in reversed(range(1, used)):

            @pl.when(target > chip)
            def _(target=target):
                @pl.when(chip > 0)
                def _():
                    to_up(s_up, target).wait_recv()
                    acc[s_up, target] = plus(acc[s_up, target], up_land[s_up, target])

                to_up(s_up, target).start()

    s_down = step - chips + chip

    @pl.when(jnp.logical_and(s_down >= 0, s_down < scenes))
    def _():
        for target in range(used):

            @pl.when(target < chip)
            def _(target=target):
                @pl.when(chip < chips - 1)
                def _():
                    to_down(s_down, target).wait_recv()
                    acc[s_down, target] = plus(acc[s_down, target], down_land[s_down, target])

                to_down(s_down, target).start()

    s_end = step - chips

    @pl.when(s_end >= 0)
    def _():
        @pl.when(chip < used)
        def _():
            grn_ref[s_end] = acc[s_end, chip].astype(F32)

            @pl.when(chip > 0)
            def _():
                to_up(s_end, chip).wait_recv()
                grn_ref[s_end] += up_land[s_end, chip].astype(F32)

            @pl.when(chip < chips - 1)
            def _():
                to_down(s_end, chip).wait_recv()
                grn_ref[s_end] += down_land[s_end, chip].astype(F32)

        @pl.when(chip >= used)
        def _():
            grn_ref[s_end] = jnp.zeros((keys, cp), F32)

    for t in range(1, steps - 1):

        @pl.when(step == t)
        def _(t=t):
            for k in range(t * each, min((t + 1) * each, sums.ops + 1)):
                sums.advance(k)
            if t * each <= sums.ops < (t + 1) * each:
                pltpu.make_async_copy(done, sum_hbm, sum_sem.at[0]).start()

    def tail(i, s):
        rhat, rstd = centered(red_ref[i], channels)
        inside = lanes((keys, cp)) < channels
        upstream = jnp.where(inside, grn_ref[s], 0.0)
        dvec_ref[0:1] += jnp.sum(upstream * rhat, 0, keepdims=True)
        dvec_ref[1:2] += jnp.sum(upstream, 0, keepdims=True)
        gred = norm_back(upstream, vec_ref[2:3], rhat, rstd, channels)
        gred = jnp.where(inside, gred, 0.0).astype(BF16)
        gred_t = gred.T
        x = widen(tok_ref[i].astype(F32), cp)
        xhat, xstd = centered(x, channels)
        low = (xhat * vec_ref[0:1] + vec_ref[1:2]).astype(BF16)
        lowf = low.astype(F32)
        for t in range(lt):
            scr[i, t] = lowf[:, t * LANE : (t + 1) * LANE]
        for b in range(2):
            part = [scr[i, t, pl.ds(b, n // 2, stride=2), :] for t in range(lt)]
            part = jnp.concatenate(part, -1).reshape(height // 2, 2, width // 2, cp)
            for a in range(2):
                ab = 2 * a + b
                dwrt[ab] += dot(gred_t, part[:, a].reshape(keys, cp).astype(BF16))
                back = dot_nt(gred, wr_ref[ab])
                for t in range(lt):
                    for r in range(height // 2):
                        gscr[i, t, pl.ds((2 * r + a) * width + b, width // 2, stride=2), :] = back[
                            r * (width // 2) : (r + 1) * (width // 2), t * LANE : (t + 1) * LANE
                        ]
        gqt = gqt_ref[s]
        dwqt[...] += dot(gqt, low)
        gn = widen(dot_nt(gqt.T, wq_ref[...]), cp)
        gn = gn + jnp.concatenate([gscr[i, t] for t in range(lt)], -1)
        dvec_ref[3:4] += jnp.sum(gn * xhat, 0, keepdims=True)
        dvec_ref[4:5] += jnp.sum(gn, 0, keepdims=True)
        gx = norm_back(gn, vec_ref[0:1], xhat, xstd, channels)
        ig_ref[i] = gres2_ref[i] + gx[:, :channels]

    @pl.when(step >= scenes)
    def _():
        for i in range(together):
            tail(i, (step - scenes) * together + i)

    @pl.when(step < scenes)
    def _():
        s = step
        for j in range(1, count):
            chunk(j)
        for h in range(HEADS):
            base = h * LANE + (0 if h % 2 == 0 else HALF)
            gqt_ref[s, h * HALF : (h + 1) * HALF] = (
                dqt[base : base + HALF, :] * head_size**-0.5
            ).astype(BF16)

    @pl.when(step == steps - 1)
    def _():
        pltpu.make_async_copy(done, sum_hbm, sum_sem.at[0]).wait()

        @pl.loop(0, scenes)
        def _(s):
            for target in range(used):

                @pl.when(target > chip)
                def _(target=target):
                    to_up(s, target).wait_send()

                @pl.when(target < chip)
                def _(target=target):
                    to_down(s, target).wait_send()


def attback(
    dims, ff, ndp, blk, used, cid, q, att, gres, ke, ve, rn, tok, red, vec, wpe, wkv, wq, wr, first
):
    scenes, height, width, channels, cp = dims
    n = height * width
    keys = n // 4
    chips = blk // 2
    lt = cp // LANE
    live = 2 * used * keys
    he = HEADS * LANE
    together = -(-scenes // chips)
    assert scenes == together * chips
    ops = 2 * len(orders_of(ndp, blk)[0])

    def early(shape):
        return pl.BlockSpec(
            (1,) + shape, lambda t: (jnp.minimum(t, scenes - 1),) + (0,) * len(shape)
        )

    def late(shape):
        return pl.BlockSpec(
            (together,) + shape, lambda t: (jnp.maximum(t - scenes, 0),) + (0,) * len(shape)
        )

    land = (scenes, used, keys, cp)
    hbm = pl.BlockSpec(memory_space=pl.ANY)
    vm = pl.BlockSpec(memory_space=pltpu.VMEM)
    return pl.pallas_call(
        functools.partial(attback_kernel, dims, ff, ndp, blk, used),
        grid=(scenes + chips,),
        in_specs=[
            early((n, he)),
            early((n, cp)),
            early((n, channels)),
            early((live, he)),
            early((live, he)),
            early((live, cp)),
            late((n, channels)),
            late((n, channels)),
            late((keys, cp)),
            vm, vm, vm, vm, vm, hbm,
        ],
        out_specs=[late((n, channels))] + [vm] * 6 + [hbm],
        out_shape=[
            jax.ShapeDtypeStruct((scenes, n, channels), F32),
            jax.ShapeDtypeStruct((channels, cp), F32),
            jax.ShapeDtypeStruct((4, cp, cp), F32),
            jax.ShapeDtypeStruct((cp, cp), F32),
            jax.ShapeDtypeStruct((cp, 2 * cp), F32),
            jax.ShapeDtypeStruct((8, cp), F32),
            jax.ShapeDtypeStruct((8, cp), F32),
            jax.ShapeDtypeStruct(first.shape, BF16),
        ],
        scratch_shapes=[
            pltpu.VMEM((n, he), BF16),
            pltpu.VMEM((he, n), F32),
            pltpu.VMEM((scenes, channels, n), BF16),
            pltpu.VMEM((scenes, keys, cp), F32),
            pltpu.VMEM((together, lt, n, LANE), F32),
            pltpu.VMEM((together, lt, n, LANE), F32),
            pltpu.VMEM((2, 2, used, keys, cp), BF16),
        ]
        + [pltpu.VMEM(land, BF16)] * 4
        + [pltpu.VMEM(first.shape, BF16)] * 3
        + [pltpu.SemaphoreType.DMA((scenes, used))] * 6
        + [pltpu.SemaphoreType.DMA((3, ops, widest(ndp, blk)))] * 2
        + [pltpu.SemaphoreType.DMA((1,))],
        compiler_params=pltpu.CompilerParams(
            vmem_limit_bytes=VMEM, collective_id=cid, has_side_effects=True
        ),
    )(q, att, gres, ke, ve, rn, tok, gres, red, vec, wpe, wkv, wq, wr, first)


def reduce_kernel(
    channels, ff, ndp, nblk, dwr, dwkv, dwp, dwq, dtap, dtb, dvec2, dvec1, dbp, cnt,
    out_hbm, small_hbm, work, recv, done, swork, srecv, sdone, send_sem, recv_sem, out_sem,
):
    ndev = ndp * nblk
    cp = up_to(channels, LANE)
    orders = orders_of(ndp, nblk)
    plan, used, sizes = rest_plan(channels, ndev)
    splan, srows = small_plan(channels, ff, ndev)
    barrier = pltpu.get_barrier_semaphore()
    peers = peers_of(orders[0])
    for peer in peers:
        pl.semaphore_signal(barrier, inc=1, device_id=peer, device_id_type=pl.DeviceIdType.MESH)

    def put(name, ref):
        at, rows, slabs = plan[name]
        for t in range(slabs):
            work[at + t * rows : at + (t + 1) * rows, :] = ref(t, rows).astype(BF16)

    def lane_slabs(ref):
        return lambda t, rows: ref[:rows, t * LANE : (t + 1) * LANE]

    per = cp // LANE
    put("wr", lambda t, rows: dwr[t // per, :rows, (t % per) * LANE : (t % per + 1) * LANE])
    put("wkv", lane_slabs(dwkv))
    put("wp", lane_slabs(dwp))
    put("wq", lane_slabs(dwq))
    if used < sum(sizes):
        work[used:, :] = jnp.zeros((sum(sizes) - used, LANE), BF16)
    swork[...] = jnp.zeros(swork.shape, F32)
    at, rows, slabs = splan["tap"]
    db = jnp.sum(dtb[...], 0, keepdims=True)
    for t in range(slabs):
        cut = slice(t * LANE, (t + 1) * LANE)
        swork[at + t * rows : at + t * rows + 9, :] = dtap[:, cut]
        swork[at + t * rows + 9 : at + t * rows + 10, :] = db[:, cut]
    at, rows, slabs = splan["vec"]
    pb = jnp.sum(dbp[...], 0, keepdims=True)
    for t in range(slabs):
        cut = slice(t * LANE, (t + 1) * LANE)
        swork[at + t * rows : at + t * rows + 3, :] = dvec2[0:3, cut]
        swork[at + t * rows + 3 : at + t * rows + 8, :] = dvec1[0:5, cut]
        swork[at + t * rows + 8 : at + t * rows + 9, :] = pb[:, cut]
    at, rows, _ = splan["count"]
    swork[at : at + rows, :] = cnt[...]

    pl.semaphore_wait(barrier, len(peers))
    parts = three_parts(work, recv, done, sizes, orders)
    parts.append((swork, srecv, sdone, 0, srows, orders[0]))
    sums = Sums(parts, send_sem, recv_sem)
    for k in range(sums.ops + 1):
        sums.advance(k)

    a = pltpu.make_async_copy(done, out_hbm, out_sem.at[0])
    b = pltpu.make_async_copy(sdone, small_hbm, out_sem.at[1])
    a.start()
    b.start()
    a.wait()
    b.wait()


def reduce_all(channels, ff, ndp, nblk, *grads):
    ndev = ndp * nblk
    ops = 2 * len(orders_of(ndp, nblk)[0])
    wide = widest(ndp, nblk)
    _, _, sizes = rest_plan(channels, ndev)
    _, srows = small_plan(channels, ff, ndev)
    total = sum(sizes)
    vm = pl.BlockSpec(memory_space=pltpu.VMEM)
    hbm = pl.BlockSpec(memory_space=pl.ANY)
    return pl.pallas_call(
        functools.partial(reduce_kernel, channels, ff, ndp, nblk),
        in_specs=[vm] * len(grads),
        out_specs=[hbm, hbm],
        out_shape=[
            jax.ShapeDtypeStruct((total, LANE), BF16),
            jax.ShapeDtypeStruct((srows, LANE), F32),
        ],
        scratch_shapes=[pltpu.VMEM((total, LANE), BF16)] * 3
        + [pltpu.VMEM((srows, LANE), F32)] * 3
        + [
            pltpu.SemaphoreType.DMA((4, ops, wide)),
            pltpu.SemaphoreType.DMA((4, ops, wide)),
            pltpu.SemaphoreType.DMA((2,)),
        ],
        compiler_params=pltpu.CompilerParams(
            vmem_limit_bytes=VMEM, collective_id=1, has_side_effects=True
        ),
    )(*grads)


def unpack_kernel(channels, ff, ndev, out_in, ig_in, first, packed, small, *outs):
    cp = up_to(channels, LANE)
    plans = ((first, ffn_plan(channels, ff, ndev)[0]), (packed, rest_plan(channels, ndev)[0]))
    splan, _ = small_plan(channels, ff, ndev)
    out, ig, g1, b1, wq, qb, wr, rb, rg, rbn, wkv, vb, wp, pb, g2, b2, we, eb, dt, db, ws, sb, cm, out_hold, ig_hold, in_sem, out_sem = (
        outs
    )
    ins, moves = [], []
    for k, (src, hold, dst) in enumerate(((out_in, out_hold, out), (ig_in, ig_hold, ig))):
        for s in range(src.shape[0]):
            ins.append(pltpu.make_async_copy(src.at[s], hold.at[s], in_sem.at[k, s]))
            moves.append(pltpu.make_async_copy(hold.at[s], dst.at[s], out_sem.at[k, s]))
    for copy in ins:
        copy.start()
    lt = cp // LANE

    for copy, move in zip(ins, moves):
        copy.wait()
        move.start()

    def slab(name, t, first=0, count=None):
        ref, plan = plans[0] if name in plans[0][1] else plans[1]
        at, rows, _ = plan[name]
        count = rows if count is None else count
        return ref[at + t * rows + first : at + t * rows + first + count, :].astype(F32)

    for t in range(ff // LANE):
        cut = slice(t * LANE, (t + 1) * LANE)
        we[:, cut] = slab("we", t, 0, channels)
        eb[cut] = slab("we", t, channels, 16)[0]
        ws[:, cut] = slab("ws", t)
        at, rows, _ = splan["tap"]
        dt[:, cut] = small[at + t * rows : at + t * rows + 9, :]
        db[cut] = small[at + t * rows + 9, :]

    def wide(name, first, count=None, base=0):
        return jnp.concatenate([slab(name, base + t, first, count) for t in range(lt)], -1)

    parts = [wide("wr", 0, base=ab * lt) for ab in range(4)]
    wr[...] = jnp.concatenate([v[:, :channels] for v in parts], -1)
    rb[...] = parts[0].T[channels]
    turned = wide("wq", 0).T
    wq[...] = turned[:channels]
    qb[...] = turned[channels]
    wp[...] = wide("wp", 0)[:, :channels]
    wkv[...] = jnp.concatenate(
        [wide("wkv", 0, channels)[:, :channels], wide("wkv", 0, channels, lt)[:, :channels]], -1
    )
    vb[...] = wide("wkv", channels, 16, lt)[1, :channels]
    at, rows, _ = splan["vec"]
    vec = jnp.concatenate([small[at + t * rows : at + (t + 1) * rows, :] for t in range(lt)], -1)
    vec = vec[:, :channels]
    for k, ref in enumerate((g2, b2, sb, rg, rbn, None, g1, b1, pb)):
        if ref is not None:
            ref[...] = vec[k]
    at, rows, _ = splan["count"]
    cm[...] = small[at : at + rows, :].astype(jnp.int32)[:CLASSES, :CLASSES]
    for move in moves:
        move.wait()


def unpack(channels, ff, ndev, out, ig, first, packed, small):
    one = (channels,)
    shapes = [
        one, one, (channels, channels), one, (channels, 4 * channels), one, one, one,
        (channels, 2 * channels), one, (channels, channels), one, one, one, (channels, ff), (ff,),
        (9, ff), (ff,), (channels, ff), one,
    ]
    outs = [jax.ShapeDtypeStruct(v, F32) for v in shapes]
    outs.append(jax.ShapeDtypeStruct((CLASSES, CLASSES), jnp.int32))
    vm = pl.BlockSpec(memory_space=pltpu.VMEM)
    hbm = pl.BlockSpec(memory_space=pl.ANY)
    return pl.pallas_call(
        functools.partial(unpack_kernel, channels, ff, ndev),
        in_specs=[hbm, hbm, vm, vm, vm],
        out_specs=[hbm, hbm] + [vm] * len(outs),
        out_shape=[jax.ShapeDtypeStruct(v.shape, v.dtype) for v in (out, ig)] + outs,
        scratch_shapes=[
            pltpu.VMEM(out.shape, out.dtype),
            pltpu.VMEM(ig.shape, ig.dtype),
            pltpu.SemaphoreType.DMA((2, out.shape[0])),
            pltpu.SemaphoreType.DMA((2, out.shape[0])),
        ],
        compiler_params=pltpu.CompilerParams(vmem_limit_bytes=VMEM),
    )(out, ig, first, packed, small)


NEG = np.float32(NEGATIVE * LOG2E)
NEG_HI = np.float32(ml_dtypes.bfloat16(NEG))
NEG_MID = np.float32(ml_dtypes.bfloat16(NEG - NEG_HI))
NEG_LO = np.float32(ml_dtypes.bfloat16(NEG - NEG_HI - NEG_MID))


def ext_row(values):
    lane = lanes((1, HEADS * LANE))
    row = jnp.zeros((1, HEADS * LANE), F32)
    for h in range(HEADS):
        for k, value in values.items():
            row = jnp.where(lane == h * LANE + ext_lane(h) + k, value, row)
    return row


def spread(value, cp):
    value = widen(value, cp)
    half = lanes((1, LANE)) // HALF
    blocks = []
    for h in range(HEADS):
        tile = value[:, (h // 2) * LANE : (h // 2 + 1) * LANE]
        blocks.append(jnp.where(half == h % 2, tile, jnp.zeros_like(tile)))
    return jnp.concatenate(blocks, -1)


def split_low(value):
    hi = value.astype(BF16).astype(F32)
    return hi, value - hi


def rows16(*rows):
    width = rows[0].shape[-1]
    at = lax.broadcasted_iota(jnp.int32, (16, width), 0)
    block = jnp.zeros((16, width), F32)
    for k, row in enumerate(rows):
        block = jnp.where(at == k, row, block)
    return block.astype(BF16)


def prep_kernel(
    channels, g1, b1, qw, qb, rw, rb, rg, rbn, kvw, vb, pw, pb, g2, b2, ew, eb, tb, sw, sb,
    vec, wq, wk, wv, wp, wpe, wkv, wr, we, ws, one, dbias, full,
):
    cp = up_to(channels, LANE)
    he = HEADS * LANE
    ff = ew.shape[1]
    head_size = channels // HEADS
    rest = cp - channels - 16

    def row(ref):
        return ref[...].reshape(1, ref.shape[-1])

    lane = lanes((1, cp))

    def padded(ref, *at):
        v = widen(row(ref), cp)
        for k in at:
            v = jnp.where(lane == channels + k, 1.0, v)
        return v

    for k, v in enumerate(
        (
            padded(g1), padded(b1, 0, 1), padded(rg), padded(rbn, 1, 2), padded(pb), padded(g2),
            padded(b2, 0, 1), padded(sb),
        )
    ):
        vec[k : k + 1, :] = v

    def fill(ref, top, *rows):
        width = ref.shape[-1]
        ref[:channels, :] = top
        ref[channels : channels + 16, :] = (
            rows16(*rows) if rows else jnp.zeros((16, width), BF16)
        )
        if rest:
            ref[channels + 16 :, :] = jnp.zeros((rest, width), BF16)

    ones = ext_row({0: 1.0, 1: 1.0, 2: 1.0})
    one[...] = ones
    dbias[...] = row(tb)
    qs = spread(qw[...], cp)
    qb_hi, qb_lo = split_low(row(qb))
    fill(wq, qs, spread(qb_hi, cp), spread(qb_lo, cp))
    kw = widen(kvw[:, :channels], cp)
    vw = widen(kvw[:, channels:], cp)
    ks = spread(kvw[:, :channels], cp)
    nil = jnp.zeros((1, he), F32)
    fill(
        wk, ks, ext_row({0: float(NEG_HI), 1: float(NEG_MID), 2: float(NEG_LO)}),
        ext_row({3: 1.0, 4: 1.0, 5: 1.0}),
    )
    vb_hi, vb_lo = split_low(row(vb))
    fill(wv, spread(kvw[:, channels:], cp), nil, spread(vb_hi, cp) + ones, spread(vb_lo, cp))
    p = widen(pw[...], cp)
    fill(wp, p)
    zero = jnp.zeros((HALF, cp), BF16)
    for h in range(HEADS):
        data, other = (0, HALF) if h % 2 == 0 else (HALF, 0)
        wpe[h * LANE + data : h * LANE + data + HALF, :] = p[h * HALF : (h + 1) * HALF]
        wpe[h * LANE + other : h * LANE + other + HALF, :] = zero
    fill(wkv, jnp.concatenate([kw, vw], -1))
    rb_rows = [widen(v, cp) for v in split_low(row(rb))]
    rw_rows = rw[...].T
    for ab in range(4):
        fill(
            wr.at[ab], widen(rw_rows[ab * channels : (ab + 1) * channels, :], cp),
            *rb_rows[ab : ab + 1],
        )
    fill(we, ew[...], *split_low(row(eb)))
    fill(ws, sw[...])

    def norm(v):
        return jnp.sqrt(jnp.sum(v * v, (0, 1), keepdims=True))

    root = channels**0.5

    def reach(gain, bias):
        top = jnp.max(jnp.abs(row(gain)), (0, 1), keepdims=True)
        return root * top + norm(row(bias))

    query_in, key_in = reach(g1, b1), reach(rg, rbn)
    qb_wide = spread(row(qb), cp)
    bound = jnp.zeros((1, 1), F32)
    for h in range(HEADS):
        cut = slice(h * LANE, (h + 1) * LANE)
        query = query_in * norm(qs[:, cut].astype(F32)) + norm(qb_wide[:, cut])
        key = key_in * norm(ks[:, cut].astype(F32))
        bound = jnp.maximum(bound, query * key)
    bound = bound * (head_size**-0.5 * 1.05)
    full[...] = jnp.where(2.0 * bound + 256.0 < -NEGATIVE, 0, 1).astype(jnp.int32)


def prep(channels, *weights):
    cp = up_to(channels, LANE)
    he = HEADS * LANE
    ff = weights[14].shape[1]
    shapes = [
        ((8, cp), F32), ((cp, he), BF16), ((cp, he), BF16), ((cp, he), BF16), ((cp, cp), BF16),
        ((he, cp), BF16), ((cp, 2 * cp), BF16), ((4, cp, cp), BF16), ((cp, ff), BF16),
        ((cp, ff), BF16), ((1, he), F32), ((1, ff), F32), ((1, 1), jnp.int32),
    ]
    return pl.pallas_call(
        functools.partial(prep_kernel, channels),
        out_shape=[jax.ShapeDtypeStruct(*v) for v in shapes],
        compiler_params=pltpu.CompilerParams(vmem_limit_bytes=VMEM),
    )(*weights)


def body(
    tokens, mask, labels, predicted, cotangent, norm1_gain, norm1_bias, query_weight, query_bias,
    reduce_weight, reduce_bias, rnorm_gain, rnorm_bias, kv_weight, value_bias, proj_weight,
    proj_bias, norm2_gain, norm2_bias, expand_weight, expand_bias, depth_weight, depth_bias,
    shrink_weight, shrink_bias,
):
    scenes, height, width, channels = tokens.shape
    ndp, blk = lax.axis_size("dp"), lax.axis_size("blk")
    n = height * width
    ff = expand_weight.shape[1]
    dims = (scenes, height, width, channels, up_to(channels, LANE))
    chips = blk // 2
    used = min(chips, -(-MASK_ROWS // (2 * height)))

    vec, wq, wk, wv, wp, wpe, wkv, wr, we, ws, ones, tap_bias, full = prep(
        channels, norm1_gain, norm1_bias, query_weight, query_bias, reduce_weight.T, reduce_bias,
        rnorm_gain, rnorm_bias, kv_weight, value_bias, proj_weight, proj_bias, norm2_gain,
        norm2_bias, expand_weight, expand_bias, depth_bias, shrink_weight.T, shrink_bias,
    )
    full = full[0, 0] > 0

    def either(call, cids, sizes, *operands):
        if used == chips:
            return call(*sizes, chips, cids[1], *operands)
        return lax.cond(
            full,
            functools.partial(call, *sizes, chips, cids[1]),
            functools.partial(call, *sizes, used, cids[0]),
            *operands,
        )

    tok = tokens.reshape(scenes, n, channels)
    ct = cotangent.reshape(scenes, n, channels)
    red, counts, q, att, ke, ve, rn, res = either(
        attend, (2, 3), (dims, blk), tok, mask, labels, predicted, vec, wr, wq, ones, wk, wv, wp
    )
    out, gres, first, dtap, dtb, dvec2 = ffn(
        dims, blk, ndp * blk, res, ct, vec, we, ws, depth_weight, tap_bias
    )
    ig, dwqt, dwrt, dwp, dwkv, dbp, dvec1, first = either(
        attback, (4, 5), (dims, ff, ndp, blk), q, att, gres, ke, ve, rn, tok, red, vec, wpe, wkv,
        query_weight, wr, first,
    )
    packed, small = reduce_all(
        channels, ff, ndp, blk, dwrt, dwkv, dwp, dwqt, dtap, dtb, dvec2, dvec1, dbp, counts
    )
    out, ig, *grads = unpack(channels, ff, ndp * blk, out, ig, first, packed, small)
    grads[4], grads[18] = grads[4].T, grads[18].T
    return (out.reshape(tokens.shape), ig.reshape(tokens.shape), *grads)


def solution(mesh):
    banded = P("dp", "blk", None, None)
    plane = P("dp", "blk", None)
    in_specs = (banded, plane, plane, plane, banded) + (P(),) * 20
    out_specs = (banded, banded) + (P(),) * 21
    return jax.shard_map(body, mesh=mesh, in_specs=in_specs, out_specs=out_specs, check_vma=False)
```

```python
import functools

import jax
import jax.numpy as jnp
from jax import lax
from jax.experimental import pallas as pl
from jax.experimental.pallas import tpu as pltpu
from jax.sharding import PartitionSpec as P
import ml_dtypes
import numpy as np

HEADS = 5
CLASSES = 19
EPSILON = 1e-06
NEGATIVE = -32768.0
LOG2E = 1.4426950408889634
LN2 = 0.6931471805599453
F32 = jnp.float32
BF16 = jnp.bfloat16
LANE = 128
HALF = 64
KEY_CHUNK = 256
MASK_ROWS = 48
VMEM = 62 * 2**20
FF_CHUNK = 256
GROUP = 8
NEG = np.float32(NEGATIVE * LOG2E)
NEG_HI = np.float32(ml_dtypes.bfloat16(NEG))
NEG_MID = np.float32(ml_dtypes.bfloat16(NEG - NEG_HI))
NEG_LO = np.float32(ml_dtypes.bfloat16(NEG - NEG_HI - NEG_MID))


def up_to(value, step):
    return -(-value // step) * step


def dot(a, b):
    return lax.dot_general(a, b, (((1,), (0,)), ((), ())), preferred_element_type=F32)


def dot_nt(a, b):
    return lax.dot_general(a, b, (((1,), (1,)), ((), ())), preferred_element_type=F32)


def dot_tn(a, b):
    return lax.dot_general(a, b, (((0,), (0,)), ((), ())), preferred_element_type=F32)


def lanes(shape):
    return lax.broadcasted_iota(jnp.int32, shape, len(shape) - 1)


def whole(shape):
    return pl.BlockSpec(shape, lambda *_: (0,) * len(shape))


def per_scene(shape):
    return pl.BlockSpec((1,) + shape, lambda s: (s,) + (0,) * len(shape))


def inside(value, channels):
    full = channels // LANE * LANE
    if full == value.shape[-1]:
        return value
    last = value[..., full:]
    last = jnp.where(lanes(last.shape) < channels - full, last, 0.0)
    return jnp.concatenate([value[..., :full], last], -1)


def head_blocks(value, free):
    half = lanes((1, LANE)) // HALF
    fills = [free(0), free(1)]
    return [
        jnp.where(half == h % 2, value[:, h // 2 * LANE : (h // 2 + 1) * LANE], fills[h % 2])
        for h in range(HEADS)
    ]


def free_row(parity, values):
    lane = lanes((1, LANE))
    row = jnp.zeros((1, LANE), F32)
    for k, value in values.items():
        row = jnp.where(lane == ext_lane(parity) + k, value, row)
    return row


def centered(value, channels):
    mean = jnp.sum(value, -1, keepdims=True) * (1.0 / channels)
    center = inside(value - mean, channels)
    var = jnp.sum(center * center, -1, keepdims=True) * (1.0 / channels)
    rstd = lax.rsqrt(var + EPSILON)
    return center * rstd, rstd


def norm_back(up, gain, xhat, rstd, channels):
    u = up * gain
    mean = jnp.sum(u, -1, keepdims=True) * (1.0 / channels)
    proj = jnp.sum(u * xhat, -1, keepdims=True) * (1.0 / channels)
    return (u - mean - xhat * proj) * rstd


def ext_lane(head):
    return HALF if head % 2 == 0 else 0


def widen(value, width):
    pad = width - value.shape[-1]
    return jnp.concatenate([value, jnp.zeros(value.shape[:-1] + (pad,), value.dtype)], -1)


def place(blk):
    me = lax.axis_index("blk")
    core = lax.rem(me, 2)
    chip = me // 2
    return chip, core, {"blk": me + 2}, {"blk": me - 2}, {"blk": me + 1 - 2 * core}


def greet(chip, chips, up, down, sib):
    barrier = pltpu.get_barrier_semaphore()
    MESH = pl.DeviceIdType.MESH
    has_up, has_down = chip < chips - 1, chip > 0
    pl.semaphore_signal(barrier, inc=1, device_id=sib, device_id_type=MESH)

    @pl.when(has_up)
    def _():
        pl.semaphore_signal(barrier, inc=1, device_id=up, device_id_type=MESH)

    @pl.when(has_down)
    def _():
        pl.semaphore_signal(barrier, inc=1, device_id=down, device_id_type=MESH)

    pl.semaphore_wait(barrier, 1 + has_up.astype(jnp.int32) + has_down.astype(jnp.int32))


def remote(src, dst, send, recv, device):
    return pltpu.make_async_remote_copy(
        src_ref=src, dst_ref=dst, send_sem=send, recv_sem=recv, device_id=device,
        device_id_type=pl.DeviceIdType.MESH,
    )


def groups_of(ndp, nblk):
    dp_bits, blk_bits = ndp.bit_length() - 1, nblk.bit_length() - 1
    assert ndp == 1 << dp_bits and nblk == 1 << blk_bits
    core = [("blk", 0, 2)] if blk_bits else []
    if dp_bits > 2:
        plane = [("dp", 0, 1 << dp_bits // 2), ("dp", dp_bits // 2, 1 << (dp_bits - dp_bits // 2))]
    else:
        plane = [("dp", 0, ndp)] if dp_bits else []
    line = [("blk", 1, nblk // 2)] if blk_bits > 1 else []
    return core, plane, line


def lay_out(items, ndev):
    plan, at = {}, 0
    for name, rows, slabs in items:
        plan[name] = (at, rows, slabs)
        at += rows * slabs
    unit = 16 * ndev
    units = -(-at // unit)
    last = units // 3 - (1 if units > 6 else 0)
    mid = (units - last) // 2
    return plan, at, [(units - last - mid) * unit, mid * unit, last * unit]


def ffn_plan(channels, ff, ndev):
    tall = up_to(channels + 2, 16)
    return lay_out([("we", tall, ff // LANE), ("ws", channels, ff // LANE)], ndev)


def rest_plan(channels, ndev):
    cp = up_to(channels, LANE)
    tall = up_to(channels + 2, 16)
    return lay_out(
        [
            ("wr", channels, 4 * cp // LANE), ("wkv", tall, 2 * cp // LANE),
            ("wp", channels, cp // LANE), ("wq", channels, cp // LANE),
        ],
        ndev,
    )


def small_plan(channels, ff, ndev):
    cp = up_to(channels, LANE)
    plan = {"tap": (0, 16, ff // LANE)}
    at = 16 * (ff // LANE)
    plan["vec"] = (at, 16, cp // LANE)
    at += 16 * (cp // LANE)
    plan["count"] = (at, 32, 1)
    at += 32
    return plan, up_to(at, 8 * ndev)


def member(group):
    axis, bit, size = group
    return lax.rem(lax.axis_index(axis) // (1 << bit), size)


def other(group, index):
    axis, bit, _ = group
    return {axis: lax.axis_index(axis) + (index - member(group)) * (1 << bit)}


def peers_of(order):
    return [
        other(group, lax.rem(member(group) + d, group[2])) for group in order for d in range(1, group[2])
    ]


class Sums:
    def __init__(self, parts, send_sem, recv_sem):
        self.parts, self.send_sem, self.recv_sem = parts, send_sem, recv_sem
        self.rounds = len(parts[0][5])
        self.ops = 2 * self.rounds

    def unit(self, p):
        return 16 if self.parts[p][0].dtype == BF16 else 8

    def segment(self, p, i):
        _, _, _, start, rows, order = self.parts[p]
        for group in order[:i]:
            rows //= group[2]
            start = start + member(group) * rows
        return start, rows

    def landing(self, p, i):
        _, _, _, first, rows, order = self.parts[p]
        for group in order[:i]:
            first += rows // group[2] * (group[2] - 1)
            rows //= group[2]
        return first

    def copies(self, p, k):
        buf, land, done, _, _, order = self.parts[p]
        unit = self.unit(p)
        halving = k < self.rounds
        i = k if halving else self.ops - 1 - k
        group = order[i]
        size = group[2]
        me = member(group)
        result = []
        for d in range(1, size):
            to = lax.rem(me + d, size)
            if halving:
                start, rows = self.segment(p, i)
                rows //= size
                src = buf.at[pl.ds(pl.multiple_of(start + to * rows, unit), rows), :]
                low = self.landing(p, i) + (size - 1 - d) * rows
                dst = land.at[pl.ds(low, rows), :]
            else:
                start, rows = self.segment(p, i + 1)
                src = done.at[pl.ds(pl.multiple_of(start, unit), rows), :]
                dst = src
            result.append(
                remote(
                    src, dst, self.send_sem.at[p, k, d - 1], self.recv_sem.at[p, k, d - 1],
                    other(group, to),
                )
            )
        return result

    def start(self, p, k):
        for copy in self.copies(p, k):
            copy.start()

    def finish(self, p, k):
        for copy in self.copies(p, k):
            copy.wait()
        if k >= self.rounds:
            return
        buf, land, done, _, _, order = self.parts[p]
        unit = self.unit(p)
        keep, rows = self.segment(p, k + 1)
        low = self.landing(p, k)
        step = next(c for c in (256, 128, 64, 32, 16, 8) if rows % c == 0)
        into = done if k == self.rounds - 1 else buf

        @pl.loop(0, rows // step)
        def _(j):
            mine = pl.ds(pl.multiple_of(keep + j * step, unit), step)
            total = buf[mine, :].astype(F32)
            for d in range(order[k][2] - 1):
                theirs = pl.ds(pl.multiple_of(low + d * rows + j * step, unit), step)
                total = total + land[theirs, :].astype(F32)
            into[mine, :] = total.astype(buf.dtype)

    def advance(self, k):
        for p in range(len(self.parts)):
            if k > 0:
                self.finish(p, k - 1)
            if k < self.ops:
                self.start(p, k)


def three_parts(buf, land, done, sizes, orders):
    parts, at = [], 0
    for size, order in zip(sizes, orders):
        if size:
            parts.append((buf, land, done, at, size, order))
        at += size
    return parts


def orders_of(ndp, nblk):
    core, plane, line = groups_of(ndp, nblk)
    return [core + plane + line, core + plane + line, core + line + plane]


def widest(ndp, nblk):
    return max(group[2] for group in orders_of(ndp, nblk)[0]) - 1


def packed_rows(keys, cp):
    return (cp // LANE - 1) * keys + keys // 2 + 16


def pack_block(value, unc, keys, cp):
    full = cp // LANE - 1
    last = value[:, full * LANE :]
    turned = pltpu.roll(last[keys // 2 :], HALF, 1)
    last = jnp.where(lanes((1, LANE)) < HALF, last[: keys // 2], turned)
    flags = jnp.broadcast_to(unc, (keys, LANE))
    if keys < LANE:
        flags = jnp.concatenate([flags, jnp.zeros((LANE - keys, LANE), F32)], 0)
    parts = [value[:, t * LANE : (t + 1) * LANE] for t in range(full)] + [last, flags.T[:16]]
    return jnp.concatenate([v.astype(BF16) for v in parts], 0)


def unpack_block(block, ones, keys, cp):
    full = cp // LANE - 1
    parts = [block[t * keys : (t + 1) * keys] for t in range(full)]
    last = block[full * keys : full * keys + keys // 2].astype(F32)
    last = jnp.concatenate([last, pltpu.roll(last, HALF, 1)], 0)
    last = jnp.where(lanes((1, LANE)) < HALF, last, ones)
    flags = block[full * keys + keys // 2 :].astype(F32)[0:1]
    flags = jnp.broadcast_to(flags, (LANE, LANE)).T[:keys]
    return jnp.concatenate(parts + [last.astype(BF16)], -1), flags


def attend_kernel(
    dims, blk, used, tok_ref, mask_ref, label_ref, pred_ref, tok2_ref, vec_ref, wr_ref, wq_ref,
    wkv_ref, wp_ref,
    red_ref, cnt_ref, q_ref, att_ref, ke_ref, ve_ref, rn_ref, res_ref,
    scr, qbuf, oe, rnbuf, up_send, down_send, sib_send, line_recv, sib_recv,
):
    scenes, height, width, channels, cp = dims
    n = height * width
    keys = n // 4
    chips = blk // 2
    lag = chips
    step = pl.program_id(0)
    head_size = channels // HEADS
    chip, core, up, down, sib = place(blk)

    @pl.when(step == 0)
    def _():
        greet(chip, chips, up, down, sib)
        cnt_ref[...] = jnp.zeros(cnt_ref.shape, F32)

    def slot(origin, c):
        return c * used + origin

    def send_up(s, origin):
        place_ = rnbuf.at[s, slot(origin, core)]
        return remote(place_, place_, up_send.at[s, origin], line_recv.at[s, origin], up)

    def send_down(s, origin):
        place_ = rnbuf.at[s, slot(origin, core)]
        return remote(place_, place_, down_send.at[s, origin], line_recv.at[s, origin], down)

    def send_sib(s, origin):
        place_ = rnbuf.at[s, slot(origin, core)]
        return remote(place_, place_, sib_send.at[s, origin], sib_recv.at[s, origin], sib)

    @pl.when(step < scenes)
    def _():
        s = step
        x = widen(tok_ref[0].astype(F32), cp)
        xhat, _ = centered(x, channels)
        low = (xhat * vec_ref[0:1] + vec_ref[1:2]).astype(BF16)
        lowf = low.astype(F32)
        for t in range(cp // LANE):
            scr[t] = lowf[:, t * LANE : (t + 1) * LANE]
        total = jnp.zeros((keys, cp), F32)
        for b in range(2):
            part = [scr[t, pl.ds(b, n // 2, stride=2), :] for t in range(cp // LANE)]
            part = jnp.concatenate(part, -1).reshape(height // 2, 2, width // 2, cp)
            for a in range(2):
                total = total + dot(part[:, a].reshape(keys, cp).astype(BF16), wr_ref[2 * a + b])
        red_ref[0] = total
        rhat, _ = centered(total, channels)
        m = mask_ref[0].astype(F32)
        shape = (width // 2, width)
        near = lanes(shape) // 2 == lax.broadcasted_iota(jnp.int32, shape, 0)
        flags = []
        for i in range(height // 2):
            both = m[2 * i : 2 * i + 1] + m[2 * i + 1 : 2 * i + 2]
            flags.append(jnp.sum(jnp.where(near, both, 0.0), -1, keepdims=True))
        unc = jnp.where(jnp.concatenate(flags, 0) > 0.0, 0.0, 1.0)
        own = pack_block(rhat * vec_ref[2:3] + vec_ref[3:4], unc, keys, cp)

        @pl.when(chip < used)
        def _():
            rnbuf[s, slot(chip, core)] = own
            send_sib(s, chip).start()

            @pl.when(chip < chips - 1)
            def _():
                send_up(s, chip).start()

            @pl.when(chip > 0)
            def _():
                send_down(s, chip).start()

        qf = dot(low, wq_ref[...]) * (LOG2E * head_size**-0.5)
        ones = head_blocks(qf, lambda e: free_row(e, {0: 1.0, 1: 1.0, 2: 1.0}))
        for h in range(HEADS):
            qbuf[lax.rem(s, lag + 1), :, h * LANE : (h + 1) * LANE] = ones[h].astype(BF16)
        shape = (cnt_ref.shape[0], width)
        classes = lax.broadcasted_iota(jnp.int32, shape, 0)
        wide = lax.broadcasted_iota(jnp.int32, (LANE, width), 0)
        total = jnp.zeros(cnt_ref.shape, F32)
        for r in range(height):
            label = jnp.where(mask_ref[0, r : r + 1] > 0, label_ref[0, r : r + 1], -1)
            hot = jnp.where(label == classes, 1.0, 0.0).astype(BF16)
            pred = jnp.where(pred_ref[0, r : r + 1] == wide, 1.0, 0.0).astype(BF16)
            total = total + dot_nt(hot, pred)
        cnt_ref[...] += total

    for age in range(1, chips):
        s = step - age

        @pl.when(jnp.logical_and(s >= 0, s < scenes))
        def _(s=s, age=age):
            below = chip - age

            @pl.when(jnp.logical_and(below >= 0, below < used))
            def _():
                send_up(s, below).wait_recv()
                send_sib(s, below).start()

                @pl.when(chip < chips - 1)
                def _():
                    send_up(s, below).start()

            above = chip + age

            @pl.when(above < used)
            def _():
                send_down(s, above).wait_recv()
                send_sib(s, above).start()

                @pl.when(chip > 0)
                def _():
                    send_down(s, above).start()

    @pl.when(step >= lag)
    def _():
        s = step - lag

        for origin in range(used):
            send_sib(s, origin).wait_recv()

        free = vec_ref[3:4, cp - LANE :]
        blocks = [unpack_block(rnbuf[s, i], free, keys, cp) for i in range(2 * used)]
        rn_all = jnp.concatenate([v[0] for v in blocks], 0)
        rn_ref[0] = rn_all
        flag = jnp.concatenate([v[1] for v in blocks], 0)
        kv = dot(rn_all, wkv_ref[...])
        negative = {0: float(NEG_HI), 1: float(NEG_MID), 2: float(NEG_LO)}
        for h, block in enumerate(
            head_blocks(
                kv[:, :cp],
                lambda e: flag * free_row(e, negative) + free_row(e, {3: 1.0, 4: 1.0, 5: 1.0}),
            )
        ):
            ke_ref[0, :, h * LANE : (h + 1) * LANE] = block.astype(BF16)
        for h, block in enumerate(
            head_blocks(kv[:, cp:], lambda e: free_row(e, {0: 1.0, 1: 1.0, 2: 1.0}))
        ):
            ve_ref[0, :, h * LANE : (h + 1) * LANE] = block.astype(BF16)
        mine = lax.rem(s, lag + 1)
        count = 2 * used * keys // KEY_CHUNK
        for h in range(HEADS):
            block = slice(h * LANE, (h + 1) * LANE)
            e = ext_lane(h)
            q = qbuf[mine, :, block]
            parts = [
                dot_nt(q, ke_ref[0, j * KEY_CHUNK : (j + 1) * KEY_CHUNK, block])
                for j in range(count)
            ]
            top = functools.reduce(jnp.maximum, parts)
            top = jnp.max(top, -1, keepdims=True)
            out = jnp.zeros((n, LANE), F32)
            for j in range(count):
                p = jnp.exp2(parts[j] - top).astype(BF16)
                out = out + dot(p, ve_ref[0, j * KEY_CHUNK : (j + 1) * KEY_CHUNK, block])
            total = out[:, e : e + 1]
            oe[h] = out / total
            lse = top + jnp.log2(total)
            hi = lse.astype(BF16).astype(F32)
            mid = (lse - hi).astype(BF16).astype(F32)
            lo = lse - hi - mid
            lane = lanes((n, LANE))
            q2 = q.astype(F32)
            q2 = jnp.where(lane == e + 3, -hi, q2)
            q2 = jnp.where(lane == e + 4, -mid, q2)
            q2 = jnp.where(lane == e + 5, -lo, q2)
            q_ref[0, :, block] = q2.astype(BF16)

        tiles = []
        low_half = lanes((n, LANE)) < HALF
        for t in range(cp // LANE):
            other = oe[2 * t + 1] if 2 * t + 1 < HEADS else jnp.zeros((n, LANE), F32)
            tiles.append(jnp.where(low_half, oe[2 * t], other))
        att = jnp.concatenate(tiles, -1)
        att_ref[0] = att
        x = widen(tok2_ref[0].astype(F32), cp)
        resid = x + dot(att.astype(BF16), wp_ref[...]) + vec_ref[4:5]
        for t in range(cp // LANE):
            for r in range(height):
                for half in range(2):
                    base = r * width + half * (width // 2)
                    at = r * scenes * width + half * scenes + s
                    res_ref[t, pl.ds(at, width // 2, stride=2 * scenes), :] = resid[
                        base : base + width // 2, t * LANE : (t + 1) * LANE
                    ]

    @pl.when(step == scenes + lag - 1)
    def _():
        @pl.loop(0, scenes)
        def _(s):
            for origin in range(used):
                send_sib(s, origin).wait_send()

                @pl.when(jnp.logical_and(origin <= chip, chip < chips - 1))
                def _(origin=origin):
                    send_up(s, origin).wait_send()

                @pl.when(jnp.logical_and(origin >= chip, chip > 0))
                def _(origin=origin):
                    send_down(s, origin).wait_send()


def attend(dims, blk, used, cid, tok, mask, labels, predicted, vec, wr, wq, wkv, wp):
    scenes, height, width, channels, cp = dims
    n = height * width
    keys = n // 4
    chips = blk // 2
    lag = chips
    k = blk * keys
    live = 2 * used * keys
    he = HEADS * LANE

    def early(shape):
        return pl.BlockSpec(
            (1,) + shape, lambda t: (jnp.minimum(t, scenes - 1),) + (0,) * len(shape)
        )

    def late(shape):
        return pl.BlockSpec((1,) + shape, lambda t: (jnp.maximum(t - lag, 0),) + (0,) * len(shape))

    return pl.pallas_call(
        functools.partial(attend_kernel, dims, blk, used),
        grid=(scenes + lag,),
        in_specs=[early((n, channels))]
        + [early((height, width))] * 3
        + [late((n, channels))]
        + [whole(v.shape) for v in (vec, wr, wq, wkv, wp)],
        out_specs=[
            early((keys, cp)),
            whole((32, LANE)),
            late((n, he)),
            late((n, cp)),
            late((live, he)),
            late((live, he)),
            late((live, cp)),
            whole((cp // LANE, scenes * n, LANE)),
        ],
        out_shape=[
            jax.ShapeDtypeStruct((scenes, keys, cp), F32),
            jax.ShapeDtypeStruct((32, LANE), F32),
            jax.ShapeDtypeStruct((scenes, n, he), BF16),
            jax.ShapeDtypeStruct((scenes, n, cp), F32),
            jax.ShapeDtypeStruct((scenes, k, he), BF16),
            jax.ShapeDtypeStruct((scenes, k, he), BF16),
            jax.ShapeDtypeStruct((scenes, k, cp), BF16),
            jax.ShapeDtypeStruct((cp // LANE, scenes * n, LANE), F32),
        ],
        scratch_shapes=[
            pltpu.VMEM((cp // LANE, n, LANE), F32),
            pltpu.VMEM((lag + 1, n, he), BF16),
            pltpu.VMEM((HEADS, n, LANE), F32),
            pltpu.VMEM((scenes, 2 * used, packed_rows(keys, cp), LANE), BF16),
        ]
        + [pltpu.SemaphoreType.DMA((scenes, used))] * 5,
        compiler_params=pltpu.CompilerParams(
            vmem_limit_bytes=VMEM, collective_id=cid, has_side_effects=True
        ),
    )(tok, mask, labels, predicted, tok, vec, wr, wq, wkv, wp)


def ffn_kernel(
    dims, ff, blk, ndev, res_hbm, ct_hbm, ew_hbm, sw_hbm, vec_ref, eb_ref, taps_ref, tb_ref,
    out_hbm, gres_hbm, pack_hbm, dtap_ref, dtb_ref, dvec_ref,
    we_ref, ws_ref, dwe_ref, dwst, packed, res_ref, ct_ref, cn, cnt, ctt, ctx, oacc, gacc, hid, gm, halo, act, back, tapacc, out_stage, gres_stage,
    weight_sem, pack_sem, res_sem, ct_sem, out_sem, gres_sem, cn_send, cn_recv, gm_send, gm_recv,
):
    scenes, height, width, channels, cp = dims
    n = height * width
    rw = scenes * width
    lt = cp // LANE
    fc = FF_CHUNK
    nchunk = ff // fc
    cols = width // 2
    pair = 2 * scenes
    group = GROUP if cols % GROUP == 0 else cols
    me = lax.axis_index("blk")
    has_left = me > 0
    has_right = me < blk - 1
    left, right = {"blk": me - 1}, {"blk": me + 1}
    MESH = pl.DeviceIdType.MESH

    def res_copy(r):
        rows = pl.ds(pl.multiple_of(r * rw, rw), rw)
        return pltpu.make_async_copy(res_hbm.at[:, rows, :], res_ref.at[:, rows, :], res_sem.at[r])

    def ct_copy(s):
        return pltpu.make_async_copy(ct_hbm.at[s], ct_ref.at[s], ct_sem.at[s])

    ew_copy = pltpu.make_async_copy(ew_hbm, we_ref.at[:channels, :], weight_sem.at[0])
    sw_copy = pltpu.make_async_copy(sw_hbm, ws_ref.at[:channels, :], weight_sem.at[1])
    for r in range(height):
        res_copy(r).start()
    for s in range(scenes):
        ct_copy(s).start()
    ew_copy.start()
    sw_copy.start()
    bias_rows = eb_ref.shape[0]
    we_ref[channels : channels + bias_rows, :] = eb_ref[...]
    if channels + bias_rows < cp:
        we_ref[channels + bias_rows :, :] = jnp.zeros((cp - channels - bias_rows, ff), BF16)
    ws_ref[channels:, :] = jnp.zeros((cp - channels, ff), BF16)

    barrier = pltpu.get_barrier_semaphore()

    @pl.when(has_left)
    def _():
        pl.semaphore_signal(barrier, inc=1, device_id=left, device_id_type=MESH)

    @pl.when(has_right)
    def _():
        pl.semaphore_signal(barrier, inc=1, device_id=right, device_id_type=MESH)

    pl.semaphore_wait(barrier, has_left.astype(jnp.int32) + has_right.astype(jnp.int32))

    def row(r, size=rw):
        return pl.ds(pl.multiple_of(r * rw, rw), size)

    g2, b2 = vec_ref[5:6], vec_ref[6:7]

    def load3(ref, r):
        return jnp.concatenate([ref[t, row(r), :] for t in range(lt)], -1)

    def store3(ref, r, value):
        for t in range(lt):
            ref[t, row(r), :] = value[:, t * LANE : (t + 1) * LANE]

    @pl.loop(0, height)
    def _(r):
        res_copy(r).wait()
        x = load3(res_ref, r)
        xhat, rstd = centered(x, channels)
        c = (xhat * g2 + b2).astype(BF16)
        cn[row(r + 1), :] = c
        cnt[:, row(r)] = c.T
        store3(oacc, r, x + vec_ref[7:8])
        store3(res_ref, r, jnp.where(lanes(xhat.shape) == channels, rstd, xhat))

    def cn_copy(up):
        return pltpu.make_async_remote_copy(
            src_ref=cn.at[row(1 if up else height), :],
            dst_ref=cn.at[row(height + 1 if up else 0), :],
            send_sem=cn_send.at[0 if up else 1],
            recv_sem=cn_recv.at[0 if up else 1],
            device_id=left if up else right,
            device_id_type=MESH,
        )

    @pl.when(has_left)
    def _():
        cn_copy(True).start()

    @pl.when(has_right)
    def _():
        cn_copy(False).start()

    @pl.loop(0, scenes)
    def _(s):
        ct_copy(s).wait()
        c = widen(ct_ref[s].astype(F32), cp)
        for t in range(lt):
            for r in range(height):
                for half in range(2):
                    base = r * width + half * cols
                    gacc[t, pl.ds(r * rw + half * scenes + s, cols, stride=pair), :] = c[
                        base : base + cols, t * LANE : (t + 1) * LANE
                    ]

    dvec_ref[...] = jnp.zeros(dvec_ref.shape, F32)

    @pl.loop(0, height)
    def _(r):
        c = load3(gacc, r)
        dvec_ref[2:3] += jnp.sum(c, 0, keepdims=True)
        low = c.astype(BF16)
        ctt[row(r), :] = low
        ctx[:, row(r)] = low.T
        store3(gacc, r, jnp.zeros((rw, cp), F32))

    ew_copy.wait()
    sw_copy.wait()
    dwe_ref[...] = jnp.zeros(dwe_ref.shape, F32)
    dwst[...] = jnp.zeros(dwst.shape, F32)

    @pl.when(has_left)
    def _():
        cn_copy(False).wait_recv()

    @pl.when(jnp.logical_not(has_left))
    def _():
        cn[row(0), :] = jnp.zeros((rw, cp), BF16)

    @pl.when(has_right)
    def _():
        cn_copy(True).wait_recv()

    @pl.when(jnp.logical_not(has_right))
    def _():
        cn[row(height + 1), :] = jnp.zeros((rw, cp), BF16)

    def put(ref, slot, r, value):
        v = value.reshape(cols, pair, fc)
        z = jnp.zeros((scenes, fc), F32)
        ref[slot, r, 1 : cols + 1] = v.astype(BF16)
        ref[slot, r, 0] = jnp.concatenate([z, v[cols - 1, :scenes]], 0).astype(BF16)
        ref[slot, r, cols + 1] = jnp.concatenate([v[0, scenes:], z], 0).astype(BF16)

    def gm_copy(k, slot, up):
        return pltpu.make_async_remote_copy(
            src_ref=gm.at[slot, 1 if up else height],
            dst_ref=halo.at[k, 1 if up else 0],
            send_sem=gm_send.at[k, 0 if up else 1],
            recv_sem=gm_recv.at[k, 0 if up else 1],
            device_id=left if up else right,
            device_id_type=MESH,
        )

    def phase_a(k, slot):
        span = pl.ds(pl.multiple_of(k * fc, fc), fc)
        taps = [
            taps_ref[pl.ds(i, 1), span].astype(BF16).reshape(1, 1, fc) for i in range(9)
        ]
        bias = tb_ref[:, span]

        def hidden(r):
            put(hid, slot, r, dot(cn[r * rw : (r + 1) * rw, :], we_ref[:, span]))

        def products(r):
            active = act[r * rw : (r + 1) * rw, :]
            o = dot_nt(active, ws_ref[:, span])
            for t in range(lt):
                oacc[t, r * rw : (r + 1) * rw, :] += o[:, t * LANE : (t + 1) * LANE]
            dwst[:, span] += dot(ctx[:, r * rw : (r + 1) * rw], active)

        hidden(0)
        hidden(1)
        hidden(2)
        sums = jnp.zeros((8, fc), F32)
        for r in range(height):
            back[...] = dot(ctt[r * rw : (r + 1) * rw, :], ws_ref[:, span])
            if r:
                products(r - 1)
            for g in range(0, cols, group):
                acc = None
                for a in range(3):
                    line = hid[slot, r + a, g : g + group + 2]
                    for b in range(3):
                        term = line[b : b + group] * taps[3 * a + b]
                        acc = term if acc is None else acc + term
                mixed = acc.astype(F32).reshape(group * pair, fc) + bias
                arg = mixed * 0.7071067811865476
                phi = 0.5 + 0.5 * lax.erf(arg)
                dens = jnp.exp2(arg * arg * -LOG2E) * mixed
                act[r * rw + g * pair : r * rw + (g + group) * pair, :] = (mixed * phi).astype(BF16)
                slope = phi + dens * 0.3989422804014327
                grad = back[g * pair : (g + group) * pair, :] * slope
                sums = sums + jnp.sum(grad.reshape(group * pair // 8, 8, fc), 0)
                v = grad.reshape(group, pair, fc)
                gm[slot, r + 1, g + 1 : g + group + 1] = v.astype(BF16)
                z = jnp.zeros((scenes, fc), F32)
                if g == 0:
                    gm[slot, r + 1, cols + 1] = jnp.concatenate([v[0, scenes:], z], 0).astype(BF16)
                if g + group == cols:
                    gm[slot, r + 1, 0] = jnp.concatenate([z, v[group - 1, :scenes]], 0).astype(BF16)
            if r + 3 < height + 2:
                hidden(r + 3)
        products(height - 1)
        dtb_ref[:, span] = sums

        @pl.when(has_left)
        def _():
            gm_copy(k, slot, True).start()

        @pl.when(has_right)
        def _():
            gm_copy(k, slot, False).start()

    def phase_b(k, slot):
        span = pl.ds(pl.multiple_of(k * fc, fc), fc)

        @pl.when(has_left)
        def _():
            gm_copy(k, slot, False).wait_recv()
            gm[slot, 0] = halo[k, 0]

        @pl.when(jnp.logical_not(has_left))
        def _():
            gm[slot, 0] = jnp.zeros((cols + 2, pair, fc), BF16)

        @pl.when(has_right)
        def _():
            gm_copy(k, slot, True).wait_recv()
            gm[slot, height + 1] = halo[k, 1]

        @pl.when(jnp.logical_not(has_right))
        def _():
            gm[slot, height + 1] = jnp.zeros((cols + 2, pair, fc), BF16)

        taps = [
            taps_ref[pl.ds(i, 1), span].astype(BF16).reshape(1, 1, fc) for i in range(9)
        ]
        tapacc[...] = jnp.zeros(tapacc.shape, F32)

        def products(r):
            low = act[r * rw : (r + 1) * rw, :]
            dwe_ref[:, span] += dot(cnt[:, r * rw : (r + 1) * rw], low)
            g = dot_nt(low, we_ref[:, span])
            for t in range(lt):
                gacc[t, r * rw : (r + 1) * rw, :] += g[:, t * LANE : (t + 1) * LANE]

        for r in range(height):
            tapsum = [None] * 9
            for g in range(0, cols, group):
                acc = None
                own = hid[slot, r + 1, g + 1 : g + group + 1]
                for a in range(3):
                    line = gm[slot, r + 2 - a, g : g + group + 2]
                    for b in range(3):
                        window = line[2 - b : 2 - b + group]
                        term = window * taps[3 * a + b]
                        acc = term if acc is None else acc + term
                        prod = own * window
                        while prod.shape[0] > 1:
                            cut = prod.shape[0] // 2
                            prod = prod[:cut] + prod[cut:]
                        i = 3 * a + b
                        tapsum[i] = prod[0] if tapsum[i] is None else tapsum[i] + prod[0]
                act[r * rw + g * pair : r * rw + (g + group) * pair, :] = acc.reshape(group * pair, fc)
            for i in range(9):
                tapacc[i] += tapsum[i].astype(F32)
        for r in range(height):
            products(r)

        for tap in range(9):
            dtap_ref[pl.ds(tap, 1), span] = jnp.sum(tapacc[tap], 0, keepdims=True)

        @pl.when(has_left)
        def _():
            gm_copy(k, slot, True).wait_send()

        @pl.when(has_right)
        def _():
            gm_copy(k, slot, False).wait_send()

    @pl.loop(0, nchunk + 1)
    def _(k):
        slot = lax.rem(k, 2)

        @pl.when(k < nchunk)
        def _():
            phase_a(k, slot)

        @pl.when(k > 0)
        def _():
            phase_b(k - 1, 1 - slot)

    @pl.when(has_left)
    def _():
        cn_copy(True).wait_send()

    @pl.when(has_right)
    def _():
        cn_copy(False).wait_send()

    plan, filled, _ = ffn_plan(channels, ff, ndev)
    for name, ref in (("we", dwe_ref), ("ws", dwst)):
        at, rows, slabs = plan[name]
        for t in range(slabs):
            packed[at + t * rows : at + (t + 1) * rows, :] = ref[
                :rows, t * LANE : (t + 1) * LANE
            ].astype(BF16)
    if filled < packed.shape[0]:
        packed[filled:, :] = jnp.zeros((packed.shape[0] - filled, LANE), BF16)
    pack_copy = pltpu.make_async_copy(packed, pack_hbm, pack_sem.at[0])
    pack_copy.start()

    def gather(ref, s):
        rows = []
        for r in range(height):
            for half in range(2):
                rows.append(
                    jnp.concatenate(
                        [
                            ref[t, pl.ds(r * rw + half * scenes + s, cols, stride=pair), :]
                            for t in range(lt)
                        ],
                        -1,
                    )
                )
        return jnp.concatenate(rows, 0)[:, :channels]

    def out_copy(s, slot):
        return pltpu.make_async_copy(out_stage.at[slot], out_hbm.at[s], out_sem.at[slot])

    def gres_copy(s, slot):
        return pltpu.make_async_copy(gres_stage.at[slot], gres_hbm.at[s], gres_sem.at[slot])

    @pl.loop(0, scenes)
    def _(s):
        slot = lax.rem(s, 2)

        @pl.when(s >= 2)
        def _():
            out_copy(s - 2, slot).wait()

        out_stage[slot] = gather(oacc, s).astype(BF16)
        out_copy(s, slot).start()

    @pl.loop(0, height)
    def _(r):
        kept = load3(res_ref, r)
        rstd = kept[:, channels : channels + 1]
        xhat = inside(kept, channels)
        upstream = load3(gacc, r)
        dvec_ref[0:1] += jnp.sum(upstream * xhat, 0, keepdims=True)
        dvec_ref[1:2] += jnp.sum(upstream, 0, keepdims=True)
        g = ctt[row(r), :].astype(F32) + norm_back(upstream, g2, xhat, rstd, channels)
        store3(gacc, r, g)

    @pl.loop(0, scenes)
    def _(s):
        slot = lax.rem(s, 2)

        @pl.when(s >= 2)
        def _():
            gres_copy(s - 2, slot).wait()

        gres_stage[slot] = gather(gacc, s)
        gres_copy(s, slot).start()

    for s in range(scenes - 2, scenes):
        out_copy(s, s % 2).wait()
        gres_copy(s, s % 2).wait()
    pack_copy.wait()


def ffn(dims, blk, ndev, res, ct, ew, sw, vec, eb, taps, tb):
    scenes, height, width, channels, cp = dims
    n = height * width
    total = scenes * n
    rw = scenes * width
    ff = sw.shape[1]
    lt = cp // LANE
    nchunk = ff // FF_CHUNK
    strip = (width // 2 + 2, 2 * scenes, FF_CHUNK)
    pack_rows = sum(ffn_plan(channels, ff, ndev)[2])
    vm = pl.BlockSpec(memory_space=pltpu.VMEM)
    hbm = pl.BlockSpec(memory_space=pl.ANY)
    return pl.pallas_call(
        functools.partial(ffn_kernel, dims, ff, blk, ndev),
        in_specs=[hbm] * 4 + [vm] * 4,
        out_specs=[hbm, hbm, hbm] + [vm] * 3,
        out_shape=[
            jax.ShapeDtypeStruct((scenes, n, channels), BF16),
            jax.ShapeDtypeStruct((scenes, n, channels), F32),
            jax.ShapeDtypeStruct((pack_rows, LANE), BF16),
            jax.ShapeDtypeStruct((9, ff), F32),
            jax.ShapeDtypeStruct((8, ff), F32),
            jax.ShapeDtypeStruct((8, cp), F32),
        ],
        scratch_shapes=[
            pltpu.VMEM((cp, ff), BF16),
            pltpu.VMEM((cp, ff), BF16),
            pltpu.VMEM((cp, ff), F32),
            pltpu.VMEM((cp, ff), F32),
            pltpu.VMEM((pack_rows, LANE), BF16),
            pltpu.VMEM((lt, total, LANE), F32),
            pltpu.VMEM((scenes, n, channels), BF16),
            pltpu.VMEM((total + 2 * rw, cp), BF16),
            pltpu.VMEM((cp, total), BF16),
            pltpu.VMEM((total, cp), BF16),
            pltpu.VMEM((cp, total), BF16),
            pltpu.VMEM((lt, total, LANE), F32),
            pltpu.VMEM((lt, total, LANE), F32),
            pltpu.VMEM((2, height + 2) + strip, BF16),
            pltpu.VMEM((2, height + 2) + strip, BF16),
            pltpu.VMEM((nchunk, 2) + strip, BF16),
            pltpu.VMEM((total, FF_CHUNK), BF16),
            pltpu.VMEM((rw, FF_CHUNK), F32),
            pltpu.VMEM((9, 2 * scenes, FF_CHUNK), F32),
            pltpu.VMEM((2, n, channels), BF16),
            pltpu.VMEM((2, n, channels), F32),
            pltpu.SemaphoreType.DMA((2,)),
            pltpu.SemaphoreType.DMA((1,)),
            pltpu.SemaphoreType.DMA((height,)),
            pltpu.SemaphoreType.DMA((scenes,)),
            pltpu.SemaphoreType.DMA((2,)),
            pltpu.SemaphoreType.DMA((2,)),
            pltpu.SemaphoreType.DMA((2,)),
            pltpu.SemaphoreType.DMA((2,)),
            pltpu.SemaphoreType.DMA((nchunk, 2)),
            pltpu.SemaphoreType.DMA((nchunk, 2)),
        ],
        compiler_params=pltpu.CompilerParams(
            vmem_limit_bytes=VMEM, collective_id=0, has_side_effects=True
        ),
    )(res, ct, ew, sw, vec, eb, taps, tb)


def attback_kernel(
    dims, ff, ndp, blk, used, q_ref, att_ref, gres_ref, ke_ref, ve_ref, rn_ref, tok_ref, gres2_ref,
    red_ref, vec_ref, wp_ref, wkv_ref, wq_ref, wr_ref, first_hbm,
    ig_ref, dwqt, dwrt, dwp_ref, dwkv_ref, dbp_ref, dvec_ref, sum_hbm,
    ge, dqt, gqt_ref, grn_ref, scr, gscr, own, acc, sib_land, up_land, down_land,
    work, land, done,
    sib_send, sib_recv, up_send, up_recv, down_send, down_recv, sum_send, sum_recv, sum_sem,
):
    scenes, height, width, channels, cp = dims
    n = height * width
    keys = n // 4
    chips = blk // 2
    lt = cp // LANE
    head_size = channels // HEADS
    step = pl.program_id(0)
    chip, core, up, down, sib = place(blk)
    count = 2 * used * keys // KEY_CHUNK
    steps = scenes + chips
    together = -(-scenes // chips)
    ndev = ndp * blk
    order = orders_of(ndp, blk)[0]
    parts = three_parts(work, land, done, ffn_plan(channels, ff, ndev)[2], [order] * 3)
    sums = Sums(parts, sum_send, sum_recv)
    each = -(-(sums.ops + 1) // (steps - 1))

    @pl.when(step == 0)
    def _():
        load = pltpu.make_async_copy(first_hbm, work, sum_sem.at[0])
        load.start()
        barrier = pltpu.get_barrier_semaphore()
        peers = peers_of(order)
        for peer in peers:
            pl.semaphore_signal(barrier, inc=1, device_id=peer, device_id_type=pl.DeviceIdType.MESH)
        pl.semaphore_wait(barrier, len(peers))
        load.wait()
        for k in range(each):
            sums.advance(k)
        dwqt[...] = jnp.zeros(dwqt.shape, F32)
        dwrt[...] = jnp.zeros(dwrt.shape, F32)
        dvec_ref[...] = jnp.zeros(dvec_ref.shape, F32)
        dwp_ref[...] = jnp.zeros(dwp_ref.shape, F32)
        dwkv_ref[...] = jnp.zeros(dwkv_ref.shape, F32)
        dbp_ref[...] = jnp.zeros(dbp_ref.shape, F32)

    def to_sib(s, target):
        return remote(
            own.at[lax.rem(s, 2), 1 - core, target], sib_land.at[s, target], sib_send.at[s, target],
            sib_recv.at[s, target], sib,
        )

    def to_up(s, target):
        return remote(
            acc.at[s, target], up_land.at[s, target], up_send.at[s, target], up_recv.at[s, target], up
        )

    def to_down(s, target):
        return remote(
            acc.at[s, target], down_land.at[s, target], down_send.at[s, target],
            down_recv.at[s, target], down,
        )

    def plus(a, b):
        return (a.astype(F32) + b.astype(F32)).astype(BF16)

    def chunk(j):
        s = step
        per = KEY_CHUNK // keys
        span = slice(j * KEY_CHUNK, (j + 1) * KEY_CHUNK)
        dks, dvs = [], []
        for h in range(HEADS):
            block = slice(h * LANE, (h + 1) * LANE)
            k, v = ke_ref[0, span, block], ve_ref[0, span, block]
            q, g = q_ref[0, :, block], ge[:, block]
            p = jnp.exp2(dot_nt(k, q))
            gs = (p * dot_nt(v, g)).astype(BF16)
            dvs.append(dot(p.astype(BF16), g))
            dks.append(dot(gs, q))
            dqt[block, :] += dot_tn(k, gs)
        low_half = lanes((KEY_CHUNK, LANE)) < HALF
        tiles = []
        for group, scale in ((dks, LN2), (dvs, 1.0)):
            for t in range(lt):
                other = (
                    group[2 * t + 1] if 2 * t + 1 < HEADS else jnp.zeros((KEY_CHUNK, LANE), F32)
                )
                tiles.append((jnp.where(low_half, group[2 * t], other) * scale).astype(BF16))
        gkv = jnp.concatenate(tiles, -1)
        grn = dot_nt(gkv, wkv_ref[...]).astype(BF16)
        for i in range(per):
            at = j * per + i
            own[lax.rem(s, 2), at // used, at % used] = grn[i * keys : (i + 1) * keys]

            @pl.when(core != at // used)
            def _(at=at):
                to_sib(s, at % used).start()

        dwkv_ref[...] += dot(rn_ref[0, span].T, gkv)

    @pl.when(step < scenes)
    def _():
        s = step
        gb = widen(gres_ref[0], cp).astype(BF16)
        dbp_ref[...] += jnp.sum(gb.astype(F32).reshape(n // 8, 8, cp), 0)
        att = att_ref[0]
        dwp_ref[...] += dot(att.astype(BF16).T, gb)
        gatt = head_blocks(dot_nt(gb, wp_ref[...]), lambda e: 0.0)
        lane = lanes((n, LANE))
        for h in range(HEADS):
            e = ext_lane(h)
            g = gatt[h].astype(BF16).astype(F32)
            o = att[:, (h // 2) * LANE : (h // 2 + 1) * LANE]
            inner = jnp.sum(g * o, -1, keepdims=True)
            hi = inner.astype(BF16).astype(F32)
            g = jnp.where(lane == e, -hi, g)
            g = jnp.where(lane == e + 1, hi - inner, g)
            ge[:, h * LANE : (h + 1) * LANE] = g.astype(BF16)
        dqt[...] = jnp.zeros(dqt.shape, F32)
        chunk(0)

    s1 = step - 1

    @pl.when(jnp.logical_and(s1 >= 0, s1 < scenes))
    def _():
        for target in range(used):
            to_sib(s1, target).wait()
            acc[s1, target] = plus(own[lax.rem(s1, 2), core, target], sib_land[s1, target])

    s_up = step - 1 - chip

    @pl.when(jnp.logical_and(s_up >= 0, s_up < scenes))
    def _():
        for target in reversed(range(1, used)):

            @pl.when(target > chip)
            def _(target=target):
                @pl.when(chip > 0)
                def _():
                    to_up(s_up, target).wait_recv()
                    acc[s_up, target] = plus(acc[s_up, target], up_land[s_up, target])

                to_up(s_up, target).start()

    s_down = step - chips + chip

    @pl.when(jnp.logical_and(s_down >= 0, s_down < scenes))
    def _():
        for target in range(used):

            @pl.when(target < chip)
            def _(target=target):
                @pl.when(chip < chips - 1)
                def _():
                    to_down(s_down, target).wait_recv()
                    acc[s_down, target] = plus(acc[s_down, target], down_land[s_down, target])

                to_down(s_down, target).start()

    s_end = step - chips

    @pl.when(s_end >= 0)
    def _():
        @pl.when(chip < used)
        def _():
            grn_ref[s_end] = acc[s_end, chip].astype(F32)

            @pl.when(chip > 0)
            def _():
                to_up(s_end, chip).wait_recv()
                grn_ref[s_end] += up_land[s_end, chip].astype(F32)

            @pl.when(chip < chips - 1)
            def _():
                to_down(s_end, chip).wait_recv()
                grn_ref[s_end] += down_land[s_end, chip].astype(F32)

        @pl.when(chip >= used)
        def _():
            grn_ref[s_end] = jnp.zeros((keys, cp), F32)

    for t in range(1, steps - 1):

        @pl.when(step == t)
        def _(t=t):
            for k in range(t * each, min((t + 1) * each, sums.ops + 1)):
                sums.advance(k)
            if t * each <= sums.ops < (t + 1) * each:
                pltpu.make_async_copy(done, sum_hbm, sum_sem.at[0]).start()

    def tail(base):
        gred, low, hats = [], [], []
        for i in range(together):
            rhat, rstd = centered(red_ref[i], channels)
            upstream = inside(grn_ref[base + i], channels)
            dvec_ref[0:1] += jnp.sum(upstream * rhat, 0, keepdims=True)
            dvec_ref[1:2] += jnp.sum(upstream, 0, keepdims=True)
            g = norm_back(upstream, vec_ref[2:3], rhat, rstd, channels)
            gred.append(inside(g, channels).astype(BF16))
            x = widen(tok_ref[i].astype(F32), cp)
            xhat, xstd = centered(x, channels)
            hats.append((xhat, xstd))
            low.append((xhat * vec_ref[0:1] + vec_ref[1:2]).astype(BF16))
            lowf = low[i].astype(F32)
            for t in range(lt):
                scr[i, t] = lowf[:, t * LANE : (t + 1) * LANE]
        gred = jnp.concatenate(gred, 0)
        gred_t = gred.T
        for b in range(2):
            patches = [[], []]
            for i in range(together):
                part = [scr[i, t, pl.ds(b, n // 2, stride=2), :] for t in range(lt)]
                part = jnp.concatenate(part, -1).reshape(height // 2, 2, width // 2, cp)
                for a in range(2):
                    patches[a].append(part[:, a].reshape(keys, cp))
            for a in range(2):
                ab = 2 * a + b
                dwrt[ab] += dot(gred_t, jnp.concatenate(patches[a], 0).astype(BF16))
                back = dot_nt(gred, wr_ref[ab])
                for i in range(together):
                    for t in range(lt):
                        for r in range(height // 2):
                            at = i * keys + r * (width // 2)
                            gscr[i, t, pl.ds((2 * r + a) * width + b, width // 2, stride=2), :] = back[
                                at : at + width // 2, t * LANE : (t + 1) * LANE
                            ]
        for i in range(together):
            gqt = gqt_ref[base + i]
            xhat, xstd = hats[i]
            dwqt[...] += dot(gqt, low[i])
            gn = widen(dot_nt(gqt.T, wq_ref[...]), cp)
            gn = gn + jnp.concatenate([gscr[i, t] for t in range(lt)], -1)
            dvec_ref[3:4] += jnp.sum(gn * xhat, 0, keepdims=True)
            dvec_ref[4:5] += jnp.sum(gn, 0, keepdims=True)
            gx = norm_back(gn, vec_ref[0:1], xhat, xstd, channels)
            ig_ref[i] = gres2_ref[i] + gx[:, :channels]

    @pl.when(step >= scenes)
    def _():
        tail((step - scenes) * together)

    @pl.when(step < scenes)
    def _():
        s = step
        for j in range(1, count):
            chunk(j)
        for h in range(HEADS):
            base = h * LANE + (0 if h % 2 == 0 else HALF)
            gqt_ref[s, h * HALF : (h + 1) * HALF] = (
                dqt[base : base + HALF, :] * head_size**-0.5
            ).astype(BF16)

    @pl.when(step == steps - 1)
    def _():
        pltpu.make_async_copy(done, sum_hbm, sum_sem.at[0]).wait()

        @pl.loop(0, scenes)
        def _(s):
            for target in range(used):

                @pl.when(target > chip)
                def _(target=target):
                    to_up(s, target).wait_send()

                @pl.when(target < chip)
                def _(target=target):
                    to_down(s, target).wait_send()


def attback(
    dims, ff, ndp, blk, used, cid, q, att, gres, ke, ve, rn, tok, red, vec, wp, wkv, wq, wr, first
):
    scenes, height, width, channels, cp = dims
    n = height * width
    keys = n // 4
    chips = blk // 2
    lt = cp // LANE
    live = 2 * used * keys
    he = HEADS * LANE
    together = -(-scenes // chips)
    assert scenes == together * chips
    ops = 2 * len(orders_of(ndp, blk)[0])

    def early(shape):
        return pl.BlockSpec(
            (1,) + shape, lambda t: (jnp.minimum(t, scenes - 1),) + (0,) * len(shape)
        )

    def late(shape):
        return pl.BlockSpec(
            (together,) + shape, lambda t: (jnp.maximum(t - scenes, 0),) + (0,) * len(shape)
        )

    land = (scenes, used, keys, cp)
    hbm = pl.BlockSpec(memory_space=pl.ANY)
    vm = pl.BlockSpec(memory_space=pltpu.VMEM)
    return pl.pallas_call(
        functools.partial(attback_kernel, dims, ff, ndp, blk, used),
        grid=(scenes + chips,),
        in_specs=[
            early((n, he)),
            early((n, cp)),
            early((n, channels)),
            early((live, he)),
            early((live, he)),
            early((live, cp)),
            late((n, channels)),
            late((n, channels)),
            late((keys, cp)),
            vm, vm, vm, vm, vm, hbm,
        ],
        out_specs=[late((n, channels))] + [vm] * 6 + [hbm],
        out_shape=[
            jax.ShapeDtypeStruct((scenes, n, channels), F32),
            jax.ShapeDtypeStruct((channels, cp), F32),
            jax.ShapeDtypeStruct((4, cp, cp), F32),
            jax.ShapeDtypeStruct((cp, cp), F32),
            jax.ShapeDtypeStruct((cp, 2 * cp), F32),
            jax.ShapeDtypeStruct((8, cp), F32),
            jax.ShapeDtypeStruct((8, cp), F32),
            jax.ShapeDtypeStruct(first.shape, BF16),
        ],
        scratch_shapes=[
            pltpu.VMEM((n, he), BF16),
            pltpu.VMEM((he, n), F32),
            pltpu.VMEM((scenes, channels, n), BF16),
            pltpu.VMEM((scenes, keys, cp), F32),
            pltpu.VMEM((together, lt, n, LANE), F32),
            pltpu.VMEM((together, lt, n, LANE), F32),
            pltpu.VMEM((2, 2, used, keys, cp), BF16),
        ]
        + [pltpu.VMEM(land, BF16)] * 4
        + [pltpu.VMEM(first.shape, BF16)] * 3
        + [pltpu.SemaphoreType.DMA((scenes, used))] * 6
        + [pltpu.SemaphoreType.DMA((3, ops, widest(ndp, blk)))] * 2
        + [pltpu.SemaphoreType.DMA((1,))],
        compiler_params=pltpu.CompilerParams(
            vmem_limit_bytes=VMEM, collective_id=cid, has_side_effects=True
        ),
    )(q, att, gres, ke, ve, rn, tok, gres, red, vec, wp, wkv, wq, wr, first)


def reduce_kernel(
    channels, ff, ndp, nblk, dwr, dwkv, dwp, dwq, dtap, dtb, dvec2, dvec1, dbp, cnt,
    out_hbm, small_hbm, work, recv, done, swork, srecv, sdone, send_sem, recv_sem, out_sem,
):
    ndev = ndp * nblk
    cp = up_to(channels, LANE)
    orders = orders_of(ndp, nblk)
    plan, used, sizes = rest_plan(channels, ndev)
    splan, srows = small_plan(channels, ff, ndev)
    barrier = pltpu.get_barrier_semaphore()
    peers = peers_of(orders[0])
    for peer in peers:
        pl.semaphore_signal(barrier, inc=1, device_id=peer, device_id_type=pl.DeviceIdType.MESH)

    def put(name, ref):
        at, rows, slabs = plan[name]
        for t in range(slabs):
            work[at + t * rows : at + (t + 1) * rows, :] = ref(t, rows).astype(BF16)

    def lane_slabs(ref):
        return lambda t, rows: ref[:rows, t * LANE : (t + 1) * LANE]

    per = cp // LANE
    put("wr", lambda t, rows: dwr[t // per, :rows, (t % per) * LANE : (t % per + 1) * LANE])
    put("wkv", lane_slabs(dwkv))
    put("wp", lane_slabs(dwp))
    put("wq", lane_slabs(dwq))
    if used < sum(sizes):
        work[used:, :] = jnp.zeros((sum(sizes) - used, LANE), BF16)
    swork[...] = jnp.zeros(swork.shape, F32)
    at, rows, slabs = splan["tap"]
    db = jnp.sum(dtb[...], 0, keepdims=True)
    for t in range(slabs):
        cut = slice(t * LANE, (t + 1) * LANE)
        swork[at + t * rows : at + t * rows + 9, :] = dtap[:, cut]
        swork[at + t * rows + 9 : at + t * rows + 10, :] = db[:, cut]
    at, rows, slabs = splan["vec"]
    pb = jnp.sum(dbp[...], 0, keepdims=True)
    for t in range(slabs):
        cut = slice(t * LANE, (t + 1) * LANE)
        swork[at + t * rows : at + t * rows + 3, :] = dvec2[0:3, cut]
        swork[at + t * rows + 3 : at + t * rows + 8, :] = dvec1[0:5, cut]
        swork[at + t * rows + 8 : at + t * rows + 9, :] = pb[:, cut]
    at, rows, _ = splan["count"]
    swork[at : at + rows, :] = cnt[...]

    pl.semaphore_wait(barrier, len(peers))
    parts = three_parts(work, recv, done, sizes, orders)
    parts.append((swork, srecv, sdone, 0, srows, orders[0]))
    sums = Sums(parts, send_sem, recv_sem)
    for k in range(sums.ops + 1):
        sums.advance(k)

    a = pltpu.make_async_copy(done, out_hbm, out_sem.at[0])
    b = pltpu.make_async_copy(sdone, small_hbm, out_sem.at[1])
    a.start()
    b.start()
    a.wait()
    b.wait()


def reduce_all(channels, ff, ndp, nblk, *grads):
    ndev = ndp * nblk
    ops = 2 * len(orders_of(ndp, nblk)[0])
    wide = widest(ndp, nblk)
    _, _, sizes = rest_plan(channels, ndev)
    _, srows = small_plan(channels, ff, ndev)
    total = sum(sizes)
    vm = pl.BlockSpec(memory_space=pltpu.VMEM)
    hbm = pl.BlockSpec(memory_space=pl.ANY)
    return pl.pallas_call(
        functools.partial(reduce_kernel, channels, ff, ndp, nblk),
        in_specs=[vm] * len(grads),
        out_specs=[hbm, hbm],
        out_shape=[
            jax.ShapeDtypeStruct((total, LANE), BF16),
            jax.ShapeDtypeStruct((srows, LANE), F32),
        ],
        scratch_shapes=[pltpu.VMEM((total, LANE), BF16)] * 3
        + [pltpu.VMEM((srows, LANE), F32)] * 3
        + [
            pltpu.SemaphoreType.DMA((4, ops, wide)),
            pltpu.SemaphoreType.DMA((4, ops, wide)),
            pltpu.SemaphoreType.DMA((2,)),
        ],
        compiler_params=pltpu.CompilerParams(
            vmem_limit_bytes=VMEM, collective_id=1, has_side_effects=True
        ),
    )(*grads)


def unpack_kernel(channels, ff, ndev, out_in, ig_in, first, packed, small, *outs):
    cp = up_to(channels, LANE)
    plans = ((first, ffn_plan(channels, ff, ndev)[0]), (packed, rest_plan(channels, ndev)[0]))
    splan, _ = small_plan(channels, ff, ndev)
    out, ig, g1, b1, wq, qb, wr, rb, rg, rbn, wkv, vb, wp, pb, g2, b2, we, eb, dt, db, ws, sb, cm, out_hold, ig_hold, in_sem, out_sem = (
        outs
    )
    ins, moves = [], []
    for k, (src, hold, dst) in enumerate(((out_in, out_hold, out), (ig_in, ig_hold, ig))):
        for s in range(src.shape[0]):
            ins.append(pltpu.make_async_copy(src.at[s], hold.at[s], in_sem.at[k, s]))
            moves.append(pltpu.make_async_copy(hold.at[s], dst.at[s], out_sem.at[k, s]))
    for copy in ins:
        copy.start()
    lt = cp // LANE

    for copy, move in zip(ins, moves):
        copy.wait()
        move.start()

    def slab(name, t, first=0, count=None):
        ref, plan = plans[0] if name in plans[0][1] else plans[1]
        at, rows, _ = plan[name]
        count = rows if count is None else count
        return ref[at + t * rows + first : at + t * rows + first + count, :].astype(F32)

    for t in range(ff // LANE):
        cut = slice(t * LANE, (t + 1) * LANE)
        we[:, cut] = slab("we", t, 0, channels)
        eb[cut] = slab("we", t, channels, 16)[0]
        ws[:, cut] = slab("ws", t)
        at, rows, _ = splan["tap"]
        dt[:, cut] = small[at + t * rows : at + t * rows + 9, :]
        db[cut] = small[at + t * rows + 9, :]

    def wide(name, first, count=None, base=0):
        return jnp.concatenate([slab(name, base + t, first, count) for t in range(lt)], -1)

    parts = [wide("wr", 0, base=ab * lt) for ab in range(4)]
    wr[...] = jnp.concatenate([v[:, :channels] for v in parts], -1)
    rb[...] = parts[0].T[channels]
    turned = wide("wq", 0).T
    wq[...] = turned[:channels]
    qb[...] = turned[channels]
    wp[...] = wide("wp", 0)[:, :channels]
    wkv[...] = jnp.concatenate(
        [wide("wkv", 0, channels)[:, :channels], wide("wkv", 0, channels, lt)[:, :channels]], -1
    )
    vb[...] = wide("wkv", channels, 16, lt)[1, :channels]
    at, rows, _ = splan["vec"]
    vec = jnp.concatenate([small[at + t * rows : at + (t + 1) * rows, :] for t in range(lt)], -1)
    vec = vec[:, :channels]
    for k, ref in enumerate((g2, b2, sb, rg, rbn, None, g1, b1, pb)):
        if ref is not None:
            ref[...] = vec[k]
    at, rows, _ = splan["count"]
    cm[...] = small[at : at + rows, :].astype(jnp.int32)[:CLASSES, :CLASSES]
    for move in moves:
        move.wait()


def unpack(channels, ff, ndev, out, ig, first, packed, small):
    one = (channels,)
    shapes = [
        one, one, (channels, channels), one, (channels, 4 * channels), one, one, one,
        (channels, 2 * channels), one, (channels, channels), one, one, one, (channels, ff), (ff,),
        (9, ff), (ff,), (channels, ff), one,
    ]
    outs = [jax.ShapeDtypeStruct(v, F32) for v in shapes]
    outs.append(jax.ShapeDtypeStruct((CLASSES, CLASSES), jnp.int32))
    vm = pl.BlockSpec(memory_space=pltpu.VMEM)
    hbm = pl.BlockSpec(memory_space=pl.ANY)
    return pl.pallas_call(
        functools.partial(unpack_kernel, channels, ff, ndev),
        in_specs=[hbm, hbm, vm, vm, vm],
        out_specs=[hbm, hbm] + [vm] * len(outs),
        out_shape=[jax.ShapeDtypeStruct(v.shape, v.dtype) for v in (out, ig)] + outs,
        scratch_shapes=[
            pltpu.VMEM(out.shape, out.dtype),
            pltpu.VMEM(ig.shape, ig.dtype),
            pltpu.SemaphoreType.DMA((2, out.shape[0])),
            pltpu.SemaphoreType.DMA((2, out.shape[0])),
        ],
        compiler_params=pltpu.CompilerParams(vmem_limit_bytes=VMEM),
    )(out, ig, first, packed, small)


def split_low(value):
    hi = value.astype(BF16).astype(F32)
    return hi, value - hi


def rows16(*rows):
    width = rows[0].shape[-1]
    at = lax.broadcasted_iota(jnp.int32, (16, width), 0)
    block = jnp.zeros((16, width), F32)
    for k, row in enumerate(rows):
        block = jnp.where(at == k, row, block)
    return block.astype(BF16)


def prep_kernel(
    channels, g1, b1, qw, qb, rw, rb, rg, rbn, kvw, vb, pw, pb, g2, b2, eb, tb, sb,
    vec, wq, wp, wkv, wr, ebias, dbias, full,
):
    cp = up_to(channels, LANE)
    head_size = channels // HEADS
    rest = cp - channels - 16

    def row(ref):
        return ref[...].reshape(1, ref.shape[-1])

    lane = lanes((1, cp))

    def padded(ref, *at):
        v = widen(row(ref), cp)
        for k in at:
            v = jnp.where(lane == channels + k, 1.0, v)
        return v

    for k, v in enumerate(
        (
            padded(g1), padded(b1, 0, 1), padded(rg), padded(rbn, 1, 2), padded(pb), padded(g2),
            padded(b2, 0, 1), padded(sb),
        )
    ):
        vec[k : k + 1, :] = v

    def fill(ref, top, *rows):
        width = ref.shape[-1]
        ref[:channels, :] = top
        ref[channels : channels + 16, :] = (
            rows16(*rows) if rows else jnp.zeros((16, width), BF16)
        )
        if rest:
            ref[channels + 16 :, :] = jnp.zeros((rest, width), BF16)

    dbias[...] = row(tb)
    ebias[...] = rows16(*split_low(row(eb)))
    q = widen(qw[...], cp)
    qb_wide = widen(row(qb), cp)
    fill(wq, q, *split_low(qb_wide))
    kw = widen(kvw[:, :channels], cp)
    vw = widen(kvw[:, channels:], cp)
    nil = jnp.zeros((1, 2 * cp), F32)
    vb_rows = [
        jnp.concatenate([jnp.zeros((1, cp), F32), widen(v, cp)], -1) for v in split_low(row(vb))
    ]
    fill(wkv, jnp.concatenate([kw, vw], -1), nil, *vb_rows)
    fill(wp, widen(pw[...], cp))
    rb_rows = [widen(v, cp) for v in split_low(row(rb))]
    rw_rows = rw[...].T
    for ab in range(4):
        fill(
            wr.at[ab], widen(rw_rows[ab * channels : (ab + 1) * channels, :], cp),
            *rb_rows[ab : ab + 1],
        )

    def norm(v):
        return jnp.sqrt(jnp.sum(v * v, (0, 1), keepdims=True))

    root = channels**0.5

    def reach(gain, bias):
        top = jnp.max(jnp.abs(row(gain)), (0, 1), keepdims=True)
        return root * top + norm(row(bias))

    def head(value, h):
        tile = value[:, h // 2 * LANE : (h // 2 + 1) * LANE].astype(F32)
        return jnp.where(lanes((1, LANE)) // HALF == h % 2, tile, 0.0)

    query_in, key_in = reach(g1, b1), reach(rg, rbn)
    bound = jnp.zeros((1, 1), F32)
    for h in range(HEADS):
        query = query_in * norm(head(q, h)) + norm(head(qb_wide, h))
        bound = jnp.maximum(bound, query * key_in * norm(head(kw, h)))
    bound = bound * (head_size**-0.5 * 1.05)
    full[...] = jnp.where(2.0 * bound + 256.0 < -NEGATIVE, 0, 1).astype(jnp.int32)


def prep(channels, ff, *weights):
    cp = up_to(channels, LANE)
    shapes = [
        ((8, cp), F32), ((cp, cp), BF16), ((cp, cp), BF16), ((cp, 2 * cp), BF16),
        ((4, cp, cp), BF16), ((16, ff), BF16), ((1, ff), F32), ((1, 1), jnp.int32),
    ]
    return pl.pallas_call(
        functools.partial(prep_kernel, channels),
        out_shape=[jax.ShapeDtypeStruct(*v) for v in shapes],
        compiler_params=pltpu.CompilerParams(vmem_limit_bytes=VMEM),
    )(*weights)


def body(
    tokens, mask, labels, predicted, cotangent, norm1_gain, norm1_bias, query_weight, query_bias,
    reduce_weight, reduce_bias, rnorm_gain, rnorm_bias, kv_weight, value_bias, proj_weight,
    proj_bias, norm2_gain, norm2_bias, expand_weight, expand_bias, depth_weight, depth_bias,
    shrink_weight, shrink_bias,
):
    scenes, height, width, channels = tokens.shape
    ndp, blk = lax.axis_size("dp"), lax.axis_size("blk")
    n = height * width
    ff = expand_weight.shape[1]
    dims = (scenes, height, width, channels, up_to(channels, LANE))
    chips = blk // 2
    used = min(chips, -(-MASK_ROWS // (2 * height)))

    vec, wq, wp, wkv, wr, expand_rows, tap_bias, full = prep(
        channels, ff, norm1_gain, norm1_bias, query_weight, query_bias, reduce_weight.T, reduce_bias,
        rnorm_gain, rnorm_bias, kv_weight, value_bias, proj_weight, proj_bias, norm2_gain,
        norm2_bias, expand_bias, depth_bias, shrink_bias,
    )
    full = full[0, 0] > 0

    def either(call, cids, sizes, *operands):
        if used == chips:
            return call(*sizes, chips, cids[1], *operands)
        return lax.cond(
            full,
            functools.partial(call, *sizes, chips, cids[1]),
            functools.partial(call, *sizes, used, cids[0]),
            *operands,
        )

    tok = tokens.reshape(scenes, n, channels)
    ct = cotangent.reshape(scenes, n, channels)
    red, counts, q, att, ke, ve, rn, res = either(
        attend, (2, 3), (dims, blk), tok, mask, labels, predicted, vec, wr, wq, wkv, wp
    )
    out, gres, first, dtap, dtb, dvec2 = ffn(
        dims, blk, ndp * blk, res, ct, expand_weight, shrink_weight.T, vec, expand_rows, depth_weight,
        tap_bias,
    )
    ig, dwqt, dwrt, dwp, dwkv, dbp, dvec1, first = either(
        attback, (4, 5), (dims, ff, ndp, blk), q, att, gres, ke, ve, rn, tok, red, vec, wp, wkv,
        query_weight, wr, first,
    )
    packed, small = reduce_all(
        channels, ff, ndp, blk, dwrt, dwkv, dwp, dwqt, dtap, dtb, dvec2, dvec1, dbp, counts
    )
    out, ig, *grads = unpack(channels, ff, ndp * blk, out, ig, first, packed, small)
    grads[4], grads[18] = grads[4].T, grads[18].T
    return (out.reshape(tokens.shape), ig.reshape(tokens.shape), *grads)


def solution(mesh):
    banded = P("dp", "blk", None, None)
    plane = P("dp", "blk", None)
    in_specs = (banded, plane, plane, plane, banded) + (P(),) * 20
    out_specs = (banded, banded) + (P(),) * 21
    return jax.shard_map(body, mesh=mesh, in_specs=in_specs, out_specs=out_specs, check_vma=False)
```

```python
import functools

import jax
import jax.numpy as jnp
from jax import lax
from jax.experimental import pallas as pl
from jax.experimental.pallas import tpu as pltpu
from jax.sharding import PartitionSpec as P
import ml_dtypes
import numpy as np

HEADS = 5
CLASSES = 19
EPSILON = 1e-06
NEGATIVE = -32768.0
LOG2E = 1.4426950408889634
LN2 = 0.6931471805599453
F32 = jnp.float32
BF16 = jnp.bfloat16
LANE = 128
HALF = 64
KEY_CHUNK = 256
MASK_ROWS = 48
VMEM = 62 * 2**20
FF_CHUNK = 256
GROUP = 8
NEG = np.float32(NEGATIVE * LOG2E)
NEG_HI = np.float32(ml_dtypes.bfloat16(NEG))
NEG_MID = np.float32(ml_dtypes.bfloat16(NEG - NEG_HI))
NEG_LO = np.float32(ml_dtypes.bfloat16(NEG - NEG_HI - NEG_MID))


def up_to(value, step):
    return -(-value // step) * step


def dot(a, b):
    return lax.dot_general(a, b, (((1,), (0,)), ((), ())), preferred_element_type=F32)


def dot_nt(a, b):
    return lax.dot_general(a, b, (((1,), (1,)), ((), ())), preferred_element_type=F32)


def dot_tn(a, b):
    return lax.dot_general(a, b, (((0,), (0,)), ((), ())), preferred_element_type=F32)


def lanes(shape):
    return lax.broadcasted_iota(jnp.int32, shape, len(shape) - 1)


def whole(shape):
    return pl.BlockSpec(shape, lambda *_: (0,) * len(shape))


def per_scene(shape):
    return pl.BlockSpec((1,) + shape, lambda s: (s,) + (0,) * len(shape))


def inside(value, channels):
    full = channels // LANE * LANE
    if full == value.shape[-1]:
        return value
    last = value[..., full:]
    last = jnp.where(lanes(last.shape) < channels - full, last, 0.0)
    return jnp.concatenate([value[..., :full], last], -1)


def head_blocks(value, free):
    half = lanes((1, LANE)) // HALF
    fills = [free(0), free(1)]
    return [
        jnp.where(half == h % 2, value[:, h // 2 * LANE : (h // 2 + 1) * LANE], fills[h % 2])
        for h in range(HEADS)
    ]


def free_row(parity, values):
    lane = lanes((1, LANE))
    row = jnp.zeros((1, LANE), F32)
    for k, value in values.items():
        row = jnp.where(lane == ext_lane(parity) + k, value, row)
    return row


def centered(value, channels):
    mean = jnp.sum(value, -1, keepdims=True) * (1.0 / channels)
    center = inside(value - mean, channels)
    var = jnp.sum(center * center, -1, keepdims=True) * (1.0 / channels)
    rstd = lax.rsqrt(var + EPSILON)
    return center * rstd, rstd


def norm_back(up, gain, xhat, rstd, channels):
    u = up * gain
    mean = jnp.sum(u, -1, keepdims=True) * (1.0 / channels)
    proj = jnp.sum(u * xhat, -1, keepdims=True) * (1.0 / channels)
    return (u - mean - xhat * proj) * rstd


def ext_lane(head):
    return HALF if head % 2 == 0 else 0


def widen(value, width):
    pad = width - value.shape[-1]
    return jnp.concatenate([value, jnp.zeros(value.shape[:-1] + (pad,), value.dtype)], -1)


def place(blk):
    me = lax.axis_index("blk")
    core = lax.rem(me, 2)
    chip = me // 2
    return chip, core, {"blk": me + 2}, {"blk": me - 2}, {"blk": me + 1 - 2 * core}


def greet(chip, chips, up, down, sib):
    barrier = pltpu.get_barrier_semaphore()
    MESH = pl.DeviceIdType.MESH
    has_up, has_down = chip < chips - 1, chip > 0
    pl.semaphore_signal(barrier, inc=1, device_id=sib, device_id_type=MESH)

    @pl.when(has_up)
    def _():
        pl.semaphore_signal(barrier, inc=1, device_id=up, device_id_type=MESH)

    @pl.when(has_down)
    def _():
        pl.semaphore_signal(barrier, inc=1, device_id=down, device_id_type=MESH)

    pl.semaphore_wait(barrier, 1 + has_up.astype(jnp.int32) + has_down.astype(jnp.int32))


def remote(src, dst, send, recv, device):
    return pltpu.make_async_remote_copy(
        src_ref=src, dst_ref=dst, send_sem=send, recv_sem=recv, device_id=device,
        device_id_type=pl.DeviceIdType.MESH,
    )


def groups_of(ndp, nblk):
    dp_bits, blk_bits = ndp.bit_length() - 1, nblk.bit_length() - 1
    assert ndp == 1 << dp_bits and nblk == 1 << blk_bits
    core = [("blk", 0, 2)] if blk_bits else []
    if dp_bits > 2:
        plane = [("dp", 0, 1 << dp_bits // 2), ("dp", dp_bits // 2, 1 << (dp_bits - dp_bits // 2))]
    else:
        plane = [("dp", 0, ndp)] if dp_bits else []
    line = [("blk", 1, nblk // 2)] if blk_bits > 1 else []
    return core, plane, line


def lay_out(items, ndev):
    plan, at = {}, 0
    for name, rows, slabs in items:
        plan[name] = (at, rows, slabs)
        at += rows * slabs
    unit = 16 * ndev
    units = -(-at // unit)
    last = units // 3 - (1 if units > 6 else 0)
    mid = (units - last) // 2
    return plan, at, [(units - last - mid) * unit, mid * unit, last * unit]


def ffn_plan(channels, ff, ndev):
    tall = up_to(channels + 2, 16)
    return lay_out([("we", tall, ff // LANE), ("ws", channels, ff // LANE)], ndev)


def middle_plan(channels, ndev):
    tall = up_to(channels + 2, 16)
    return lay_out(
        [("wkv", tall, 2 * channels // LANE), ("wp", channels, channels // LANE)], ndev
    )


def rest_plan(channels, ndev):
    assert 4 * channels % LANE == 0 and 2 * channels % LANE == 0 and channels % LANE == HALF
    return lay_out(
        [
            ("wr", channels, 4 * channels // LANE), ("wq", channels, channels // LANE),
            ("halves", channels, 1),
        ],
        ndev,
    )


def small_plan(channels, ff, ndev):
    cp = up_to(channels, LANE)
    plan = {"tap": (0, 16, ff // LANE)}
    at = 16 * (ff // LANE)
    plan["vec"] = (at, 16, cp // LANE)
    at += 16 * (cp // LANE)
    plan["count"] = (at, 32, 1)
    at += 32
    return plan, up_to(at, 8 * ndev)


def member(group):
    axis, bit, size = group
    return lax.rem(lax.axis_index(axis) // (1 << bit), size)


def other(group, index):
    axis, bit, _ = group
    return {axis: lax.axis_index(axis) + (index - member(group)) * (1 << bit)}


def peers_of(order):
    return [
        other(group, lax.rem(member(group) + d, group[2])) for group in order for d in range(1, group[2])
    ]


class Sums:
    def __init__(self, parts, send_sem, recv_sem):
        self.parts, self.send_sem, self.recv_sem = parts, send_sem, recv_sem
        self.rounds = len(parts[0][5])
        self.ops = 2 * self.rounds

    def unit(self, p):
        return 16 if self.parts[p][0].dtype == BF16 else 8

    def segment(self, p, i):
        _, _, _, start, rows, order = self.parts[p]
        for group in order[:i]:
            rows //= group[2]
            start = start + member(group) * rows
        return start, rows

    def landing(self, p, i):
        _, _, _, first, rows, order = self.parts[p]
        for group in order[:i]:
            first += rows // group[2] * (group[2] - 1)
            rows //= group[2]
        return first

    def copies(self, p, k):
        buf, land, done, _, _, order = self.parts[p]
        unit = self.unit(p)
        halving = k < self.rounds
        i = k if halving else self.ops - 1 - k
        group = order[i]
        size = group[2]
        me = member(group)
        result = []
        for d in range(1, size):
            to = lax.rem(me + d, size)
            if halving:
                start, rows = self.segment(p, i)
                rows //= size
                src = buf.at[pl.ds(pl.multiple_of(start + to * rows, unit), rows), :]
                low = self.landing(p, i) + (size - 1 - d) * rows
                dst = land.at[pl.ds(low, rows), :]
            else:
                start, rows = self.segment(p, i + 1)
                src = done.at[pl.ds(pl.multiple_of(start, unit), rows), :]
                dst = src
            result.append(
                remote(
                    src, dst, self.send_sem.at[p, k, d - 1], self.recv_sem.at[p, k, d - 1],
                    other(group, to),
                )
            )
        return result

    def start(self, p, k):
        for copy in self.copies(p, k):
            copy.start()

    def finish(self, p, k):
        for copy in self.copies(p, k):
            copy.wait()
        if k >= self.rounds:
            return
        buf, land, done, _, _, order = self.parts[p]
        unit = self.unit(p)
        keep, rows = self.segment(p, k + 1)
        low = self.landing(p, k)
        step = next(c for c in (256, 128, 64, 32, 16, 8) if rows % c == 0)
        into = done if k == self.rounds - 1 else buf

        @pl.loop(0, rows // step)
        def _(j):
            mine = pl.ds(pl.multiple_of(keep + j * step, unit), step)
            total = buf[mine, :].astype(F32)
            for d in range(order[k][2] - 1):
                theirs = pl.ds(pl.multiple_of(low + d * rows + j * step, unit), step)
                total = total + land[theirs, :].astype(F32)
            into[mine, :] = total.astype(buf.dtype)

    def advance(self, k):
        for p in range(len(self.parts)):
            if k > 0:
                self.finish(p, k - 1)
            if k < self.ops:
                self.start(p, k)


def three_parts(buf, land, done, sizes, orders):
    parts, at = [], 0
    for size, order in zip(sizes, orders):
        if size:
            parts.append((buf, land, done, at, size, order))
        at += size
    return parts


def orders_of(ndp, nblk):
    core, plane, line = groups_of(ndp, nblk)
    return [core + plane + line, core + plane + line, core + line + plane]


def widest(ndp, nblk):
    return max(group[2] for group in orders_of(ndp, nblk)[0]) - 1


def packed_rows(keys, cp):
    return (cp // LANE - 1) * keys + keys // 2 + 16


def pack_block(value, unc, keys, cp):
    full = cp // LANE - 1
    last = value[:, full * LANE :]
    turned = pltpu.roll(last[keys // 2 :], HALF, 1)
    last = jnp.where(lanes((1, LANE)) < HALF, last[: keys // 2], turned)
    flags = jnp.broadcast_to(unc, (keys, LANE))
    if keys < LANE:
        flags = jnp.concatenate([flags, jnp.zeros((LANE - keys, LANE), F32)], 0)
    parts = [value[:, t * LANE : (t + 1) * LANE] for t in range(full)] + [last, flags.T[:16]]
    return jnp.concatenate([v.astype(BF16) for v in parts], 0)


def unpack_block(block, ones, keys, cp):
    full = cp // LANE - 1
    parts = [block[t * keys : (t + 1) * keys] for t in range(full)]
    last = block[full * keys : full * keys + keys // 2].astype(F32)
    last = jnp.concatenate([last, pltpu.roll(last, HALF, 1)], 0)
    last = jnp.where(lanes((1, LANE)) < HALF, last, ones)
    flags = block[full * keys + keys // 2 :].astype(F32)[0:1]
    flags = jnp.broadcast_to(flags, (LANE, LANE)).T[:keys]
    return jnp.concatenate(parts + [last.astype(BF16)], -1), flags


def attend_kernel(
    dims, blk, used, tok_ref, mask_ref, label_ref, pred_ref, tok2_ref, vec_ref, wr_ref, wq_ref,
    wkv_ref, wp_ref,
    red_ref, cnt_ref, q_ref, att_ref, ke_ref, ve_ref, rn_ref, res_ref,
    scr, qbuf, oe, rnbuf, up_send, down_send, sib_send, line_recv, sib_recv,
):
    scenes, height, width, channels, cp = dims
    n = height * width
    keys = n // 4
    chips = blk // 2
    lag = chips
    step = pl.program_id(0)
    head_size = channels // HEADS
    chip, core, up, down, sib = place(blk)

    @pl.when(step == 0)
    def _():
        greet(chip, chips, up, down, sib)
        cnt_ref[...] = jnp.zeros(cnt_ref.shape, F32)

    def slot(origin, c):
        return c * used + origin

    def send_up(s, origin):
        place_ = rnbuf.at[s, slot(origin, core)]
        return remote(place_, place_, up_send.at[s, origin], line_recv.at[s, origin], up)

    def send_down(s, origin):
        place_ = rnbuf.at[s, slot(origin, core)]
        return remote(place_, place_, down_send.at[s, origin], line_recv.at[s, origin], down)

    def send_sib(s, origin):
        place_ = rnbuf.at[s, slot(origin, core)]
        return remote(place_, place_, sib_send.at[s, origin], sib_recv.at[s, origin], sib)

    @pl.when(step < scenes)
    def _():
        s = step
        x = widen(tok_ref[0].astype(F32), cp)
        xhat, _ = centered(x, channels)
        low = (xhat * vec_ref[0:1] + vec_ref[1:2]).astype(BF16)
        lowf = low.astype(F32)
        for t in range(cp // LANE):
            scr[t] = lowf[:, t * LANE : (t + 1) * LANE]
        total = jnp.zeros((keys, cp), F32)
        for b in range(2):
            part = [scr[t, pl.ds(b, n // 2, stride=2), :] for t in range(cp // LANE)]
            part = jnp.concatenate(part, -1).reshape(height // 2, 2, width // 2, cp)
            for a in range(2):
                total = total + dot(part[:, a].reshape(keys, cp).astype(BF16), wr_ref[2 * a + b])
        red_ref[0] = total
        rhat, _ = centered(total, channels)
        m = mask_ref[0].astype(F32)
        shape = (width // 2, width)
        near = lanes(shape) // 2 == lax.broadcasted_iota(jnp.int32, shape, 0)
        flags = []
        for i in range(height // 2):
            both = m[2 * i : 2 * i + 1] + m[2 * i + 1 : 2 * i + 2]
            flags.append(jnp.sum(jnp.where(near, both, 0.0), -1, keepdims=True))
        unc = jnp.where(jnp.concatenate(flags, 0) > 0.0, 0.0, 1.0)
        own = pack_block(rhat * vec_ref[2:3] + vec_ref[3:4], unc, keys, cp)

        @pl.when(chip < used)
        def _():
            rnbuf[s, slot(chip, core)] = own
            send_sib(s, chip).start()

            @pl.when(chip < chips - 1)
            def _():
                send_up(s, chip).start()

            @pl.when(chip > 0)
            def _():
                send_down(s, chip).start()

        qf = dot(low, wq_ref[...]) * (LOG2E * head_size**-0.5)
        ones = head_blocks(qf, lambda e: free_row(e, {0: 1.0, 1: 1.0, 2: 1.0}))
        for h in range(HEADS):
            qbuf[lax.rem(s, lag + 1), :, h * LANE : (h + 1) * LANE] = ones[h].astype(BF16)
        shape = (cnt_ref.shape[0], width)
        classes = lax.broadcasted_iota(jnp.int32, shape, 0)
        wide = lax.broadcasted_iota(jnp.int32, (LANE, width), 0)
        total = jnp.zeros(cnt_ref.shape, F32)
        for r in range(height):
            label = jnp.where(mask_ref[0, r : r + 1] > 0, label_ref[0, r : r + 1], -1)
            hot = jnp.where(label == classes, 1.0, 0.0).astype(BF16)
            pred = jnp.where(pred_ref[0, r : r + 1] == wide, 1.0, 0.0).astype(BF16)
            total = total + dot_nt(hot, pred)
        cnt_ref[...] += total

    for age in range(1, chips):
        s = step - age

        @pl.when(jnp.logical_and(s >= 0, s < scenes))
        def _(s=s, age=age):
            below = chip - age

            @pl.when(jnp.logical_and(below >= 0, below < used))
            def _():
                send_up(s, below).wait_recv()
                send_sib(s, below).start()

                @pl.when(chip < chips - 1)
                def _():
                    send_up(s, below).start()

            above = chip + age

            @pl.when(above < used)
            def _():
                send_down(s, above).wait_recv()
                send_sib(s, above).start()

                @pl.when(chip > 0)
                def _():
                    send_down(s, above).start()

    @pl.when(step >= lag)
    def _():
        s = step - lag

        for origin in range(used):
            send_sib(s, origin).wait_recv()

        free = vec_ref[3:4, cp - LANE :]
        blocks = [unpack_block(rnbuf[s, i], free, keys, cp) for i in range(2 * used)]
        rn_all = jnp.concatenate([v[0] for v in blocks], 0)
        rn_ref[0] = rn_all
        flag = jnp.concatenate([v[1] for v in blocks], 0)
        kv = dot(rn_all, wkv_ref[...])
        negative = {0: float(NEG_HI), 1: float(NEG_MID), 2: float(NEG_LO)}
        for h, block in enumerate(
            head_blocks(
                kv[:, :cp],
                lambda e: flag * free_row(e, negative) + free_row(e, {3: 1.0, 4: 1.0, 5: 1.0}),
            )
        ):
            ke_ref[0, :, h * LANE : (h + 1) * LANE] = block.astype(BF16)
        for h, block in enumerate(
            head_blocks(kv[:, cp:], lambda e: free_row(e, {0: 1.0, 1: 1.0, 2: 1.0}))
        ):
            ve_ref[0, :, h * LANE : (h + 1) * LANE] = block.astype(BF16)
        mine = lax.rem(s, lag + 1)
        count = 2 * used * keys // KEY_CHUNK
        for h in range(HEADS):
            block = slice(h * LANE, (h + 1) * LANE)
            e = ext_lane(h)
            q = qbuf[mine, :, block]
            parts = [
                dot_nt(q, ke_ref[0, j * KEY_CHUNK : (j + 1) * KEY_CHUNK, block])
                for j in range(count)
            ]
            top = functools.reduce(jnp.maximum, parts)
            top = jnp.max(top, -1, keepdims=True)
            out = jnp.zeros((n, LANE), F32)
            for j in range(count):
                p = jnp.exp2(parts[j] - top).astype(BF16)
                out = out + dot(p, ve_ref[0, j * KEY_CHUNK : (j + 1) * KEY_CHUNK, block])
            total = out[:, e : e + 1]
            oe[h] = out / total
            lse = top + jnp.log2(total)
            hi = lse.astype(BF16).astype(F32)
            mid = (lse - hi).astype(BF16).astype(F32)
            lo = lse - hi - mid
            lane = lanes((n, LANE))
            q2 = q.astype(F32)
            q2 = jnp.where(lane == e + 3, -hi, q2)
            q2 = jnp.where(lane == e + 4, -mid, q2)
            q2 = jnp.where(lane == e + 5, -lo, q2)
            q_ref[0, :, block] = q2.astype(BF16)

        tiles = []
        low_half = lanes((n, LANE)) < HALF
        for t in range(cp // LANE):
            other = oe[2 * t + 1] if 2 * t + 1 < HEADS else jnp.zeros((n, LANE), F32)
            tiles.append(jnp.where(low_half, oe[2 * t], other))
        att = jnp.concatenate(tiles, -1)
        att_ref[0] = att
        x = widen(tok2_ref[0].astype(F32), cp)
        resid = x + dot(att.astype(BF16), wp_ref[...]) + vec_ref[4:5]
        for t in range(cp // LANE):
            for r in range(height):
                for half in range(2):
                    base = r * width + half * (width // 2)
                    at = r * scenes * width + half * scenes + s
                    res_ref[t, pl.ds(at, width // 2, stride=2 * scenes), :] = resid[
                        base : base + width // 2, t * LANE : (t + 1) * LANE
                    ]

    @pl.when(step == scenes + lag - 1)
    def _():
        @pl.loop(0, scenes)
        def _(s):
            for origin in range(used):
                send_sib(s, origin).wait_send()

                @pl.when(jnp.logical_and(origin <= chip, chip < chips - 1))
                def _(origin=origin):
                    send_up(s, origin).wait_send()

                @pl.when(jnp.logical_and(origin >= chip, chip > 0))
                def _(origin=origin):
                    send_down(s, origin).wait_send()


def attend(dims, blk, used, cid, tok, mask, labels, predicted, vec, wr, wq, wkv, wp):
    scenes, height, width, channels, cp = dims
    n = height * width
    keys = n // 4
    chips = blk // 2
    lag = chips
    k = blk * keys
    live = 2 * used * keys
    he = HEADS * LANE

    def early(shape):
        return pl.BlockSpec(
            (1,) + shape, lambda t: (jnp.minimum(t, scenes - 1),) + (0,) * len(shape)
        )

    def late(shape):
        return pl.BlockSpec((1,) + shape, lambda t: (jnp.maximum(t - lag, 0),) + (0,) * len(shape))

    return pl.pallas_call(
        functools.partial(attend_kernel, dims, blk, used),
        grid=(scenes + lag,),
        in_specs=[early((n, channels))]
        + [early((height, width))] * 3
        + [late((n, channels))]
        + [whole(v.shape) for v in (vec, wr, wq, wkv, wp)],
        out_specs=[
            early((keys, cp)),
            whole((32, LANE)),
            late((n, he)),
            late((n, cp)),
            late((live, he)),
            late((live, he)),
            late((live, cp)),
            whole((cp // LANE, scenes * n, LANE)),
        ],
        out_shape=[
            jax.ShapeDtypeStruct((scenes, keys, cp), F32),
            jax.ShapeDtypeStruct((32, LANE), F32),
            jax.ShapeDtypeStruct((scenes, n, he), BF16),
            jax.ShapeDtypeStruct((scenes, n, cp), F32),
            jax.ShapeDtypeStruct((scenes, k, he), BF16),
            jax.ShapeDtypeStruct((scenes, k, he), BF16),
            jax.ShapeDtypeStruct((scenes, k, cp), BF16),
            jax.ShapeDtypeStruct((cp // LANE, scenes * n, LANE), F32),
        ],
        scratch_shapes=[
            pltpu.VMEM((cp // LANE, n, LANE), F32),
            pltpu.VMEM((lag + 1, n, he), BF16),
            pltpu.VMEM((HEADS, n, LANE), F32),
            pltpu.VMEM((scenes, 2 * used, packed_rows(keys, cp), LANE), BF16),
        ]
        + [pltpu.SemaphoreType.DMA((scenes, used))] * 5,
        compiler_params=pltpu.CompilerParams(
            vmem_limit_bytes=VMEM, collective_id=cid, has_side_effects=True
        ),
    )(tok, mask, labels, predicted, tok, vec, wr, wq, wkv, wp)


def ffn_kernel(
    dims, ff, blk, ndev, res_hbm, ct_hbm, ew_hbm, sw_hbm, vec_ref, eb_ref, taps_ref, tb_ref,
    out_hbm, gres_hbm, pack_hbm, dtap_ref, dtb_ref, dvec_ref,
    we_ref, ws_ref, dwe_ref, dwst, packed, res_ref, ct_ref, cn, cnt, ctt, ctx, oacc, gacc, hid, gm, halo, act, back, tapacc, out_stage, gres_stage,
    weight_sem, pack_sem, res_sem, ct_sem, out_sem, gres_sem, cn_send, cn_recv, gm_send, gm_recv,
):
    scenes, height, width, channels, cp = dims
    n = height * width
    rw = scenes * width
    lt = cp // LANE
    fc = FF_CHUNK
    nchunk = ff // fc
    cols = width // 2
    pair = 2 * scenes
    group = GROUP if cols % GROUP == 0 else cols
    me = lax.axis_index("blk")
    has_left = me > 0
    has_right = me < blk - 1
    left, right = {"blk": me - 1}, {"blk": me + 1}
    MESH = pl.DeviceIdType.MESH

    def res_copy(r):
        rows = pl.ds(pl.multiple_of(r * rw, rw), rw)
        return pltpu.make_async_copy(res_hbm.at[:, rows, :], res_ref.at[:, rows, :], res_sem.at[r])

    def ct_copy(s):
        return pltpu.make_async_copy(ct_hbm.at[s], ct_ref.at[s], ct_sem.at[s])

    ew_copy = pltpu.make_async_copy(ew_hbm, we_ref.at[:channels, :], weight_sem.at[0])
    sw_copy = pltpu.make_async_copy(sw_hbm, ws_ref.at[:channels, :], weight_sem.at[1])
    for r in range(height):
        res_copy(r).start()
    for s in range(scenes):
        ct_copy(s).start()
    ew_copy.start()
    sw_copy.start()
    bias_rows = eb_ref.shape[0]
    we_ref[channels : channels + bias_rows, :] = eb_ref[...]
    if channels + bias_rows < cp:
        we_ref[channels + bias_rows :, :] = jnp.zeros((cp - channels - bias_rows, ff), BF16)
    ws_ref[channels:, :] = jnp.zeros((cp - channels, ff), BF16)

    barrier = pltpu.get_barrier_semaphore()

    @pl.when(has_left)
    def _():
        pl.semaphore_signal(barrier, inc=1, device_id=left, device_id_type=MESH)

    @pl.when(has_right)
    def _():
        pl.semaphore_signal(barrier, inc=1, device_id=right, device_id_type=MESH)

    pl.semaphore_wait(barrier, has_left.astype(jnp.int32) + has_right.astype(jnp.int32))

    def row(r, size=rw):
        return pl.ds(pl.multiple_of(r * rw, rw), size)

    g2, b2 = vec_ref[5:6], vec_ref[6:7]

    def load3(ref, r):
        return jnp.concatenate([ref[t, row(r), :] for t in range(lt)], -1)

    def store3(ref, r, value):
        for t in range(lt):
            ref[t, row(r), :] = value[:, t * LANE : (t + 1) * LANE]

    @pl.loop(0, height)
    def _(r):
        res_copy(r).wait()
        x = load3(res_ref, r)
        xhat, rstd = centered(x, channels)
        c = (xhat * g2 + b2).astype(BF16)
        cn[row(r + 1), :] = c
        cnt[:, row(r)] = c.T
        store3(oacc, r, x + vec_ref[7:8])
        store3(res_ref, r, jnp.where(lanes(xhat.shape) == channels, rstd, xhat))

    def cn_copy(up):
        return pltpu.make_async_remote_copy(
            src_ref=cn.at[row(1 if up else height), :],
            dst_ref=cn.at[row(height + 1 if up else 0), :],
            send_sem=cn_send.at[0 if up else 1],
            recv_sem=cn_recv.at[0 if up else 1],
            device_id=left if up else right,
            device_id_type=MESH,
        )

    @pl.when(has_left)
    def _():
        cn_copy(True).start()

    @pl.when(has_right)
    def _():
        cn_copy(False).start()

    @pl.loop(0, scenes)
    def _(s):
        ct_copy(s).wait()
        c = widen(ct_ref[s].astype(F32), cp)
        for t in range(lt):
            for r in range(height):
                for half in range(2):
                    base = r * width + half * cols
                    gacc[t, pl.ds(r * rw + half * scenes + s, cols, stride=pair), :] = c[
                        base : base + cols, t * LANE : (t + 1) * LANE
                    ]

    dvec_ref[...] = jnp.zeros(dvec_ref.shape, F32)

    @pl.loop(0, height)
    def _(r):
        c = load3(gacc, r)
        dvec_ref[2:3] += jnp.sum(c, 0, keepdims=True)
        low = c.astype(BF16)
        ctt[row(r), :] = low
        ctx[:, row(r)] = low.T
        store3(gacc, r, jnp.zeros((rw, cp), F32))

    ew_copy.wait()
    sw_copy.wait()
    dwe_ref[...] = jnp.zeros(dwe_ref.shape, F32)
    dwst[...] = jnp.zeros(dwst.shape, F32)

    @pl.when(has_left)
    def _():
        cn_copy(False).wait_recv()

    @pl.when(jnp.logical_not(has_left))
    def _():
        cn[row(0), :] = jnp.zeros((rw, cp), BF16)

    @pl.when(has_right)
    def _():
        cn_copy(True).wait_recv()

    @pl.when(jnp.logical_not(has_right))
    def _():
        cn[row(height + 1), :] = jnp.zeros((rw, cp), BF16)

    def put(ref, slot, r, value):
        v = value.reshape(cols, pair, fc)
        z = jnp.zeros((scenes, fc), F32)
        ref[slot, r, 1 : cols + 1] = v.astype(BF16)
        ref[slot, r, 0] = jnp.concatenate([z, v[cols - 1, :scenes]], 0).astype(BF16)
        ref[slot, r, cols + 1] = jnp.concatenate([v[0, scenes:], z], 0).astype(BF16)

    def gm_copy(k, slot, up):
        return pltpu.make_async_remote_copy(
            src_ref=gm.at[slot, 1 if up else height],
            dst_ref=halo.at[k, 1 if up else 0],
            send_sem=gm_send.at[k, 0 if up else 1],
            recv_sem=gm_recv.at[k, 0 if up else 1],
            device_id=left if up else right,
            device_id_type=MESH,
        )

    def phase_a(k, slot):
        span = pl.ds(pl.multiple_of(k * fc, fc), fc)
        taps = [
            taps_ref[pl.ds(i, 1), span].astype(BF16).reshape(1, 1, fc) for i in range(9)
        ]
        bias = tb_ref[:, span]

        def hidden(r):
            put(hid, slot, r, dot(cn[r * rw : (r + 1) * rw, :], we_ref[:, span]))

        def products(r):
            active = act[r * rw : (r + 1) * rw, :]
            o = dot_nt(active, ws_ref[:, span])
            for t in range(lt):
                oacc[t, r * rw : (r + 1) * rw, :] += o[:, t * LANE : (t + 1) * LANE]
            dwst[:, span] += dot(ctx[:, r * rw : (r + 1) * rw], active)

        hidden(0)
        hidden(1)
        hidden(2)
        sums = jnp.zeros((8, fc), F32)
        for r in range(height):
            back[...] = dot(ctt[r * rw : (r + 1) * rw, :], ws_ref[:, span])
            if r:
                products(r - 1)
            for g in range(0, cols, group):
                acc = None
                for a in range(3):
                    line = hid[slot, r + a, g : g + group + 2]
                    for b in range(3):
                        term = line[b : b + group] * taps[3 * a + b]
                        acc = term if acc is None else acc + term
                mixed = acc.astype(F32).reshape(group * pair, fc) + bias
                arg = mixed * 0.7071067811865476
                phi = 0.5 + 0.5 * lax.erf(arg)
                dens = jnp.exp2(arg * arg * -LOG2E) * mixed
                act[r * rw + g * pair : r * rw + (g + group) * pair, :] = (mixed * phi).astype(BF16)
                slope = phi + dens * 0.3989422804014327
                grad = back[g * pair : (g + group) * pair, :] * slope
                sums = sums + jnp.sum(grad.reshape(group * pair // 8, 8, fc), 0)
                v = grad.reshape(group, pair, fc)
                gm[slot, r + 1, g + 1 : g + group + 1] = v.astype(BF16)
                z = jnp.zeros((scenes, fc), F32)
                if g == 0:
                    gm[slot, r + 1, cols + 1] = jnp.concatenate([v[0, scenes:], z], 0).astype(BF16)
                if g + group == cols:
                    gm[slot, r + 1, 0] = jnp.concatenate([z, v[group - 1, :scenes]], 0).astype(BF16)
            if r + 3 < height + 2:
                hidden(r + 3)
        products(height - 1)
        dtb_ref[:, span] = sums

        @pl.when(has_left)
        def _():
            gm_copy(k, slot, True).start()

        @pl.when(has_right)
        def _():
            gm_copy(k, slot, False).start()

    def phase_b(k, slot):
        span = pl.ds(pl.multiple_of(k * fc, fc), fc)

        @pl.when(has_left)
        def _():
            gm_copy(k, slot, False).wait_recv()
            gm[slot, 0] = halo[k, 0]

        @pl.when(jnp.logical_not(has_left))
        def _():
            gm[slot, 0] = jnp.zeros((cols + 2, pair, fc), BF16)

        @pl.when(has_right)
        def _():
            gm_copy(k, slot, True).wait_recv()
            gm[slot, height + 1] = halo[k, 1]

        @pl.when(jnp.logical_not(has_right))
        def _():
            gm[slot, height + 1] = jnp.zeros((cols + 2, pair, fc), BF16)

        taps = [
            taps_ref[pl.ds(i, 1), span].astype(BF16).reshape(1, 1, fc) for i in range(9)
        ]
        tapacc[...] = jnp.zeros(tapacc.shape, F32)

        def products(r):
            low = act[r * rw : (r + 1) * rw, :]
            dwe_ref[:, span] += dot(cnt[:, r * rw : (r + 1) * rw], low)
            g = dot_nt(low, we_ref[:, span])
            for t in range(lt):
                gacc[t, r * rw : (r + 1) * rw, :] += g[:, t * LANE : (t + 1) * LANE]

        for r in range(height):
            tapsum = [None] * 9
            for g in range(0, cols, group):
                acc = None
                own = hid[slot, r + 1, g + 1 : g + group + 1]
                for a in range(3):
                    line = gm[slot, r + 2 - a, g : g + group + 2]
                    for b in range(3):
                        window = line[2 - b : 2 - b + group]
                        term = window * taps[3 * a + b]
                        acc = term if acc is None else acc + term
                        prod = own * window
                        while prod.shape[0] > 1:
                            cut = prod.shape[0] // 2
                            prod = prod[:cut] + prod[cut:]
                        i = 3 * a + b
                        tapsum[i] = prod[0] if tapsum[i] is None else tapsum[i] + prod[0]
                act[r * rw + g * pair : r * rw + (g + group) * pair, :] = acc.reshape(group * pair, fc)
            for i in range(9):
                tapacc[i] += tapsum[i].astype(F32)
        for r in range(height):
            products(r)

        for tap in range(9):
            dtap_ref[pl.ds(tap, 1), span] = jnp.sum(tapacc[tap], 0, keepdims=True)

        @pl.when(has_left)
        def _():
            gm_copy(k, slot, True).wait_send()

        @pl.when(has_right)
        def _():
            gm_copy(k, slot, False).wait_send()

    @pl.loop(0, nchunk + 1)
    def _(k):
        slot = lax.rem(k, 2)

        @pl.when(k < nchunk)
        def _():
            phase_a(k, slot)

        @pl.when(k > 0)
        def _():
            phase_b(k - 1, 1 - slot)

    @pl.when(has_left)
    def _():
        cn_copy(True).wait_send()

    @pl.when(has_right)
    def _():
        cn_copy(False).wait_send()

    plan, filled, _ = ffn_plan(channels, ff, ndev)
    for name, ref in (("we", dwe_ref), ("ws", dwst)):
        at, rows, slabs = plan[name]
        for t in range(slabs):
            packed[at + t * rows : at + (t + 1) * rows, :] = ref[
                :rows, t * LANE : (t + 1) * LANE
            ].astype(BF16)
    if filled < packed.shape[0]:
        packed[filled:, :] = jnp.zeros((packed.shape[0] - filled, LANE), BF16)
    pack_copy = pltpu.make_async_copy(packed, pack_hbm, pack_sem.at[0])
    pack_copy.start()

    def gather(ref, s):
        rows = []
        for r in range(height):
            for half in range(2):
                rows.append(
                    jnp.concatenate(
                        [
                            ref[t, pl.ds(r * rw + half * scenes + s, cols, stride=pair), :]
                            for t in range(lt)
                        ],
                        -1,
                    )
                )
        return jnp.concatenate(rows, 0)[:, :channels]

    def out_copy(s, slot):
        return pltpu.make_async_copy(out_stage.at[slot], out_hbm.at[s], out_sem.at[slot])

    def gres_copy(s, slot):
        return pltpu.make_async_copy(gres_stage.at[slot], gres_hbm.at[s], gres_sem.at[slot])

    @pl.loop(0, scenes)
    def _(s):
        slot = lax.rem(s, 2)

        @pl.when(s >= 2)
        def _():
            out_copy(s - 2, slot).wait()

        out_stage[slot] = gather(oacc, s).astype(BF16)
        out_copy(s, slot).start()

    @pl.loop(0, height)
    def _(r):
        kept = load3(res_ref, r)
        rstd = kept[:, channels : channels + 1]
        xhat = inside(kept, channels)
        upstream = load3(gacc, r)
        dvec_ref[0:1] += jnp.sum(upstream * xhat, 0, keepdims=True)
        dvec_ref[1:2] += jnp.sum(upstream, 0, keepdims=True)
        g = ctt[row(r), :].astype(F32) + norm_back(upstream, g2, xhat, rstd, channels)
        store3(gacc, r, g)

    @pl.loop(0, scenes)
    def _(s):
        slot = lax.rem(s, 2)

        @pl.when(s >= 2)
        def _():
            gres_copy(s - 2, slot).wait()

        gres_stage[slot] = gather(gacc, s)
        gres_copy(s, slot).start()

    for s in range(scenes - 2, scenes):
        out_copy(s, s % 2).wait()
        gres_copy(s, s % 2).wait()
    pack_copy.wait()


def ffn(dims, blk, ndev, res, ct, ew, sw, vec, eb, taps, tb):
    scenes, height, width, channels, cp = dims
    n = height * width
    total = scenes * n
    rw = scenes * width
    ff = sw.shape[1]
    lt = cp // LANE
    nchunk = ff // FF_CHUNK
    strip = (width // 2 + 2, 2 * scenes, FF_CHUNK)
    pack_rows = sum(ffn_plan(channels, ff, ndev)[2])
    vm = pl.BlockSpec(memory_space=pltpu.VMEM)
    hbm = pl.BlockSpec(memory_space=pl.ANY)
    return pl.pallas_call(
        functools.partial(ffn_kernel, dims, ff, blk, ndev),
        in_specs=[hbm] * 4 + [vm] * 4,
        out_specs=[hbm, hbm, hbm] + [vm] * 3,
        out_shape=[
            jax.ShapeDtypeStruct((scenes, n, channels), BF16),
            jax.ShapeDtypeStruct((scenes, n, channels), F32),
            jax.ShapeDtypeStruct((pack_rows, LANE), BF16),
            jax.ShapeDtypeStruct((9, ff), F32),
            jax.ShapeDtypeStruct((8, ff), F32),
            jax.ShapeDtypeStruct((8, cp), F32),
        ],
        scratch_shapes=[
            pltpu.VMEM((cp, ff), BF16),
            pltpu.VMEM((cp, ff), BF16),
            pltpu.VMEM((cp, ff), F32),
            pltpu.VMEM((cp, ff), F32),
            pltpu.VMEM((pack_rows, LANE), BF16),
            pltpu.VMEM((lt, total, LANE), F32),
            pltpu.VMEM((scenes, n, channels), BF16),
            pltpu.VMEM((total + 2 * rw, cp), BF16),
            pltpu.VMEM((cp, total), BF16),
            pltpu.VMEM((total, cp), BF16),
            pltpu.VMEM((cp, total), BF16),
            pltpu.VMEM((lt, total, LANE), F32),
            pltpu.VMEM((lt, total, LANE), F32),
            pltpu.VMEM((2, height + 2) + strip, BF16),
            pltpu.VMEM((2, height + 2) + strip, BF16),
            pltpu.VMEM((nchunk, 2) + strip, BF16),
            pltpu.VMEM((total, FF_CHUNK), BF16),
            pltpu.VMEM((rw, FF_CHUNK), F32),
            pltpu.VMEM((9, 2 * scenes, FF_CHUNK), F32),
            pltpu.VMEM((2, n, channels), BF16),
            pltpu.VMEM((2, n, channels), F32),
            pltpu.SemaphoreType.DMA((2,)),
            pltpu.SemaphoreType.DMA((1,)),
            pltpu.SemaphoreType.DMA((height,)),
            pltpu.SemaphoreType.DMA((scenes,)),
            pltpu.SemaphoreType.DMA((2,)),
            pltpu.SemaphoreType.DMA((2,)),
            pltpu.SemaphoreType.DMA((2,)),
            pltpu.SemaphoreType.DMA((2,)),
            pltpu.SemaphoreType.DMA((nchunk, 2)),
            pltpu.SemaphoreType.DMA((nchunk, 2)),
        ],
        compiler_params=pltpu.CompilerParams(
            vmem_limit_bytes=VMEM, collective_id=0, has_side_effects=True
        ),
    )(res, ct, ew, sw, vec, eb, taps, tb)


def attback_kernel(
    dims, ff, ndp, blk, used, q_ref, att_ref, gres_ref, ke_ref, ve_ref, rn_ref, tok_ref, gres2_ref,
    red_ref, vec_ref, wp_ref, wkv_ref, wq_ref, wr_ref, dtap, dtb, dvec2, cnt, first_hbm,
    ig_ref, sum_hbm, mid_hbm, rest_hbm, small_hbm,
    dwqt, dwrt, dwp_ref, dwkv_ref, dbp_ref, dvec_ref, ge, dqt, gqt_ref, grn_ref, scr, gscr, own, acc, sib_land, up_land, down_land,
    gkv_ref, work, land, done, mid_work, mid_land, mid_done, rest_work, rest_land, rest_done, small_work, small_land, small_done,
    sib_send, sib_recv, up_send, up_recv, down_send, down_recv, sum_send, sum_recv,
    mid_send, mid_recv, rest_send, rest_recv, sum_sem,
):
    scenes, height, width, channels, cp = dims
    n = height * width
    keys = n // 4
    chips = blk // 2
    lt = cp // LANE
    head_size = channels // HEADS
    step = pl.program_id(0)
    chip, core, up, down, sib = place(blk)
    count = 2 * used * keys // KEY_CHUNK
    steps = scenes + chips
    together = -(-scenes // chips)
    ndev = ndp * blk
    order = orders_of(ndp, blk)[0]
    parts = three_parts(work, land, done, ffn_plan(channels, ff, ndev)[2], [order] * 3)
    sums = Sums(parts, sum_send, sum_recv)
    each = -(-(sums.ops + 1) // (steps - 1))
    mid_plan, mid_used, mid_sizes = middle_plan(channels, ndev)
    mid = Sums(
        three_parts(mid_work, mid_land, mid_done, mid_sizes, [order] * 3), mid_send, mid_recv
    )
    early = min(chips, mid.ops)

    def put(buf, plan, name, value):
        at, rows, slabs = plan[name]
        for t in range(slabs):
            buf[at + t * rows : at + (t + 1) * rows, :] = value(t, rows).astype(BF16)

    def cut_of(value):
        return lambda t, rows: value[:rows, t * LANE : (t + 1) * LANE]

    @pl.when(step == 0)
    def _():
        load = pltpu.make_async_copy(first_hbm, work, sum_sem.at[0])
        load.start()
        barrier = pltpu.get_barrier_semaphore()
        peers = peers_of(order)
        for peer in peers:
            pl.semaphore_signal(barrier, inc=1, device_id=peer, device_id_type=pl.DeviceIdType.MESH)
        pl.semaphore_wait(barrier, len(peers))
        load.wait()
        for k in range(each):
            sums.advance(k)
        dwqt[...] = jnp.zeros(dwqt.shape, F32)
        dwrt[...] = jnp.zeros(dwrt.shape, F32)
        dvec_ref[...] = jnp.zeros(dvec_ref.shape, F32)
        dwp_ref[...] = jnp.zeros(dwp_ref.shape, F32)
        dwkv_ref[...] = jnp.zeros(dwkv_ref.shape, F32)
        dbp_ref[...] = jnp.zeros(dbp_ref.shape, F32)

    def to_sib(s, target):
        return remote(
            own.at[lax.rem(s, 2), 1 - core, target], sib_land.at[s, target], sib_send.at[s, target],
            sib_recv.at[s, target], sib,
        )

    def to_up(s, target):
        return remote(
            acc.at[s, target], up_land.at[s, target], up_send.at[s, target], up_recv.at[s, target], up
        )

    def to_down(s, target):
        return remote(
            acc.at[s, target], down_land.at[s, target], down_send.at[s, target],
            down_recv.at[s, target], down,
        )

    def plus(a, b):
        return (a.astype(F32) + b.astype(F32)).astype(BF16)

    def chunk(j):
        s = step
        per = KEY_CHUNK // keys
        span = slice(j * KEY_CHUNK, (j + 1) * KEY_CHUNK)
        dks, dvs = [], []
        for h in range(HEADS):
            block = slice(h * LANE, (h + 1) * LANE)
            k, v = ke_ref[0, span, block], ve_ref[0, span, block]
            q, g = q_ref[0, :, block], ge[:, block]
            p = jnp.exp2(dot_nt(k, q))
            gs = (p * dot_nt(v, g)).astype(BF16)
            dvs.append(dot(p.astype(BF16), g))
            dks.append(dot(gs, q))
            dqt[block, :] += dot_tn(k, gs)
        low_half = lanes((KEY_CHUNK, LANE)) < HALF
        tiles = []
        for group, scale in ((dks, LN2), (dvs, 1.0)):
            for t in range(lt):
                other = (
                    group[2 * t + 1] if 2 * t + 1 < HEADS else jnp.zeros((KEY_CHUNK, LANE), F32)
                )
                tiles.append((jnp.where(low_half, group[2 * t], other) * scale).astype(BF16))
        gkv = jnp.concatenate(tiles, -1)
        grn = dot_nt(gkv, wkv_ref[...]).astype(BF16)
        for i in range(per):
            at = j * per + i
            own[lax.rem(s, 2), at // used, at % used] = grn[i * keys : (i + 1) * keys]

            @pl.when(core != at // used)
            def _(at=at):
                to_sib(s, at % used).start()

        gkv_ref[span, :] = gkv

    @pl.when(step < scenes)
    def _():
        s = step
        gb = widen(gres_ref[0], cp).astype(BF16)
        dbp_ref[...] += jnp.sum(gb.astype(F32).reshape(n // 8, 8, cp), 0)
        att = att_ref[0]
        dwp_ref[...] += dot(att.astype(BF16).T, gb)
        gatt = head_blocks(dot_nt(gb, wp_ref[...]), lambda e: 0.0)
        lane = lanes((n, LANE))
        for h in range(HEADS):
            e = ext_lane(h)
            g = gatt[h].astype(BF16).astype(F32)
            o = att[:, (h // 2) * LANE : (h // 2 + 1) * LANE]
            inner = jnp.sum(g * o, -1, keepdims=True)
            hi = inner.astype(BF16).astype(F32)
            g = jnp.where(lane == e, -hi, g)
            g = jnp.where(lane == e + 1, hi - inner, g)
            ge[:, h * LANE : (h + 1) * LANE] = g.astype(BF16)
        dqt[...] = jnp.zeros(dqt.shape, F32)
        chunk(0)

    s1 = step - 1

    @pl.when(jnp.logical_and(s1 >= 0, s1 < scenes))
    def _():
        for target in range(used):
            to_sib(s1, target).wait()
            acc[s1, target] = plus(own[lax.rem(s1, 2), core, target], sib_land[s1, target])

    s_up = step - 1 - chip

    @pl.when(jnp.logical_and(s_up >= 0, s_up < scenes))
    def _():
        for target in reversed(range(1, used)):

            @pl.when(target > chip)
            def _(target=target):
                @pl.when(chip > 0)
                def _():
                    to_up(s_up, target).wait_recv()
                    acc[s_up, target] = plus(acc[s_up, target], up_land[s_up, target])

                to_up(s_up, target).start()

    s_down = step - chips + chip

    @pl.when(jnp.logical_and(s_down >= 0, s_down < scenes))
    def _():
        for target in range(used):

            @pl.when(target < chip)
            def _(target=target):
                @pl.when(chip < chips - 1)
                def _():
                    to_down(s_down, target).wait_recv()
                    acc[s_down, target] = plus(acc[s_down, target], down_land[s_down, target])

                to_down(s_down, target).start()

    s_end = step - chips

    @pl.when(s_end >= 0)
    def _():
        @pl.when(chip < used)
        def _():
            grn_ref[s_end] = acc[s_end, chip].astype(F32)

            @pl.when(chip > 0)
            def _():
                to_up(s_end, chip).wait_recv()
                grn_ref[s_end] += up_land[s_end, chip].astype(F32)

            @pl.when(chip < chips - 1)
            def _():
                to_down(s_end, chip).wait_recv()
                grn_ref[s_end] += down_land[s_end, chip].astype(F32)

        @pl.when(chip >= used)
        def _():
            grn_ref[s_end] = jnp.zeros((keys, cp), F32)

    for t in range(1, steps - 1):

        @pl.when(step == t)
        def _(t=t):
            for k in range(t * each, min((t + 1) * each, sums.ops + 1)):
                sums.advance(k)
            if t * each <= sums.ops < (t + 1) * each:
                pltpu.make_async_copy(done, sum_hbm, sum_sem.at[0]).start()

    def tail(base):
        gred, low, hats = [], [], []
        for i in range(together):
            rhat, rstd = centered(red_ref[i], channels)
            upstream = inside(grn_ref[base + i], channels)
            dvec_ref[0:1] += jnp.sum(upstream * rhat, 0, keepdims=True)
            dvec_ref[1:2] += jnp.sum(upstream, 0, keepdims=True)
            g = norm_back(upstream, vec_ref[2:3], rhat, rstd, channels)
            gred.append(inside(g, channels).astype(BF16))
            dvec_ref[2:3] += jnp.sum(gred[i].astype(F32), 0, keepdims=True)
            x = widen(tok_ref[i].astype(F32), cp)
            xhat, xstd = centered(x, channels)
            hats.append((xhat, xstd))
            low.append((xhat * vec_ref[0:1] + vec_ref[1:2]).astype(BF16))
            lowf = low[i].astype(F32)
            for t in range(lt):
                scr[i, t] = lowf[:, t * LANE : (t + 1) * LANE]
        gred = jnp.concatenate(gred, 0)
        gred_t = gred.T
        for b in range(2):
            patches = [[], []]
            for i in range(together):
                part = [scr[i, t, pl.ds(b, n // 2, stride=2), :] for t in range(lt)]
                part = jnp.concatenate(part, -1).reshape(height // 2, 2, width // 2, cp)
                for a in range(2):
                    patches[a].append(part[:, a].reshape(keys, cp))
            for a in range(2):
                ab = 2 * a + b
                dwrt[ab] += dot(gred_t, jnp.concatenate(patches[a], 0).astype(BF16))
                back = dot_nt(gred, wr_ref[ab])
                for i in range(together):
                    for t in range(lt):
                        for r in range(height // 2):
                            at = i * keys + r * (width // 2)
                            gscr[i, t, pl.ds((2 * r + a) * width + b, width // 2, stride=2), :] = back[
                                at : at + width // 2, t * LANE : (t + 1) * LANE
                            ]
        for i in range(together):
            gqt = gqt_ref[base + i]
            xhat, xstd = hats[i]
            dwqt[...] += dot(gqt, low[i])
            gn = widen(dot_nt(gqt.T, wq_ref[...]), cp)
            gn = gn + jnp.concatenate([gscr[i, t] for t in range(lt)], -1)
            dvec_ref[3:4] += jnp.sum(gn * xhat, 0, keepdims=True)
            dvec_ref[4:5] += jnp.sum(gn, 0, keepdims=True)
            gx = norm_back(gn, vec_ref[0:1], xhat, xstd, channels)
            ig_ref[i] = gres2_ref[i] + gx[:, :channels]

    @pl.when(step == scenes)
    def _():
        joined = jnp.concatenate([dwkv_ref[:, :channels], dwkv_ref[:, cp : cp + channels]], -1)
        put(mid_work, mid_plan, "wkv", cut_of(joined))
        put(mid_work, mid_plan, "wp", cut_of(dwp_ref))
        if mid_used < mid_work.shape[0]:
            mid_work[mid_used:, :] = jnp.zeros((mid_work.shape[0] - mid_used, LANE), BF16)

    for t in range(early):

        @pl.when(step == scenes + t)
        def _(t=t):
            mid.advance(t)

    @pl.when(step >= scenes)
    def _():
        tail((step - scenes) * together)

    @pl.when(step < scenes)
    def _():
        s = step
        for j in range(1, count):
            chunk(j)
        dwkv_ref[...] += dot(rn_ref[0].T, gkv_ref[...])
        for h in range(HEADS):
            base = h * LANE + (0 if h % 2 == 0 else HALF)
            gqt_ref[s, h * HALF : (h + 1) * HALF] = (
                dqt[base : base + HALF, :] * head_size**-0.5
            ).astype(BF16)

    @pl.when(step == steps - 1)
    def _():
        plan, filled, sizes = rest_plan(channels, ndev)
        splan, srows = small_plan(channels, ff, ndev)
        full = channels // LANE

        joined = jnp.concatenate([dwrt[ab, :channels, :channels] for ab in range(4)], -1)
        put(rest_work, plan, "wr", cut_of(joined))
        put(rest_work, plan, "wq", cut_of(dwqt))
        last = pltpu.roll(dwqt[:, full * LANE :], HALF, 1)
        put(
            rest_work,
            plan,
            "halves",
            lambda t, rows: jnp.where(
                lanes((1, LANE)) < HALF, dwp_ref[:rows, full * LANE :], last
            ),
        )
        if filled < rest_work.shape[0]:
            rest_work[filled:, :] = jnp.zeros((rest_work.shape[0] - filled, LANE), BF16)
        small_work[...] = jnp.zeros(small_work.shape, F32)
        at, rows, slabs = splan["tap"]
        db = jnp.sum(dtb[...], 0, keepdims=True)
        for t in range(slabs):
            cut = slice(t * LANE, (t + 1) * LANE)
            small_work[at + t * rows : at + t * rows + 9, :] = dtap[:, cut]
            small_work[at + t * rows + 9 : at + t * rows + 10, :] = db[:, cut]
        at, rows, slabs = splan["vec"]
        pb = jnp.sum(dbp_ref[...], 0, keepdims=True)
        qb = widen(dwqt[:, full * LANE :].T[HALF : HALF + 1], cp)
        for t in range(slabs):
            cut = slice(t * LANE, (t + 1) * LANE)
            low = at + t * rows
            small_work[low : low + 3, :] = dvec2[0:3, cut]
            small_work[low + 3 : low + 8, :] = dvec_ref[0:5, cut]
            small_work[low + 8 : low + 9, :] = pb[:, cut]
            small_work[low + 9 : low + 10, :] = qb[:, cut]
        at, rows, _ = splan["count"]
        small_work[at : at + rows, :] = cnt[...]

        orders = orders_of(ndp, blk)
        rest_parts = three_parts(rest_work, rest_land, rest_done, sizes, orders)
        rest_parts.append((small_work, small_land, small_done, 0, srows, orders[0]))
        rest = Sums(rest_parts, rest_send, rest_recv)
        for k in range(max(rest.ops, mid.ops - early) + 1):
            if k <= rest.ops:
                rest.advance(k)
            if k + early <= mid.ops:
                mid.advance(k + early)
        leave = [
            pltpu.make_async_copy(rest_done, rest_hbm, sum_sem.at[1]),
            pltpu.make_async_copy(small_done, small_hbm, sum_sem.at[2]),
            pltpu.make_async_copy(mid_done, mid_hbm, sum_sem.at[3]),
        ]
        for copy in leave:
            copy.start()
        for copy in leave:
            copy.wait()
        pltpu.make_async_copy(done, sum_hbm, sum_sem.at[0]).wait()

        @pl.loop(0, scenes)
        def _(s):
            for target in range(used):

                @pl.when(target > chip)
                def _(target=target):
                    to_up(s, target).wait_send()

                @pl.when(target < chip)
                def _(target=target):
                    to_down(s, target).wait_send()


def attback(
    dims, ff, ndp, blk, used, cid, q, att, gres, ke, ve, rn, tok, red, vec, wp, wkv, wq, wr,
    dtap, dtb, dvec2, cnt, first
):
    scenes, height, width, channels, cp = dims
    n = height * width
    keys = n // 4
    chips = blk // 2
    lt = cp // LANE
    live = 2 * used * keys
    he = HEADS * LANE
    together = -(-scenes // chips)
    assert scenes == together * chips
    mid_rows = sum(middle_plan(channels, ndp * blk)[2])
    rest_rows = sum(rest_plan(channels, ndp * blk)[2])
    small_rows = small_plan(channels, ff, ndp * blk)[1]
    ops = 2 * len(orders_of(ndp, blk)[0])

    def early(shape):
        return pl.BlockSpec(
            (1,) + shape, lambda t: (jnp.minimum(t, scenes - 1),) + (0,) * len(shape)
        )

    def late(shape):
        return pl.BlockSpec(
            (together,) + shape, lambda t: (jnp.maximum(t - scenes, 0),) + (0,) * len(shape)
        )

    land = (scenes, used, keys, cp)
    hbm = pl.BlockSpec(memory_space=pl.ANY)
    vm = pl.BlockSpec(memory_space=pltpu.VMEM)
    return pl.pallas_call(
        functools.partial(attback_kernel, dims, ff, ndp, blk, used),
        grid=(scenes + chips,),
        in_specs=[
            early((n, he)),
            early((n, cp)),
            early((n, channels)),
            early((live, he)),
            early((live, he)),
            early((live, cp)),
            late((n, channels)),
            late((n, channels)),
            late((keys, cp)),
        ]
        + [vm] * 9
        + [hbm],
        out_specs=[late((n, channels))] + [hbm] * 4,
        out_shape=[
            jax.ShapeDtypeStruct((scenes, n, channels), F32),
            jax.ShapeDtypeStruct(first.shape, BF16),
            jax.ShapeDtypeStruct((mid_rows, LANE), BF16),
            jax.ShapeDtypeStruct((rest_rows, LANE), BF16),
            jax.ShapeDtypeStruct((small_rows, LANE), F32),
        ],
        scratch_shapes=[
            pltpu.VMEM((channels, cp), F32),
            pltpu.VMEM((4, cp, cp), F32),
            pltpu.VMEM((cp, cp), F32),
            pltpu.VMEM((cp, 2 * cp), F32),
            pltpu.VMEM((8, cp), F32),
            pltpu.VMEM((8, cp), F32),
            pltpu.VMEM((n, he), BF16),
            pltpu.VMEM((he, n), F32),
            pltpu.VMEM((scenes, channels, n), BF16),
            pltpu.VMEM((scenes, keys, cp), F32),
            pltpu.VMEM((together, lt, n, LANE), F32),
            pltpu.VMEM((together, lt, n, LANE), F32),
            pltpu.VMEM((2, 2, used, keys, cp), BF16),
        ]
        + [pltpu.VMEM(land, BF16)] * 4
        + [pltpu.VMEM((live, 2 * cp), BF16)]
        + [pltpu.VMEM(first.shape, BF16)] * 3
        + [pltpu.VMEM((mid_rows, LANE), BF16)] * 3
        + [pltpu.VMEM((rest_rows, LANE), BF16)] * 3
        + [pltpu.VMEM((small_rows, LANE), F32)] * 3
        + [pltpu.SemaphoreType.DMA((scenes, used))] * 6
        + [pltpu.SemaphoreType.DMA((3, ops, widest(ndp, blk)))] * 4
        + [pltpu.SemaphoreType.DMA((4, ops, widest(ndp, blk)))] * 2
        + [pltpu.SemaphoreType.DMA((4,))],
        compiler_params=pltpu.CompilerParams(
            vmem_limit_bytes=VMEM, collective_id=cid, has_side_effects=True
        ),
    )(q, att, gres, ke, ve, rn, tok, gres, red, vec, wp, wkv, wq, wr, dtap, dtb, dvec2, cnt, first)


def unpack_kernel(channels, ff, ndev, out_in, ig_in, first_in, middle_in, packed_in, small, *refs):
    cp = up_to(channels, LANE)
    splan, _ = small_plan(channels, ff, ndev)
    names = (
        ("out", "ig", "g1", "b1", "wq", "qb", "wr", "rb", "rg", "rbn", "wkv", "vb")
        + ("wp", "pb", "g2", "b2", "we", "eb", "dt", "db", "ws", "sb", "cm")
    )
    outs = dict(zip(names, refs[: len(names)]))
    out_hold, ig_hold, first, middle, packed, we, ws, wr, wkv, in_sem, out_sem, sem = refs[len(names) :]
    lt = cp // LANE
    full = channels // LANE
    loads = [
        pltpu.make_async_copy(first_in, first, sem.at[0]),
        pltpu.make_async_copy(middle_in, middle, sem.at[1]),
        pltpu.make_async_copy(packed_in, packed, sem.at[2]),
    ]
    ins, moves = [], []
    pairs = ((out_in, out_hold, outs["out"]), (ig_in, ig_hold, outs["ig"]))
    for k, (src, hold, dst) in enumerate(pairs):
        for s in range(src.shape[0]):
            ins.append(pltpu.make_async_copy(src.at[s], hold.at[s], in_sem.at[k, s]))
            moves.append(pltpu.make_async_copy(hold.at[s], dst.at[s], out_sem.at[k, s]))
    for copy in loads + ins:
        copy.start()
    plans = (
        (first, ffn_plan(channels, ff, ndev)[0]), (middle, middle_plan(channels, ndev)[0]),
        (packed, rest_plan(channels, ndev)[0]),
    )
    stores = [
        pltpu.make_async_copy(src, outs[name], sem.at[3 + k])
        for k, (src, name) in enumerate(((we, "we"), (ws, "ws"), (wr, "wr"), (wkv, "wkv")))
    ]

    def slab(name, t, low=0, count=None):
        ref, plan = next(v for v in plans if name in v[1])
        at, rows, _ = plan[name]
        count = rows if count is None else count
        return ref[at + t * rows + low : at + t * rows + low + count, :].astype(F32)

    def move(count):
        for copy, on in list(zip(ins, moves))[count : count + len(ins) // 2]:
            copy.wait()
            on.start()

    loads[0].wait()
    for t in range(ff // LANE):
        cut = slice(t * LANE, (t + 1) * LANE)
        we[:, cut] = slab("we", t, 0, channels)
        outs["eb"][cut] = slab("we", t, channels, 16)[0]
        ws[:, cut] = slab("ws", t)
        at, rows, _ = splan["tap"]
        outs["dt"][:, cut] = small[at + t * rows : at + t * rows + 9, :]
        outs["db"][cut] = small[at + t * rows + 9, :]
    stores[0].start()
    stores[1].start()
    move(0)
    loads[1].wait()
    loads[2].wait()
    for t in range(4 * channels // LANE):
        wr[:, t * LANE : (t + 1) * LANE] = slab("wr", t)
    stores[2].start()
    for t in range(2 * channels // LANE):
        wkv[:, t * LANE : (t + 1) * LANE] = slab("wkv", t, 0, channels)
    stores[3].start()
    tall = [slab("wkv", t, channels, 16) for t in range(2 * channels // LANE)]
    outs["vb"][...] = jnp.concatenate(tall, -1)[1, channels:]
    halves = slab("halves", 0)
    wp = [slab("wp", t) for t in range(full)] + [halves]
    outs["wp"][...] = jnp.concatenate(wp, -1)[:, :channels]
    wq = [slab("wq", t) for t in range(full)] + [pltpu.roll(halves, HALF, 1)]
    outs["wq"][...] = jnp.concatenate(wq, -1).T[:channels]
    at, rows, _ = splan["vec"]
    vec = jnp.concatenate([small[at + t * rows : at + (t + 1) * rows, :] for t in range(lt)], -1)
    vec = vec[:, :channels]
    order = ("g2", "b2", "sb", "rg", "rbn", "rb", "g1", "b1", "pb", "qb")
    for k, name in enumerate(order):
        outs[name][...] = vec[k]
    at, rows, _ = splan["count"]
    outs["cm"][...] = small[at : at + rows, :].astype(jnp.int32)[:CLASSES, :CLASSES]
    move(len(ins) // 2)
    for copy in moves + stores:
        copy.wait()


def unpack(channels, ff, ndev, out, ig, first, middle, packed, small):
    one = (channels,)
    shapes = [
        one, one, (channels, channels), one, (channels, 4 * channels), one, one, one,
        (channels, 2 * channels), one, (channels, channels), one, one, one, (channels, ff), (ff,),
        (9, ff), (ff,), (channels, ff), one,
    ]
    outs = [jax.ShapeDtypeStruct(v, F32) for v in shapes]
    outs.append(jax.ShapeDtypeStruct((CLASSES, CLASSES), jnp.int32))
    vm = pl.BlockSpec(memory_space=pltpu.VMEM)
    hbm = pl.BlockSpec(memory_space=pl.ANY)
    big = {4, 8, 14, 18}
    return pl.pallas_call(
        functools.partial(unpack_kernel, channels, ff, ndev),
        in_specs=[hbm] * 5 + [vm],
        out_specs=[hbm, hbm] + [hbm if k in big else vm for k in range(len(outs))],
        out_shape=[jax.ShapeDtypeStruct(v.shape, v.dtype) for v in (out, ig)] + outs,
        scratch_shapes=[
            pltpu.VMEM(out.shape, out.dtype),
            pltpu.VMEM(ig.shape, ig.dtype),
            pltpu.VMEM(first.shape, first.dtype),
            pltpu.VMEM(middle.shape, middle.dtype),
            pltpu.VMEM(packed.shape, packed.dtype),
            pltpu.VMEM((channels, ff), F32),
            pltpu.VMEM((channels, ff), F32),
            pltpu.VMEM((channels, 4 * channels), F32),
            pltpu.VMEM((channels, 2 * channels), F32),
            pltpu.SemaphoreType.DMA((2, out.shape[0])),
            pltpu.SemaphoreType.DMA((2, out.shape[0])),
            pltpu.SemaphoreType.DMA((7,)),
        ],
        compiler_params=pltpu.CompilerParams(vmem_limit_bytes=VMEM),
    )(out, ig, first, middle, packed, small)


def split_low(value):
    hi = value.astype(BF16).astype(F32)
    return hi, value - hi


def rows16(*rows):
    width = rows[0].shape[-1]
    at = lax.broadcasted_iota(jnp.int32, (16, width), 0)
    block = jnp.zeros((16, width), F32)
    for k, row in enumerate(rows):
        block = jnp.where(at == k, row, block)
    return block.astype(BF16)


def prep_kernel(
    channels, g1, b1, qw, qb, rw, rb, rg, rbn, kvw, vb, pw, pb, g2, b2, eb, tb, sb,
    vec, wq, wp, wkv, wr, ebias, dbias, full,
):
    cp = up_to(channels, LANE)
    head_size = channels // HEADS
    rest = cp - channels - 16

    def row(ref):
        return ref[...].reshape(1, ref.shape[-1])

    lane = lanes((1, cp))

    def padded(ref, *at):
        v = widen(row(ref), cp)
        for k in at:
            v = jnp.where(lane == channels + k, 1.0, v)
        return v

    for k, v in enumerate(
        (
            padded(g1), padded(b1, 0, 1), padded(rg), padded(rbn, 1, 2), padded(pb), padded(g2),
            padded(b2, 0, 1), padded(sb),
        )
    ):
        vec[k : k + 1, :] = v

    def fill(ref, top, *rows):
        width = ref.shape[-1]
        ref[:channels, :] = top
        ref[channels : channels + 16, :] = (
            rows16(*rows) if rows else jnp.zeros((16, width), BF16)
        )
        if rest:
            ref[channels + 16 :, :] = jnp.zeros((rest, width), BF16)

    dbias[...] = row(tb)
    ebias[...] = rows16(*split_low(row(eb)))
    q = widen(qw[...], cp)
    qb_wide = widen(row(qb), cp)
    fill(wq, q, *split_low(qb_wide))
    kw = widen(kvw[:, :channels], cp)
    vw = widen(kvw[:, channels:], cp)
    nil = jnp.zeros((1, 2 * cp), F32)
    vb_rows = [
        jnp.concatenate([jnp.zeros((1, cp), F32), widen(v, cp)], -1) for v in split_low(row(vb))
    ]
    fill(wkv, jnp.concatenate([kw, vw], -1), nil, *vb_rows)
    fill(wp, widen(pw[...], cp))
    rb_rows = [widen(v, cp) for v in split_low(row(rb))]
    rw_rows = rw[...].T
    for ab in range(4):
        fill(
            wr.at[ab], widen(rw_rows[ab * channels : (ab + 1) * channels, :], cp),
            *rb_rows[ab : ab + 1],
        )

    def norm(v):
        return jnp.sqrt(jnp.sum(v * v, (0, 1), keepdims=True))

    root = channels**0.5

    def reach(gain, bias):
        top = jnp.max(jnp.abs(row(gain)), (0, 1), keepdims=True)
        return root * top + norm(row(bias))

    def head(value, h):
        tile = value[:, h // 2 * LANE : (h // 2 + 1) * LANE].astype(F32)
        return jnp.where(lanes((1, LANE)) // HALF == h % 2, tile, 0.0)

    query_in, key_in = reach(g1, b1), reach(rg, rbn)
    bound = jnp.zeros((1, 1), F32)
    for h in range(HEADS):
        query = query_in * norm(head(q, h)) + norm(head(qb_wide, h))
        bound = jnp.maximum(bound, query * key_in * norm(head(kw, h)))
    bound = bound * (head_size**-0.5 * 1.05)
    full[...] = jnp.where(2.0 * bound + 256.0 < -NEGATIVE, 0, 1).astype(jnp.int32)


def prep(channels, ff, *weights):
    cp = up_to(channels, LANE)
    shapes = [
        ((8, cp), F32), ((cp, cp), BF16), ((cp, cp), BF16), ((cp, 2 * cp), BF16),
        ((4, cp, cp), BF16), ((16, ff), BF16), ((1, ff), F32), ((1, 1), jnp.int32),
    ]
    return pl.pallas_call(
        functools.partial(prep_kernel, channels),
        out_shape=[jax.ShapeDtypeStruct(*v) for v in shapes],
        compiler_params=pltpu.CompilerParams(vmem_limit_bytes=VMEM),
    )(*weights)


def body(
    tokens, mask, labels, predicted, cotangent, norm1_gain, norm1_bias, query_weight, query_bias,
    reduce_weight, reduce_bias, rnorm_gain, rnorm_bias, kv_weight, value_bias, proj_weight,
    proj_bias, norm2_gain, norm2_bias, expand_weight, expand_bias, depth_weight, depth_bias,
    shrink_weight, shrink_bias,
):
    scenes, height, width, channels = tokens.shape
    ndp, blk = lax.axis_size("dp"), lax.axis_size("blk")
    n = height * width
    ff = expand_weight.shape[1]
    dims = (scenes, height, width, channels, up_to(channels, LANE))
    chips = blk // 2
    used = min(chips, -(-MASK_ROWS // (2 * height)))

    vec, wq, wp, wkv, wr, expand_rows, tap_bias, full = prep(
        channels, ff, norm1_gain, norm1_bias, query_weight, query_bias, reduce_weight.T, reduce_bias,
        rnorm_gain, rnorm_bias, kv_weight, value_bias, proj_weight, proj_bias, norm2_gain,
        norm2_bias, expand_bias, depth_bias, shrink_bias,
    )
    full = full[0, 0] > 0

    def either(call, cids, sizes, *operands):
        if used == chips:
            return call(*sizes, chips, cids[1], *operands)
        return lax.cond(
            full,
            functools.partial(call, *sizes, chips, cids[1]),
            functools.partial(call, *sizes, used, cids[0]),
            *operands,
        )

    tok = tokens.reshape(scenes, n, channels)
    ct = cotangent.reshape(scenes, n, channels)
    red, counts, q, att, ke, ve, rn, res = either(
        attend, (2, 3), (dims, blk), tok, mask, labels, predicted, vec, wr, wq, wkv, wp
    )
    out, gres, first, dtap, dtb, dvec2 = ffn(
        dims, blk, ndp * blk, res, ct, expand_weight, shrink_weight.T, vec, expand_rows, depth_weight,
        tap_bias,
    )
    ig, first, middle, packed, small = either(
        attback, (4, 5), (dims, ff, ndp, blk), q, att, gres, ke, ve, rn, tok, red, vec, wp, wkv,
        query_weight, wr, dtap, dtb, dvec2, counts, first,
    )
    out, ig, *grads = unpack(channels, ff, ndp * blk, out, ig, first, middle, packed, small)
    grads[4], grads[18] = grads[4].T, grads[18].T
    return (out.reshape(tokens.shape), ig.reshape(tokens.shape), *grads)


def solution(mesh):
    banded = P("dp", "blk", None, None)
    plane = P("dp", "blk", None)
    in_specs = (banded, plane, plane, plane, banded) + (P(),) * 20
    out_specs = (banded, banded) + (P(),) * 21
    return jax.shard_map(body, mesh=mesh, in_specs=in_specs, out_specs=out_specs, check_vma=False)
```

```python
import functools

import jax
import jax.numpy as jnp
from jax import lax
from jax.experimental import pallas as pl
from jax.experimental.pallas import tpu as pltpu
from jax.sharding import PartitionSpec as P
import ml_dtypes
import numpy as np

HEADS = 5
CLASSES = 19
EPSILON = 1e-06
NEGATIVE = -32768.0
LOG2E = 1.4426950408889634
LN2 = 0.6931471805599453
F32 = jnp.float32
BF16 = jnp.bfloat16
LANE = 128
HALF = 64
KEY_CHUNK = 256
MASK_ROWS = 48
VMEM = 62 * 2**20
FF_CHUNK = 256
GROUP = 8
NEG = np.float32(NEGATIVE * LOG2E)
NEG_HI = np.float32(ml_dtypes.bfloat16(NEG))
NEG_MID = np.float32(ml_dtypes.bfloat16(NEG - NEG_HI))
NEG_LO = np.float32(ml_dtypes.bfloat16(NEG - NEG_HI - NEG_MID))


def up_to(value, step):
    return -(-value // step) * step


def dot(a, b):
    return lax.dot_general(a, b, (((1,), (0,)), ((), ())), preferred_element_type=F32)


def dot_nt(a, b):
    return lax.dot_general(a, b, (((1,), (1,)), ((), ())), preferred_element_type=F32)


def dot_tn(a, b):
    return lax.dot_general(a, b, (((0,), (0,)), ((), ())), preferred_element_type=F32)


def lanes(shape):
    return lax.broadcasted_iota(jnp.int32, shape, len(shape) - 1)


def whole(shape):
    return pl.BlockSpec(shape, lambda *_: (0,) * len(shape))


def per_scene(shape):
    return pl.BlockSpec((1,) + shape, lambda s: (s,) + (0,) * len(shape))


def inside(value, channels):
    full = channels // LANE * LANE
    if full == value.shape[-1]:
        return value
    last = value[..., full:]
    last = jnp.where(lanes(last.shape) < channels - full, last, 0.0)
    return jnp.concatenate([value[..., :full], last], -1)


def head_blocks(value, free):
    half = lanes((1, LANE)) // HALF
    fills = [free(0), free(1)]
    return [
        jnp.where(half == h % 2, value[:, h // 2 * LANE : (h // 2 + 1) * LANE], fills[h % 2])
        for h in range(HEADS)
    ]


def free_row(parity, values):
    lane = lanes((1, LANE))
    row = jnp.zeros((1, LANE), F32)
    for k, value in values.items():
        row = jnp.where(lane == ext_lane(parity) + k, value, row)
    return row


def centered(value, channels):
    mean = jnp.sum(value, -1, keepdims=True) * (1.0 / channels)
    center = inside(value - mean, channels)
    var = jnp.sum(center * center, -1, keepdims=True) * (1.0 / channels)
    rstd = lax.rsqrt(var + EPSILON)
    return center * rstd, rstd


def norm_back(up, gain, xhat, rstd, channels):
    u = up * gain
    mean = jnp.sum(u, -1, keepdims=True) * (1.0 / channels)
    proj = jnp.sum(u * xhat, -1, keepdims=True) * (1.0 / channels)
    return (u - mean - xhat * proj) * rstd


def ext_lane(head):
    return HALF if head % 2 == 0 else 0


def widen(value, width):
    pad = width - value.shape[-1]
    return jnp.concatenate([value, jnp.zeros(value.shape[:-1] + (pad,), value.dtype)], -1)


def place(blk):
    me = lax.axis_index("blk")
    core = lax.rem(me, 2)
    chip = me // 2
    return chip, core, {"blk": me + 2}, {"blk": me - 2}, {"blk": me + 1 - 2 * core}


def greet(chip, chips, up, down, sib):
    barrier = pltpu.get_barrier_semaphore()
    MESH = pl.DeviceIdType.MESH
    has_up, has_down = chip < chips - 1, chip > 0
    pl.semaphore_signal(barrier, inc=1, device_id=sib, device_id_type=MESH)

    @pl.when(has_up)
    def _():
        pl.semaphore_signal(barrier, inc=1, device_id=up, device_id_type=MESH)

    @pl.when(has_down)
    def _():
        pl.semaphore_signal(barrier, inc=1, device_id=down, device_id_type=MESH)

    pl.semaphore_wait(barrier, 1 + has_up.astype(jnp.int32) + has_down.astype(jnp.int32))


def remote(src, dst, send, recv, device):
    return pltpu.make_async_remote_copy(
        src_ref=src, dst_ref=dst, send_sem=send, recv_sem=recv, device_id=device,
        device_id_type=pl.DeviceIdType.MESH,
    )


def groups_of(ndp, nblk):
    dp_bits, blk_bits = ndp.bit_length() - 1, nblk.bit_length() - 1
    assert ndp == 1 << dp_bits and nblk == 1 << blk_bits
    core = [("blk", 0, 2)] if blk_bits else []
    if dp_bits > 2:
        plane = [("dp", 0, 1 << dp_bits // 2), ("dp", dp_bits // 2, 1 << (dp_bits - dp_bits // 2))]
    else:
        plane = [("dp", 0, ndp)] if dp_bits else []
    line = [("blk", 1, nblk // 2)] if blk_bits > 1 else []
    return core, plane, line


def lay_out(items, ndev):
    plan, at = {}, 0
    for name, rows, slabs in items:
        plan[name] = (at, rows, slabs)
        at += rows * slabs
    unit = 16 * ndev
    units = -(-at // unit)
    last = units // 3 - (1 if units > 6 else 0)
    mid = (units - last) // 2
    return plan, at, [(units - last - mid) * unit, mid * unit, last * unit]


def ffn_plan(channels, ff, ndev):
    tall = up_to(channels + 2, 16)
    return lay_out([("we", tall, ff // LANE), ("ws", channels, ff // LANE)], ndev)


def middle_plan(channels, ndev):
    tall = up_to(channels + 2, 16)
    return lay_out(
        [("wkv", tall, 2 * channels // LANE), ("wp", channels, channels // LANE)], ndev
    )


def rest_plan(channels, ndev):
    assert 4 * channels % LANE == 0 and 2 * channels % LANE == 0 and channels % LANE == HALF
    return lay_out(
        [
            ("wr", channels, 4 * channels // LANE), ("wq", channels, channels // LANE),
            ("halves", channels, 1),
        ],
        ndev,
    )


def small_plan(channels, ff, ndev):
    cp = up_to(channels, LANE)
    plan = {"tap": (0, 16, ff // LANE)}
    at = 16 * (ff // LANE)
    plan["vec"] = (at, 16, cp // LANE)
    at += 16 * (cp // LANE)
    plan["count"] = (at, 32, 1)
    at += 32
    return plan, up_to(at, 8 * ndev)


def member(group):
    axis, bit, size = group
    return lax.rem(lax.axis_index(axis) // (1 << bit), size)


def other(group, index):
    axis, bit, _ = group
    return {axis: lax.axis_index(axis) + (index - member(group)) * (1 << bit)}


def peers_of(order):
    return [
        other(group, lax.rem(member(group) + d, group[2])) for group in order for d in range(1, group[2])
    ]


class Sums:
    def __init__(self, parts, send_sem, recv_sem):
        self.parts, self.send_sem, self.recv_sem = parts, send_sem, recv_sem
        self.rounds = len(parts[0][5])
        self.ops = 2 * self.rounds

    def unit(self, p):
        return 16 if self.parts[p][0].dtype == BF16 else 8

    def segment(self, p, i):
        _, _, _, start, rows, order = self.parts[p]
        for group in order[:i]:
            rows //= group[2]
            start = start + member(group) * rows
        return start, rows

    def landing(self, p, i):
        _, _, _, first, rows, order = self.parts[p]
        for group in order[:i]:
            first += rows // group[2] * (group[2] - 1)
            rows //= group[2]
        return first

    def copies(self, p, k):
        buf, land, done, _, _, order = self.parts[p]
        unit = self.unit(p)
        halving = k < self.rounds
        i = k if halving else self.ops - 1 - k
        group = order[i]
        size = group[2]
        me = member(group)
        result = []
        for d in range(1, size):
            to = lax.rem(me + d, size)
            if halving:
                start, rows = self.segment(p, i)
                rows //= size
                src = buf.at[pl.ds(pl.multiple_of(start + to * rows, unit), rows), :]
                low = self.landing(p, i) + (size - 1 - d) * rows
                dst = land.at[pl.ds(low, rows), :]
            else:
                start, rows = self.segment(p, i + 1)
                src = done.at[pl.ds(pl.multiple_of(start, unit), rows), :]
                dst = src
            result.append(
                remote(
                    src, dst, self.send_sem.at[p, k, d - 1], self.recv_sem.at[p, k, d - 1],
                    other(group, to),
                )
            )
        return result

    def start(self, p, k):
        for copy in self.copies(p, k):
            copy.start()

    def finish(self, p, k):
        for copy in self.copies(p, k):
            copy.wait()
        if k >= self.rounds:
            return
        buf, land, done, _, _, order = self.parts[p]
        unit = self.unit(p)
        keep, rows = self.segment(p, k + 1)
        low = self.landing(p, k)
        step = next(c for c in (256, 128, 64, 32, 16, 8) if rows % c == 0)
        into = done if k == self.rounds - 1 else buf

        @pl.loop(0, rows // step)
        def _(j):
            mine = pl.ds(pl.multiple_of(keep + j * step, unit), step)
            total = buf[mine, :].astype(F32)
            for d in range(order[k][2] - 1):
                theirs = pl.ds(pl.multiple_of(low + d * rows + j * step, unit), step)
                total = total + land[theirs, :].astype(F32)
            into[mine, :] = total.astype(buf.dtype)

    def advance(self, k):
        for p in range(len(self.parts)):
            if k > 0:
                self.finish(p, k - 1)
            if k < self.ops:
                self.start(p, k)


def three_parts(buf, land, done, sizes, orders):
    parts, at = [], 0
    for size, order in zip(sizes, orders):
        if size:
            parts.append((buf, land, done, at, size, order))
        at += size
    return parts


def orders_of(ndp, nblk):
    core, plane, line = groups_of(ndp, nblk)
    return [core + plane + line, core + plane + line, core + line + plane]


def widest(ndp, nblk):
    return max(group[2] for group in orders_of(ndp, nblk)[0]) - 1


def packed_rows(keys, cp):
    return (cp // LANE - 1) * keys + keys // 2 + 16


def pack_block(value, unc, keys, cp):
    full = cp // LANE - 1
    last = value[:, full * LANE :]
    turned = pltpu.roll(last[keys // 2 :], HALF, 1)
    last = jnp.where(lanes((1, LANE)) < HALF, last[: keys // 2], turned)
    flags = jnp.broadcast_to(unc, (keys, LANE))
    if keys < LANE:
        flags = jnp.concatenate([flags, jnp.zeros((LANE - keys, LANE), F32)], 0)
    parts = [value[:, t * LANE : (t + 1) * LANE] for t in range(full)] + [last, flags.T[:16]]
    return jnp.concatenate([v.astype(BF16) for v in parts], 0)


def unpack_block(block, ones, keys, cp):
    full = cp // LANE - 1
    parts = [block[t * keys : (t + 1) * keys] for t in range(full)]
    last = block[full * keys : full * keys + keys // 2].astype(F32)
    last = jnp.concatenate([last, pltpu.roll(last, HALF, 1)], 0)
    last = jnp.where(lanes((1, LANE)) < HALF, last, ones)
    flags = block[full * keys + keys // 2 :].astype(F32)[0:1]
    flags = jnp.broadcast_to(flags, (LANE, LANE)).T[:keys]
    return jnp.concatenate(parts + [last.astype(BF16)], -1), flags


def attend_kernel(
    dims, blk, used, tok_ref, mask_ref, label_ref, pred_ref, tok2_ref, vec_ref, wr_ref, wq_ref,
    wkv_ref, wp_ref,
    red_ref, cnt_ref, q_ref, att_ref, ke_ref, ve_ref, rn_ref, res_ref,
    scr, qbuf, oe, rnbuf, up_send, down_send, sib_send, line_recv, sib_recv,
):
    scenes, height, width, channels, cp = dims
    n = height * width
    keys = n // 4
    chips = blk // 2
    lag = chips
    step = pl.program_id(0)
    head_size = channels // HEADS
    chip, core, up, down, sib = place(blk)

    @pl.when(step == 0)
    def _():
        greet(chip, chips, up, down, sib)
        cnt_ref[...] = jnp.zeros(cnt_ref.shape, F32)

    def slot(origin, c):
        return c * used + origin

    def send_up(s, origin):
        place_ = rnbuf.at[s, slot(origin, core)]
        return remote(place_, place_, up_send.at[s, origin], line_recv.at[s, origin], up)

    def send_down(s, origin):
        place_ = rnbuf.at[s, slot(origin, core)]
        return remote(place_, place_, down_send.at[s, origin], line_recv.at[s, origin], down)

    def send_sib(s, origin):
        place_ = rnbuf.at[s, slot(origin, core)]
        return remote(place_, place_, sib_send.at[s, origin], sib_recv.at[s, origin], sib)

    @pl.when(step < scenes)
    def _():
        s = step
        x = widen(tok_ref[0].astype(F32), cp)
        xhat, _ = centered(x, channels)
        low = (xhat * vec_ref[0:1] + vec_ref[1:2]).astype(BF16)
        lowf = low.astype(F32)
        for t in range(cp // LANE):
            scr[t, :n] = lowf[:, t * LANE : (t + 1) * LANE]
        total = jnp.zeros((keys, cp), F32)
        for b in range(2):
            part = [scr[t, pl.ds(b, n // 2, stride=2), :] for t in range(cp // LANE)]
            part = jnp.concatenate(part, -1).reshape(height // 2, 2, width // 2, cp)
            for a in range(2):
                total = total + dot(part[:, a].reshape(keys, cp).astype(BF16), wr_ref[2 * a + b])
        red_ref[0] = total
        rhat, _ = centered(total, channels)
        m = mask_ref[0].astype(F32)
        shape = (width // 2, width)
        near = lanes(shape) // 2 == lax.broadcasted_iota(jnp.int32, shape, 0)
        flags = []
        for i in range(height // 2):
            both = m[2 * i : 2 * i + 1] + m[2 * i + 1 : 2 * i + 2]
            flags.append(jnp.sum(jnp.where(near, both, 0.0), -1, keepdims=True))
        unc = jnp.where(jnp.concatenate(flags, 0) > 0.0, 0.0, 1.0)
        own = pack_block(rhat * vec_ref[2:3] + vec_ref[3:4], unc, keys, cp)

        @pl.when(chip < used)
        def _():
            rnbuf[s, slot(chip, core)] = own
            send_sib(s, chip).start()

            @pl.when(chip < chips - 1)
            def _():
                send_up(s, chip).start()

            @pl.when(chip > 0)
            def _():
                send_down(s, chip).start()

        qf = dot(low, wq_ref[...]) * (LOG2E * head_size**-0.5)
        ones = head_blocks(qf, lambda e: free_row(e, {0: 1.0, 1: 1.0, 2: 1.0}))
        for h in range(HEADS):
            qbuf[lax.rem(s, lag + 1), :, h * LANE : (h + 1) * LANE] = ones[h].astype(BF16)
        shape = (cnt_ref.shape[0], width)
        classes = lax.broadcasted_iota(jnp.int32, shape, 0)
        wide = lax.broadcasted_iota(jnp.int32, (LANE, width), 0)
        total = jnp.zeros(cnt_ref.shape, F32)
        for r in range(height):
            label = jnp.where(mask_ref[0, r : r + 1] > 0, label_ref[0, r : r + 1], -1)
            hot = jnp.where(label == classes, 1.0, 0.0).astype(BF16)
            pred = jnp.where(pred_ref[0, r : r + 1] == wide, 1.0, 0.0).astype(BF16)
            total = total + dot_nt(hot, pred)
        cnt_ref[...] += total

    for age in range(1, chips):
        s = step - age

        @pl.when(jnp.logical_and(s >= 0, s < scenes))
        def _(s=s, age=age):
            below = chip - age

            @pl.when(jnp.logical_and(below >= 0, below < used))
            def _():
                send_up(s, below).wait_recv()
                send_sib(s, below).start()

                @pl.when(chip < chips - 1)
                def _():
                    send_up(s, below).start()

            above = chip + age

            @pl.when(above < used)
            def _():
                send_down(s, above).wait_recv()
                send_sib(s, above).start()

                @pl.when(chip > 0)
                def _():
                    send_down(s, above).start()

    @pl.when(step >= lag)
    def _():
        s = step - lag

        for origin in range(used):
            send_sib(s, origin).wait_recv()

        free = vec_ref[3:4, cp - LANE :]
        blocks = [unpack_block(rnbuf[s, i], free, keys, cp) for i in range(2 * used)]
        rn_all = jnp.concatenate([v[0] for v in blocks], 0)
        rn_ref[0] = rn_all
        flag = jnp.concatenate([v[1] for v in blocks], 0)
        kv = dot(rn_all, wkv_ref[...])
        negative = {0: float(NEG_HI), 1: float(NEG_MID), 2: float(NEG_LO)}
        for h, block in enumerate(
            head_blocks(
                kv[:, :cp],
                lambda e: flag * free_row(e, negative) + free_row(e, {3: 1.0, 4: 1.0, 5: 1.0}),
            )
        ):
            ke_ref[0, :, h * LANE : (h + 1) * LANE] = block.astype(BF16)
        for h, block in enumerate(
            head_blocks(kv[:, cp:], lambda e: free_row(e, {0: 1.0, 1: 1.0, 2: 1.0}))
        ):
            ve_ref[0, :, h * LANE : (h + 1) * LANE] = block.astype(BF16)
        mine = lax.rem(s, lag + 1)
        count = 2 * used * keys // KEY_CHUNK
        for h in range(HEADS):
            block = slice(h * LANE, (h + 1) * LANE)
            e = ext_lane(h)
            q = qbuf[mine, :, block]
            parts = [
                dot_nt(q, ke_ref[0, j * KEY_CHUNK : (j + 1) * KEY_CHUNK, block])
                for j in range(count)
            ]
            top = functools.reduce(jnp.maximum, parts)
            top = jnp.max(top, -1, keepdims=True)
            out = jnp.zeros((n, LANE), F32)
            for j in range(count):
                p = jnp.exp2(parts[j] - top).astype(BF16)
                out = out + dot(p, ve_ref[0, j * KEY_CHUNK : (j + 1) * KEY_CHUNK, block])
            total = out[:, e : e + 1]
            oe[h] = out / total
            lse = top + jnp.log2(total)
            hi = lse.astype(BF16).astype(F32)
            mid = (lse - hi).astype(BF16).astype(F32)
            lo = lse - hi - mid
            lane = lanes((n, LANE))
            q2 = q.astype(F32)
            q2 = jnp.where(lane == e + 3, -hi, q2)
            q2 = jnp.where(lane == e + 4, -mid, q2)
            q2 = jnp.where(lane == e + 5, -lo, q2)
            q_ref[0, :, block] = q2.astype(BF16)

        tiles = []
        low_half = lanes((n, LANE)) < HALF
        for t in range(cp // LANE):
            other = oe[2 * t + 1] if 2 * t + 1 < HEADS else jnp.zeros((n, LANE), F32)
            tiles.append(jnp.where(low_half, oe[2 * t], other))
        att = jnp.concatenate(tiles, -1)
        att_ref[0] = att
        x = widen(tok2_ref[0].astype(F32), cp)
        resid = x + dot(att.astype(BF16), wp_ref[...]) + vec_ref[4:5]
        for t in range(cp // LANE):
            for r in range(height):
                for half in range(2):
                    base = r * width + half * (width // 2)
                    at = r * scenes * width + half * scenes + s
                    res_ref[t, pl.ds(at, width // 2, stride=2 * scenes), :] = resid[
                        base : base + width // 2, t * LANE : (t + 1) * LANE
                    ]

    @pl.when(step == scenes + lag - 1)
    def _():
        @pl.loop(0, scenes)
        def _(s):
            for origin in range(used):
                send_sib(s, origin).wait_send()

                @pl.when(jnp.logical_and(origin <= chip, chip < chips - 1))
                def _(origin=origin):
                    send_up(s, origin).wait_send()

                @pl.when(jnp.logical_and(origin >= chip, chip > 0))
                def _(origin=origin):
                    send_down(s, origin).wait_send()


def attend(dims, blk, used, cid, tok, mask, labels, predicted, vec, wr, wq, wkv, wp):
    scenes, height, width, channels, cp = dims
    n = height * width
    keys = n // 4
    chips = blk // 2
    lag = chips
    k = blk * keys
    live = 2 * used * keys
    he = HEADS * LANE

    def early(shape):
        return pl.BlockSpec(
            (1,) + shape, lambda t: (jnp.minimum(t, scenes - 1),) + (0,) * len(shape)
        )

    def late(shape):
        return pl.BlockSpec((1,) + shape, lambda t: (jnp.maximum(t - lag, 0),) + (0,) * len(shape))

    return pl.pallas_call(
        functools.partial(attend_kernel, dims, blk, used),
        grid=(scenes + lag,),
        in_specs=[early((n, channels))]
        + [early((height, width))] * 3
        + [late((n, channels))]
        + [whole(v.shape) for v in (vec, wr, wq, wkv, wp)],
        out_specs=[
            early((keys, cp)),
            whole((32, LANE)),
            late((n, he)),
            late((n, cp)),
            late((live, he)),
            late((live, he)),
            late((live, cp)),
            whole((cp // LANE, scenes * n + 2 * scenes, LANE)),
        ],
        out_shape=[
            jax.ShapeDtypeStruct((scenes, keys, cp), F32),
            jax.ShapeDtypeStruct((32, LANE), F32),
            jax.ShapeDtypeStruct((scenes, n, he), BF16),
            jax.ShapeDtypeStruct((scenes, n, cp), F32),
            jax.ShapeDtypeStruct((scenes, k, he), BF16),
            jax.ShapeDtypeStruct((scenes, k, he), BF16),
            jax.ShapeDtypeStruct((scenes, k, cp), BF16),
            jax.ShapeDtypeStruct((cp // LANE, scenes * n + 2 * scenes, LANE), F32),
        ],
        scratch_shapes=[
            pltpu.VMEM((cp // LANE, n + 8, LANE), F32),
            pltpu.VMEM((lag + 1, n, he), BF16),
            pltpu.VMEM((HEADS, n, LANE), F32),
            pltpu.VMEM((scenes, 2 * used, packed_rows(keys, cp), LANE), BF16),
        ]
        + [pltpu.SemaphoreType.DMA((scenes, used))] * 5,
        compiler_params=pltpu.CompilerParams(
            vmem_limit_bytes=VMEM, collective_id=cid, has_side_effects=True
        ),
    )(tok, mask, labels, predicted, tok, vec, wr, wq, wkv, wp)


def ffn_kernel(
    dims, ff, blk, ndev, res_hbm, ct_hbm, ew_hbm, sw_hbm, vec_ref, eb_ref, taps_ref, tb_ref,
    out_hbm, gres_hbm, pack_hbm, dtap_ref, dtb_ref, dvec_ref,
    we_ref, ws_ref, dwe_ref, dwst, packed, res_ref, ct_ref, cn, cnt, ctt, ctx, oacc, gacc, hid, gm, halo, act, back, tapacc, out_stage, gres_stage,
    weight_sem, pack_sem, res_sem, ct_sem, out_sem, gres_sem, cn_send, cn_recv, gm_send, gm_recv,
):
    scenes, height, width, channels, cp = dims
    n = height * width
    rw = scenes * width
    lt = cp // LANE
    fc = FF_CHUNK
    nchunk = ff // fc
    cols = width // 2
    pair = 2 * scenes
    group = GROUP if cols % GROUP == 0 else cols
    me = lax.axis_index("blk")
    has_left = me > 0
    has_right = me < blk - 1
    left, right = {"blk": me - 1}, {"blk": me + 1}
    MESH = pl.DeviceIdType.MESH

    def res_copy(r):
        rows = pl.ds(pl.multiple_of(r * rw, rw), rw)
        return pltpu.make_async_copy(res_hbm.at[:, rows, :], res_ref.at[:, rows, :], res_sem.at[r])

    def ct_copy(s):
        return pltpu.make_async_copy(ct_hbm.at[s], ct_ref.at[s], ct_sem.at[s])

    ew_copy = pltpu.make_async_copy(ew_hbm, we_ref.at[:channels, :], weight_sem.at[0])
    sw_copy = pltpu.make_async_copy(sw_hbm, ws_ref.at[:channels, :], weight_sem.at[1])
    for r in range(height):
        res_copy(r).start()
    for s in range(scenes):
        ct_copy(s).start()
    ew_copy.start()
    sw_copy.start()
    bias_rows = eb_ref.shape[0]
    we_ref[channels : channels + bias_rows, :] = eb_ref[...]
    if channels + bias_rows < cp:
        we_ref[channels + bias_rows :, :] = jnp.zeros((cp - channels - bias_rows, ff), BF16)
    ws_ref[channels:, :] = jnp.zeros((cp - channels, ff), BF16)

    barrier = pltpu.get_barrier_semaphore()

    @pl.when(has_left)
    def _():
        pl.semaphore_signal(barrier, inc=1, device_id=left, device_id_type=MESH)

    @pl.when(has_right)
    def _():
        pl.semaphore_signal(barrier, inc=1, device_id=right, device_id_type=MESH)

    pl.semaphore_wait(barrier, has_left.astype(jnp.int32) + has_right.astype(jnp.int32))

    def row(r, size=rw):
        return pl.ds(pl.multiple_of(r * rw, rw), size)

    g2, b2 = vec_ref[5:6], vec_ref[6:7]

    def load3(ref, r):
        return jnp.concatenate([ref[t, row(r), :] for t in range(lt)], -1)

    def store3(ref, r, value):
        for t in range(lt):
            ref[t, row(r), :] = value[:, t * LANE : (t + 1) * LANE]

    @pl.loop(0, height)
    def _(r):
        res_copy(r).wait()
        x = load3(res_ref, r)
        xhat, rstd = centered(x, channels)
        c = (xhat * g2 + b2).astype(BF16)
        cn[row(r + 1), :] = c
        cnt[:, row(r)] = c.T
        store3(oacc, r, x + vec_ref[7:8])
        store3(res_ref, r, jnp.where(lanes(xhat.shape) == channels, rstd, xhat))

    def cn_copy(up):
        return pltpu.make_async_remote_copy(
            src_ref=cn.at[row(1 if up else height), :],
            dst_ref=cn.at[row(height + 1 if up else 0), :],
            send_sem=cn_send.at[0 if up else 1],
            recv_sem=cn_recv.at[0 if up else 1],
            device_id=left if up else right,
            device_id_type=MESH,
        )

    @pl.when(has_left)
    def _():
        cn_copy(True).start()

    @pl.when(has_right)
    def _():
        cn_copy(False).start()

    @pl.loop(0, scenes)
    def _(s):
        ct_copy(s).wait()
        c = widen(ct_ref[s].astype(F32), cp)
        for t in range(lt):
            for r in range(height):
                for half in range(2):
                    base = r * width + half * cols
                    gacc[t, pl.ds(r * rw + half * scenes + s, cols, stride=pair), :] = c[
                        base : base + cols, t * LANE : (t + 1) * LANE
                    ]

    dvec_ref[...] = jnp.zeros(dvec_ref.shape, F32)

    @pl.loop(0, height)
    def _(r):
        c = load3(gacc, r)
        dvec_ref[2:3] += jnp.sum(c, 0, keepdims=True)
        low = c.astype(BF16)
        ctt[row(r), :] = low
        ctx[:, row(r)] = low.T
        store3(gacc, r, jnp.zeros((rw, cp), F32))

    ew_copy.wait()
    sw_copy.wait()
    dwe_ref[...] = jnp.zeros(dwe_ref.shape, F32)
    dwst[...] = jnp.zeros(dwst.shape, F32)

    @pl.when(has_left)
    def _():
        cn_copy(False).wait_recv()

    @pl.when(jnp.logical_not(has_left))
    def _():
        cn[row(0), :] = jnp.zeros((rw, cp), BF16)

    @pl.when(has_right)
    def _():
        cn_copy(True).wait_recv()

    @pl.when(jnp.logical_not(has_right))
    def _():
        cn[row(height + 1), :] = jnp.zeros((rw, cp), BF16)

    def put(ref, slot, r, value):
        v = value.reshape(cols, pair, fc)
        z = jnp.zeros((scenes, fc), F32)
        ref[slot, r, 1 : cols + 1] = v.astype(BF16)
        ref[slot, r, 0] = jnp.concatenate([z, v[cols - 1, :scenes]], 0).astype(BF16)
        ref[slot, r, cols + 1] = jnp.concatenate([v[0, scenes:], z], 0).astype(BF16)

    def gm_copy(k, slot, up):
        return pltpu.make_async_remote_copy(
            src_ref=gm.at[slot, 1 if up else height],
            dst_ref=halo.at[k, 1 if up else 0],
            send_sem=gm_send.at[k, 0 if up else 1],
            recv_sem=gm_recv.at[k, 0 if up else 1],
            device_id=left if up else right,
            device_id_type=MESH,
        )

    def phase_a(k, slot):
        span = pl.ds(pl.multiple_of(k * fc, fc), fc)
        taps = [
            taps_ref[pl.ds(i, 1), span].astype(BF16).reshape(1, 1, fc) for i in range(9)
        ]
        bias = tb_ref[:, span]

        def hidden(r):
            put(hid, slot, r, dot(cn[r * rw : (r + 1) * rw, :], we_ref[:, span]))

        def products(r):
            active = act[r * rw : (r + 1) * rw, :]
            o = dot_nt(active, ws_ref[:, span])
            for t in range(lt):
                oacc[t, r * rw : (r + 1) * rw, :] += o[:, t * LANE : (t + 1) * LANE]
            dwst[:, span] += dot(ctx[:, r * rw : (r + 1) * rw], active)

        hidden(0)
        hidden(1)
        hidden(2)
        sums = jnp.zeros((8, fc), F32)
        for r in range(height):
            back[...] = dot(ctt[r * rw : (r + 1) * rw, :], ws_ref[:, span])
            if r:
                products(r - 1)
            for g in range(0, cols, group):
                acc = None
                for a in range(3):
                    line = hid[slot, r + a, g : g + group + 2]
                    for b in range(3):
                        term = line[b : b + group] * taps[3 * a + b]
                        acc = term if acc is None else acc + term
                mixed = acc.astype(F32).reshape(group * pair, fc) + bias
                arg = mixed * 0.7071067811865476
                phi = 0.5 + 0.5 * lax.erf(arg)
                dens = jnp.exp2(arg * arg * -LOG2E) * mixed
                act[r * rw + g * pair : r * rw + (g + group) * pair, :] = (mixed * phi).astype(BF16)
                slope = phi + dens * 0.3989422804014327
                grad = back[g * pair : (g + group) * pair, :] * slope
                sums = sums + jnp.sum(grad.reshape(group * pair // 8, 8, fc), 0)
                v = grad.reshape(group, pair, fc)
                gm[slot, r + 1, g + 1 : g + group + 1] = v.astype(BF16)
                z = jnp.zeros((scenes, fc), F32)
                if g == 0:
                    gm[slot, r + 1, cols + 1] = jnp.concatenate([v[0, scenes:], z], 0).astype(BF16)
                if g + group == cols:
                    gm[slot, r + 1, 0] = jnp.concatenate([z, v[group - 1, :scenes]], 0).astype(BF16)
            if r + 3 < height + 2:
                hidden(r + 3)
        products(height - 1)
        dtb_ref[:, span] = sums

        @pl.when(has_left)
        def _():
            gm_copy(k, slot, True).start()

        @pl.when(has_right)
        def _():
            gm_copy(k, slot, False).start()

    def phase_b(k, slot):
        span = pl.ds(pl.multiple_of(k * fc, fc), fc)

        @pl.when(has_left)
        def _():
            gm_copy(k, slot, False).wait_recv()
            gm[slot, 0] = halo[k, 0]

        @pl.when(jnp.logical_not(has_left))
        def _():
            gm[slot, 0] = jnp.zeros((cols + 2, pair, fc), BF16)

        @pl.when(has_right)
        def _():
            gm_copy(k, slot, True).wait_recv()
            gm[slot, height + 1] = halo[k, 1]

        @pl.when(jnp.logical_not(has_right))
        def _():
            gm[slot, height + 1] = jnp.zeros((cols + 2, pair, fc), BF16)

        taps = [
            taps_ref[pl.ds(i, 1), span].astype(BF16).reshape(1, 1, fc) for i in range(9)
        ]
        tapacc[...] = jnp.zeros(tapacc.shape, F32)

        def products(r):
            low = act[r * rw : (r + 1) * rw, :]
            dwe_ref[:, span] += dot(cnt[:, r * rw : (r + 1) * rw], low)
            g = dot_nt(low, we_ref[:, span])
            for t in range(lt):
                gacc[t, r * rw : (r + 1) * rw, :] += g[:, t * LANE : (t + 1) * LANE]

        for r in range(height):
            tapsum = [None] * 9
            for g in range(0, cols, group):
                acc = None
                own = hid[slot, r + 1, g + 1 : g + group + 1]
                for a in range(3):
                    line = gm[slot, r + 2 - a, g : g + group + 2]
                    for b in range(3):
                        window = line[2 - b : 2 - b + group]
                        term = window * taps[3 * a + b]
                        acc = term if acc is None else acc + term
                        prod = own * window
                        while prod.shape[0] > 1:
                            cut = prod.shape[0] // 2
                            prod = prod[:cut] + prod[cut:]
                        i = 3 * a + b
                        tapsum[i] = prod[0] if tapsum[i] is None else tapsum[i] + prod[0]
                act[r * rw + g * pair : r * rw + (g + group) * pair, :] = acc.reshape(group * pair, fc)
            for i in range(9):
                tapacc[i] += tapsum[i].astype(F32)
        for r in range(height):
            products(r)

        for tap in range(9):
            dtap_ref[pl.ds(tap, 1), span] = jnp.sum(tapacc[tap], 0, keepdims=True)

        @pl.when(has_left)
        def _():
            gm_copy(k, slot, True).wait_send()

        @pl.when(has_right)
        def _():
            gm_copy(k, slot, False).wait_send()

    @pl.loop(0, nchunk + 1)
    def _(k):
        slot = lax.rem(k, 2)

        @pl.when(k < nchunk)
        def _():
            phase_a(k, slot)

        @pl.when(k > 0)
        def _():
            phase_b(k - 1, 1 - slot)

    @pl.when(has_left)
    def _():
        cn_copy(True).wait_send()

    @pl.when(has_right)
    def _():
        cn_copy(False).wait_send()

    plan, filled, _ = ffn_plan(channels, ff, ndev)
    for name, ref in (("we", dwe_ref), ("ws", dwst)):
        at, rows, slabs = plan[name]
        for t in range(slabs):
            packed[at + t * rows : at + (t + 1) * rows, :] = ref[
                :rows, t * LANE : (t + 1) * LANE
            ].astype(BF16)
    if filled < packed.shape[0]:
        packed[filled:, :] = jnp.zeros((packed.shape[0] - filled, LANE), BF16)
    pack_copy = pltpu.make_async_copy(packed, pack_hbm, pack_sem.at[0])
    pack_copy.start()

    def gather(ref, s):
        rows = []
        for r in range(height):
            for half in range(2):
                rows.append(
                    jnp.concatenate(
                        [
                            ref[t, pl.ds(r * rw + half * scenes + s, cols, stride=pair), :]
                            for t in range(lt)
                        ],
                        -1,
                    )
                )
        return jnp.concatenate(rows, 0)[:, :channels]

    def out_copy(s, slot):
        return pltpu.make_async_copy(out_stage.at[slot], out_hbm.at[s], out_sem.at[slot])

    def gres_copy(s, slot):
        return pltpu.make_async_copy(gres_stage.at[slot], gres_hbm.at[s], gres_sem.at[slot])

    @pl.loop(0, scenes)
    def _(s):
        slot = lax.rem(s, 2)

        @pl.when(s >= 2)
        def _():
            out_copy(s - 2, slot).wait()

        out_stage[slot] = gather(oacc, s).astype(BF16)
        out_copy(s, slot).start()

    @pl.loop(0, height)
    def _(r):
        kept = load3(res_ref, r)
        rstd = kept[:, channels : channels + 1]
        xhat = inside(kept, channels)
        upstream = load3(gacc, r)
        dvec_ref[0:1] += jnp.sum(upstream * xhat, 0, keepdims=True)
        dvec_ref[1:2] += jnp.sum(upstream, 0, keepdims=True)
        g = ctt[row(r), :].astype(F32) + norm_back(upstream, g2, xhat, rstd, channels)
        store3(gacc, r, g)

    @pl.loop(0, scenes)
    def _(s):
        slot = lax.rem(s, 2)

        @pl.when(s >= 2)
        def _():
            gres_copy(s - 2, slot).wait()

        gres_stage[slot] = gather(gacc, s)
        gres_copy(s, slot).start()

    for s in range(scenes - 2, scenes):
        out_copy(s, s % 2).wait()
        gres_copy(s, s % 2).wait()
    pack_copy.wait()


def ffn(dims, blk, ndev, res, ct, ew, sw, vec, eb, taps, tb):
    scenes, height, width, channels, cp = dims
    n = height * width
    total = scenes * n
    rw = scenes * width
    ff = sw.shape[1]
    lt = cp // LANE
    nchunk = ff // FF_CHUNK
    strip = (width // 2 + 2, 2 * scenes, FF_CHUNK)
    pack_rows = sum(ffn_plan(channels, ff, ndev)[2])
    vm = pl.BlockSpec(memory_space=pltpu.VMEM)
    hbm = pl.BlockSpec(memory_space=pl.ANY)
    return pl.pallas_call(
        functools.partial(ffn_kernel, dims, ff, blk, ndev),
        in_specs=[hbm] * 4 + [vm] * 4,
        out_specs=[hbm, hbm, hbm] + [vm] * 3,
        out_shape=[
            jax.ShapeDtypeStruct((scenes, n, channels), BF16),
            jax.ShapeDtypeStruct((scenes, n, channels), F32),
            jax.ShapeDtypeStruct((pack_rows, LANE), BF16),
            jax.ShapeDtypeStruct((9, ff), F32),
            jax.ShapeDtypeStruct((8, ff), F32),
            jax.ShapeDtypeStruct((8, cp), F32),
        ],
        scratch_shapes=[
            pltpu.VMEM((cp, ff), BF16),
            pltpu.VMEM((cp, ff), BF16),
            pltpu.VMEM((cp, ff), F32),
            pltpu.VMEM((cp, ff), F32),
            pltpu.VMEM((pack_rows, LANE), BF16),
            pltpu.VMEM((lt, total, LANE), F32),
            pltpu.VMEM((scenes, n, channels), BF16),
            pltpu.VMEM((total + 2 * rw, cp), BF16),
            pltpu.VMEM((cp, total), BF16),
            pltpu.VMEM((total, cp), BF16),
            pltpu.VMEM((cp, total), BF16),
            pltpu.VMEM((lt, total + 2 * scenes, LANE), F32),
            pltpu.VMEM((lt, total + 2 * scenes, LANE), F32),
            pltpu.VMEM((2, height + 2) + strip, BF16),
            pltpu.VMEM((2, height + 2) + strip, BF16),
            pltpu.VMEM((nchunk, 2) + strip, BF16),
            pltpu.VMEM((total, FF_CHUNK), BF16),
            pltpu.VMEM((rw, FF_CHUNK), F32),
            pltpu.VMEM((9, 2 * scenes, FF_CHUNK), F32),
            pltpu.VMEM((2, n, channels), BF16),
            pltpu.VMEM((2, n, channels), F32),
            pltpu.SemaphoreType.DMA((2,)),
            pltpu.SemaphoreType.DMA((1,)),
            pltpu.SemaphoreType.DMA((height,)),
            pltpu.SemaphoreType.DMA((scenes,)),
            pltpu.SemaphoreType.DMA((2,)),
            pltpu.SemaphoreType.DMA((2,)),
            pltpu.SemaphoreType.DMA((2,)),
            pltpu.SemaphoreType.DMA((2,)),
            pltpu.SemaphoreType.DMA((nchunk, 2)),
            pltpu.SemaphoreType.DMA((nchunk, 2)),
        ],
        compiler_params=pltpu.CompilerParams(
            vmem_limit_bytes=VMEM, collective_id=0, has_side_effects=True
        ),
    )(res, ct, ew, sw, vec, eb, taps, tb)


def attback_kernel(
    dims, ff, ndp, blk, used, q_ref, att_ref, gres_ref, ke_ref, ve_ref, rn_ref, tok_ref, gres2_ref,
    red_ref, vec_ref, wp_ref, wkv_ref, wq_ref, wr_ref, dtap, dtb, dvec2, cnt, first_hbm,
    ig_ref, sum_hbm, mid_hbm, rest_hbm, small_hbm,
    dwqt, dwrt, dwp_ref, dwkv_ref, dbp_ref, dvec_ref, ge, dqt, gqt_ref, grn_ref, scr, gscr, own, acc, sib_land, up_land, down_land,
    gkv_ref, work, land, done, mid_work, mid_land, mid_done, rest_work, rest_land, rest_done, small_work, small_land, small_done,
    sib_send, sib_recv, up_send, up_recv, down_send, down_recv, sum_send, sum_recv,
    mid_send, mid_recv, rest_send, rest_recv, sum_sem,
):
    scenes, height, width, channels, cp = dims
    n = height * width
    keys = n // 4
    chips = blk // 2
    lt = cp // LANE
    head_size = channels // HEADS
    step = pl.program_id(0)
    chip, core, up, down, sib = place(blk)
    count = 2 * used * keys // KEY_CHUNK
    steps = scenes + chips
    together = -(-scenes // chips)
    ndev = ndp * blk
    order = orders_of(ndp, blk)[0]
    parts = three_parts(work, land, done, ffn_plan(channels, ff, ndev)[2], [order] * 3)
    sums = Sums(parts, sum_send, sum_recv)
    each = -(-(sums.ops + 1) // (steps - 1))
    mid_plan, mid_used, mid_sizes = middle_plan(channels, ndev)
    mid = Sums(
        three_parts(mid_work, mid_land, mid_done, mid_sizes, [order] * 3), mid_send, mid_recv
    )
    early = min(chips, mid.ops)

    def put(buf, plan, name, value):
        at, rows, slabs = plan[name]
        for t in range(slabs):
            buf[at + t * rows : at + (t + 1) * rows, :] = value(t, rows).astype(BF16)

    def cut_of(value):
        return lambda t, rows: value[:rows, t * LANE : (t + 1) * LANE]

    @pl.when(step == 0)
    def _():
        load = pltpu.make_async_copy(first_hbm, work, sum_sem.at[0])
        load.start()
        barrier = pltpu.get_barrier_semaphore()
        peers = peers_of(order)
        for peer in peers:
            pl.semaphore_signal(barrier, inc=1, device_id=peer, device_id_type=pl.DeviceIdType.MESH)
        pl.semaphore_wait(barrier, len(peers))
        load.wait()
        for k in range(each):
            sums.advance(k)
        dwqt[...] = jnp.zeros(dwqt.shape, F32)
        dwrt[...] = jnp.zeros(dwrt.shape, F32)
        dvec_ref[...] = jnp.zeros(dvec_ref.shape, F32)
        dwp_ref[...] = jnp.zeros(dwp_ref.shape, F32)
        dwkv_ref[...] = jnp.zeros(dwkv_ref.shape, F32)
        dbp_ref[...] = jnp.zeros(dbp_ref.shape, F32)

    def to_sib(s, target):
        return remote(
            own.at[lax.rem(s, 2), 1 - core, target], sib_land.at[s, target], sib_send.at[s, target],
            sib_recv.at[s, target], sib,
        )

    def to_up(s, target):
        return remote(
            acc.at[s, target], up_land.at[s, target], up_send.at[s, target], up_recv.at[s, target], up
        )

    def to_down(s, target):
        return remote(
            acc.at[s, target], down_land.at[s, target], down_send.at[s, target],
            down_recv.at[s, target], down,
        )

    def plus(a, b):
        return (a.astype(F32) + b.astype(F32)).astype(BF16)

    def chunk(j):
        s = step
        per = KEY_CHUNK // keys
        span = slice(j * KEY_CHUNK, (j + 1) * KEY_CHUNK)
        dks, dvs = [], []
        for h in range(HEADS):
            block = slice(h * LANE, (h + 1) * LANE)
            k, v = ke_ref[0, span, block], ve_ref[0, span, block]
            q, g = q_ref[0, :, block], ge[:, block]
            p = jnp.exp2(dot_nt(k, q))
            gs = (p * dot_nt(v, g)).astype(BF16)
            dvs.append(dot(p.astype(BF16), g))
            dks.append(dot(gs, q))
            dqt[block, :] += dot_tn(k, gs)
        low_half = lanes((KEY_CHUNK, LANE)) < HALF
        tiles = []
        for group, scale in ((dks, LN2), (dvs, 1.0)):
            for t in range(lt):
                other = (
                    group[2 * t + 1] if 2 * t + 1 < HEADS else jnp.zeros((KEY_CHUNK, LANE), F32)
                )
                tiles.append((jnp.where(low_half, group[2 * t], other) * scale).astype(BF16))
        gkv = jnp.concatenate(tiles, -1)
        grn = dot_nt(gkv, wkv_ref[...]).astype(BF16)
        for i in range(per):
            at = j * per + i
            own[lax.rem(s, 2), at // used, at % used] = grn[i * keys : (i + 1) * keys]

            @pl.when(core != at // used)
            def _(at=at):
                to_sib(s, at % used).start()

        gkv_ref[span, :] = gkv

    @pl.when(step < scenes)
    def _():
        s = step
        gb = widen(gres_ref[0], cp).astype(BF16)
        dbp_ref[...] += jnp.sum(gb.astype(F32).reshape(n // 8, 8, cp), 0)
        att = att_ref[0]
        dwp_ref[...] += dot(att.astype(BF16).T, gb)
        gatt = head_blocks(dot_nt(gb, wp_ref[...]), lambda e: 0.0)
        lane = lanes((n, LANE))
        for h in range(HEADS):
            e = ext_lane(h)
            g = gatt[h].astype(BF16).astype(F32)
            o = att[:, (h // 2) * LANE : (h // 2 + 1) * LANE]
            inner = jnp.sum(g * o, -1, keepdims=True)
            hi = inner.astype(BF16).astype(F32)
            g = jnp.where(lane == e, -hi, g)
            g = jnp.where(lane == e + 1, hi - inner, g)
            ge[:, h * LANE : (h + 1) * LANE] = g.astype(BF16)
        dqt[...] = jnp.zeros(dqt.shape, F32)
        chunk(0)

    s1 = step - 1

    @pl.when(jnp.logical_and(s1 >= 0, s1 < scenes))
    def _():
        for target in range(used):
            to_sib(s1, target).wait()
            acc[s1, target] = plus(own[lax.rem(s1, 2), core, target], sib_land[s1, target])

    s_up = step - 1 - chip

    @pl.when(jnp.logical_and(s_up >= 0, s_up < scenes))
    def _():
        for target in reversed(range(1, used)):

            @pl.when(target > chip)
            def _(target=target):
                @pl.when(chip > 0)
                def _():
                    to_up(s_up, target).wait_recv()
                    acc[s_up, target] = plus(acc[s_up, target], up_land[s_up, target])

                to_up(s_up, target).start()

    s_down = step - chips + chip

    @pl.when(jnp.logical_and(s_down >= 0, s_down < scenes))
    def _():
        for target in range(used):

            @pl.when(target < chip)
            def _(target=target):
                @pl.when(chip < chips - 1)
                def _():
                    to_down(s_down, target).wait_recv()
                    acc[s_down, target] = plus(acc[s_down, target], down_land[s_down, target])

                to_down(s_down, target).start()

    s_end = step - chips

    @pl.when(s_end >= 0)
    def _():
        @pl.when(chip < used)
        def _():
            grn_ref[s_end] = acc[s_end, chip].astype(F32)

            @pl.when(chip > 0)
            def _():
                to_up(s_end, chip).wait_recv()
                grn_ref[s_end] += up_land[s_end, chip].astype(F32)

            @pl.when(chip < chips - 1)
            def _():
                to_down(s_end, chip).wait_recv()
                grn_ref[s_end] += down_land[s_end, chip].astype(F32)

        @pl.when(chip >= used)
        def _():
            grn_ref[s_end] = jnp.zeros((keys, cp), F32)

    for t in range(1, steps - 1):

        @pl.when(step == t)
        def _(t=t):
            for k in range(t * each, min((t + 1) * each, sums.ops + 1)):
                sums.advance(k)
            if t * each <= sums.ops < (t + 1) * each:
                pltpu.make_async_copy(done, sum_hbm, sum_sem.at[0]).start()

    def tail(base):
        gred, low, hats = [], [], []
        for i in range(together):
            rhat, rstd = centered(red_ref[i], channels)
            upstream = inside(grn_ref[base + i], channels)
            dvec_ref[0:1] += jnp.sum(upstream * rhat, 0, keepdims=True)
            dvec_ref[1:2] += jnp.sum(upstream, 0, keepdims=True)
            g = norm_back(upstream, vec_ref[2:3], rhat, rstd, channels)
            gred.append(inside(g, channels).astype(BF16))
            dvec_ref[2:3] += jnp.sum(gred[i].astype(F32), 0, keepdims=True)
            x = widen(tok_ref[i].astype(F32), cp)
            xhat, xstd = centered(x, channels)
            hats.append((xhat, xstd))
            low.append((xhat * vec_ref[0:1] + vec_ref[1:2]).astype(BF16))
            lowf = low[i].astype(F32)
            for t in range(lt):
                scr[i, t, :n] = lowf[:, t * LANE : (t + 1) * LANE]
        gred = jnp.concatenate(gred, 0)
        gred_t = gred.T
        for b in range(2):
            patches = [[], []]
            for i in range(together):
                part = [scr[i, t, pl.ds(b, n // 2, stride=2), :] for t in range(lt)]
                part = jnp.concatenate(part, -1).reshape(height // 2, 2, width // 2, cp)
                for a in range(2):
                    patches[a].append(part[:, a].reshape(keys, cp))
            for a in range(2):
                ab = 2 * a + b
                dwrt[ab] += dot(gred_t, jnp.concatenate(patches[a], 0).astype(BF16))
                back = dot_nt(gred, wr_ref[ab])
                for i in range(together):
                    for t in range(lt):
                        for r in range(height // 2):
                            at = i * keys + r * (width // 2)
                            gscr[i, t, pl.ds((2 * r + a) * width + b, width // 2, stride=2), :] = back[
                                at : at + width // 2, t * LANE : (t + 1) * LANE
                            ]
        for i in range(together):
            gqt = gqt_ref[base + i]
            xhat, xstd = hats[i]
            dwqt[...] += dot(gqt, low[i])
            gn = widen(dot_nt(gqt.T, wq_ref[...]), cp)
            gn = gn + jnp.concatenate([gscr[i, t, :n] for t in range(lt)], -1)
            dvec_ref[3:4] += jnp.sum(gn * xhat, 0, keepdims=True)
            dvec_ref[4:5] += jnp.sum(gn, 0, keepdims=True)
            gx = norm_back(gn, vec_ref[0:1], xhat, xstd, channels)
            ig_ref[i] = gres2_ref[i] + gx[:, :channels]

    @pl.when(step == scenes)
    def _():
        joined = jnp.concatenate([dwkv_ref[:, :channels], dwkv_ref[:, cp : cp + channels]], -1)
        put(mid_work, mid_plan, "wkv", cut_of(joined))
        put(mid_work, mid_plan, "wp", cut_of(dwp_ref))
        if mid_used < mid_work.shape[0]:
            mid_work[mid_used:, :] = jnp.zeros((mid_work.shape[0] - mid_used, LANE), BF16)

    for t in range(early):

        @pl.when(step == scenes + t)
        def _(t=t):
            mid.advance(t)

    @pl.when(step >= scenes)
    def _():
        tail((step - scenes) * together)

    @pl.when(step < scenes)
    def _():
        s = step
        for j in range(1, count):
            chunk(j)
        dwkv_ref[...] += dot(rn_ref[0].T, gkv_ref[...])
        for h in range(HEADS):
            base = h * LANE + (0 if h % 2 == 0 else HALF)
            gqt_ref[s, h * HALF : (h + 1) * HALF] = (
                dqt[base : base + HALF, :] * head_size**-0.5
            ).astype(BF16)

    @pl.when(step == steps - 1)
    def _():
        plan, filled, sizes = rest_plan(channels, ndev)
        splan, srows = small_plan(channels, ff, ndev)
        full = channels // LANE

        joined = jnp.concatenate([dwrt[ab, :channels, :channels] for ab in range(4)], -1)
        put(rest_work, plan, "wr", cut_of(joined))
        put(rest_work, plan, "wq", cut_of(dwqt))
        last = pltpu.roll(dwqt[:, full * LANE :], HALF, 1)
        put(
            rest_work,
            plan,
            "halves",
            lambda t, rows: jnp.where(
                lanes((1, LANE)) < HALF, dwp_ref[:rows, full * LANE :], last
            ),
        )
        if filled < rest_work.shape[0]:
            rest_work[filled:, :] = jnp.zeros((rest_work.shape[0] - filled, LANE), BF16)
        small_work[...] = jnp.zeros(small_work.shape, F32)
        at, rows, slabs = splan["tap"]
        db = jnp.sum(dtb[...], 0, keepdims=True)
        for t in range(slabs):
            cut = slice(t * LANE, (t + 1) * LANE)
            small_work[at + t * rows : at + t * rows + 9, :] = dtap[:, cut]
            small_work[at + t * rows + 9 : at + t * rows + 10, :] = db[:, cut]
        at, rows, slabs = splan["vec"]
        pb = jnp.sum(dbp_ref[...], 0, keepdims=True)
        qb = widen(dwqt[:, full * LANE :].T[HALF : HALF + 1], cp)
        for t in range(slabs):
            cut = slice(t * LANE, (t + 1) * LANE)
            low = at + t * rows
            small_work[low : low + 3, :] = dvec2[0:3, cut]
            small_work[low + 3 : low + 8, :] = dvec_ref[0:5, cut]
            small_work[low + 8 : low + 9, :] = pb[:, cut]
            small_work[low + 9 : low + 10, :] = qb[:, cut]
        at, rows, _ = splan["count"]
        small_work[at : at + rows, :] = cnt[...]

        orders = orders_of(ndp, blk)
        rest_parts = three_parts(rest_work, rest_land, rest_done, sizes, orders)
        rest_parts.append((small_work, small_land, small_done, 0, srows, orders[0]))
        rest = Sums(rest_parts, rest_send, rest_recv)
        for k in range(max(rest.ops, mid.ops - early) + 1):
            if k <= rest.ops:
                rest.advance(k)
            if k + early <= mid.ops:
                mid.advance(k + early)
        leave = [
            pltpu.make_async_copy(rest_done, rest_hbm, sum_sem.at[1]),
            pltpu.make_async_copy(small_done, small_hbm, sum_sem.at[2]),
            pltpu.make_async_copy(mid_done, mid_hbm, sum_sem.at[3]),
        ]
        for copy in leave:
            copy.start()
        for copy in leave:
            copy.wait()
        pltpu.make_async_copy(done, sum_hbm, sum_sem.at[0]).wait()

        @pl.loop(0, scenes)
        def _(s):
            for target in range(used):

                @pl.when(target > chip)
                def _(target=target):
                    to_up(s, target).wait_send()

                @pl.when(target < chip)
                def _(target=target):
                    to_down(s, target).wait_send()


def attback(
    dims, ff, ndp, blk, used, cid, q, att, gres, ke, ve, rn, tok, red, vec, wp, wkv, wq, wr,
    dtap, dtb, dvec2, cnt, first
):
    scenes, height, width, channels, cp = dims
    n = height * width
    keys = n // 4
    chips = blk // 2
    lt = cp // LANE
    live = 2 * used * keys
    he = HEADS * LANE
    together = -(-scenes // chips)
    assert scenes == together * chips
    mid_rows = sum(middle_plan(channels, ndp * blk)[2])
    rest_rows = sum(rest_plan(channels, ndp * blk)[2])
    small_rows = small_plan(channels, ff, ndp * blk)[1]
    ops = 2 * len(orders_of(ndp, blk)[0])

    def early(shape):
        return pl.BlockSpec(
            (1,) + shape, lambda t: (jnp.minimum(t, scenes - 1),) + (0,) * len(shape)
        )

    def late(shape):
        return pl.BlockSpec(
            (together,) + shape, lambda t: (jnp.maximum(t - scenes, 0),) + (0,) * len(shape)
        )

    land = (scenes, used, keys, cp)
    hbm = pl.BlockSpec(memory_space=pl.ANY)
    vm = pl.BlockSpec(memory_space=pltpu.VMEM)
    return pl.pallas_call(
        functools.partial(attback_kernel, dims, ff, ndp, blk, used),
        grid=(scenes + chips,),
        in_specs=[
            early((n, he)),
            early((n, cp)),
            early((n, channels)),
            early((live, he)),
            early((live, he)),
            early((live, cp)),
            late((n, channels)),
            late((n, channels)),
            late((keys, cp)),
        ]
        + [vm] * 9
        + [hbm],
        out_specs=[late((n, channels))] + [hbm] * 4,
        out_shape=[
            jax.ShapeDtypeStruct((scenes, n, channels), F32),
            jax.ShapeDtypeStruct(first.shape, BF16),
            jax.ShapeDtypeStruct((mid_rows, LANE), BF16),
            jax.ShapeDtypeStruct((rest_rows, LANE), BF16),
            jax.ShapeDtypeStruct((small_rows, LANE), F32),
        ],
        scratch_shapes=[
            pltpu.VMEM((channels, cp), F32),
            pltpu.VMEM((4, cp, cp), F32),
            pltpu.VMEM((cp, cp), F32),
            pltpu.VMEM((cp, 2 * cp), F32),
            pltpu.VMEM((8, cp), F32),
            pltpu.VMEM((8, cp), F32),
            pltpu.VMEM((n, he), BF16),
            pltpu.VMEM((he, n), F32),
            pltpu.VMEM((scenes, channels, n), BF16),
            pltpu.VMEM((scenes, keys, cp), F32),
            pltpu.VMEM((together, lt, n + 8, LANE), F32),
            pltpu.VMEM((together, lt, n + 8, LANE), F32),
            pltpu.VMEM((2, 2, used, keys, cp), BF16),
        ]
        + [pltpu.VMEM(land, BF16)] * 4
        + [pltpu.VMEM((live, 2 * cp), BF16)]
        + [pltpu.VMEM(first.shape, BF16)] * 3
        + [pltpu.VMEM((mid_rows, LANE), BF16)] * 3
        + [pltpu.VMEM((rest_rows, LANE), BF16)] * 3
        + [pltpu.VMEM((small_rows, LANE), F32)] * 3
        + [pltpu.SemaphoreType.DMA((scenes, used))] * 6
        + [pltpu.SemaphoreType.DMA((3, ops, widest(ndp, blk)))] * 4
        + [pltpu.SemaphoreType.DMA((4, ops, widest(ndp, blk)))] * 2
        + [pltpu.SemaphoreType.DMA((4,))],
        compiler_params=pltpu.CompilerParams(
            vmem_limit_bytes=VMEM, collective_id=cid, has_side_effects=True
        ),
    )(q, att, gres, ke, ve, rn, tok, gres, red, vec, wp, wkv, wq, wr, dtap, dtb, dvec2, cnt, first)


def unpack_kernel(channels, ff, ndev, out_in, ig_in, first_in, middle_in, packed_in, small, *refs):
    cp = up_to(channels, LANE)
    splan, _ = small_plan(channels, ff, ndev)
    names = (
        ("out", "ig", "g1", "b1", "wq", "qb", "wr", "rb", "rg", "rbn", "wkv", "vb")
        + ("wp", "pb", "g2", "b2", "we", "eb", "dt", "db", "ws", "sb", "cm")
    )
    outs = dict(zip(names, refs[: len(names)]))
    out_hold, ig_hold, first, middle, packed, we, ws, wr, wkv, in_sem, out_sem, sem = refs[len(names) :]
    lt = cp // LANE
    full = channels // LANE
    loads = [
        pltpu.make_async_copy(first_in, first, sem.at[0]),
        pltpu.make_async_copy(middle_in, middle, sem.at[1]),
        pltpu.make_async_copy(packed_in, packed, sem.at[2]),
    ]
    ins, moves = [], []
    pairs = ((out_in, out_hold, outs["out"]), (ig_in, ig_hold, outs["ig"]))
    for k, (src, hold, dst) in enumerate(pairs):
        for s in range(src.shape[0]):
            ins.append(pltpu.make_async_copy(src.at[s], hold.at[s], in_sem.at[k, s]))
            moves.append(pltpu.make_async_copy(hold.at[s], dst.at[s], out_sem.at[k, s]))
    for copy in loads + ins:
        copy.start()
    plans = (
        (first, ffn_plan(channels, ff, ndev)[0]), (middle, middle_plan(channels, ndev)[0]),
        (packed, rest_plan(channels, ndev)[0]),
    )
    stores = [
        pltpu.make_async_copy(src, outs[name], sem.at[3 + k])
        for k, (src, name) in enumerate(((we, "we"), (ws, "ws"), (wr, "wr"), (wkv, "wkv")))
    ]

    def slab(name, t, low=0, count=None):
        ref, plan = next(v for v in plans if name in v[1])
        at, rows, _ = plan[name]
        count = rows if count is None else count
        return ref[at + t * rows + low : at + t * rows + low + count, :].astype(F32)

    def move(count):
        for copy, on in list(zip(ins, moves))[count : count + len(ins) // 2]:
            copy.wait()
            on.start()

    loads[0].wait()
    for t in range(ff // LANE):
        cut = slice(t * LANE, (t + 1) * LANE)
        we[:, cut] = slab("we", t, 0, channels)
        outs["eb"][cut] = slab("we", t, channels, 16)[0]
        ws[:, cut] = slab("ws", t)
        at, rows, _ = splan["tap"]
        outs["dt"][:, cut] = small[at + t * rows : at + t * rows + 9, :]
        outs["db"][cut] = small[at + t * rows + 9, :]
    stores[0].start()
    stores[1].start()
    move(0)
    loads[1].wait()
    loads[2].wait()
    for t in range(4 * channels // LANE):
        wr[:, t * LANE : (t + 1) * LANE] = slab("wr", t)
    stores[2].start()
    for t in range(2 * channels // LANE):
        wkv[:, t * LANE : (t + 1) * LANE] = slab("wkv", t, 0, channels)
    stores[3].start()
    tall = [slab("wkv", t, channels, 16) for t in range(2 * channels // LANE)]
    outs["vb"][...] = jnp.concatenate(tall, -1)[1, channels:]
    halves = slab("halves", 0)
    wp = [slab("wp", t) for t in range(full)] + [halves]
    outs["wp"][...] = jnp.concatenate(wp, -1)[:, :channels]
    wq = [slab("wq", t) for t in range(full)] + [pltpu.roll(halves, HALF, 1)]
    outs["wq"][...] = jnp.concatenate(wq, -1).T[:channels]
    at, rows, _ = splan["vec"]
    vec = jnp.concatenate([small[at + t * rows : at + (t + 1) * rows, :] for t in range(lt)], -1)
    vec = vec[:, :channels]
    order = ("g2", "b2", "sb", "rg", "rbn", "rb", "g1", "b1", "pb", "qb")
    for k, name in enumerate(order):
        outs[name][...] = vec[k]
    at, rows, _ = splan["count"]
    outs["cm"][...] = small[at : at + rows, :].astype(jnp.int32)[:CLASSES, :CLASSES]
    move(len(ins) // 2)
    for copy in moves + stores:
        copy.wait()


def unpack(channels, ff, ndev, out, ig, first, middle, packed, small):
    one = (channels,)
    shapes = [
        one, one, (channels, channels), one, (channels, 4 * channels), one, one, one,
        (channels, 2 * channels), one, (channels, channels), one, one, one, (channels, ff), (ff,),
        (9, ff), (ff,), (channels, ff), one,
    ]
    outs = [jax.ShapeDtypeStruct(v, F32) for v in shapes]
    outs.append(jax.ShapeDtypeStruct((CLASSES, CLASSES), jnp.int32))
    vm = pl.BlockSpec(memory_space=pltpu.VMEM)
    hbm = pl.BlockSpec(memory_space=pl.ANY)
    big = {4, 8, 14, 18}
    return pl.pallas_call(
        functools.partial(unpack_kernel, channels, ff, ndev),
        in_specs=[hbm] * 5 + [vm],
        out_specs=[hbm, hbm] + [hbm if k in big else vm for k in range(len(outs))],
        out_shape=[jax.ShapeDtypeStruct(v.shape, v.dtype) for v in (out, ig)] + outs,
        scratch_shapes=[
            pltpu.VMEM(out.shape, out.dtype),
            pltpu.VMEM(ig.shape, ig.dtype),
            pltpu.VMEM(first.shape, first.dtype),
            pltpu.VMEM(middle.shape, middle.dtype),
            pltpu.VMEM(packed.shape, packed.dtype),
            pltpu.VMEM((channels, ff), F32),
            pltpu.VMEM((channels, ff), F32),
            pltpu.VMEM((channels, 4 * channels), F32),
            pltpu.VMEM((channels, 2 * channels), F32),
            pltpu.SemaphoreType.DMA((2, out.shape[0])),
            pltpu.SemaphoreType.DMA((2, out.shape[0])),
            pltpu.SemaphoreType.DMA((7,)),
        ],
        compiler_params=pltpu.CompilerParams(vmem_limit_bytes=VMEM),
    )(out, ig, first, middle, packed, small)


def split_low(value):
    hi = value.astype(BF16).astype(F32)
    return hi, value - hi


def rows16(*rows):
    width = rows[0].shape[-1]
    at = lax.broadcasted_iota(jnp.int32, (16, width), 0)
    block = jnp.zeros((16, width), F32)
    for k, row in enumerate(rows):
        block = jnp.where(at == k, row, block)
    return block.astype(BF16)


def prep_kernel(
    channels, g1, b1, qw, qb, rw, rb, rg, rbn, kvw, vb, pw, pb, g2, b2, eb, tb, sb,
    vec, wq, wp, wkv, wr, ebias, dbias, full,
):
    cp = up_to(channels, LANE)
    head_size = channels // HEADS
    rest = cp - channels - 16

    def row(ref):
        return ref[...].reshape(1, ref.shape[-1])

    lane = lanes((1, cp))

    def padded(ref, *at):
        v = widen(row(ref), cp)
        for k in at:
            v = jnp.where(lane == channels + k, 1.0, v)
        return v

    for k, v in enumerate(
        (
            padded(g1), padded(b1, 0, 1), padded(rg), padded(rbn, 1, 2), padded(pb), padded(g2),
            padded(b2, 0, 1), padded(sb),
        )
    ):
        vec[k : k + 1, :] = v

    def fill(ref, top, *rows):
        width = ref.shape[-1]
        ref[:channels, :] = top
        ref[channels : channels + 16, :] = (
            rows16(*rows) if rows else jnp.zeros((16, width), BF16)
        )
        if rest:
            ref[channels + 16 :, :] = jnp.zeros((rest, width), BF16)

    dbias[...] = row(tb)
    ebias[...] = rows16(*split_low(row(eb)))
    q = widen(qw[...], cp)
    qb_wide = widen(row(qb), cp)
    fill(wq, q, *split_low(qb_wide))
    kw = widen(kvw[:, :channels], cp)
    vw = widen(kvw[:, channels:], cp)
    nil = jnp.zeros((1, 2 * cp), F32)
    vb_rows = [
        jnp.concatenate([jnp.zeros((1, cp), F32), widen(v, cp)], -1) for v in split_low(row(vb))
    ]
    fill(wkv, jnp.concatenate([kw, vw], -1), nil, *vb_rows)
    fill(wp, widen(pw[...], cp))
    rb_rows = [widen(v, cp) for v in split_low(row(rb))]
    rw_rows = rw[...].T
    for ab in range(4):
        fill(
            wr.at[ab], widen(rw_rows[ab * channels : (ab + 1) * channels, :], cp),
            *rb_rows[ab : ab + 1],
        )

    def norm(v):
        return jnp.sqrt(jnp.sum(v * v, (0, 1), keepdims=True))

    root = channels**0.5

    def reach(gain, bias):
        top = jnp.max(jnp.abs(row(gain)), (0, 1), keepdims=True)
        return root * top + norm(row(bias))

    def head(value, h):
        tile = value[:, h // 2 * LANE : (h // 2 + 1) * LANE].astype(F32)
        return jnp.where(lanes((1, LANE)) // HALF == h % 2, tile, 0.0)

    query_in, key_in = reach(g1, b1), reach(rg, rbn)
    bound = jnp.zeros((1, 1), F32)
    for h in range(HEADS):
        query = query_in * norm(head(q, h)) + norm(head(qb_wide, h))
        bound = jnp.maximum(bound, query * key_in * norm(head(kw, h)))
    bound = bound * (head_size**-0.5 * 1.05)
    full[...] = jnp.where(2.0 * bound + 256.0 < -NEGATIVE, 0, 1).astype(jnp.int32)


def prep(channels, ff, *weights):
    cp = up_to(channels, LANE)
    shapes = [
        ((8, cp), F32), ((cp, cp), BF16), ((cp, cp), BF16), ((cp, 2 * cp), BF16),
        ((4, cp, cp), BF16), ((16, ff), BF16), ((1, ff), F32), ((1, 1), jnp.int32),
    ]
    return pl.pallas_call(
        functools.partial(prep_kernel, channels),
        out_shape=[jax.ShapeDtypeStruct(*v) for v in shapes],
        compiler_params=pltpu.CompilerParams(vmem_limit_bytes=VMEM),
    )(*weights)


def body(
    tokens, mask, labels, predicted, cotangent, norm1_gain, norm1_bias, query_weight, query_bias,
    reduce_weight, reduce_bias, rnorm_gain, rnorm_bias, kv_weight, value_bias, proj_weight,
    proj_bias, norm2_gain, norm2_bias, expand_weight, expand_bias, depth_weight, depth_bias,
    shrink_weight, shrink_bias,
):
    scenes, height, width, channels = tokens.shape
    ndp, blk = lax.axis_size("dp"), lax.axis_size("blk")
    n = height * width
    ff = expand_weight.shape[1]
    dims = (scenes, height, width, channels, up_to(channels, LANE))
    chips = blk // 2
    used = min(chips, -(-MASK_ROWS // (2 * height)))

    vec, wq, wp, wkv, wr, expand_rows, tap_bias, full = prep(
        channels, ff, norm1_gain, norm1_bias, query_weight, query_bias, reduce_weight.T, reduce_bias,
        rnorm_gain, rnorm_bias, kv_weight, value_bias, proj_weight, proj_bias, norm2_gain,
        norm2_bias, expand_bias, depth_bias, shrink_bias,
    )
    full = full[0, 0] > 0

    def either(call, cids, sizes, *operands):
        if used == chips:
            return call(*sizes, chips, cids[1], *operands)
        return lax.cond(
            full,
            functools.partial(call, *sizes, chips, cids[1]),
            functools.partial(call, *sizes, used, cids[0]),
            *operands,
        )

    tok = tokens.reshape(scenes, n, channels)
    ct = cotangent.reshape(scenes, n, channels)
    red, counts, q, att, ke, ve, rn, res = either(
        attend, (2, 3), (dims, blk), tok, mask, labels, predicted, vec, wr, wq, wkv, wp
    )
    out, gres, first, dtap, dtb, dvec2 = ffn(
        dims, blk, ndp * blk, res, ct, expand_weight, shrink_weight.T, vec, expand_rows, depth_weight,
        tap_bias,
    )
    ig, first, middle, packed, small = either(
        attback, (4, 5), (dims, ff, ndp, blk), q, att, gres, ke, ve, rn, tok, red, vec, wp, wkv,
        query_weight, wr, dtap, dtb, dvec2, counts, first,
    )
    out, ig, *grads = unpack(channels, ff, ndp * blk, out, ig, first, middle, packed, small)
    grads[4], grads[18] = grads[4].T, grads[18].T
    return (out.reshape(tokens.shape), ig.reshape(tokens.shape), *grads)


def solution(mesh):
    banded = P("dp", "blk", None, None)
    plane = P("dp", "blk", None)
    in_specs = (banded, plane, plane, plane, banded) + (P(),) * 20
    out_specs = (banded, banded) + (P(),) * 21
    return jax.shard_map(body, mesh=mesh, in_specs=in_specs, out_specs=out_specs, check_vma=False)
```

```python
import functools

import jax
import jax.numpy as jnp
from jax import lax
from jax.experimental import pallas as pl
from jax.experimental.pallas import tpu as pltpu
from jax.sharding import PartitionSpec as P
import ml_dtypes
import numpy as np

HEADS = 5
CLASSES = 19
EPSILON = 1e-06
NEGATIVE = -32768.0
LOG2E = 1.4426950408889634
LN2 = 0.6931471805599453
F32 = jnp.float32
BF16 = jnp.bfloat16
LANE = 128
HALF = 64
KEY_CHUNK = 256
MASK_ROWS = 48
VMEM = 62 * 2**20
FF_CHUNK = 256
GROUP = 8
NEG = np.float32(NEGATIVE * LOG2E)
NEG_HI = np.float32(ml_dtypes.bfloat16(NEG))
NEG_MID = np.float32(ml_dtypes.bfloat16(NEG - NEG_HI))
NEG_LO = np.float32(ml_dtypes.bfloat16(NEG - NEG_HI - NEG_MID))


def up_to(value, step):
    return -(-value // step) * step


def dot(a, b):
    return lax.dot_general(a, b, (((1,), (0,)), ((), ())), preferred_element_type=F32)


def dot_nt(a, b):
    return lax.dot_general(a, b, (((1,), (1,)), ((), ())), preferred_element_type=F32)


def dot_tn(a, b):
    return lax.dot_general(a, b, (((0,), (0,)), ((), ())), preferred_element_type=F32)


def lanes(shape):
    return lax.broadcasted_iota(jnp.int32, shape, len(shape) - 1)


def whole(shape):
    return pl.BlockSpec(shape, lambda *_: (0,) * len(shape))


def per_scene(shape):
    return pl.BlockSpec((1,) + shape, lambda s: (s,) + (0,) * len(shape))


def inside(value, channels):
    full = channels // LANE * LANE
    if full == value.shape[-1]:
        return value
    last = value[..., full:]
    last = jnp.where(lanes(last.shape) < channels - full, last, 0.0)
    return jnp.concatenate([value[..., :full], last], -1)


def head_blocks(value, free):
    half = lanes((1, LANE)) // HALF
    fills = [free(0), free(1)]
    return [
        jnp.where(half == h % 2, value[:, h // 2 * LANE : (h // 2 + 1) * LANE], fills[h % 2])
        for h in range(HEADS)
    ]


def free_row(parity, values):
    lane = lanes((1, LANE))
    row = jnp.zeros((1, LANE), F32)
    for k, value in values.items():
        row = jnp.where(lane == ext_lane(parity) + k, value, row)
    return row


def centered(value, channels):
    mean = jnp.sum(value, -1, keepdims=True) * (1.0 / channels)
    center = inside(value - mean, channels)
    var = jnp.sum(center * center, -1, keepdims=True) * (1.0 / channels)
    rstd = lax.rsqrt(var + EPSILON)
    return center * rstd, rstd


def norm_back(up, gain, xhat, rstd, channels):
    u = up * gain
    mean = jnp.sum(u, -1, keepdims=True) * (1.0 / channels)
    proj = jnp.sum(u * xhat, -1, keepdims=True) * (1.0 / channels)
    return (u - mean - xhat * proj) * rstd


def ext_lane(head):
    return HALF if head % 2 == 0 else 0


def widen(value, width):
    pad = width - value.shape[-1]
    return jnp.concatenate([value, jnp.zeros(value.shape[:-1] + (pad,), value.dtype)], -1)


def place(blk):
    me = lax.axis_index("blk")
    core = lax.rem(me, 2)
    chip = me // 2
    return chip, core, {"blk": me + 2}, {"blk": me - 2}, {"blk": me + 1 - 2 * core}


def greet(chip, chips, up, down, sib):
    barrier = pltpu.get_barrier_semaphore()
    MESH = pl.DeviceIdType.MESH
    has_up, has_down = chip < chips - 1, chip > 0
    pl.semaphore_signal(barrier, inc=1, device_id=sib, device_id_type=MESH)

    @pl.when(has_up)
    def _():
        pl.semaphore_signal(barrier, inc=1, device_id=up, device_id_type=MESH)

    @pl.when(has_down)
    def _():
        pl.semaphore_signal(barrier, inc=1, device_id=down, device_id_type=MESH)

    pl.semaphore_wait(barrier, 1 + has_up.astype(jnp.int32) + has_down.astype(jnp.int32))


def remote(src, dst, send, recv, device):
    return pltpu.make_async_remote_copy(
        src_ref=src, dst_ref=dst, send_sem=send, recv_sem=recv, device_id=device,
        device_id_type=pl.DeviceIdType.MESH,
    )


def groups_of(ndp, nblk):
    dp_bits, blk_bits = ndp.bit_length() - 1, nblk.bit_length() - 1
    assert ndp == 1 << dp_bits and nblk == 1 << blk_bits
    core = [("blk", 0, 2)] if blk_bits else []
    if dp_bits > 2:
        plane = [("dp", 0, 1 << dp_bits // 2), ("dp", dp_bits // 2, 1 << (dp_bits - dp_bits // 2))]
    else:
        plane = [("dp", 0, ndp)] if dp_bits else []
    line = [("blk", 1, nblk // 2)] if blk_bits > 1 else []
    return core, plane, line


def lay_out(items, ndev):
    plan, at = {}, 0
    for name, rows, slabs in items:
        plan[name] = (at, rows, slabs)
        at += rows * slabs
    unit = 16 * ndev
    units = -(-at // unit)
    last = units // 3 - (1 if units > 6 else 0)
    mid = (units - last) // 2
    return plan, at, [(units - last - mid) * unit, mid * unit, last * unit]


def ffn_plan(channels, ff, ndev):
    tall = up_to(channels + 2, 16)
    return lay_out([("we", tall, ff // LANE), ("ws", channels, ff // LANE)], ndev)


def middle_plan(channels, ndev):
    tall = up_to(channels + 2, 16)
    return lay_out(
        [("wkv", tall, 2 * channels // LANE), ("wp", channels, channels // LANE)], ndev
    )


def rest_plan(channels, ndev):
    assert 4 * channels % LANE == 0 and 2 * channels % LANE == 0 and channels % LANE == HALF
    return lay_out(
        [
            ("wr", channels, 4 * channels // LANE), ("wq", channels, channels // LANE),
            ("halves", channels, 1),
        ],
        ndev,
    )


def small_plan(channels, ff, ndev):
    cp = up_to(channels, LANE)
    plan = {"tap": (0, 16, ff // LANE)}
    at = 16 * (ff // LANE)
    plan["vec"] = (at, 16, cp // LANE)
    at += 16 * (cp // LANE)
    plan["count"] = (at, 32, 1)
    at += 32
    return plan, up_to(at, 8 * ndev)


def member(group):
    axis, bit, size = group
    return lax.rem(lax.axis_index(axis) // (1 << bit), size)


def other(group, index):
    axis, bit, _ = group
    return {axis: lax.axis_index(axis) + (index - member(group)) * (1 << bit)}


def peers_of(order):
    return [
        other(group, lax.rem(member(group) + d, group[2])) for group in order for d in range(1, group[2])
    ]


class Sums:
    def __init__(self, parts, send_sem, recv_sem):
        self.parts, self.send_sem, self.recv_sem = parts, send_sem, recv_sem
        self.rounds = len(parts[0][5])
        self.ops = 2 * self.rounds

    def unit(self, p):
        return 16 if self.parts[p][0].dtype == BF16 else 8

    def segment(self, p, i):
        _, _, _, start, rows, order = self.parts[p]
        for group in order[:i]:
            rows //= group[2]
            start = start + member(group) * rows
        return start, rows

    def landing(self, p, i):
        _, _, _, first, rows, order = self.parts[p]
        for group in order[:i]:
            first += rows // group[2] * (group[2] - 1)
            rows //= group[2]
        return first

    def copies(self, p, k):
        buf, land, done, _, _, order = self.parts[p]
        unit = self.unit(p)
        halving = k < self.rounds
        i = k if halving else self.ops - 1 - k
        group = order[i]
        size = group[2]
        me = member(group)
        result = []
        for d in range(1, size):
            to = lax.rem(me + d, size)
            if halving:
                start, rows = self.segment(p, i)
                rows //= size
                src = buf.at[pl.ds(pl.multiple_of(start + to * rows, unit), rows), :]
                low = self.landing(p, i) + (size - 1 - d) * rows
                dst = land.at[pl.ds(low, rows), :]
            else:
                start, rows = self.segment(p, i + 1)
                src = done.at[pl.ds(pl.multiple_of(start, unit), rows), :]
                dst = src
            result.append(
                remote(
                    src, dst, self.send_sem.at[p, k, d - 1], self.recv_sem.at[p, k, d - 1],
                    other(group, to),
                )
            )
        return result

    def start(self, p, k):
        for copy in self.copies(p, k):
            copy.start()

    def finish(self, p, k):
        for copy in self.copies(p, k):
            copy.wait()
        if k >= self.rounds:
            return
        buf, land, done, _, _, order = self.parts[p]
        unit = self.unit(p)
        keep, rows = self.segment(p, k + 1)
        low = self.landing(p, k)
        step = next(c for c in (256, 128, 64, 32, 16, 8) if rows % c == 0)
        into = done if k == self.rounds - 1 else buf

        @pl.loop(0, rows // step)
        def _(j):
            mine = pl.ds(pl.multiple_of(keep + j * step, unit), step)
            total = buf[mine, :].astype(F32)
            for d in range(order[k][2] - 1):
                theirs = pl.ds(pl.multiple_of(low + d * rows + j * step, unit), step)
                total = total + land[theirs, :].astype(F32)
            into[mine, :] = total.astype(buf.dtype)

    def advance(self, k):
        for p in range(len(self.parts)):
            if k > 0:
                self.finish(p, k - 1)
            if k < self.ops:
                self.start(p, k)


def three_parts(buf, land, done, sizes, orders):
    parts, at = [], 0
    for size, order in zip(sizes, orders):
        if size:
            parts.append((buf, land, done, at, size, order))
        at += size
    return parts


def orders_of(ndp, nblk):
    core, plane, line = groups_of(ndp, nblk)
    return [core + plane + line, core + plane + line, core + line + plane]


def widest(ndp, nblk):
    return max(group[2] for group in orders_of(ndp, nblk)[0]) - 1


def packed_rows(keys, cp):
    return (cp // LANE - 1) * keys + keys // 2 + 16


def pack_block(value, unc, keys, cp):
    full = cp // LANE - 1
    last = value[:, full * LANE :]
    turned = pltpu.roll(last[keys // 2 :], HALF, 1)
    last = jnp.where(lanes((1, LANE)) < HALF, last[: keys // 2], turned)
    flags = jnp.broadcast_to(unc, (keys, LANE))
    if keys < LANE:
        flags = jnp.concatenate([flags, jnp.zeros((LANE - keys, LANE), F32)], 0)
    parts = [value[:, t * LANE : (t + 1) * LANE] for t in range(full)] + [last, flags.T[:16]]
    return jnp.concatenate([v.astype(BF16) for v in parts], 0)


def unpack_block(block, ones, keys, cp):
    full = cp // LANE - 1
    parts = [block[t * keys : (t + 1) * keys] for t in range(full)]
    last = block[full * keys : full * keys + keys // 2].astype(F32)
    last = jnp.concatenate([last, pltpu.roll(last, HALF, 1)], 0)
    last = jnp.where(lanes((1, LANE)) < HALF, last, ones)
    flags = block[full * keys + keys // 2 :].astype(F32)[0:1]
    flags = jnp.broadcast_to(flags, (LANE, LANE)).T[:keys]
    return jnp.concatenate(parts + [last.astype(BF16)], -1), flags


def attend_kernel(
    dims, blk, used, tok_ref, mask_ref, label_ref, pred_ref, tok2_ref, vec_ref, wr_ref, wq_ref,
    wkv_ref, wp_ref,
    red_ref, cnt_ref, q_ref, att_ref, ke_ref, ve_ref, rn_ref, res_ref,
    scr, qbuf, oe, rnbuf, up_send, down_send, sib_send, line_recv, sib_recv,
):
    scenes, height, width, channels, cp = dims
    n = height * width
    keys = n // 4
    chips = blk // 2
    lag = chips
    step = pl.program_id(0)
    head_size = channels // HEADS
    chip, core, up, down, sib = place(blk)

    @pl.when(step == 0)
    def _():
        greet(chip, chips, up, down, sib)
        cnt_ref[...] = jnp.zeros(cnt_ref.shape, F32)

    def slot(origin, c):
        return c * used + origin

    def send_up(s, origin):
        place_ = rnbuf.at[s, slot(origin, core)]
        return remote(place_, place_, up_send.at[s, origin], line_recv.at[s, origin], up)

    def send_down(s, origin):
        place_ = rnbuf.at[s, slot(origin, core)]
        return remote(place_, place_, down_send.at[s, origin], line_recv.at[s, origin], down)

    def send_sib(s, origin):
        place_ = rnbuf.at[s, slot(origin, core)]
        return remote(place_, place_, sib_send.at[s, origin], sib_recv.at[s, origin], sib)

    @pl.when(step < scenes)
    def _():
        s = step
        x = widen(tok_ref[0].astype(F32), cp)
        xhat, _ = centered(x, channels)
        low = (xhat * vec_ref[0:1] + vec_ref[1:2]).astype(BF16)
        lowf = low.astype(F32)
        for t in range(cp // LANE):
            scr[t, :n] = lowf[:, t * LANE : (t + 1) * LANE]
        total = jnp.zeros((keys, cp), F32)
        for b in range(2):
            part = [scr[t, pl.ds(b, n // 2, stride=2), :] for t in range(cp // LANE)]
            part = jnp.concatenate(part, -1).reshape(height // 2, 2, width // 2, cp)
            for a in range(2):
                total = total + dot(part[:, a].reshape(keys, cp).astype(BF16), wr_ref[2 * a + b])
        red_ref[0] = total
        rhat, _ = centered(total, channels)
        m = mask_ref[0].astype(F32)
        shape = (width // 2, width)
        near = lanes(shape) // 2 == lax.broadcasted_iota(jnp.int32, shape, 0)
        flags = []
        for i in range(height // 2):
            both = m[2 * i : 2 * i + 1] + m[2 * i + 1 : 2 * i + 2]
            flags.append(jnp.sum(jnp.where(near, both, 0.0), -1, keepdims=True))
        unc = jnp.where(jnp.concatenate(flags, 0) > 0.0, 0.0, 1.0)
        own = pack_block(rhat * vec_ref[2:3] + vec_ref[3:4], unc, keys, cp)

        @pl.when(chip < used)
        def _():
            rnbuf[s, slot(chip, core)] = own

            @pl.when(chip < chips - 1)
            def _():
                send_up(s, chip).start()

            @pl.when(chip > 0)
            def _():
                send_down(s, chip).start()

            send_sib(s, chip).start()

        qf = dot(low, wq_ref[...]) * (LOG2E * head_size**-0.5)
        ones = head_blocks(qf, lambda e: free_row(e, {0: 1.0, 1: 1.0, 2: 1.0}))
        for h in range(HEADS):
            qbuf[lax.rem(s, lag + 1), :, h * LANE : (h + 1) * LANE] = ones[h].astype(BF16)
        shape = (cnt_ref.shape[0], width)
        classes = lax.broadcasted_iota(jnp.int32, shape, 0)
        wide = lax.broadcasted_iota(jnp.int32, (LANE, width), 0)
        total = jnp.zeros(cnt_ref.shape, F32)
        for r in range(height):
            label = jnp.where(mask_ref[0, r : r + 1] > 0, label_ref[0, r : r + 1], -1)
            hot = jnp.where(label == classes, 1.0, 0.0).astype(BF16)
            pred = jnp.where(pred_ref[0, r : r + 1] == wide, 1.0, 0.0).astype(BF16)
            total = total + dot_nt(hot, pred)
        cnt_ref[...] += total

    for age in range(1, chips):
        s = step - age

        @pl.when(jnp.logical_and(s >= 0, s < scenes))
        def _(s=s, age=age):
            below = chip - age

            @pl.when(jnp.logical_and(below >= 0, below < used))
            def _():
                send_up(s, below).wait_recv()

                @pl.when(chip < chips - 1)
                def _():
                    send_up(s, below).start()

                send_sib(s, below).start()

            above = chip + age

            @pl.when(above < used)
            def _():
                send_down(s, above).wait_recv()

                @pl.when(chip > 0)
                def _():
                    send_down(s, above).start()

                send_sib(s, above).start()

    @pl.when(step >= lag)
    def _():
        s = step - lag

        for origin in range(used):
            send_sib(s, origin).wait_recv()

        free = vec_ref[3:4, cp - LANE :]
        blocks = [unpack_block(rnbuf[s, i], free, keys, cp) for i in range(2 * used)]
        rn_all = jnp.concatenate([v[0] for v in blocks], 0)
        rn_ref[0] = rn_all
        flag = jnp.concatenate([v[1] for v in blocks], 0)
        kv = dot(rn_all, wkv_ref[...])
        negative = {0: float(NEG_HI), 1: float(NEG_MID), 2: float(NEG_LO)}
        for h, block in enumerate(
            head_blocks(
                kv[:, :cp],
                lambda e: flag * free_row(e, negative) + free_row(e, {3: 1.0, 4: 1.0, 5: 1.0}),
            )
        ):
            ke_ref[0, :, h * LANE : (h + 1) * LANE] = block.astype(BF16)
        for h, block in enumerate(
            head_blocks(kv[:, cp:], lambda e: free_row(e, {0: 1.0, 1: 1.0, 2: 1.0}))
        ):
            ve_ref[0, :, h * LANE : (h + 1) * LANE] = block.astype(BF16)
        mine = lax.rem(s, lag + 1)
        count = 2 * used * keys // KEY_CHUNK
        for h in range(HEADS):
            block = slice(h * LANE, (h + 1) * LANE)
            e = ext_lane(h)
            q = qbuf[mine, :, block]
            parts = [
                dot_nt(q, ke_ref[0, j * KEY_CHUNK : (j + 1) * KEY_CHUNK, block])
                for j in range(count)
            ]
            top = functools.reduce(jnp.maximum, parts)
            top = jnp.max(top, -1, keepdims=True)
            out = jnp.zeros((n, LANE), F32)
            for j in range(count):
                p = jnp.exp2(parts[j] - top).astype(BF16)
                out = out + dot(p, ve_ref[0, j * KEY_CHUNK : (j + 1) * KEY_CHUNK, block])
            total = out[:, e : e + 1]
            oe[h] = out / total
            lse = top + jnp.log2(total)
            hi = lse.astype(BF16).astype(F32)
            mid = (lse - hi).astype(BF16).astype(F32)
            lo = lse - hi - mid
            lane = lanes((n, LANE))
            q2 = q.astype(F32)
            q2 = jnp.where(lane == e + 3, -hi, q2)
            q2 = jnp.where(lane == e + 4, -mid, q2)
            q2 = jnp.where(lane == e + 5, -lo, q2)
            q_ref[0, :, block] = q2.astype(BF16)

        tiles = []
        low_half = lanes((n, LANE)) < HALF
        for t in range(cp // LANE):
            other = oe[2 * t + 1] if 2 * t + 1 < HEADS else jnp.zeros((n, LANE), F32)
            tiles.append(jnp.where(low_half, oe[2 * t], other))
        att = jnp.concatenate(tiles, -1)
        att_ref[0] = att
        x = widen(tok2_ref[0].astype(F32), cp)
        resid = x + dot(att.astype(BF16), wp_ref[...]) + vec_ref[4:5]
        for t in range(cp // LANE):
            for r in range(height):
                for half in range(2):
                    base = r * width + half * (width // 2)
                    at = r * scenes * width + half * scenes + s
                    res_ref[t, pl.ds(at, width // 2, stride=2 * scenes), :] = resid[
                        base : base + width // 2, t * LANE : (t + 1) * LANE
                    ]

    @pl.when(step == scenes + lag - 1)
    def _():
        @pl.loop(0, scenes)
        def _(s):
            for origin in range(used):
                send_sib(s, origin).wait_send()

                @pl.when(jnp.logical_and(origin <= chip, chip < chips - 1))
                def _(origin=origin):
                    send_up(s, origin).wait_send()

                @pl.when(jnp.logical_and(origin >= chip, chip > 0))
                def _(origin=origin):
                    send_down(s, origin).wait_send()


def attend(dims, blk, used, cid, tok, mask, labels, predicted, vec, wr, wq, wkv, wp):
    scenes, height, width, channels, cp = dims
    n = height * width
    keys = n // 4
    chips = blk // 2
    lag = chips
    k = blk * keys
    live = 2 * used * keys
    he = HEADS * LANE

    def early(shape):
        return pl.BlockSpec(
            (1,) + shape, lambda t: (jnp.minimum(t, scenes - 1),) + (0,) * len(shape)
        )

    def late(shape):
        return pl.BlockSpec((1,) + shape, lambda t: (jnp.maximum(t - lag, 0),) + (0,) * len(shape))

    return pl.pallas_call(
        functools.partial(attend_kernel, dims, blk, used),
        grid=(scenes + lag,),
        in_specs=[early((n, channels))]
        + [early((height, width))] * 3
        + [late((n, channels))]
        + [whole(v.shape) for v in (vec, wr, wq, wkv, wp)],
        out_specs=[
            early((keys, cp)),
            whole((32, LANE)),
            late((n, he)),
            late((n, cp)),
            late((live, he)),
            late((live, he)),
            late((live, cp)),
            whole((cp // LANE, scenes * n + 2 * scenes, LANE)),
        ],
        out_shape=[
            jax.ShapeDtypeStruct((scenes, keys, cp), F32),
            jax.ShapeDtypeStruct((32, LANE), F32),
            jax.ShapeDtypeStruct((scenes, n, he), BF16),
            jax.ShapeDtypeStruct((scenes, n, cp), F32),
            jax.ShapeDtypeStruct((scenes, k, he), BF16),
            jax.ShapeDtypeStruct((scenes, k, he), BF16),
            jax.ShapeDtypeStruct((scenes, k, cp), BF16),
            jax.ShapeDtypeStruct((cp // LANE, scenes * n + 2 * scenes, LANE), F32),
        ],
        scratch_shapes=[
            pltpu.VMEM((cp // LANE, n + 8, LANE), F32),
            pltpu.VMEM((lag + 1, n, he), BF16),
            pltpu.VMEM((HEADS, n, LANE), F32),
            pltpu.VMEM((scenes, 2 * used, packed_rows(keys, cp), LANE), BF16),
        ]
        + [pltpu.SemaphoreType.DMA((scenes, used))] * 5,
        compiler_params=pltpu.CompilerParams(
            vmem_limit_bytes=VMEM, collective_id=cid, has_side_effects=True
        ),
    )(tok, mask, labels, predicted, tok, vec, wr, wq, wkv, wp)


def ffn_kernel(
    dims, ff, blk, ndev, res_hbm, ct_hbm, ew_hbm, sw_hbm, vec_ref, eb_ref, taps_ref, tb_ref,
    out_hbm, gres_hbm, pack_hbm, dtap_ref, dtb_ref, dvec_ref,
    we_ref, ws_ref, dwe_ref, dwst, packed, res_ref, ct_ref, cn, cnt, ctt, ctx, oacc, gacc, hid, gm, halo, act, back, tapacc, out_stage, gres_stage,
    weight_sem, pack_sem, res_sem, ct_sem, out_sem, gres_sem, cn_send, cn_recv, gm_send, gm_recv,
):
    scenes, height, width, channels, cp = dims
    n = height * width
    rw = scenes * width
    lt = cp // LANE
    fc = FF_CHUNK
    nchunk = ff // fc
    cols = width // 2
    pair = 2 * scenes
    group = GROUP if cols % GROUP == 0 else cols
    me = lax.axis_index("blk")
    has_left = me > 0
    has_right = me < blk - 1
    left, right = {"blk": me - 1}, {"blk": me + 1}
    MESH = pl.DeviceIdType.MESH

    def res_copy(r):
        rows = pl.ds(pl.multiple_of(r * rw, rw), rw)
        return pltpu.make_async_copy(res_hbm.at[:, rows, :], res_ref.at[:, rows, :], res_sem.at[r])

    def ct_copy(s):
        return pltpu.make_async_copy(ct_hbm.at[s], ct_ref.at[s], ct_sem.at[s])

    ew_copy = pltpu.make_async_copy(ew_hbm, we_ref.at[:channels, :], weight_sem.at[0])
    sw_copy = pltpu.make_async_copy(sw_hbm, ws_ref.at[:channels, :], weight_sem.at[1])
    for r in range(height):
        res_copy(r).start()
    for s in range(scenes):
        ct_copy(s).start()
    ew_copy.start()
    sw_copy.start()
    bias_rows = eb_ref.shape[0]
    we_ref[channels : channels + bias_rows, :] = eb_ref[...]
    if channels + bias_rows < cp:
        we_ref[channels + bias_rows :, :] = jnp.zeros((cp - channels - bias_rows, ff), BF16)
    ws_ref[channels:, :] = jnp.zeros((cp - channels, ff), BF16)

    barrier = pltpu.get_barrier_semaphore()

    @pl.when(has_left)
    def _():
        pl.semaphore_signal(barrier, inc=1, device_id=left, device_id_type=MESH)

    @pl.when(has_right)
    def _():
        pl.semaphore_signal(barrier, inc=1, device_id=right, device_id_type=MESH)

    pl.semaphore_wait(barrier, has_left.astype(jnp.int32) + has_right.astype(jnp.int32))

    def row(r, size=rw):
        return pl.ds(pl.multiple_of(r * rw, rw), size)

    g2, b2 = vec_ref[5:6], vec_ref[6:7]

    def load3(ref, r):
        return jnp.concatenate([ref[t, row(r), :] for t in range(lt)], -1)

    def store3(ref, r, value):
        for t in range(lt):
            ref[t, row(r), :] = value[:, t * LANE : (t + 1) * LANE]

    @pl.loop(0, height)
    def _(r):
        res_copy(r).wait()
        x = load3(res_ref, r)
        xhat, rstd = centered(x, channels)
        c = (xhat * g2 + b2).astype(BF16)
        cn[row(r + 1), :] = c
        cnt[:, row(r)] = c.T
        store3(oacc, r, x + vec_ref[7:8])
        store3(res_ref, r, jnp.where(lanes(xhat.shape) == channels, rstd, xhat))

    def cn_copy(up):
        return pltpu.make_async_remote_copy(
            src_ref=cn.at[row(1 if up else height), :],
            dst_ref=cn.at[row(height + 1 if up else 0), :],
            send_sem=cn_send.at[0 if up else 1],
            recv_sem=cn_recv.at[0 if up else 1],
            device_id=left if up else right,
            device_id_type=MESH,
        )

    @pl.when(has_left)
    def _():
        cn_copy(True).start()

    @pl.when(has_right)
    def _():
        cn_copy(False).start()

    @pl.loop(0, scenes)
    def _(s):
        ct_copy(s).wait()
        c = widen(ct_ref[s].astype(F32), cp)
        for t in range(lt):
            for r in range(height):
                for half in range(2):
                    base = r * width + half * cols
                    gacc[t, pl.ds(r * rw + half * scenes + s, cols, stride=pair), :] = c[
                        base : base + cols, t * LANE : (t + 1) * LANE
                    ]

    dvec_ref[...] = jnp.zeros(dvec_ref.shape, F32)

    @pl.loop(0, height)
    def _(r):
        c = load3(gacc, r)
        dvec_ref[2:3] += jnp.sum(c, 0, keepdims=True)
        low = c.astype(BF16)
        ctt[row(r), :] = low
        ctx[:, row(r)] = low.T
        store3(gacc, r, jnp.zeros((rw, cp), F32))

    ew_copy.wait()
    sw_copy.wait()
    dwe_ref[...] = jnp.zeros(dwe_ref.shape, F32)
    dwst[...] = jnp.zeros(dwst.shape, F32)

    @pl.when(has_left)
    def _():
        cn_copy(False).wait_recv()

    @pl.when(jnp.logical_not(has_left))
    def _():
        cn[row(0), :] = jnp.zeros((rw, cp), BF16)

    @pl.when(has_right)
    def _():
        cn_copy(True).wait_recv()

    @pl.when(jnp.logical_not(has_right))
    def _():
        cn[row(height + 1), :] = jnp.zeros((rw, cp), BF16)

    def put(ref, slot, r, value):
        v = value.reshape(cols, pair, fc)
        z = jnp.zeros((scenes, fc), F32)
        ref[slot, r, 1 : cols + 1] = v.astype(BF16)
        ref[slot, r, 0] = jnp.concatenate([z, v[cols - 1, :scenes]], 0).astype(BF16)
        ref[slot, r, cols + 1] = jnp.concatenate([v[0, scenes:], z], 0).astype(BF16)

    def gm_copy(k, slot, up):
        return pltpu.make_async_remote_copy(
            src_ref=gm.at[slot, 1 if up else height],
            dst_ref=halo.at[k, 1 if up else 0],
            send_sem=gm_send.at[k, 0 if up else 1],
            recv_sem=gm_recv.at[k, 0 if up else 1],
            device_id=left if up else right,
            device_id_type=MESH,
        )

    def phase_a(k, slot):
        span = pl.ds(pl.multiple_of(k * fc, fc), fc)
        taps = [
            taps_ref[pl.ds(i, 1), span].astype(BF16).reshape(1, 1, fc) for i in range(9)
        ]
        bias = tb_ref[:, span]

        def hidden(r):
            put(hid, slot, r, dot(cn[r * rw : (r + 1) * rw, :], we_ref[:, span]))

        def products(r):
            active = act[r * rw : (r + 1) * rw, :]
            o = dot_nt(active, ws_ref[:, span])
            for t in range(lt):
                oacc[t, r * rw : (r + 1) * rw, :] += o[:, t * LANE : (t + 1) * LANE]
            dwst[:, span] += dot(ctx[:, r * rw : (r + 1) * rw], active)

        hidden(0)
        hidden(1)
        hidden(2)
        sums = jnp.zeros((8, fc), F32)
        for r in range(height):
            back[...] = dot(ctt[r * rw : (r + 1) * rw, :], ws_ref[:, span])
            if r:
                products(r - 1)
            for g in range(0, cols, group):
                acc = None
                for a in range(3):
                    line = hid[slot, r + a, g : g + group + 2]
                    for b in range(3):
                        term = line[b : b + group] * taps[3 * a + b]
                        acc = term if acc is None else acc + term
                mixed = acc.astype(F32).reshape(group * pair, fc) + bias
                arg = mixed * 0.7071067811865476
                phi = 0.5 + 0.5 * lax.erf(arg)
                dens = jnp.exp2(arg * arg * -LOG2E) * mixed
                act[r * rw + g * pair : r * rw + (g + group) * pair, :] = (mixed * phi).astype(BF16)
                slope = phi + dens * 0.3989422804014327
                grad = back[g * pair : (g + group) * pair, :] * slope
                sums = sums + jnp.sum(grad.reshape(group * pair // 8, 8, fc), 0)
                v = grad.reshape(group, pair, fc)
                gm[slot, r + 1, g + 1 : g + group + 1] = v.astype(BF16)
                z = jnp.zeros((scenes, fc), F32)
                if g == 0:
                    gm[slot, r + 1, cols + 1] = jnp.concatenate([v[0, scenes:], z], 0).astype(BF16)
                if g + group == cols:
                    gm[slot, r + 1, 0] = jnp.concatenate([z, v[group - 1, :scenes]], 0).astype(BF16)
            if r + 3 < height + 2:
                hidden(r + 3)
        products(height - 1)
        dtb_ref[:, span] = sums

        @pl.when(has_left)
        def _():
            gm_copy(k, slot, True).start()

        @pl.when(has_right)
        def _():
            gm_copy(k, slot, False).start()

    def phase_b(k, slot):
        span = pl.ds(pl.multiple_of(k * fc, fc), fc)

        @pl.when(has_left)
        def _():
            gm_copy(k, slot, False).wait_recv()
            gm[slot, 0] = halo[k, 0]

        @pl.when(jnp.logical_not(has_left))
        def _():
            gm[slot, 0] = jnp.zeros((cols + 2, pair, fc), BF16)

        @pl.when(has_right)
        def _():
            gm_copy(k, slot, True).wait_recv()
            gm[slot, height + 1] = halo[k, 1]

        @pl.when(jnp.logical_not(has_right))
        def _():
            gm[slot, height + 1] = jnp.zeros((cols + 2, pair, fc), BF16)

        taps = [
            taps_ref[pl.ds(i, 1), span].astype(BF16).reshape(1, 1, fc) for i in range(9)
        ]
        tapacc[...] = jnp.zeros(tapacc.shape, F32)

        def products(r):
            low = act[r * rw : (r + 1) * rw, :]
            dwe_ref[:, span] += dot(cnt[:, r * rw : (r + 1) * rw], low)
            g = dot_nt(low, we_ref[:, span])
            for t in range(lt):
                gacc[t, r * rw : (r + 1) * rw, :] += g[:, t * LANE : (t + 1) * LANE]

        for r in range(height):
            tapsum = [None] * 9
            for g in range(0, cols, group):
                acc = None
                own = hid[slot, r + 1, g + 1 : g + group + 1]
                for a in range(3):
                    line = gm[slot, r + 2 - a, g : g + group + 2]
                    for b in range(3):
                        window = line[2 - b : 2 - b + group]
                        term = window * taps[3 * a + b]
                        acc = term if acc is None else acc + term
                        prod = own * window
                        while prod.shape[0] > 1:
                            cut = prod.shape[0] // 2
                            prod = prod[:cut] + prod[cut:]
                        i = 3 * a + b
                        tapsum[i] = prod[0] if tapsum[i] is None else tapsum[i] + prod[0]
                act[r * rw + g * pair : r * rw + (g + group) * pair, :] = acc.reshape(group * pair, fc)
            for i in range(9):
                tapacc[i] += tapsum[i].astype(F32)
        for r in range(height):
            products(r)

        for tap in range(9):
            dtap_ref[pl.ds(tap, 1), span] = jnp.sum(tapacc[tap], 0, keepdims=True)

        @pl.when(has_left)
        def _():
            gm_copy(k, slot, True).wait_send()

        @pl.when(has_right)
        def _():
            gm_copy(k, slot, False).wait_send()

    @pl.loop(0, nchunk + 1)
    def _(k):
        slot = lax.rem(k, 2)

        @pl.when(k < nchunk)
        def _():
            phase_a(k, slot)

        @pl.when(k > 0)
        def _():
            phase_b(k - 1, 1 - slot)

    @pl.when(has_left)
    def _():
        cn_copy(True).wait_send()

    @pl.when(has_right)
    def _():
        cn_copy(False).wait_send()

    plan, filled, _ = ffn_plan(channels, ff, ndev)
    for name, ref in (("we", dwe_ref), ("ws", dwst)):
        at, rows, slabs = plan[name]
        for t in range(slabs):
            packed[at + t * rows : at + (t + 1) * rows, :] = ref[
                :rows, t * LANE : (t + 1) * LANE
            ].astype(BF16)
    if filled < packed.shape[0]:
        packed[filled:, :] = jnp.zeros((packed.shape[0] - filled, LANE), BF16)
    pack_copy = pltpu.make_async_copy(packed, pack_hbm, pack_sem.at[0])
    pack_copy.start()

    def gather(ref, s):
        rows = []
        for r in range(height):
            for half in range(2):
                rows.append(
                    jnp.concatenate(
                        [
                            ref[t, pl.ds(r * rw + half * scenes + s, cols, stride=pair), :]
                            for t in range(lt)
                        ],
                        -1,
                    )
                )
        return jnp.concatenate(rows, 0)[:, :channels]

    def out_copy(s, slot):
        return pltpu.make_async_copy(out_stage.at[slot], out_hbm.at[s], out_sem.at[slot])

    def gres_copy(s, slot):
        return pltpu.make_async_copy(gres_stage.at[slot], gres_hbm.at[s], gres_sem.at[slot])

    @pl.loop(0, scenes)
    def _(s):
        slot = lax.rem(s, 2)

        @pl.when(s >= 2)
        def _():
            out_copy(s - 2, slot).wait()

        out_stage[slot] = gather(oacc, s).astype(BF16)
        out_copy(s, slot).start()

    @pl.loop(0, height)
    def _(r):
        kept = load3(res_ref, r)
        rstd = kept[:, channels : channels + 1]
        xhat = inside(kept, channels)
        upstream = load3(gacc, r)
        dvec_ref[0:1] += jnp.sum(upstream * xhat, 0, keepdims=True)
        dvec_ref[1:2] += jnp.sum(upstream, 0, keepdims=True)
        g = ctt[row(r), :].astype(F32) + norm_back(upstream, g2, xhat, rstd, channels)
        store3(gacc, r, g)

    @pl.loop(0, scenes)
    def _(s):
        slot = lax.rem(s, 2)

        @pl.when(s >= 2)
        def _():
            gres_copy(s - 2, slot).wait()

        gres_stage[slot] = gather(gacc, s)
        gres_copy(s, slot).start()

    for s in range(scenes - 2, scenes):
        out_copy(s, s % 2).wait()
        gres_copy(s, s % 2).wait()
    pack_copy.wait()


def ffn(dims, blk, ndev, res, ct, ew, sw, vec, eb, taps, tb):
    scenes, height, width, channels, cp = dims
    n = height * width
    total = scenes * n
    rw = scenes * width
    ff = sw.shape[1]
    lt = cp // LANE
    nchunk = ff // FF_CHUNK
    strip = (width // 2 + 2, 2 * scenes, FF_CHUNK)
    pack_rows = sum(ffn_plan(channels, ff, ndev)[2])
    vm = pl.BlockSpec(memory_space=pltpu.VMEM)
    hbm = pl.BlockSpec(memory_space=pl.ANY)
    return pl.pallas_call(
        functools.partial(ffn_kernel, dims, ff, blk, ndev),
        in_specs=[hbm] * 4 + [vm] * 4,
        out_specs=[hbm, hbm, hbm] + [vm] * 3,
        out_shape=[
            jax.ShapeDtypeStruct((scenes, n, channels), BF16),
            jax.ShapeDtypeStruct((scenes, n, channels), F32),
            jax.ShapeDtypeStruct((pack_rows, LANE), BF16),
            jax.ShapeDtypeStruct((9, ff), F32),
            jax.ShapeDtypeStruct((8, ff), F32),
            jax.ShapeDtypeStruct((8, cp), F32),
        ],
        scratch_shapes=[
            pltpu.VMEM((cp, ff), BF16),
            pltpu.VMEM((cp, ff), BF16),
            pltpu.VMEM((cp, ff), F32),
            pltpu.VMEM((cp, ff), F32),
            pltpu.VMEM((pack_rows, LANE), BF16),
            pltpu.VMEM((lt, total, LANE), F32),
            pltpu.VMEM((scenes, n, channels), BF16),
            pltpu.VMEM((total + 2 * rw, cp), BF16),
            pltpu.VMEM((cp, total), BF16),
            pltpu.VMEM((total, cp), BF16),
            pltpu.VMEM((cp, total), BF16),
            pltpu.VMEM((lt, total + 2 * scenes, LANE), F32),
            pltpu.VMEM((lt, total + 2 * scenes, LANE), F32),
            pltpu.VMEM((2, height + 2) + strip, BF16),
            pltpu.VMEM((2, height + 2) + strip, BF16),
            pltpu.VMEM((nchunk, 2) + strip, BF16),
            pltpu.VMEM((total, FF_CHUNK), BF16),
            pltpu.VMEM((rw, FF_CHUNK), F32),
            pltpu.VMEM((9, 2 * scenes, FF_CHUNK), F32),
            pltpu.VMEM((2, n, channels), BF16),
            pltpu.VMEM((2, n, channels), F32),
            pltpu.SemaphoreType.DMA((2,)),
            pltpu.SemaphoreType.DMA((1,)),
            pltpu.SemaphoreType.DMA((height,)),
            pltpu.SemaphoreType.DMA((scenes,)),
            pltpu.SemaphoreType.DMA((2,)),
            pltpu.SemaphoreType.DMA((2,)),
            pltpu.SemaphoreType.DMA((2,)),
            pltpu.SemaphoreType.DMA((2,)),
            pltpu.SemaphoreType.DMA((nchunk, 2)),
            pltpu.SemaphoreType.DMA((nchunk, 2)),
        ],
        compiler_params=pltpu.CompilerParams(
            vmem_limit_bytes=VMEM, collective_id=0, has_side_effects=True
        ),
    )(res, ct, ew, sw, vec, eb, taps, tb)


def attback_kernel(
    dims, ff, ndp, blk, used, q_ref, att_ref, gres_ref, ke_ref, ve_ref, rn_ref, tok_ref, gres2_ref,
    red_ref, vec_ref, wp_ref, wkv_ref, wq_ref, wr_ref, dtap, dtb, dvec2, cnt, first_hbm,
    ig_ref, sum_hbm, mid_hbm, rest_hbm, small_hbm,
    dwqt, dwrt, dwp_ref, dwkv_ref, dbp_ref, dvec_ref, ge, dqt, gqt_ref, grn_ref, scr, gscr, own, acc, sib_land, up_land, down_land,
    gkv_ref, work, land, done, mid_work, mid_land, mid_done, rest_work, rest_land, rest_done, small_work, small_land, small_done,
    sib_send, sib_recv, up_send, up_recv, down_send, down_recv, sum_send, sum_recv,
    mid_send, mid_recv, rest_send, rest_recv, sum_sem,
):
    scenes, height, width, channels, cp = dims
    n = height * width
    keys = n // 4
    chips = blk // 2
    lt = cp // LANE
    head_size = channels // HEADS
    step = pl.program_id(0)
    chip, core, up, down, sib = place(blk)
    count = 2 * used * keys // KEY_CHUNK
    steps = scenes + chips
    together = -(-scenes // chips)
    ndev = ndp * blk
    order = orders_of(ndp, blk)[0]
    parts = three_parts(work, land, done, ffn_plan(channels, ff, ndev)[2], [order] * 3)
    sums = Sums(parts, sum_send, sum_recv)
    each = -(-(sums.ops + 1) // (steps - 1))
    mid_plan, mid_used, mid_sizes = middle_plan(channels, ndev)
    mid = Sums(
        three_parts(mid_work, mid_land, mid_done, mid_sizes, [order] * 3), mid_send, mid_recv
    )
    early = min(chips, mid.ops)

    def put(buf, plan, name, value):
        at, rows, slabs = plan[name]
        for t in range(slabs):
            buf[at + t * rows : at + (t + 1) * rows, :] = value(t, rows).astype(BF16)

    def cut_of(value):
        return lambda t, rows: value[:rows, t * LANE : (t + 1) * LANE]

    @pl.when(step == 0)
    def _():
        load = pltpu.make_async_copy(first_hbm, work, sum_sem.at[0])
        load.start()
        barrier = pltpu.get_barrier_semaphore()
        peers = peers_of(order)
        for peer in peers:
            pl.semaphore_signal(barrier, inc=1, device_id=peer, device_id_type=pl.DeviceIdType.MESH)
        pl.semaphore_wait(barrier, len(peers))
        load.wait()
        for k in range(each):
            sums.advance(k)
        dwqt[...] = jnp.zeros(dwqt.shape, F32)
        dwrt[...] = jnp.zeros(dwrt.shape, F32)
        dvec_ref[...] = jnp.zeros(dvec_ref.shape, F32)
        dwp_ref[...] = jnp.zeros(dwp_ref.shape, F32)
        dwkv_ref[...] = jnp.zeros(dwkv_ref.shape, F32)
        dbp_ref[...] = jnp.zeros(dbp_ref.shape, F32)

    def to_sib(s, target):
        return remote(
            own.at[lax.rem(s, 2), 1 - core, target], sib_land.at[s, target], sib_send.at[s, target],
            sib_recv.at[s, target], sib,
        )

    def to_up(s, target):
        return remote(
            acc.at[s, target], up_land.at[s, target], up_send.at[s, target], up_recv.at[s, target], up
        )

    def to_down(s, target):
        return remote(
            acc.at[s, target], down_land.at[s, target], down_send.at[s, target],
            down_recv.at[s, target], down,
        )

    def plus(a, b):
        return (a.astype(F32) + b.astype(F32)).astype(BF16)

    def chunk(j):
        s = step
        per = KEY_CHUNK // keys
        span = slice(j * KEY_CHUNK, (j + 1) * KEY_CHUNK)
        dks, dvs = [], []
        for h in range(HEADS):
            block = slice(h * LANE, (h + 1) * LANE)
            k, v = ke_ref[0, span, block], ve_ref[0, span, block]
            q, g = q_ref[0, :, block], ge[:, block]
            p = jnp.exp2(dot_nt(k, q))
            gs = (p * dot_nt(v, g)).astype(BF16)
            dvs.append(dot(p.astype(BF16), g))
            dks.append(dot(gs, q))
            dqt[block, :] += dot_tn(k, gs)
        low_half = lanes((KEY_CHUNK, LANE)) < HALF
        tiles = []
        for group, scale in ((dks, LN2), (dvs, 1.0)):
            for t in range(lt):
                other = (
                    group[2 * t + 1] if 2 * t + 1 < HEADS else jnp.zeros((KEY_CHUNK, LANE), F32)
                )
                tiles.append((jnp.where(low_half, group[2 * t], other) * scale).astype(BF16))
        gkv = jnp.concatenate(tiles, -1)
        grn = dot_nt(gkv, wkv_ref[...]).astype(BF16)
        for i in range(per):
            at = j * per + i
            own[lax.rem(s, 2), at // used, at % used] = grn[i * keys : (i + 1) * keys]

            @pl.when(core != at // used)
            def _(at=at):
                to_sib(s, at % used).start()

        gkv_ref[span, :] = gkv

    @pl.when(step < scenes)
    def _():
        s = step
        gb = widen(gres_ref[0], cp).astype(BF16)
        dbp_ref[...] += jnp.sum(gb.astype(F32).reshape(n // 8, 8, cp), 0)
        att = att_ref[0]
        dwp_ref[...] += dot(att.astype(BF16).T, gb)
        gatt = head_blocks(dot_nt(gb, wp_ref[...]), lambda e: 0.0)
        lane = lanes((n, LANE))
        for h in range(HEADS):
            e = ext_lane(h)
            g = gatt[h].astype(BF16).astype(F32)
            o = att[:, (h // 2) * LANE : (h // 2 + 1) * LANE]
            inner = jnp.sum(g * o, -1, keepdims=True)
            hi = inner.astype(BF16).astype(F32)
            g = jnp.where(lane == e, -hi, g)
            g = jnp.where(lane == e + 1, hi - inner, g)
            ge[:, h * LANE : (h + 1) * LANE] = g.astype(BF16)
        dqt[...] = jnp.zeros(dqt.shape, F32)
        chunk(0)

    s1 = step - 1

    @pl.when(jnp.logical_and(s1 >= 0, s1 < scenes))
    def _():
        for target in range(used):
            to_sib(s1, target).wait()
            acc[s1, target] = plus(own[lax.rem(s1, 2), core, target], sib_land[s1, target])

    s_up = step - 1 - chip

    @pl.when(jnp.logical_and(s_up >= 0, s_up < scenes))
    def _():
        for target in reversed(range(1, used)):

            @pl.when(target > chip)
            def _(target=target):
                @pl.when(chip > 0)
                def _():
                    to_up(s_up, target).wait_recv()
                    acc[s_up, target] = plus(acc[s_up, target], up_land[s_up, target])

                to_up(s_up, target).start()

    s_down = step - chips + chip

    @pl.when(jnp.logical_and(s_down >= 0, s_down < scenes))
    def _():
        for target in range(used):

            @pl.when(target < chip)
            def _(target=target):
                @pl.when(chip < chips - 1)
                def _():
                    to_down(s_down, target).wait_recv()
                    acc[s_down, target] = plus(acc[s_down, target], down_land[s_down, target])

                to_down(s_down, target).start()

    s_end = step - chips

    @pl.when(s_end >= 0)
    def _():
        @pl.when(chip < used)
        def _():
            grn_ref[s_end] = acc[s_end, chip].astype(F32)

            @pl.when(chip > 0)
            def _():
                to_up(s_end, chip).wait_recv()
                grn_ref[s_end] += up_land[s_end, chip].astype(F32)

            @pl.when(chip < chips - 1)
            def _():
                to_down(s_end, chip).wait_recv()
                grn_ref[s_end] += down_land[s_end, chip].astype(F32)

        @pl.when(chip >= used)
        def _():
            grn_ref[s_end] = jnp.zeros((keys, cp), F32)

    for t in range(1, steps - 1):

        @pl.when(step == t)
        def _(t=t):
            for k in range(t * each, min((t + 1) * each, sums.ops + 1)):
                sums.advance(k)
            if t * each <= sums.ops < (t + 1) * each:
                pltpu.make_async_copy(done, sum_hbm, sum_sem.at[0]).start()

    def tail(base):
        gred, low, hats = [], [], []
        for i in range(together):
            rhat, rstd = centered(red_ref[i], channels)
            upstream = inside(grn_ref[base + i], channels)
            dvec_ref[0:1] += jnp.sum(upstream * rhat, 0, keepdims=True)
            dvec_ref[1:2] += jnp.sum(upstream, 0, keepdims=True)
            g = norm_back(upstream, vec_ref[2:3], rhat, rstd, channels)
            gred.append(inside(g, channels).astype(BF16))
            dvec_ref[2:3] += jnp.sum(gred[i].astype(F32), 0, keepdims=True)
            x = widen(tok_ref[i].astype(F32), cp)
            xhat, xstd = centered(x, channels)
            hats.append((xhat, xstd))
            low.append((xhat * vec_ref[0:1] + vec_ref[1:2]).astype(BF16))
            lowf = low[i].astype(F32)
            for t in range(lt):
                scr[i, t, :n] = lowf[:, t * LANE : (t + 1) * LANE]
        gred = jnp.concatenate(gred, 0)
        gred_t = gred.T
        for b in range(2):
            patches = [[], []]
            for i in range(together):
                part = [scr[i, t, pl.ds(b, n // 2, stride=2), :] for t in range(lt)]
                part = jnp.concatenate(part, -1).reshape(height // 2, 2, width // 2, cp)
                for a in range(2):
                    patches[a].append(part[:, a].reshape(keys, cp))
            for a in range(2):
                ab = 2 * a + b
                dwrt[ab] += dot(gred_t, jnp.concatenate(patches[a], 0).astype(BF16))
                back = dot_nt(gred, wr_ref[ab])
                for i in range(together):
                    for t in range(lt):
                        for r in range(height // 2):
                            at = i * keys + r * (width // 2)
                            gscr[i, t, pl.ds((2 * r + a) * width + b, width // 2, stride=2), :] = back[
                                at : at + width // 2, t * LANE : (t + 1) * LANE
                            ]
        for i in range(together):
            gqt = gqt_ref[base + i]
            xhat, xstd = hats[i]
            dwqt[...] += dot(gqt, low[i])
            gn = widen(dot_nt(gqt.T, wq_ref[...]), cp)
            gn = gn + jnp.concatenate([gscr[i, t, :n] for t in range(lt)], -1)
            dvec_ref[3:4] += jnp.sum(gn * xhat, 0, keepdims=True)
            dvec_ref[4:5] += jnp.sum(gn, 0, keepdims=True)
            gx = norm_back(gn, vec_ref[0:1], xhat, xstd, channels)
            ig_ref[i] = gres2_ref[i] + gx[:, :channels]

    @pl.when(step == scenes)
    def _():
        joined = jnp.concatenate([dwkv_ref[:, :channels], dwkv_ref[:, cp : cp + channels]], -1)
        put(mid_work, mid_plan, "wkv", cut_of(joined))
        put(mid_work, mid_plan, "wp", cut_of(dwp_ref))
        if mid_used < mid_work.shape[0]:
            mid_work[mid_used:, :] = jnp.zeros((mid_work.shape[0] - mid_used, LANE), BF16)

    for t in range(early):

        @pl.when(step == scenes + t)
        def _(t=t):
            mid.advance(t)

    @pl.when(step >= scenes)
    def _():
        tail((step - scenes) * together)

    @pl.when(step < scenes)
    def _():
        s = step
        for j in range(1, count):
            chunk(j)
        dwkv_ref[...] += dot(rn_ref[0].T, gkv_ref[...])
        for h in range(HEADS):
            base = h * LANE + (0 if h % 2 == 0 else HALF)
            gqt_ref[s, h * HALF : (h + 1) * HALF] = (
                dqt[base : base + HALF, :] * head_size**-0.5
            ).astype(BF16)

    @pl.when(step == steps - 1)
    def _():
        plan, filled, sizes = rest_plan(channels, ndev)
        splan, srows = small_plan(channels, ff, ndev)
        full = channels // LANE

        joined = jnp.concatenate([dwrt[ab, :channels, :channels] for ab in range(4)], -1)
        put(rest_work, plan, "wr", cut_of(joined))
        put(rest_work, plan, "wq", cut_of(dwqt))
        last = pltpu.roll(dwqt[:, full * LANE :], HALF, 1)
        put(
            rest_work,
            plan,
            "halves",
            lambda t, rows: jnp.where(
                lanes((1, LANE)) < HALF, dwp_ref[:rows, full * LANE :], last
            ),
        )
        if filled < rest_work.shape[0]:
            rest_work[filled:, :] = jnp.zeros((rest_work.shape[0] - filled, LANE), BF16)
        small_work[...] = jnp.zeros(small_work.shape, F32)
        at, rows, slabs = splan["tap"]
        db = jnp.sum(dtb[...], 0, keepdims=True)
        for t in range(slabs):
            cut = slice(t * LANE, (t + 1) * LANE)
            small_work[at + t * rows : at + t * rows + 9, :] = dtap[:, cut]
            small_work[at + t * rows + 9 : at + t * rows + 10, :] = db[:, cut]
        at, rows, slabs = splan["vec"]
        pb = jnp.sum(dbp_ref[...], 0, keepdims=True)
        qb = widen(dwqt[:, full * LANE :].T[HALF : HALF + 1], cp)
        for t in range(slabs):
            cut = slice(t * LANE, (t + 1) * LANE)
            low = at + t * rows
            small_work[low : low + 3, :] = dvec2[0:3, cut]
            small_work[low + 3 : low + 8, :] = dvec_ref[0:5, cut]
            small_work[low + 8 : low + 9, :] = pb[:, cut]
            small_work[low + 9 : low + 10, :] = qb[:, cut]
        at, rows, _ = splan["count"]
        small_work[at : at + rows, :] = cnt[...]

        orders = orders_of(ndp, blk)
        rest_parts = three_parts(rest_work, rest_land, rest_done, sizes, orders)
        rest_parts.append((small_work, small_land, small_done, 0, srows, orders[0]))
        rest = Sums(rest_parts, rest_send, rest_recv)
        for k in range(max(rest.ops, mid.ops - early) + 1):
            if k <= rest.ops:
                rest.advance(k)
            if k + early <= mid.ops:
                mid.advance(k + early)
        leave = [
            pltpu.make_async_copy(rest_done, rest_hbm, sum_sem.at[1]),
            pltpu.make_async_copy(small_done, small_hbm, sum_sem.at[2]),
            pltpu.make_async_copy(mid_done, mid_hbm, sum_sem.at[3]),
        ]
        for copy in leave:
            copy.start()
        for copy in leave:
            copy.wait()
        pltpu.make_async_copy(done, sum_hbm, sum_sem.at[0]).wait()

        @pl.loop(0, scenes)
        def _(s):
            for target in range(used):

                @pl.when(target > chip)
                def _(target=target):
                    to_up(s, target).wait_send()

                @pl.when(target < chip)
                def _(target=target):
                    to_down(s, target).wait_send()


def attback(
    dims, ff, ndp, blk, used, cid, q, att, gres, ke, ve, rn, tok, red, vec, wp, wkv, wq, wr,
    dtap, dtb, dvec2, cnt, first
):
    scenes, height, width, channels, cp = dims
    n = height * width
    keys = n // 4
    chips = blk // 2
    lt = cp // LANE
    live = 2 * used * keys
    he = HEADS * LANE
    together = -(-scenes // chips)
    assert scenes == together * chips
    mid_rows = sum(middle_plan(channels, ndp * blk)[2])
    rest_rows = sum(rest_plan(channels, ndp * blk)[2])
    small_rows = small_plan(channels, ff, ndp * blk)[1]
    ops = 2 * len(orders_of(ndp, blk)[0])

    def early(shape):
        return pl.BlockSpec(
            (1,) + shape, lambda t: (jnp.minimum(t, scenes - 1),) + (0,) * len(shape)
        )

    def late(shape):
        return pl.BlockSpec(
            (together,) + shape, lambda t: (jnp.maximum(t - scenes, 0),) + (0,) * len(shape)
        )

    land = (scenes, used, keys, cp)
    hbm = pl.BlockSpec(memory_space=pl.ANY)
    vm = pl.BlockSpec(memory_space=pltpu.VMEM)
    return pl.pallas_call(
        functools.partial(attback_kernel, dims, ff, ndp, blk, used),
        grid=(scenes + chips,),
        in_specs=[
            early((n, he)),
            early((n, cp)),
            early((n, channels)),
            early((live, he)),
            early((live, he)),
            early((live, cp)),
            late((n, channels)),
            late((n, channels)),
            late((keys, cp)),
        ]
        + [vm] * 9
        + [hbm],
        out_specs=[late((n, channels))] + [hbm] * 4,
        out_shape=[
            jax.ShapeDtypeStruct((scenes, n, channels), F32),
            jax.ShapeDtypeStruct(first.shape, BF16),
            jax.ShapeDtypeStruct((mid_rows, LANE), BF16),
            jax.ShapeDtypeStruct((rest_rows, LANE), BF16),
            jax.ShapeDtypeStruct((small_rows, LANE), F32),
        ],
        scratch_shapes=[
            pltpu.VMEM((channels, cp), F32),
            pltpu.VMEM((4, cp, cp), F32),
            pltpu.VMEM((cp, cp), F32),
            pltpu.VMEM((cp, 2 * cp), F32),
            pltpu.VMEM((8, cp), F32),
            pltpu.VMEM((8, cp), F32),
            pltpu.VMEM((n, he), BF16),
            pltpu.VMEM((he, n), F32),
            pltpu.VMEM((scenes, channels, n), BF16),
            pltpu.VMEM((scenes, keys, cp), F32),
            pltpu.VMEM((together, lt, n + 8, LANE), F32),
            pltpu.VMEM((together, lt, n + 8, LANE), F32),
            pltpu.VMEM((2, 2, used, keys, cp), BF16),
        ]
        + [pltpu.VMEM(land, BF16)] * 4
        + [pltpu.VMEM((live, 2 * cp), BF16)]
        + [pltpu.VMEM(first.shape, BF16)] * 3
        + [pltpu.VMEM((mid_rows, LANE), BF16)] * 3
        + [pltpu.VMEM((rest_rows, LANE), BF16)] * 3
        + [pltpu.VMEM((small_rows, LANE), F32)] * 3
        + [pltpu.SemaphoreType.DMA((scenes, used))] * 6
        + [pltpu.SemaphoreType.DMA((3, ops, widest(ndp, blk)))] * 4
        + [pltpu.SemaphoreType.DMA((4, ops, widest(ndp, blk)))] * 2
        + [pltpu.SemaphoreType.DMA((4,))],
        compiler_params=pltpu.CompilerParams(
            vmem_limit_bytes=VMEM, collective_id=cid, has_side_effects=True
        ),
    )(q, att, gres, ke, ve, rn, tok, gres, red, vec, wp, wkv, wq, wr, dtap, dtb, dvec2, cnt, first)


def unpack_kernel(channels, ff, ndev, out_in, ig_in, first_in, middle_in, packed_in, small, *refs):
    cp = up_to(channels, LANE)
    splan, _ = small_plan(channels, ff, ndev)
    names = (
        ("out", "ig", "g1", "b1", "wq", "qb", "wr", "rb", "rg", "rbn", "wkv", "vb")
        + ("wp", "pb", "g2", "b2", "we", "eb", "dt", "db", "ws", "sb", "cm")
    )
    outs = dict(zip(names, refs[: len(names)]))
    out_hold, ig_hold, first, middle, packed, we, ws, wr, wkv, in_sem, out_sem, sem = refs[len(names) :]
    lt = cp // LANE
    full = channels // LANE
    loads = [
        pltpu.make_async_copy(first_in, first, sem.at[0]),
        pltpu.make_async_copy(middle_in, middle, sem.at[1]),
        pltpu.make_async_copy(packed_in, packed, sem.at[2]),
    ]
    ins, moves = [], []
    pairs = ((out_in, out_hold, outs["out"]), (ig_in, ig_hold, outs["ig"]))
    for k, (src, hold, dst) in enumerate(pairs):
        for s in range(src.shape[0]):
            ins.append(pltpu.make_async_copy(src.at[s], hold.at[s], in_sem.at[k, s]))
            moves.append(pltpu.make_async_copy(hold.at[s], dst.at[s], out_sem.at[k, s]))
    for copy in loads + ins:
        copy.start()
    plans = (
        (first, ffn_plan(channels, ff, ndev)[0]), (middle, middle_plan(channels, ndev)[0]),
        (packed, rest_plan(channels, ndev)[0]),
    )
    stores = [
        pltpu.make_async_copy(src, outs[name], sem.at[3 + k])
        for k, (src, name) in enumerate(((we, "we"), (ws, "ws"), (wr, "wr"), (wkv, "wkv")))
    ]

    def slab(name, t, low=0, count=None):
        ref, plan = next(v for v in plans if name in v[1])
        at, rows, _ = plan[name]
        count = rows if count is None else count
        return ref[at + t * rows + low : at + t * rows + low + count, :].astype(F32)

    def move(count):
        for copy, on in list(zip(ins, moves))[count : count + len(ins) // 2]:
            copy.wait()
            on.start()

    loads[0].wait()
    for t in range(ff // LANE):
        cut = slice(t * LANE, (t + 1) * LANE)
        we[:, cut] = slab("we", t, 0, channels)
        outs["eb"][cut] = slab("we", t, channels, 16)[0]
        ws[:, cut] = slab("ws", t)
        at, rows, _ = splan["tap"]
        outs["dt"][:, cut] = small[at + t * rows : at + t * rows + 9, :]
        outs["db"][cut] = small[at + t * rows + 9, :]
    stores[0].start()
    stores[1].start()
    move(0)
    loads[1].wait()
    loads[2].wait()
    for t in range(4 * channels // LANE):
        wr[:, t * LANE : (t + 1) * LANE] = slab("wr", t)
    stores[2].start()
    for t in range(2 * channels // LANE):
        wkv[:, t * LANE : (t + 1) * LANE] = slab("wkv", t, 0, channels)
    stores[3].start()
    tall = [slab("wkv", t, channels, 16) for t in range(2 * channels // LANE)]
    outs["vb"][...] = jnp.concatenate(tall, -1)[1, channels:]
    halves = slab("halves", 0)
    wp = [slab("wp", t) for t in range(full)] + [halves]
    outs["wp"][...] = jnp.concatenate(wp, -1)[:, :channels]
    wq = [slab("wq", t) for t in range(full)] + [pltpu.roll(halves, HALF, 1)]
    outs["wq"][...] = jnp.concatenate(wq, -1).T[:channels]
    at, rows, _ = splan["vec"]
    vec = jnp.concatenate([small[at + t * rows : at + (t + 1) * rows, :] for t in range(lt)], -1)
    vec = vec[:, :channels]
    order = ("g2", "b2", "sb", "rg", "rbn", "rb", "g1", "b1", "pb", "qb")
    for k, name in enumerate(order):
        outs[name][...] = vec[k]
    at, rows, _ = splan["count"]
    outs["cm"][...] = small[at : at + rows, :].astype(jnp.int32)[:CLASSES, :CLASSES]
    move(len(ins) // 2)
    for copy in moves + stores:
        copy.wait()


def unpack(channels, ff, ndev, out, ig, first, middle, packed, small):
    one = (channels,)
    shapes = [
        one, one, (channels, channels), one, (channels, 4 * channels), one, one, one,
        (channels, 2 * channels), one, (channels, channels), one, one, one, (channels, ff), (ff,),
        (9, ff), (ff,), (channels, ff), one,
    ]
    outs = [jax.ShapeDtypeStruct(v, F32) for v in shapes]
    outs.append(jax.ShapeDtypeStruct((CLASSES, CLASSES), jnp.int32))
    vm = pl.BlockSpec(memory_space=pltpu.VMEM)
    hbm = pl.BlockSpec(memory_space=pl.ANY)
    big = {4, 8, 14, 18}
    return pl.pallas_call(
        functools.partial(unpack_kernel, channels, ff, ndev),
        in_specs=[hbm] * 5 + [vm],
        out_specs=[hbm, hbm] + [hbm if k in big else vm for k in range(len(outs))],
        out_shape=[jax.ShapeDtypeStruct(v.shape, v.dtype) for v in (out, ig)] + outs,
        scratch_shapes=[
            pltpu.VMEM(out.shape, out.dtype),
            pltpu.VMEM(ig.shape, ig.dtype),
            pltpu.VMEM(first.shape, first.dtype),
            pltpu.VMEM(middle.shape, middle.dtype),
            pltpu.VMEM(packed.shape, packed.dtype),
            pltpu.VMEM((channels, ff), F32),
            pltpu.VMEM((channels, ff), F32),
            pltpu.VMEM((channels, 4 * channels), F32),
            pltpu.VMEM((channels, 2 * channels), F32),
            pltpu.SemaphoreType.DMA((2, out.shape[0])),
            pltpu.SemaphoreType.DMA((2, out.shape[0])),
            pltpu.SemaphoreType.DMA((7,)),
        ],
        compiler_params=pltpu.CompilerParams(vmem_limit_bytes=VMEM),
    )(out, ig, first, middle, packed, small)


def split_low(value):
    hi = value.astype(BF16).astype(F32)
    return hi, value - hi


def rows16(*rows):
    width = rows[0].shape[-1]
    at = lax.broadcasted_iota(jnp.int32, (16, width), 0)
    block = jnp.zeros((16, width), F32)
    for k, row in enumerate(rows):
        block = jnp.where(at == k, row, block)
    return block.astype(BF16)


def prep_kernel(
    channels, g1, b1, qw, qb, rw, rb, rg, rbn, kvw, vb, pw, pb, g2, b2, eb, tb, sb,
    vec, wq, wp, wkv, wr, ebias, dbias, full,
):
    cp = up_to(channels, LANE)
    head_size = channels // HEADS
    rest = cp - channels - 16

    def row(ref):
        return ref[...].reshape(1, ref.shape[-1])

    lane = lanes((1, cp))

    def padded(ref, *at):
        v = widen(row(ref), cp)
        for k in at:
            v = jnp.where(lane == channels + k, 1.0, v)
        return v

    for k, v in enumerate(
        (
            padded(g1), padded(b1, 0, 1), padded(rg), padded(rbn, 1, 2), padded(pb), padded(g2),
            padded(b2, 0, 1), padded(sb),
        )
    ):
        vec[k : k + 1, :] = v

    def fill(ref, top, *rows):
        width = ref.shape[-1]
        ref[:channels, :] = top
        ref[channels : channels + 16, :] = (
            rows16(*rows) if rows else jnp.zeros((16, width), BF16)
        )
        if rest:
            ref[channels + 16 :, :] = jnp.zeros((rest, width), BF16)

    dbias[...] = row(tb)
    ebias[...] = rows16(*split_low(row(eb)))
    q = widen(qw[...], cp)
    qb_wide = widen(row(qb), cp)
    fill(wq, q, *split_low(qb_wide))
    kw = widen(kvw[:, :channels], cp)
    vw = widen(kvw[:, channels:], cp)
    nil = jnp.zeros((1, 2 * cp), F32)
    vb_rows = [
        jnp.concatenate([jnp.zeros((1, cp), F32), widen(v, cp)], -1) for v in split_low(row(vb))
    ]
    fill(wkv, jnp.concatenate([kw, vw], -1), nil, *vb_rows)
    fill(wp, widen(pw[...], cp))
    rb_rows = [widen(v, cp) for v in split_low(row(rb))]
    rw_rows = rw[...].T
    for ab in range(4):
        fill(
            wr.at[ab], widen(rw_rows[ab * channels : (ab + 1) * channels, :], cp),
            *rb_rows[ab : ab + 1],
        )

    def norm(v):
        return jnp.sqrt(jnp.sum(v * v, (0, 1), keepdims=True))

    root = channels**0.5

    def reach(gain, bias):
        top = jnp.max(jnp.abs(row(gain)), (0, 1), keepdims=True)
        return root * top + norm(row(bias))

    def head(value, h):
        tile = value[:, h // 2 * LANE : (h // 2 + 1) * LANE].astype(F32)
        return jnp.where(lanes((1, LANE)) // HALF == h % 2, tile, 0.0)

    query_in, key_in = reach(g1, b1), reach(rg, rbn)
    bound = jnp.zeros((1, 1), F32)
    for h in range(HEADS):
        query = query_in * norm(head(q, h)) + norm(head(qb_wide, h))
        bound = jnp.maximum(bound, query * key_in * norm(head(kw, h)))
    bound = bound * (head_size**-0.5 * 1.05)
    full[...] = jnp.where(2.0 * bound + 256.0 < -NEGATIVE, 0, 1).astype(jnp.int32)


def prep(channels, ff, *weights):
    cp = up_to(channels, LANE)
    shapes = [
        ((8, cp), F32), ((cp, cp), BF16), ((cp, cp), BF16), ((cp, 2 * cp), BF16),
        ((4, cp, cp), BF16), ((16, ff), BF16), ((1, ff), F32), ((1, 1), jnp.int32),
    ]
    return pl.pallas_call(
        functools.partial(prep_kernel, channels),
        out_shape=[jax.ShapeDtypeStruct(*v) for v in shapes],
        compiler_params=pltpu.CompilerParams(vmem_limit_bytes=VMEM),
    )(*weights)


def body(
    tokens, mask, labels, predicted, cotangent, norm1_gain, norm1_bias, query_weight, query_bias,
    reduce_weight, reduce_bias, rnorm_gain, rnorm_bias, kv_weight, value_bias, proj_weight,
    proj_bias, norm2_gain, norm2_bias, expand_weight, expand_bias, depth_weight, depth_bias,
    shrink_weight, shrink_bias,
):
    scenes, height, width, channels = tokens.shape
    ndp, blk = lax.axis_size("dp"), lax.axis_size("blk")
    n = height * width
    ff = expand_weight.shape[1]
    dims = (scenes, height, width, channels, up_to(channels, LANE))
    chips = blk // 2
    used = min(chips, -(-MASK_ROWS // (2 * height)))

    vec, wq, wp, wkv, wr, expand_rows, tap_bias, full = prep(
        channels, ff, norm1_gain, norm1_bias, query_weight, query_bias, reduce_weight.T, reduce_bias,
        rnorm_gain, rnorm_bias, kv_weight, value_bias, proj_weight, proj_bias, norm2_gain,
        norm2_bias, expand_bias, depth_bias, shrink_bias,
    )
    full = full[0, 0] > 0

    def either(call, cids, sizes, *operands):
        if used == chips:
            return call(*sizes, chips, cids[1], *operands)
        return lax.cond(
            full,
            functools.partial(call, *sizes, chips, cids[1]),
            functools.partial(call, *sizes, used, cids[0]),
            *operands,
        )

    tok = tokens.reshape(scenes, n, channels)
    ct = cotangent.reshape(scenes, n, channels)
    red, counts, q, att, ke, ve, rn, res = either(
        attend, (2, 3), (dims, blk), tok, mask, labels, predicted, vec, wr, wq, wkv, wp
    )
    out, gres, first, dtap, dtb, dvec2 = ffn(
        dims, blk, ndp * blk, res, ct, expand_weight, shrink_weight.T, vec, expand_rows, depth_weight,
        tap_bias,
    )
    ig, first, middle, packed, small = either(
        attback, (4, 5), (dims, ff, ndp, blk), q, att, gres, ke, ve, rn, tok, red, vec, wp, wkv,
        query_weight, wr, dtap, dtb, dvec2, counts, first,
    )
    out, ig, *grads = unpack(channels, ff, ndp * blk, out, ig, first, middle, packed, small)
    grads[4], grads[18] = grads[4].T, grads[18].T
    return (out.reshape(tokens.shape), ig.reshape(tokens.shape), *grads)


def solution(mesh):
    banded = P("dp", "blk", None, None)
    plane = P("dp", "blk", None)
    in_specs = (banded, plane, plane, plane, banded) + (P(),) * 20
    out_specs = (banded, banded) + (P(),) * 21
    return jax.shard_map(body, mesh=mesh, in_specs=in_specs, out_specs=out_specs, check_vma=False)
```
